32 devices in a mesh: blk: 8 (over y, x, core), head: 4 (over z).
Axes of the slice: x: 2, y: 2, z: 4, core: 2. Of those that a mesh axis runs over, the one named last changes fastest.
Arguments:
- tokens: bfloat16 [2, 2048, 1024], P(None, ('blk', 'head')), may hold values from -6 to 6
- w_query: bfloat16 [1024, 1024], P('blk', 'head'), may hold values from -0.1875 to 0.1875
- w_key: bfloat16 [1024, 1024], P('blk', 'head'), may hold values from -0.1875 to 0.1875
- w_value: bfloat16 [1024, 1024], P('blk', 'head'), may hold values from -0.1875 to 0.1875
- w_out: bfloat16 [1024, 1024], P('head', 'blk'), may hold values from -6 to 6
- b_query: bfloat16 [1024], P(('blk', 'head')), may hold values from -3 to 3
- b_value: bfloat16 [1024], P(('blk', 'head')), may hold values from -3 to 3
- b_out: bfloat16 [1024], P(('blk', 'head')), may hold values from -2 to 2
- norm1_gain: bfloat16 [1024], P(('blk', 'head')), may hold values from 0.5 to 1.5
- norm1_shift: bfloat16 [1024], P(('blk', 'head')), may hold values from -2 to 2
- w_in: bfloat16 [1024, 4096], P('blk', 'head'), may hold values from -0.1875 to 0.1875
- w_back: bfloat16 [1024, 4096], P('blk', 'head'), may hold values from -0.09375 to 0.09375
- b_in: bfloat16 [4096], P(('blk', 'head')), may hold values from -3 to 3
- b_back: bfloat16 [1024], P(('blk', 'head')), may hold values from -2 to 2
- norm2_gain: bfloat16 [1024], P(('blk', 'head')), may hold values from 0.5 to 1.5
- norm2_shift: bfloat16 [1024], P(('blk', 'head')), may hold values from -2 to 2
- cotangent: bfloat16 [2, 2048, 1024], P(None, ('blk', 'head')), may hold values from -6 to 6
Outputs:
- output: bfloat16 [2, 2048, 1024], P(None, ('blk', 'head'))
- grad_tokens: bfloat16 [2, 2048, 1024], P(None, ('blk', 'head'))
- grad_w_query: float32 [1024, 1024], P('blk', 'head')
- grad_w_key: float32 [1024, 1024], P('blk', 'head')
- grad_w_value: float32 [1024, 1024], P('blk', 'head')
- grad_w_out: float32 [1024, 1024], P('head', 'blk')
- grad_b_query: float32 [1024], P(('blk', 'head'))
- grad_b_value: float32 [1024], P(('blk', 'head'))
- grad_b_out: float32 [1024], P(('blk', 'head'))
- grad_norm1_gain: float32 [1024], P(('blk', 'head'))
- grad_norm1_shift: float32 [1024], P(('blk', 'head'))
- grad_w_in: float32 [1024, 4096], P('blk', 'head')
- grad_w_back: float32 [1024, 4096], P('blk', 'head')
- grad_b_in: float32 [4096], P(('blk', 'head'))
- grad_b_back: float32 [1024], P(('blk', 'head'))
- grad_norm2_gain: float32 [1024], P(('blk', 'head'))
- grad_norm2_shift: float32 [1024], P(('blk', 'head'))
The draws below stay inside these ranges and needn't reach their ends.
All inputs are finite; a program needn't handle non-finite values.
Results may differ from the reference program's by a relative error of at most 0.02.
Values may be sent and summed in bfloat16 or wider, within the bound.
A program may use at most 704 MiB of HBM per device.

```python
import jax
import jax.numpy as jnp
from jax import lax

D = 1024
HEADS = 16
FF = 4096
HEAD_DIM = 64
SEQS = 2
LENGTH = 2048


def strengthened(drawn, own_key, source, target, parts, factor):
    owner, partner = [(jnp.arange(drawn.shape[axis_at]) // (drawn.shape[axis_at] // parts)).reshape([-1 if axis == axis_at else 1 for axis in range(drawn.ndim)]) for axis_at in (source, target)]
    chosen = jax.random.permutation(own_key, parts)[partner]
    strong = (owner == chosen) | (owner == (partner + parts // 2) % parts)
    return jnp.where(strong, factor * drawn, drawn)


def level_of(rng, extent, pieces, least, largest):
    factor_of = 1.0
    for position, shards_of in pieces:
        heights = jax.random.uniform(jax.random.fold_in(jax.random.fold_in(rng, 6), position), (shards_of,), jnp.float32, least / len(pieces), largest / len(pieces))
        factor_of = factor_of * jnp.repeat(jnp.exp(heights), extent[position] // shards_of).reshape((-1,) + (1,) * (len(extent) - 1 - position))
    return factor_of


def noise(stream_key, extent, scale, limit, cuts=(), kind=jnp.bfloat16):
    level = level_of(stream_key, extent, cuts, -0.22, 0.18) if cuts else 1.0
    array = jax.random.normal(stream_key, extent, jnp.float32) * scale * level
    return jnp.minimum(jnp.maximum(array, -limit), limit).astype(kind)


def gaussian_with(rng, dims, scale, most, shards, heavy, kind=jnp.bfloat16):
    drawn = scale * jax.random.normal(rng, dims, jnp.float32)
    if shards:
        drawn = drawn * level_of(rng, dims, shards, -0.22, 0.18)
    return jnp.clip(strengthened(drawn, jax.random.fold_in(rng, 3), *heavy), -most, most).astype(kind)


def setup_inputs(seed: int = 0) -> dict:
    arg_keys = jax.random.split(jax.random.key(seed), 18)
    tokens = noise(arg_keys[0], (SEQS, LENGTH, D), 1.0, 6.0, ((1, 32),))
    w_query = noise(arg_keys[1], (D, D), D ** -0.5, 0.1875, ((0, 8), (1, 4)))
    w_key = noise(arg_keys[2], (D, D), D ** -0.5, 0.1875, ((0, 8), (1, 4)))
    w_value = noise(arg_keys[3], (D, D), D ** -0.5, 0.1875, ((0, 8), (1, 4)))
    w_out = noise(arg_keys[4], (D, D), (max(3 * D // LENGTH, 1)) ** -0.5, 6.0, ((0, 4), (1, 8)))
    b_query = noise(arg_keys[5], (D,), 0.5, 3.0, ((0, 32),))
    b_value = noise(arg_keys[6], (D,), 0.5, 3.0, ((0, 32),))
    b_out = noise(arg_keys[7], (D,), 0.3, 2.0, ((0, 32),))
    norm1_gain = jnp.clip(1.0 + 0.1 * jax.random.normal(arg_keys[8], (D,), jnp.float32), 0.5, 1.5).astype(jnp.bfloat16)
    norm1_shift = noise(arg_keys[9], (D,), 0.3, 2.0, ((0, 32),))
    w_in = noise(arg_keys[10], (D, FF), D ** -0.5, 0.1875, ((0, 8), (1, 4)))
    w_back = noise(arg_keys[11], (D, FF), FF ** -0.5, 0.09375, ((0, 8), (1, 4)))
    b_in = noise(arg_keys[12], (FF,), 0.5, 3.0, ((0, 32),))
    b_back = noise(arg_keys[13], (D,), 0.3, 2.0, ((0, 32),))
    norm2_gain = jnp.clip(1.0 + 0.1 * jax.random.normal(arg_keys[14], (D,), jnp.float32), 0.5, 1.5).astype(jnp.bfloat16)
    norm2_shift = noise(arg_keys[15], (D,), 0.3, 2.0, ((0, 32),))
    cotangent = gaussian_with(arg_keys[16], (SEQS, LENGTH, D), 1.0, 6.0, ((1, 32),), (1, 2, 32, 2.75))
    return {"tokens": tokens, "w_query": w_query, "w_key": w_key, "w_value": w_value, "w_out": w_out, "b_query": b_query, "b_value": b_value, "b_out": b_out, "norm1_gain": norm1_gain, "norm1_shift": norm1_shift, "w_in": w_in, "w_back": w_back, "b_in": b_in, "b_back": b_back, "norm2_gain": norm2_gain, "norm2_shift": norm2_shift, "cotangent": cotangent}


@jax.custom_vjp
def low(v):
    return lax.optimization_barrier(v.astype(jnp.bfloat16)).astype(jnp.float32)

@jax.custom_vjp
def low_back(v):
    return v

def low_keep(v):
    return (low(v), None)

def low_pass(kept, grad):
    return (grad,)

def back_keep(v):
    return (v, None)

def back_low(kept, grad):
    return (low(grad),)
low.defvjp(low_keep, low_pass)
low_back.defvjp(back_keep, back_low)
NORM_EPS = 1e-05
HIGH = lax.Precision.HIGHEST

def layer_norm(summed, gain, shift):
    centre = lax.optimization_barrier(jnp.mean(summed, axis=-1, keepdims=True))
    centred = summed - centre
    spread = lax.optimization_barrier(jnp.mean(centred * centred, axis=-1, keepdims=True))
    return centred * lax.rsqrt(spread + NORM_EPS) * gain + shift

def project(left, right):
    return jnp.dot(left, right, precision=HIGH, preferred_element_type=jnp.float32)

def attend_block(block_queries, keys_all, values_all):
    raw = jnp.einsum('sqhe,skhe->shqk', block_queries, keys_all, precision=HIGH)
    scores = low_back(raw) * HEAD_DIM ** (-0.5)
    maxima = lax.optimization_barrier(jnp.max(scores, axis=-1, keepdims=True))
    weights = jnp.exp(scores - maxima)
    weights = low(weights / lax.optimization_barrier(jnp.sum(weights, axis=-1, keepdims=True)))
    return jnp.einsum('shqk,skhe->sqhe', weights, values_all, precision=HIGH)

def forward(tokens, w_query, w_key, w_value, w_out, b_query, b_value, b_out, norm1_gain, norm1_shift, w_in, w_back, b_in, b_back, norm2_gain, norm2_shift):
    flat_rows = tokens.reshape(SEQS * LENGTH, D)
    queries = low_back(low(project(flat_rows, w_query) + b_query))
    keys_all = low_back(low(project(flat_rows, w_key)))
    values_all = low_back(low(project(flat_rows, w_value) + b_value))
    head_shape = (SEQS, LENGTH, HEADS, HEAD_DIM)
    queries = queries.reshape(head_shape)
    keys_all = keys_all.reshape(head_shape)
    values_all = values_all.reshape(head_shape)
    block_rows = min(LENGTH, 128)
    blocked = queries.reshape(SEQS, LENGTH // block_rows, block_rows, HEADS, HEAD_DIM).transpose(1, 0, 2, 3, 4)

    def one_block(block_queries):
        return attend_block(block_queries, keys_all, values_all)
    mixed = lax.map(jax.checkpoint(one_block), blocked)
    attended = mixed.transpose(1, 0, 2, 3, 4).reshape(SEQS * LENGTH, D)
    attended = low_back(low(attended))
    branch = low_back(project(attended, w_out) + b_out)
    normed = layer_norm(flat_rows + branch, norm1_gain, norm1_shift)
    pre_act = low_back(project(low(normed), w_in) + b_in)
    hidden = low(jax.nn.gelu(pre_act, approximate=False))
    ffn_out = low_back(project(hidden, w_back.T) + b_back)
    final = layer_norm(normed + ffn_out, norm2_gain, norm2_shift)
    return final.reshape(SEQS, LENGTH, D)

def reference(tokens, w_query, w_key, w_value, w_out, b_query, b_value, b_out, norm1_gain, norm1_shift, w_in, w_back, b_in, b_back, norm2_gain, norm2_shift, cotangent):
    inputs = [arg.astype(jnp.float32) for arg in (tokens, w_query, w_key, w_value, w_out, b_query, b_value, b_out, norm1_gain, norm1_shift, w_in, w_back, b_in, b_back, norm2_gain, norm2_shift)]
    final, pull = jax.vjp(forward, *inputs)
    grads = pull(cotangent.astype(jnp.float32))
    return (final.astype(jnp.bfloat16), grads[0].astype(jnp.bfloat16), grads[1], grads[2], grads[3], grads[4], grads[5], grads[6], grads[7], grads[8], grads[9], grads[10], grads[11], grads[12], grads[13], grads[14], grads[15])
```

```python
import functools
import math

import jax
import jax.numpy as jnp
from jax import lax
from jax.experimental import pallas as pl
from jax.experimental.pallas import tpu as pltpu
from jax.sharding import PartitionSpec as P

HEAD_DIM = 64


NORM_EPS = 1e-05


def layer_norm(summed, gain, shift):
    centre = jnp.mean(summed, axis=-1, keepdims=True)
    centred = summed - centre
    spread = jnp.mean(centred * centred, axis=-1, keepdims=True)
    return centred * lax.rsqrt(spread + NORM_EPS) * gain + shift


def gelu_exact(inputs):
    return jax.nn.gelu(inputs, approximate=False)


def split_heads(packed):
    return packed.reshape(packed.shape[0], packed.shape[1], -1, HEAD_DIM)


def contract_rows(left, right):
    return lax.dot_general(
        left, right, (((0,), (0,)), ((), ())), preferred_element_type=jnp.float32
    )


def contract_cols(left, right):
    return lax.dot_general(
        left, right, (((1,), (1,)), ((), ())), preferred_element_type=jnp.float32
    )


def score_block(queries4, keys4):
    return jnp.einsum(
        "sqge,skge->sqgk", queries4, keys4, preferred_element_type=jnp.float32
    ) * HEAD_DIM ** (-0.5)


def score_grads(queries4, keys4, values4, grads4, log_sums, deltas):
    probs = jnp.exp(score_block(queries4, keys4) - log_sums[..., None])
    d_probs = jnp.einsum("sqge,skge->sqgk", grads4, values4, preferred_element_type=jnp.float32)
    d_scores = (probs * (d_probs - deltas[..., None])).astype(jnp.bfloat16)
    return (probs.astype(jnp.bfloat16), d_scores)


def token_rows(local):
    return lax.all_gather(local, "head", axis=1, tiled=True)


def token_partials(terms):
    return lax.psum_scatter(
        terms.astype(jnp.bfloat16), "head", scatter_dimension=1, tiled=True
    ).astype(jnp.float32)


def place_part(part, full_len, start):
    return lax.dynamic_update_slice_in_dim(jnp.zeros((full_len,), jnp.float32), part, start, 0)


def per_device(
    tokens,
    w_query,
    w_key,
    w_value,
    w_out,
    b_query,
    b_value,
    b_out,
    norm1_gain,
    norm1_shift,
    w_in,
    w_back,
    b_in,
    b_back,
    norm2_gain,
    norm2_shift,
    cotangent,
):
    f32 = jnp.float32
    bf16 = jnp.bfloat16
    score_scale = HEAD_DIM ** (-0.5)
    bq_full, bv_full, bo_full, gain_one, shift_one, bin_full, bback_full, gain_two, shift_two = (
        lax.all_gather(b_query, ("blk", "head"), axis=0, tiled=True),
        lax.all_gather(b_value, ("blk", "head"), axis=0, tiled=True),
        lax.all_gather(b_out, ("blk", "head"), axis=0, tiled=True),
        lax.all_gather(norm1_gain, ("blk", "head"), axis=0, tiled=True),
        lax.all_gather(norm1_shift, ("blk", "head"), axis=0, tiled=True),
        lax.all_gather(b_in, ("blk", "head"), axis=0, tiled=True),
        lax.all_gather(b_back, ("blk", "head"), axis=0, tiled=True),
        lax.all_gather(norm2_gain, ("blk", "head"), axis=0, tiled=True),
        lax.all_gather(norm2_shift, ("blk", "head"), axis=0, tiled=True),
    )
    attn_cols, out_rows, ffn_cols = (
        lax.all_gather(jnp.stack((w_query, w_key, w_value)), "blk", axis=1, tiled=True),
        lax.all_gather(w_out, "blk", axis=1, tiled=True),
        lax.all_gather(jnp.stack((w_in, w_back)), "blk", axis=1, tiled=True),
    )
    seq_count, local_len, model_dim = tokens.shape
    token_shape = (seq_count, local_len, model_dim)
    head_id = lax.axis_index("head")
    width_part = attn_cols.shape[2]
    bq_part = lax.dynamic_slice_in_dim(bq_full, head_id * width_part, width_part).astype(f32)
    bv_part = lax.dynamic_slice_in_dim(bv_full, head_id * width_part, width_part).astype(f32)
    wide_rows = token_rows(tokens)
    wide_len = wide_rows.shape[1]
    wide_flat = wide_rows.reshape(-1, model_dim)
    head_shape = (seq_count, wide_len, width_part)
    wide_shape = (seq_count, wide_len, model_dim)
    query_heads = (
        (jnp.dot(wide_flat, attn_cols[0], preferred_element_type=f32) + bq_part)
        .astype(bf16)
        .reshape(head_shape)
    )
    key_heads = (
        jnp.dot(wide_flat, attn_cols[1], preferred_element_type=f32)
        .astype(bf16)
        .reshape(head_shape)
    )
    value_heads = (
        (jnp.dot(wide_flat, attn_cols[2], preferred_element_type=f32) + bv_part)
        .astype(bf16)
        .reshape(head_shape)
    )
    query4 = split_heads(query_heads)
    key4 = split_heads(key_heads)
    value4 = split_heads(value_heads)
    stat_shape = query4.shape[:3]
    pieces = (
        lax.all_gather(key_heads, "blk", axis=1, tiled=True),
        lax.all_gather(value_heads, "blk", axis=1, tiled=True),
    )
    maxima = jnp.full(stat_shape, -1e30, f32)
    scores = score_block(query4, split_heads(pieces[0]))
    new_max = jnp.maximum(maxima, jnp.max(scores, axis=-1))
    weights = jnp.exp(scores - new_max[..., None])
    totals = jnp.sum(weights, axis=-1)
    summed = jnp.einsum(
        "sqgk,skge->sqge", weights.astype(bf16), split_heads(pieces[1]), preferred_element_type=f32
    )
    maxima, totals, summed = (new_max, totals, summed)
    log_sums = maxima + jnp.log(totals)
    attended4 = summed / totals[..., None]
    attended_heads = attended4.reshape(head_shape).astype(bf16)
    attended_flat = attended_heads.reshape(-1, width_part)
    branch_terms = jnp.dot(attended_flat, out_rows, preferred_element_type=f32).reshape(wide_shape)
    branch = token_partials(branch_terms).reshape(-1, model_dim) + bo_full.astype(f32)
    flat_rows = tokens.reshape(-1, model_dim)
    normed, norm1_pull = jax.vjp(
        layer_norm, flat_rows.astype(f32) + branch, gain_one.astype(f32), shift_one.astype(f32)
    )
    normed_low = normed.astype(bf16)
    ffn_full = lax.all_gather(ffn_cols, "head", axis=2, tiled=True)
    pre_act = jnp.dot(normed_low, ffn_full[0], preferred_element_type=f32) + bin_full.astype(f32)
    hidden_act, gelu_pull = jax.vjp(gelu_exact, pre_act)
    hidden_low = hidden_act.astype(bf16)
    ffn_out = contract_cols(hidden_low, ffn_full[1]) + bback_full.astype(f32)
    final, norm2_pull = jax.vjp(
        layer_norm, normed + ffn_out, gain_two.astype(f32), shift_two.astype(f32)
    )
    output = final.astype(bf16).reshape(token_shape)
    d_second, grad_norm2_gain, grad_norm2_shift = norm2_pull(
        cotangent.reshape(-1, model_dim).astype(f32)
    )
    d_ffn = d_second.astype(bf16)
    grad_b_back = jnp.sum(d_ffn.astype(f32), axis=0)
    grad_back_whole = contract_rows(d_ffn, hidden_low)
    d_hidden = jnp.dot(d_ffn, ffn_full[1], preferred_element_type=f32)
    d_pre = gelu_pull(d_hidden)[0].astype(bf16)
    grad_b_in = jnp.sum(d_pre.astype(f32), axis=0)
    grad_in_whole = contract_rows(normed_low, d_pre)
    ffn_grad_parts = lax.psum_scatter(
        jnp.stack((grad_in_whole, grad_back_whole)).astype(jnp.bfloat16),
        "head",
        scatter_dimension=2,
        tiled=True,
    ).astype(jnp.float32)
    d_normed = d_second + contract_cols(d_pre, ffn_full[0])
    d_first, grad_norm1_gain, grad_norm1_shift = norm1_pull(d_normed)
    d_branch = d_first.astype(bf16)
    grad_b_out = jnp.sum(d_branch.astype(f32), axis=0)
    wide_dbranch = token_rows(d_branch.reshape(token_shape)).reshape(-1, model_dim)
    grad_out_part = contract_rows(attended_flat, wide_dbranch)
    grad_heads = contract_cols(wide_dbranch, out_rows).astype(bf16).reshape(head_shape)
    grads4 = split_heads(grad_heads)
    deltas = jnp.sum(grads4.astype(f32) * attended4, axis=-1)
    row_stats = (
        lax.all_gather(log_sums, "blk", axis=1, tiled=True),
        lax.all_gather(deltas, "blk", axis=1, tiled=True),
    )
    pieces = (
        lax.all_gather(key_heads, "blk", axis=1, tiled=True),
        lax.all_gather(value_heads, "blk", axis=1, tiled=True),
        lax.all_gather(query_heads, "blk", axis=1, tiled=True),
        lax.all_gather(grad_heads, "blk", axis=1, tiled=True),
    )
    piece_keys = split_heads(pieces[0])
    piece_values = split_heads(pieces[1])
    piece_queries = split_heads(pieces[2])
    piece_grads = split_heads(pieces[3])
    piece_sums = row_stats[0]
    piece_deltas = row_stats[1]
    own_probs, own_scores = score_grads(query4, piece_keys, piece_values, grads4, log_sums, deltas)
    d_query = score_scale * jnp.einsum(
        "sqgk,skge->sqge", own_scores, piece_keys, preferred_element_type=f32
    )
    probs_low, d_scores = score_grads(
        piece_queries, key4, value4, piece_grads, piece_sums, piece_deltas
    )
    key_acc = score_scale * jnp.einsum(
        "sqgk,sqge->skge", d_scores, piece_queries, preferred_element_type=f32
    )
    value_acc = jnp.einsum("sqgk,sqge->skge", probs_low, piece_grads, preferred_element_type=f32)
    d_query_low = d_query.reshape(-1, width_part).astype(bf16)
    d_key_low = key_acc.reshape(-1, width_part).astype(bf16)
    d_value_low = value_acc.reshape(-1, width_part).astype(bf16)
    grad_b_query = place_part(
        jnp.sum(d_query_low.astype(f32), axis=0), model_dim, head_id * width_part
    )
    grad_b_value = place_part(
        jnp.sum(d_value_low.astype(f32), axis=0), model_dim, head_id * width_part
    )
    attn_grad_parts = jnp.stack(
        (
            contract_rows(wide_flat, d_query_low),
            contract_rows(wide_flat, d_key_low),
            contract_rows(wide_flat, d_value_low),
        )
    )
    token_terms = (
        contract_cols(d_query_low, attn_cols[0])
        + contract_cols(d_key_low, attn_cols[1])
        + contract_cols(d_value_low, attn_cols[2])
    )
    d_tokens = d_first + token_partials(token_terms.reshape(wide_shape)).reshape(-1, model_dim)
    grad_tokens = d_tokens.astype(bf16).reshape(token_shape)
    attn_sums, grad_w_out, ffn_sums = (
        lax.psum_scatter(attn_grad_parts, "blk", scatter_dimension=1, tiled=True),
        lax.psum_scatter(grad_out_part, "blk", scatter_dimension=1, tiled=True),
        lax.psum_scatter(ffn_grad_parts, "blk", scatter_dimension=1, tiled=True),
    )
    (
        grad_b_query,
        grad_b_value,
        grad_b_out,
        grad_norm1_gain,
        grad_norm1_shift,
        grad_b_in,
        grad_b_back,
        grad_norm2_gain,
        grad_norm2_shift,
    ) = (
        lax.psum_scatter(grad_b_query, ("blk", "head"), scatter_dimension=0, tiled=True),
        lax.psum_scatter(grad_b_value, ("blk", "head"), scatter_dimension=0, tiled=True),
        lax.psum_scatter(grad_b_out, ("blk", "head"), scatter_dimension=0, tiled=True),
        lax.psum_scatter(grad_norm1_gain, ("blk", "head"), scatter_dimension=0, tiled=True),
        lax.psum_scatter(grad_norm1_shift, ("blk", "head"), scatter_dimension=0, tiled=True),
        lax.psum_scatter(grad_b_in, ("blk", "head"), scatter_dimension=0, tiled=True),
        lax.psum_scatter(grad_b_back, ("blk", "head"), scatter_dimension=0, tiled=True),
        lax.psum_scatter(grad_norm2_gain, ("blk", "head"), scatter_dimension=0, tiled=True),
        lax.psum_scatter(grad_norm2_shift, ("blk", "head"), scatter_dimension=0, tiled=True),
    )
    return (
        output,
        grad_tokens,
        attn_sums[0],
        attn_sums[1],
        attn_sums[2],
        grad_w_out,
        grad_b_query,
        grad_b_value,
        grad_b_out,
        grad_norm1_gain,
        grad_norm1_shift,
        ffn_sums[0],
        ffn_sums[1],
        grad_b_in,
        grad_b_back,
        grad_norm2_gain,
        grad_norm2_shift,
    )


MESH = pl.DeviceIdType.MESH
F32 = jnp.float32
BF16 = jnp.bfloat16
VMEM_LIMIT = 60 * 2**20


def dot_nn(left, right):
    return jnp.dot(left, right, preferred_element_type=F32)


class Place:
    def __init__(self):
        self.b = lax.axis_index("blk")
        self.z = lax.axis_index("head")
        self.y = self.b // 4
        self.x = (self.b // 2) % 2
        self.c = self.b % 2
        self.q = self.b // 2

    def chip(self, r):
        return ((self.y + r // 2) % 2) * 2 + (self.x + r % 2) % 2

    def peer(self, r):
        return (2 * self.chip(r) + self.c, self.z)

    def sibling(self):
        return (2 * self.q + 1 - self.c, self.z)


def remote(src, dst, send_sem, recv_sem, device):
    return pltpu.make_async_remote_copy(
        src_ref=src,
        dst_ref=dst,
        send_sem=send_sem,
        recv_sem=recv_sem,
        device_id=device,
        device_id_type=MESH,
    )


def wait_bytes(view, sem):
    pltpu.make_async_copy(view, view, sem).wait()


def greet_all(at):
    barrier = pltpu.get_barrier_semaphore()
    flat = at.b * 4 + at.z

    def greet(step, carry):
        other = (flat + step) % 32
        pl.semaphore_signal(
            barrier, inc=1, device_id=(other // 4, other % 4), device_id_type=MESH
        )
        return carry

    lax.fori_loop(1, 32, greet, 0)
    pl.semaphore_wait(barrier, 31)


def half(core):
    return pl.ds(pl.multiple_of(core * 128, 128), 128)


def lanes(index):
    return pl.ds(pl.multiple_of(index * 128, 128), 128)


def by_rows(count, size, step):
    def body(i, carry):
        step(pl.ds(pl.multiple_of(i * size, size), size))
        return carry

    lax.fori_loop(0, count // size, body, 0)


def row_sums(count, size, width, step):
    def body(i, carry):
        parts = step(pl.ds(pl.multiple_of(i * size, size), size))
        return tuple(
            kept + jnp.sum(part.reshape(size // 8, 8, width), axis=0)
            for kept, part in zip(carry, parts)
        )

    n = step.count
    sums = lax.fori_loop(
        0, count // size, body, tuple(jnp.zeros((8, width), F32) for _ in range(n))
    )
    return tuple(jnp.sum(s, axis=0, keepdims=True) for s in sums)


class Exchange:
    def __init__(self, at, send, recv, send_sib, recv_sib):
        self.at, self.send, self.recv = at, send, recv
        self.send_sib, self.recv_sib = send_sib, recv_sib

    def gather_start(self, slots):
        at = self.at
        mine = slots.at[at.q, half(at.c)]
        for r in (1, 2, 3):
            remote(mine, mine, self.send.at[r], self.recv.at[r], at.peer(r)).start()
        remote(mine, mine, self.send_sib.at[0], self.recv_sib.at[0], at.sibling()).start()

    def gather_step(self, slots, r):
        at = self.at
        chip = at.chip(r)
        block = slots.at[chip, half(at.c)]
        if r:
            wait_bytes(block, self.recv.at[r])
            remote(
                block, block, self.send_sib.at[r], self.recv_sib.at[r], at.sibling()
            ).start()
        wait_bytes(slots.at[chip, half(1 - at.c)], self.recv_sib.at[r])
        return chip

    def gather_end(self, slots):
        at = self.at
        for r in range(4):
            block = slots.at[at.chip(r), half(at.c)]
            if r:
                wait_bytes(slots.at[at.q, half(at.c)], self.send.at[r])
            wait_bytes(block, self.send_sib.at[r])

    def scatter_put(self, terms, out_sib, in_sib, r):
        at = self.at
        out_sib[r] = terms[r, half(1 - at.c)].astype(BF16)
        remote(
            out_sib.at[r], in_sib.at[r], self.send_sib.at[r], self.recv_sib.at[r], at.sibling()
        ).start()

    def scatter_pass(self, terms, in_sib, out, into, r):
        at = self.at
        wait_bytes(in_sib.at[r], self.recv_sib.at[r])
        total = terms[r, half(at.c)] + in_sib[r].astype(F32)
        if r:
            out[r] = total.astype(BF16)
            remote(out.at[r], into.at[r], self.send.at[r], self.recv.at[r], at.peer(r)).start()
        else:
            terms[0, half(at.c)] = total

    def scatter_arrive(self, into):
        for r in (1, 2, 3):
            wait_bytes(into.at[r], self.recv.at[r])

    def scatter_end(self, out_sib, out):
        for r in range(4):
            wait_bytes(out_sib.at[r], self.send_sib.at[r])
            if r:
                wait_bytes(out.at[r], self.send.at[r])


def norm_rows(values):
    centre = jnp.mean(values, axis=-1, keepdims=True)
    centred = values - centre
    spread = jnp.mean(centred * centred, axis=-1, keepdims=True)
    scale = lax.rsqrt(spread + NORM_EPS)
    return centred * scale, scale


def norm_back(grad, unit, scale):
    centre = jnp.mean(grad, axis=-1, keepdims=True)
    along = jnp.mean(grad * unit, axis=-1, keepdims=True)
    return (grad - centre - unit * along) * scale


def ffn_kernel(
    x_ref,
    att_ref,
    wo_ref,
    cot_ref,
    par_ref,
    bin_ref,
    win_ref,
    wback_ref,
    out_ref,
    d1_ref,
    db_ref,
    gwin_ref,
    gwback_ref,
    pg_ref,
    gbin_ref,
    wi,
    wb,
    n1,
    unit1,
    scale1,
    d2,
    norm_slots,
    grad_slots,
    hid,
    slope,
    pre,
    terms,
    sib_out,
    sib_in,
    peer_out,
    peer_in,
    gsend,
    grecv_in,
    grecv_back,
    send,
    recv,
    send_sib,
    recv_sib,
    w_send,
    w_recv,
    g_send,
    g_recv,
):
    at = Place()
    flat = at.b * 4 + at.z
    greet_all(at)

    mine_rows = lanes(at.b)
    mine_cols = lanes(at.z)
    local = []
    for k, (src, dst) in enumerate(((win_ref, wi), (wback_ref, wb))):
        cp = pltpu.make_async_copy(
            src.at[:, lanes(at.b)], dst.at[mine_rows, mine_cols], w_recv.at[k]
        )
        cp.start()

        def push(step, carry, src=src, dst=dst, k=k):
            other = (flat + step) % 32
            remote(
                src.at[:, lanes(other // 4)],
                dst.at[mine_rows, mine_cols],
                w_send.at[k],
                w_recv.at[k],
                (other // 4, other % 4),
            ).start()
            return carry

        lax.fori_loop(1, 32, push, 0)

    def param(i):
        return par_ref[i : i + 1, :]

    n1[...] = dot_nn(att_ref[...], wo_ref[...])

    def first_norm(rows):
        unit, scale = norm_rows(x_ref[rows].astype(F32) + n1[rows] + param(2))
        unit1[rows] = unit
        scale1[rows] = jnp.broadcast_to(scale, (32, 128))
        n1[rows] = unit * param(3) + param(4)

    by_rows(128, 32, first_norm)
    norm_slots[at.q, half(at.c)] = n1[...].astype(BF16)
    gather = Exchange(at, send.at[0], recv.at[0], send_sib.at[0], recv_sib.at[0])
    gather.gather_start(norm_slots)

    wait_bytes(wi, w_recv.at[0])
    wait_bytes(wb, w_recv.at[1])

    scatter = Exchange(at, send.at[1], recv.at[1], send_sib.at[1], recv_sib.at[1])
    for r in range(4):
        chip = gather.gather_step(norm_slots, r)
        pre[...] = dot_nn(norm_slots[chip], wi[...])

        def activate(rows, r=r):
            u = pre[rows] + bin_ref[...]
            cdf = 0.5 * (1.0 + lax.erf(u * math.sqrt(0.5)))
            bell = jnp.exp(-0.5 * u * u) * (1.0 / math.sqrt(2.0 * math.pi))
            hid[r, rows] = (u * cdf).astype(BF16)
            slope[r, rows] = cdf + u * bell

        by_rows(256, 32, activate)
        terms[r] = contract_cols(hid[r], wb[...])
        scatter.scatter_put(terms, sib_out.at[0], sib_in.at[0], r)
        if r:
            scatter.scatter_pass(terms, sib_in.at[0], peer_out.at[0], peer_in.at[0], r - 1)
    scatter.scatter_pass(terms, sib_in.at[0], peer_out.at[0], peer_in.at[0], 3)
    scatter.scatter_arrive(peer_in.at[0])

    core_rows = pl.multiple_of(at.c * 128, 128)

    def second_norm(rows):
        own = pl.ds(pl.multiple_of(core_rows + rows.start, 32), 32)
        total = (
            terms[0, own]
            + peer_in[0, 1, rows].astype(F32)
            + peer_in[0, 2, rows].astype(F32)
            + peer_in[0, 3, rows].astype(F32)
        )
        unit, scale = norm_rows(n1[rows] + total + param(5))
        out_ref[rows] = (unit * param(6) + param(7)).astype(BF16)
        g = cot_ref[rows].astype(F32)
        d = norm_back(g * param(6), unit, scale)
        d2[rows] = d
        low = d.astype(BF16)
        grad_slots[at.q, own] = low
        return g * unit, g, low.astype(F32)

    second_norm.count = 3
    sums = row_sums(128, 32, 1024, second_norm)
    pg_ref[6:7, :] = sums[0]
    pg_ref[7:8, :] = sums[1]
    pg_ref[5:6, :] = sums[2]

    gather2 = Exchange(at, send.at[2], recv.at[2], send_sib.at[2], recv_sib.at[2])
    gather2.gather_start(grad_slots)
    scatter2 = Exchange(at, send.at[3], recv.at[3], send_sib.at[3], recv_sib.at[3])
    gbin = jnp.zeros((1, 512), F32)
    for r in range(4):
        chip = gather2.gather_step(grad_slots, r)
        pre[...] = dot_nn(grad_slots[chip], wb[...])

        def deactivate(rows, r=r):
            low = (pre[rows] * slope[r, rows]).astype(BF16)
            pre[rows] = low.astype(F32)
            return (low.astype(F32),)

        deactivate.count = 1
        gbin = gbin + row_sums(256, 32, 512, deactivate)[0]
        dpre = pre[...].astype(BF16)
        slope[r] = pre[...]
        terms[r] = contract_cols(dpre, wi[...])
        if r == 0:
            scatter.scatter_end(sib_out.at[0], peer_out.at[0])
        scatter2.scatter_put(terms, sib_out.at[1], sib_in.at[1], r)
        if r:
            scatter2.scatter_pass(terms, sib_in.at[1], peer_out.at[1], peer_in.at[1], r - 1)
    scatter2.scatter_pass(terms, sib_in.at[1], peer_out.at[1], peer_in.at[1], 3)
    gbin_ref[...] = gbin

    def weight_grad(slots, right, which, into):
        def one(step, carry):
            other = (at.b + step) % 8
            total = jnp.zeros((128, 512), F32)
            for r in range(4):
                total += contract_rows(slots[at.chip(r), :, lanes(other)], right(r))
            gsend[which, other] = total.astype(BF16)
            for k in range(4):
                plane = (at.z + k) % 4
                src = gsend.at[which, other, :, lanes(plane)]
                dst = into.at[at.z, :, lanes(at.b)]

                def away():
                    remote(
                        src, dst, g_send.at[which], g_recv.at[which], (other, plane)
                    ).start()

                if k:
                    away()
                else:
                    pl.when(step != 0)(away)

                    @pl.when(step == 0)
                    def _():
                        pltpu.make_async_copy(src, dst, g_recv.at[which]).start()

            return carry

        lax.fori_loop(0, 8, one, 0)

    weight_grad(grad_slots, lambda r: hid[r], 1, grecv_back)
    weight_grad(norm_slots, lambda r: slope[r].astype(BF16), 0, grecv_in)

    scatter2.scatter_arrive(peer_in.at[1])

    def first_back(rows):
        own = pl.ds(pl.multiple_of(core_rows + rows.start, 32), 32)
        total = (
            d2[rows]
            + terms[0, own]
            + peer_in[1, 1, rows].astype(F32)
            + peer_in[1, 2, rows].astype(F32)
            + peer_in[1, 3, rows].astype(F32)
        )
        unit = unit1[rows]
        d = norm_back(total * param(3), unit, scale1[rows][:, :1])
        d1_ref[rows] = d
        low = d.astype(BF16)
        db_ref[rows] = low
        return total * unit, total, low.astype(F32)

    first_back.count = 3
    sums = row_sums(128, 32, 1024, first_back)
    pg_ref[3:4, :] = sums[0]
    pg_ref[4:5, :] = sums[1]
    pg_ref[2:3, :] = sums[2]
    pg_ref[0:2, :] = jnp.zeros((2, 1024), F32)

    for which, into, dest in ((1, grecv_back, gwback_ref), (0, grecv_in, gwin_ref)):
        wait_bytes(into, g_recv.at[which])

        def add(rows, into=into, dest=dest):
            dest[rows] = (
                into[0, rows].astype(F32)
                + into[1, rows].astype(F32)
                + into[2, rows].astype(F32)
                + into[3, rows].astype(F32)
            )

        by_rows(128, 32, add)

    gather.gather_end(norm_slots)
    gather2.gather_end(grad_slots)
    scatter2.scatter_end(sib_out.at[1], peer_out.at[1])
    for k in range(2):
        wait_bytes(wi.at[pl.ds(0, 992)], w_send.at[k])
        wait_bytes(wi.at[pl.ds(0, 992)], g_send.at[k])


def vmem():
    return pl.BlockSpec(memory_space=pltpu.VMEM)


def run_ffn(x, att, wo, cot, par, bins, win, wback):
    shapes = (
        ((128, 1024), BF16),
        ((128, 1024), F32),
        ((128, 1024), BF16),
        ((128, 1024), F32),
        ((128, 1024), F32),
        ((8, 1024), F32),
        ((1, 512), F32),
    )
    dma = pltpu.SemaphoreType.DMA
    return pl.pallas_call(
        ffn_kernel,
        out_shape=[jax.ShapeDtypeStruct(s, t) for s, t in shapes],
        in_specs=[vmem()] * 8,
        out_specs=[vmem()] * 7,
        scratch_shapes=[
            pltpu.VMEM((1024, 512), BF16),
            pltpu.VMEM((1024, 512), BF16),
            pltpu.VMEM((128, 1024), F32),
            pltpu.VMEM((128, 1024), F32),
            pltpu.VMEM((128, 128), F32),
            pltpu.VMEM((128, 1024), F32),
            pltpu.VMEM((4, 256, 1024), BF16),
            pltpu.VMEM((4, 256, 1024), BF16),
            pltpu.VMEM((4, 256, 512), BF16),
            pltpu.VMEM((4, 256, 512), F32),
            pltpu.VMEM((256, 512), F32),
            pltpu.VMEM((4, 256, 1024), F32),
            pltpu.VMEM((2, 4, 128, 1024), BF16),
            pltpu.VMEM((2, 4, 128, 1024), BF16),
            pltpu.VMEM((2, 4, 128, 1024), BF16),
            pltpu.VMEM((2, 4, 128, 1024), BF16),
            pltpu.VMEM((2, 8, 128, 512), BF16),
            pltpu.VMEM((4, 128, 1024), BF16),
            pltpu.VMEM((4, 128, 1024), BF16),
            dma((4, 4)),
            dma((4, 4)),
            dma((4, 4)),
            dma((4, 4)),
            dma((2,)),
            dma((2,)),
            dma((2,)),
            dma((2,)),
        ],
        compiler_params=pltpu.CompilerParams(
            collective_id=1, has_side_effects=True, vmem_limit_bytes=VMEM_LIMIT
        ),
    )(x, att, wo, cot, par, bins, win, wback)


def fast_device(
    tokens,
    w_query,
    w_key,
    w_value,
    w_out,
    b_query,
    b_value,
    b_out,
    norm1_gain,
    norm1_shift,
    w_in,
    w_back,
    b_in,
    b_back,
    norm2_gain,
    norm2_shift,
    cotangent,
):
    f32 = jnp.float32
    bf16 = jnp.bfloat16
    score_scale = HEAD_DIM ** (-0.5)
    b_id = lax.axis_index("blk")
    small = jnp.concatenate(
        (b_query, b_value, b_out, norm1_gain, norm1_shift, b_back, norm2_gain, norm2_shift, b_in)
    )
    smalls = lax.all_gather(small, ("blk", "head"), axis=0)
    vectors = smalls[:, :256].reshape(32, 8, 32).transpose(1, 0, 2).reshape(8, 1024).astype(f32)
    bin_full = smalls[:, 256:].reshape(4, 8, 128)
    bins = lax.dynamic_index_in_dim(bin_full, b_id, 1, False).reshape(1, 512).astype(f32)
    attn_cols, out_rows = (
        lax.all_gather(jnp.stack((w_query, w_key, w_value)), "blk", axis=1, tiled=True),
        lax.all_gather(w_out, "blk", axis=1, tiled=True),
    )
    seq_count, local_len, model_dim = tokens.shape
    token_shape = (seq_count, local_len, model_dim)
    head_id = lax.axis_index("head")
    width_part = attn_cols.shape[2]
    bq_part = lax.dynamic_slice_in_dim(vectors[0], head_id * width_part, width_part)
    bv_part = lax.dynamic_slice_in_dim(vectors[1], head_id * width_part, width_part)
    wide_rows = token_rows(tokens)
    wide_len = wide_rows.shape[1]
    wide_flat = wide_rows.reshape(-1, model_dim)
    head_shape = (seq_count, wide_len, width_part)
    wide_shape = (seq_count, wide_len, model_dim)
    query_heads = (
        (jnp.dot(wide_flat, attn_cols[0], preferred_element_type=f32) + bq_part)
        .astype(bf16)
        .reshape(head_shape)
    )
    key_heads = (
        jnp.dot(wide_flat, attn_cols[1], preferred_element_type=f32)
        .astype(bf16)
        .reshape(head_shape)
    )
    value_heads = (
        (jnp.dot(wide_flat, attn_cols[2], preferred_element_type=f32) + bv_part)
        .astype(bf16)
        .reshape(head_shape)
    )
    query4 = split_heads(query_heads)
    key4 = split_heads(key_heads)
    value4 = split_heads(value_heads)
    pieces = (
        lax.all_gather(key_heads, "blk", axis=1, tiled=True),
        lax.all_gather(value_heads, "blk", axis=1, tiled=True),
    )
    scores = score_block(query4, split_heads(pieces[0]))
    maxima = jnp.max(scores, axis=-1)
    weights = jnp.exp(scores - maxima[..., None])
    totals = jnp.sum(weights, axis=-1)
    summed = jnp.einsum(
        "sqgk,skge->sqge", weights.astype(bf16), split_heads(pieces[1]), preferred_element_type=f32
    )
    log_sums = maxima + jnp.log(totals)
    attended4 = summed / totals[..., None]
    attended_heads = attended4.reshape(head_shape).astype(bf16)
    attended_flat = attended_heads.reshape(-1, width_part)
    att = lax.all_to_all(attended_heads, "head", split_axis=1, concat_axis=2, tiled=True)
    wo = lax.all_gather(out_rows, "head", axis=0, tiled=True)
    flat_rows = tokens.reshape(-1, model_dim)
    output, d_first, d_branch, gw_in, gw_back, pg, gbin = run_ffn(
        flat_rows,
        att.reshape(-1, model_dim),
        wo,
        cotangent.reshape(-1, model_dim),
        vectors,
        bins,
        w_in,
        w_back,
    )
    wide_dbranch = token_rows(d_branch.reshape(token_shape)).reshape(-1, model_dim)
    grad_out_part = contract_rows(attended_flat, wide_dbranch)
    grad_heads = contract_cols(wide_dbranch, out_rows).astype(bf16).reshape(head_shape)
    grads4 = split_heads(grad_heads)
    deltas = jnp.sum(grads4.astype(f32) * attended4, axis=-1)
    row_stats = (
        lax.all_gather(log_sums, "blk", axis=1, tiled=True),
        lax.all_gather(deltas, "blk", axis=1, tiled=True),
    )
    piece_keys = split_heads(pieces[0])
    piece_values = split_heads(pieces[1])
    piece_queries = split_heads(lax.all_gather(query_heads, "blk", axis=1, tiled=True))
    piece_grads = split_heads(lax.all_gather(grad_heads, "blk", axis=1, tiled=True))
    own_probs, own_scores = score_grads(query4, piece_keys, piece_values, grads4, log_sums, deltas)
    d_query = score_scale * jnp.einsum(
        "sqgk,skge->sqge", own_scores, piece_keys, preferred_element_type=f32
    )
    probs_low, d_scores = score_grads(
        piece_queries, key4, value4, piece_grads, row_stats[0], row_stats[1]
    )
    key_acc = score_scale * jnp.einsum(
        "sqgk,sqge->skge", d_scores, piece_queries, preferred_element_type=f32
    )
    value_acc = jnp.einsum("sqgk,sqge->skge", probs_low, piece_grads, preferred_element_type=f32)
    d_query_low = d_query.reshape(-1, width_part).astype(bf16)
    d_key_low = key_acc.reshape(-1, width_part).astype(bf16)
    d_value_low = value_acc.reshape(-1, width_part).astype(bf16)
    grad_b_query = place_part(
        jnp.sum(d_query_low.astype(f32), axis=0), model_dim, head_id * width_part
    )
    grad_b_value = place_part(
        jnp.sum(d_value_low.astype(f32), axis=0), model_dim, head_id * width_part
    )
    attn_grad_parts = jnp.stack(
        (
            contract_rows(wide_flat, d_query_low),
            contract_rows(wide_flat, d_key_low),
            contract_rows(wide_flat, d_value_low),
        )
    )
    token_terms = (
        contract_cols(d_query_low, attn_cols[0])
        + contract_cols(d_key_low, attn_cols[1])
        + contract_cols(d_value_low, attn_cols[2])
    )
    d_tokens = d_first + token_partials(token_terms.reshape(wide_shape)).reshape(-1, model_dim)
    grad_tokens = d_tokens.astype(bf16).reshape(token_shape)
    attn_sums, grad_w_out = (
        lax.psum_scatter(attn_grad_parts, "blk", scatter_dimension=1, tiled=True),
        lax.psum_scatter(grad_out_part, "blk", scatter_dimension=1, tiled=True),
    )
    gb_in = lax.dynamic_update_slice(
        jnp.zeros((4, 8, 128), f32), gbin.reshape(4, 1, 128), (0, b_id, 0)
    )
    vec = jnp.concatenate(
        (grad_b_query[None], grad_b_value[None], pg[2:]), axis=0
    )
    vec = vec.reshape(8, 32, 32).transpose(1, 0, 2).reshape(32, 256)
    vec = jnp.concatenate((vec, gb_in.reshape(32, 128)), axis=1)
    own = lax.psum_scatter(vec, ("blk", "head"), scatter_dimension=0, tiled=True).reshape(384)
    parts = [own[32 * i : 32 * i + 32] for i in range(8)]
    return (
        output.reshape(token_shape),
        grad_tokens,
        attn_sums[0],
        attn_sums[1],
        attn_sums[2],
        grad_w_out,
        parts[0],
        parts[1],
        parts[2],
        parts[3],
        parts[4],
        gw_in,
        gw_back,
        own[256:],
        parts[5],
        parts[6],
        parts[7],
    )


def solution(mesh):
    in_specs = (
        P(None, ("blk", "head"), None),
        P("blk", "head"),
        P("blk", "head"),
        P("blk", "head"),
        P("head", "blk"),
        P(("blk", "head")),
        P(("blk", "head")),
        P(("blk", "head")),
        P(("blk", "head")),
        P(("blk", "head")),
        P("blk", "head"),
        P("blk", "head"),
        P(("blk", "head")),
        P(("blk", "head")),
        P(("blk", "head")),
        P(("blk", "head")),
        P(None, ("blk", "head"), None),
    )
    out_specs = (
        P(None, ("blk", "head"), None),
        P(None, ("blk", "head"), None),
        P("blk", "head"),
        P("blk", "head"),
        P("blk", "head"),
        P("head", "blk"),
        P(("blk", "head")),
        P(("blk", "head")),
        P(("blk", "head")),
        P(("blk", "head")),
        P(("blk", "head")),
        P("blk", "head"),
        P("blk", "head"),
        P(("blk", "head")),
        P(("blk", "head")),
        P(("blk", "head")),
        P(("blk", "head")),
    )
    sizes = (mesh.shape["blk"], mesh.shape["head"])
    body = fast_device if sizes == (8, 4) else per_device
    return jax.shard_map(
        body, mesh=mesh, in_specs=in_specs, out_specs=out_specs, check_vma=False
    )
```

```python
import functools
import math

import jax
import jax.numpy as jnp
from jax import lax
from jax.experimental import pallas as pl
from jax.experimental.pallas import tpu as pltpu
from jax.sharding import PartitionSpec as P

HEAD_DIM = 64


NORM_EPS = 1e-05


def layer_norm(summed, gain, shift):
    centre = jnp.mean(summed, axis=-1, keepdims=True)
    centred = summed - centre
    spread = jnp.mean(centred * centred, axis=-1, keepdims=True)
    return centred * lax.rsqrt(spread + NORM_EPS) * gain + shift


def gelu_exact(inputs):
    return jax.nn.gelu(inputs, approximate=False)


def split_heads(packed):
    return packed.reshape(packed.shape[0], packed.shape[1], -1, HEAD_DIM)


def contract_rows(left, right):
    return lax.dot_general(
        left, right, (((0,), (0,)), ((), ())), preferred_element_type=jnp.float32
    )


def contract_cols(left, right):
    return lax.dot_general(
        left, right, (((1,), (1,)), ((), ())), preferred_element_type=jnp.float32
    )


def score_block(queries4, keys4):
    return jnp.einsum(
        "sqge,skge->sqgk", queries4, keys4, preferred_element_type=jnp.float32
    ) * HEAD_DIM ** (-0.5)


def score_grads(queries4, keys4, values4, grads4, log_sums, deltas):
    probs = jnp.exp(score_block(queries4, keys4) - log_sums[..., None])
    d_probs = jnp.einsum("sqge,skge->sqgk", grads4, values4, preferred_element_type=jnp.float32)
    d_scores = (probs * (d_probs - deltas[..., None])).astype(jnp.bfloat16)
    return (probs.astype(jnp.bfloat16), d_scores)


def token_rows(local):
    return lax.all_gather(local, "head", axis=1, tiled=True)


def token_partials(terms):
    return lax.psum_scatter(
        terms.astype(jnp.bfloat16), "head", scatter_dimension=1, tiled=True
    ).astype(jnp.float32)


def place_part(part, full_len, start):
    return lax.dynamic_update_slice_in_dim(jnp.zeros((full_len,), jnp.float32), part, start, 0)


def per_device(
    tokens,
    w_query,
    w_key,
    w_value,
    w_out,
    b_query,
    b_value,
    b_out,
    norm1_gain,
    norm1_shift,
    w_in,
    w_back,
    b_in,
    b_back,
    norm2_gain,
    norm2_shift,
    cotangent,
):
    f32 = jnp.float32
    bf16 = jnp.bfloat16
    score_scale = HEAD_DIM ** (-0.5)
    bq_full, bv_full, bo_full, gain_one, shift_one, bin_full, bback_full, gain_two, shift_two = (
        lax.all_gather(b_query, ("blk", "head"), axis=0, tiled=True),
        lax.all_gather(b_value, ("blk", "head"), axis=0, tiled=True),
        lax.all_gather(b_out, ("blk", "head"), axis=0, tiled=True),
        lax.all_gather(norm1_gain, ("blk", "head"), axis=0, tiled=True),
        lax.all_gather(norm1_shift, ("blk", "head"), axis=0, tiled=True),
        lax.all_gather(b_in, ("blk", "head"), axis=0, tiled=True),
        lax.all_gather(b_back, ("blk", "head"), axis=0, tiled=True),
        lax.all_gather(norm2_gain, ("blk", "head"), axis=0, tiled=True),
        lax.all_gather(norm2_shift, ("blk", "head"), axis=0, tiled=True),
    )
    attn_cols, out_rows, ffn_cols = (
        lax.all_gather(jnp.stack((w_query, w_key, w_value)), "blk", axis=1, tiled=True),
        lax.all_gather(w_out, "blk", axis=1, tiled=True),
        lax.all_gather(jnp.stack((w_in, w_back)), "blk", axis=1, tiled=True),
    )
    seq_count, local_len, model_dim = tokens.shape
    token_shape = (seq_count, local_len, model_dim)
    head_id = lax.axis_index("head")
    width_part = attn_cols.shape[2]
    bq_part = lax.dynamic_slice_in_dim(bq_full, head_id * width_part, width_part).astype(f32)
    bv_part = lax.dynamic_slice_in_dim(bv_full, head_id * width_part, width_part).astype(f32)
    wide_rows = token_rows(tokens)
    wide_len = wide_rows.shape[1]
    wide_flat = wide_rows.reshape(-1, model_dim)
    head_shape = (seq_count, wide_len, width_part)
    wide_shape = (seq_count, wide_len, model_dim)
    query_heads = (
        (jnp.dot(wide_flat, attn_cols[0], preferred_element_type=f32) + bq_part)
        .astype(bf16)
        .reshape(head_shape)
    )
    key_heads = (
        jnp.dot(wide_flat, attn_cols[1], preferred_element_type=f32)
        .astype(bf16)
        .reshape(head_shape)
    )
    value_heads = (
        (jnp.dot(wide_flat, attn_cols[2], preferred_element_type=f32) + bv_part)
        .astype(bf16)
        .reshape(head_shape)
    )
    query4 = split_heads(query_heads)
    key4 = split_heads(key_heads)
    value4 = split_heads(value_heads)
    stat_shape = query4.shape[:3]
    pieces = (
        lax.all_gather(key_heads, "blk", axis=1, tiled=True),
        lax.all_gather(value_heads, "blk", axis=1, tiled=True),
    )
    maxima = jnp.full(stat_shape, -1e30, f32)
    scores = score_block(query4, split_heads(pieces[0]))
    new_max = jnp.maximum(maxima, jnp.max(scores, axis=-1))
    weights = jnp.exp(scores - new_max[..., None])
    totals = jnp.sum(weights, axis=-1)
    summed = jnp.einsum(
        "sqgk,skge->sqge", weights.astype(bf16), split_heads(pieces[1]), preferred_element_type=f32
    )
    maxima, totals, summed = (new_max, totals, summed)
    log_sums = maxima + jnp.log(totals)
    attended4 = summed / totals[..., None]
    attended_heads = attended4.reshape(head_shape).astype(bf16)
    attended_flat = attended_heads.reshape(-1, width_part)
    branch_terms = jnp.dot(attended_flat, out_rows, preferred_element_type=f32).reshape(wide_shape)
    branch = token_partials(branch_terms).reshape(-1, model_dim) + bo_full.astype(f32)
    flat_rows = tokens.reshape(-1, model_dim)
    normed, norm1_pull = jax.vjp(
        layer_norm, flat_rows.astype(f32) + branch, gain_one.astype(f32), shift_one.astype(f32)
    )
    normed_low = normed.astype(bf16)
    ffn_full = lax.all_gather(ffn_cols, "head", axis=2, tiled=True)
    pre_act = jnp.dot(normed_low, ffn_full[0], preferred_element_type=f32) + bin_full.astype(f32)
    hidden_act, gelu_pull = jax.vjp(gelu_exact, pre_act)
    hidden_low = hidden_act.astype(bf16)
    ffn_out = contract_cols(hidden_low, ffn_full[1]) + bback_full.astype(f32)
    final, norm2_pull = jax.vjp(
        layer_norm, normed + ffn_out, gain_two.astype(f32), shift_two.astype(f32)
    )
    output = final.astype(bf16).reshape(token_shape)
    d_second, grad_norm2_gain, grad_norm2_shift = norm2_pull(
        cotangent.reshape(-1, model_dim).astype(f32)
    )
    d_ffn = d_second.astype(bf16)
    grad_b_back = jnp.sum(d_ffn.astype(f32), axis=0)
    grad_back_whole = contract_rows(d_ffn, hidden_low)
    d_hidden = jnp.dot(d_ffn, ffn_full[1], preferred_element_type=f32)
    d_pre = gelu_pull(d_hidden)[0].astype(bf16)
    grad_b_in = jnp.sum(d_pre.astype(f32), axis=0)
    grad_in_whole = contract_rows(normed_low, d_pre)
    ffn_grad_parts = lax.psum_scatter(
        jnp.stack((grad_in_whole, grad_back_whole)).astype(jnp.bfloat16),
        "head",
        scatter_dimension=2,
        tiled=True,
    ).astype(jnp.float32)
    d_normed = d_second + contract_cols(d_pre, ffn_full[0])
    d_first, grad_norm1_gain, grad_norm1_shift = norm1_pull(d_normed)
    d_branch = d_first.astype(bf16)
    grad_b_out = jnp.sum(d_branch.astype(f32), axis=0)
    wide_dbranch = token_rows(d_branch.reshape(token_shape)).reshape(-1, model_dim)
    grad_out_part = contract_rows(attended_flat, wide_dbranch)
    grad_heads = contract_cols(wide_dbranch, out_rows).astype(bf16).reshape(head_shape)
    grads4 = split_heads(grad_heads)
    deltas = jnp.sum(grads4.astype(f32) * attended4, axis=-1)
    row_stats = (
        lax.all_gather(log_sums, "blk", axis=1, tiled=True),
        lax.all_gather(deltas, "blk", axis=1, tiled=True),
    )
    pieces = (
        lax.all_gather(key_heads, "blk", axis=1, tiled=True),
        lax.all_gather(value_heads, "blk", axis=1, tiled=True),
        lax.all_gather(query_heads, "blk", axis=1, tiled=True),
        lax.all_gather(grad_heads, "blk", axis=1, tiled=True),
    )
    piece_keys = split_heads(pieces[0])
    piece_values = split_heads(pieces[1])
    piece_queries = split_heads(pieces[2])
    piece_grads = split_heads(pieces[3])
    piece_sums = row_stats[0]
    piece_deltas = row_stats[1]
    own_probs, own_scores = score_grads(query4, piece_keys, piece_values, grads4, log_sums, deltas)
    d_query = score_scale * jnp.einsum(
        "sqgk,skge->sqge", own_scores, piece_keys, preferred_element_type=f32
    )
    probs_low, d_scores = score_grads(
        piece_queries, key4, value4, piece_grads, piece_sums, piece_deltas
    )
    key_acc = score_scale * jnp.einsum(
        "sqgk,sqge->skge", d_scores, piece_queries, preferred_element_type=f32
    )
    value_acc = jnp.einsum("sqgk,sqge->skge", probs_low, piece_grads, preferred_element_type=f32)
    d_query_low = d_query.reshape(-1, width_part).astype(bf16)
    d_key_low = key_acc.reshape(-1, width_part).astype(bf16)
    d_value_low = value_acc.reshape(-1, width_part).astype(bf16)
    grad_b_query = place_part(
        jnp.sum(d_query_low.astype(f32), axis=0), model_dim, head_id * width_part
    )
    grad_b_value = place_part(
        jnp.sum(d_value_low.astype(f32), axis=0), model_dim, head_id * width_part
    )
    attn_grad_parts = jnp.stack(
        (
            contract_rows(wide_flat, d_query_low),
            contract_rows(wide_flat, d_key_low),
            contract_rows(wide_flat, d_value_low),
        )
    )
    token_terms = (
        contract_cols(d_query_low, attn_cols[0])
        + contract_cols(d_key_low, attn_cols[1])
        + contract_cols(d_value_low, attn_cols[2])
    )
    d_tokens = d_first + token_partials(token_terms.reshape(wide_shape)).reshape(-1, model_dim)
    grad_tokens = d_tokens.astype(bf16).reshape(token_shape)
    attn_sums, grad_w_out, ffn_sums = (
        lax.psum_scatter(attn_grad_parts, "blk", scatter_dimension=1, tiled=True),
        lax.psum_scatter(grad_out_part, "blk", scatter_dimension=1, tiled=True),
        lax.psum_scatter(ffn_grad_parts, "blk", scatter_dimension=1, tiled=True),
    )
    (
        grad_b_query,
        grad_b_value,
        grad_b_out,
        grad_norm1_gain,
        grad_norm1_shift,
        grad_b_in,
        grad_b_back,
        grad_norm2_gain,
        grad_norm2_shift,
    ) = (
        lax.psum_scatter(grad_b_query, ("blk", "head"), scatter_dimension=0, tiled=True),
        lax.psum_scatter(grad_b_value, ("blk", "head"), scatter_dimension=0, tiled=True),
        lax.psum_scatter(grad_b_out, ("blk", "head"), scatter_dimension=0, tiled=True),
        lax.psum_scatter(grad_norm1_gain, ("blk", "head"), scatter_dimension=0, tiled=True),
        lax.psum_scatter(grad_norm1_shift, ("blk", "head"), scatter_dimension=0, tiled=True),
        lax.psum_scatter(grad_b_in, ("blk", "head"), scatter_dimension=0, tiled=True),
        lax.psum_scatter(grad_b_back, ("blk", "head"), scatter_dimension=0, tiled=True),
        lax.psum_scatter(grad_norm2_gain, ("blk", "head"), scatter_dimension=0, tiled=True),
        lax.psum_scatter(grad_norm2_shift, ("blk", "head"), scatter_dimension=0, tiled=True),
    )
    return (
        output,
        grad_tokens,
        attn_sums[0],
        attn_sums[1],
        attn_sums[2],
        grad_w_out,
        grad_b_query,
        grad_b_value,
        grad_b_out,
        grad_norm1_gain,
        grad_norm1_shift,
        ffn_sums[0],
        ffn_sums[1],
        grad_b_in,
        grad_b_back,
        grad_norm2_gain,
        grad_norm2_shift,
    )


MESH = pl.DeviceIdType.MESH
F32 = jnp.float32
BF16 = jnp.bfloat16
VMEM_LIMIT = 60 * 2**20


def dot_nn(left, right):
    return jnp.dot(left, right, preferred_element_type=F32)


class Place:
    def __init__(self):
        self.b = lax.axis_index("blk")
        self.z = lax.axis_index("head")
        self.y = self.b // 4
        self.x = (self.b // 2) % 2
        self.c = self.b % 2
        self.q = self.b // 2

    def chip(self, r):
        return ((self.y + r // 2) % 2) * 2 + (self.x + r % 2) % 2

    def peer(self, r):
        return (2 * self.chip(r) + self.c, self.z)

    def sibling(self):
        return (2 * self.q + 1 - self.c, self.z)


def remote(src, dst, send_sem, recv_sem, device):
    return pltpu.make_async_remote_copy(
        src_ref=src,
        dst_ref=dst,
        send_sem=send_sem,
        recv_sem=recv_sem,
        device_id=device,
        device_id_type=MESH,
    )


def wait_bytes(view, sem):
    pltpu.make_async_copy(view, view, sem).wait()


def greet_all(at):
    barrier = pltpu.get_barrier_semaphore()
    flat = at.b * 4 + at.z

    def greet(step, carry):
        other = (flat + step) % 32
        pl.semaphore_signal(
            barrier, inc=1, device_id=(other // 4, other % 4), device_id_type=MESH
        )
        return carry

    lax.fori_loop(1, 32, greet, 0)
    pl.semaphore_wait(barrier, 31)


def half(core):
    return pl.ds(pl.multiple_of(core * 128, 128), 128)


def lanes(index):
    return pl.ds(pl.multiple_of(index * 128, 128), 128)


def by_rows(count, size, step):
    def body(i, carry):
        step(pl.ds(pl.multiple_of(i * size, size), size))
        return carry

    lax.fori_loop(0, count // size, body, 0)


def row_sums(count, size, width, step):
    def body(i, carry):
        parts = step(pl.ds(pl.multiple_of(i * size, size), size))
        return tuple(
            kept + jnp.sum(part.reshape(size // 8, 8, width), axis=0)
            for kept, part in zip(carry, parts)
        )

    n = step.count
    sums = lax.fori_loop(
        0, count // size, body, tuple(jnp.zeros((8, width), F32) for _ in range(n))
    )
    return tuple(jnp.sum(s, axis=0, keepdims=True) for s in sums)


class Exchange:
    def __init__(self, at, send, recv, send_sib, recv_sib):
        self.at, self.send, self.recv = at, send, recv
        self.send_sib, self.recv_sib = send_sib, recv_sib

    def gather_start(self, slots):
        at = self.at
        mine = slots.at[at.q, half(at.c)]
        for r in (1, 2, 3):
            remote(mine, mine, self.send.at[r], self.recv.at[r], at.peer(r)).start()
        remote(mine, mine, self.send_sib.at[0], self.recv_sib.at[0], at.sibling()).start()

    def gather_step(self, slots, r):
        at = self.at
        chip = at.chip(r)
        block = slots.at[chip, half(at.c)]
        if r:
            wait_bytes(block, self.recv.at[r])
            remote(
                block, block, self.send_sib.at[r], self.recv_sib.at[r], at.sibling()
            ).start()
        wait_bytes(slots.at[chip, half(1 - at.c)], self.recv_sib.at[r])
        return chip

    def gather_end(self, slots):
        at = self.at
        for r in range(4):
            block = slots.at[at.chip(r), half(at.c)]
            if r:
                wait_bytes(slots.at[at.q, half(at.c)], self.send.at[r])
            wait_bytes(block, self.send_sib.at[r])

    def scatter_put(self, terms, out_sib, in_sib, r):
        at = self.at
        out_sib[r] = terms[r, half(1 - at.c)].astype(BF16)
        remote(
            out_sib.at[r], in_sib.at[r], self.send_sib.at[r], self.recv_sib.at[r], at.sibling()
        ).start()

    def scatter_pass(self, terms, in_sib, out, into, r):
        at = self.at
        wait_bytes(in_sib.at[r], self.recv_sib.at[r])
        total = terms[r, half(at.c)] + in_sib[r].astype(F32)
        if r:
            out[r] = total.astype(BF16)
            remote(out.at[r], into.at[r], self.send.at[r], self.recv.at[r], at.peer(r)).start()
        else:
            terms[0, half(at.c)] = total

    def scatter_arrive(self, into):
        for r in (1, 2, 3):
            wait_bytes(into.at[r], self.recv.at[r])

    def scatter_end(self, out_sib, out):
        for r in range(4):
            wait_bytes(out_sib.at[r], self.send_sib.at[r])
            if r:
                wait_bytes(out.at[r], self.send.at[r])


def norm_rows(values):
    centre = jnp.mean(values, axis=-1, keepdims=True)
    centred = values - centre
    spread = jnp.mean(centred * centred, axis=-1, keepdims=True)
    scale = lax.rsqrt(spread + NORM_EPS)
    return centred * scale, scale


def norm_back(grad, unit, scale):
    centre = jnp.mean(grad, axis=-1, keepdims=True)
    along = jnp.mean(grad * unit, axis=-1, keepdims=True)
    return (grad - centre - unit * along) * scale


def send_or_copy(src, dst, send_sem, recv_sem, device, own):
    def away():
        remote(src, dst, send_sem, recv_sem, device).start()

    if own is None:
        away()
        return
    pl.when(jnp.logical_not(own))(away)

    @pl.when(own)
    def _():
        pltpu.make_async_copy(src, dst, recv_sem).start()


def push_weights(at, src, dst, send_sem, recv_sem):
    rows, cols = lanes(at.b), lanes(at.z)
    flat = at.b * 4 + at.z
    pltpu.make_async_copy(src.at[:, lanes(at.b)], dst.at[rows, cols], recv_sem).start()

    def push(step, carry):
        other = (flat + step) % 32
        remote(
            src.at[:, lanes(other // 4)],
            dst.at[rows, cols],
            send_sem,
            recv_sem,
            (other // 4, other % 4),
        ).start()
        return carry

    lax.fori_loop(1, 32, push, 0)


def push_grads(at, blocks, into, send_sem, recv_sem):
    def one(step, carry):
        other = (at.b + step) % 8
        for k in range(4):
            plane = (at.z + k) % 4
            send_or_copy(
                blocks.at[other, :, lanes(plane)],
                into.at[at.z, :, lanes(at.b)],
                send_sem,
                recv_sem,
                (other, plane),
                step == 0 if k == 0 else None,
            )
        return carry

    lax.fori_loop(0, 8, one, 0)


def take_grads(into, dest, recv_sem):
    wait_bytes(into, recv_sem)

    def add(rows):
        dest[rows] = (
            into[0, rows].astype(F32)
            + into[1, rows].astype(F32)
            + into[2, rows].astype(F32)
            + into[3, rows].astype(F32)
        )

    by_rows(128, 32, add)


def ffn_kernel(
    x_ref,
    att_ref,
    wo_ref,
    cot_ref,
    par_ref,
    bin_ref,
    wi,
    wback_ref,
    out_ref,
    d1_ref,
    db_ref,
    da_ref,
    gin_ref,
    gwback_ref,
    pg_ref,
    gbin_ref,
    wb,
    n1,
    unit1,
    scale1,
    d2,
    norm_slots,
    grad_slots,
    hid,
    slope,
    pre,
    terms,
    sib_out,
    sib_in,
    peer_out,
    peer_in,
    gsend,
    grecv_back,
    da_send,
    send,
    recv,
    send_sib,
    recv_sib,
    w_send,
    w_recv,
    g_send,
    g_recv,
    a_send,
    a_recv,
):
    at = Place()
    flat = at.b * 4 + at.z
    greet_all(at)

    push_weights(at, wback_ref, wb, w_send, w_recv)

    def param(i):
        return par_ref[i : i + 1, :]

    n1[...] = dot_nn(att_ref[...], wo_ref[...])

    def first_norm(rows):
        unit, scale = norm_rows(x_ref[rows].astype(F32) + n1[rows] + param(2))
        unit1[rows] = unit
        scale1[rows] = jnp.broadcast_to(scale, (32, 128))
        n1[rows] = unit * param(3) + param(4)

    by_rows(128, 32, first_norm)
    norm_slots[at.q, half(at.c)] = n1[...].astype(BF16)
    gather = Exchange(at, send.at[0], recv.at[0], send_sib.at[0], recv_sib.at[0])
    gather.gather_start(norm_slots)

    wait_bytes(wb, w_recv)

    scatter = Exchange(at, send.at[1], recv.at[1], send_sib.at[1], recv_sib.at[1])
    for r in range(4):
        chip = gather.gather_step(norm_slots, r)
        pre[...] = dot_nn(norm_slots[chip], wi[...])

        def activate(rows, r=r):
            u = pre[rows] + bin_ref[...]
            cdf = 0.5 * (1.0 + lax.erf(u * math.sqrt(0.5)))
            bell = jnp.exp(-0.5 * u * u) * (1.0 / math.sqrt(2.0 * math.pi))
            hid[r, rows] = (u * cdf).astype(BF16)
            slope[r, rows] = cdf + u * bell

        by_rows(256, 32, activate)
        terms[r] = contract_cols(hid[r], wb[...])
        scatter.scatter_put(terms, sib_out.at[0], sib_in.at[0], r)
        if r:
            scatter.scatter_pass(terms, sib_in.at[0], peer_out.at[0], peer_in.at[0], r - 1)
    scatter.scatter_pass(terms, sib_in.at[0], peer_out.at[0], peer_in.at[0], 3)
    scatter.scatter_arrive(peer_in.at[0])

    core_rows = pl.multiple_of(at.c * 128, 128)

    def second_norm(rows):
        own = pl.ds(pl.multiple_of(core_rows + rows.start, 32), 32)
        total = (
            terms[0, own]
            + peer_in[0, 1, rows].astype(F32)
            + peer_in[0, 2, rows].astype(F32)
            + peer_in[0, 3, rows].astype(F32)
        )
        unit, scale = norm_rows(n1[rows] + total + param(5))
        out_ref[rows] = (unit * param(6) + param(7)).astype(BF16)
        g = cot_ref[rows].astype(F32)
        d = norm_back(g * param(6), unit, scale)
        d2[rows] = d
        low = d.astype(BF16)
        grad_slots[at.q, own] = low
        return g * unit, g, low.astype(F32)

    second_norm.count = 3
    sums = row_sums(128, 32, 1024, second_norm)
    pg_ref[6:7, :] = sums[0]
    pg_ref[7:8, :] = sums[1]
    pg_ref[5:6, :] = sums[2]

    gather2 = Exchange(at, send.at[2], recv.at[2], send_sib.at[2], recv_sib.at[2])
    gather2.gather_start(grad_slots)
    scatter2 = Exchange(at, send.at[3], recv.at[3], send_sib.at[3], recv_sib.at[3])
    gbin = jnp.zeros((1, 512), F32)
    for r in range(4):
        chip = gather2.gather_step(grad_slots, r)
        pre[...] = dot_nn(grad_slots[chip], wb[...])

        def deactivate(rows, r=r):
            low = (pre[rows] * slope[r, rows]).astype(BF16)
            pre[rows] = low.astype(F32)
            return (low.astype(F32),)

        deactivate.count = 1
        gbin = gbin + row_sums(256, 32, 512, deactivate)[0]
        dpre = pre[...].astype(BF16)
        slope[r] = pre[...]
        terms[r] = contract_cols(dpre, wi[...])
        if r == 0:
            scatter.scatter_end(sib_out.at[0], peer_out.at[0])
        scatter2.scatter_put(terms, sib_out.at[1], sib_in.at[1], r)
        if r:
            scatter2.scatter_pass(terms, sib_in.at[1], peer_out.at[1], peer_in.at[1], r - 1)
    scatter2.scatter_pass(terms, sib_in.at[1], peer_out.at[1], peer_in.at[1], 3)
    gbin_ref[...] = gbin

    def weight_grad(slots, right, into):
        def one(step, carry):
            other = (at.b + step) % 8
            total = jnp.zeros((128, 512), F32)
            for r in range(4):
                total += contract_rows(slots[at.chip(r), :, lanes(other)], right(r))
            into[other] = total.astype(BF16)
            return carry

        lax.fori_loop(0, 8, one, 0)

    weight_grad(grad_slots, lambda r: hid[r], gsend)
    push_grads(at, gsend, grecv_back, g_send, g_recv)
    weight_grad(norm_slots, lambda r: slope[r].astype(BF16), gin_ref)

    scatter2.scatter_arrive(peer_in.at[1])

    def first_back(rows):
        own = pl.ds(pl.multiple_of(core_rows + rows.start, 32), 32)
        total = (
            d2[rows]
            + terms[0, own]
            + peer_in[1, 1, rows].astype(F32)
            + peer_in[1, 2, rows].astype(F32)
            + peer_in[1, 3, rows].astype(F32)
        )
        unit = unit1[rows]
        d = norm_back(total * param(3), unit, scale1[rows][:, :1])
        d1_ref[rows] = d
        low = d.astype(BF16)
        db_ref[rows] = low
        return total * unit, total, low.astype(F32)

    first_back.count = 3
    sums = row_sums(128, 32, 1024, first_back)
    pg_ref[3:4, :] = sums[0]
    pg_ref[4:5, :] = sums[1]
    pg_ref[2:3, :] = sums[2]
    pg_ref[0:2, :] = jnp.zeros((2, 1024), F32)

    da_send[...] = contract_cols(db_ref[...], wo_ref[...]).astype(BF16)
    place = at.q * 4 + at.z

    def give(step, carry):
        for k in range(4):
            chip = (at.q + step) % 4
            plane = (at.z + k) % 4
            pair = 4 * (plane // 2) + chip
            src = da_send.at[pl.ds(pl.multiple_of((plane % 2) * 64, 64), 64), lanes(pair)]
            dst = da_ref.at[pl.ds(pl.multiple_of(place * 64, 64), 64)]
            send_or_copy(
                src, dst, a_send, a_recv, (2 * chip + at.c, plane), step == 0 if k == 0 else None
            )
        return carry

    lax.fori_loop(0, 4, give, 0)
    wait_bytes(da_ref, a_recv)
    wait_bytes(da_ref.at[pl.ds(0, 960)], a_send)
    take_grads(grecv_back, gwback_ref, g_recv)

    gather.gather_end(norm_slots)
    gather2.gather_end(grad_slots)
    scatter2.scatter_end(sib_out.at[1], peer_out.at[1])
    wait_bytes(wb.at[pl.ds(0, 992)], w_send)
    wait_bytes(wb.at[pl.ds(0, 992)], g_send)


def vmem():
    return pl.BlockSpec(memory_space=pltpu.VMEM)


DMA = pltpu.SemaphoreType.DMA


def head_mask(h):
    lane = lax.broadcasted_iota(jnp.int32, (1, 128), 1)
    return jnp.where(lane // HEAD_DIM == h, 1.0, 0.0).astype(F32)


def slot_rows(index):
    return pl.ds(pl.multiple_of(index * 64, 64), 64)


def chip_rows(index):
    return pl.ds(pl.multiple_of(index * 256, 256), 256)


def core_rows(index):
    return pl.ds(pl.multiple_of(index * 1024, 1024), 1024)


def attend_kernel(
    x_ref,
    wq_ref,
    wk_ref,
    wv_ref,
    wout_ref,
    small_ref,
    win_ref,
    xs,
    wqkv,
    queries,
    keys_all,
    values_all,
    mixed,
    log_sums,
    att,
    wo,
    par,
    bins,
    wi,
    smalls,
    proj,
    scores,
    att_send,
    z_send,
    z_recv,
    p_send,
    p_recv,
    w_send,
    w_recv,
    o_send,
    o_recv,
    k_send,
    k_recv,
    misc_send,
    misc_recv,
):
    at = Place()
    flat = at.b * 4 + at.z
    place = at.q * 4 + at.z
    parity = at.z % 2
    greet_all(at)

    for dz in (1, 3, 2):
        plane = (at.z + dz) % 4
        remote(
            x_ref.at[slot_rows(plane % 2)],
            xs.at[slot_rows(place)],
            z_send.at[dz],
            z_recv.at[dz],
            (at.b, plane),
        ).start()
    own = pltpu.make_async_copy(x_ref.at[slot_rows(parity)], xs.at[slot_rows(place)], z_recv.at[0])
    own.start()

    for dx in range(2):
        for dz in range(2):
            column = (at.x + dx) % 2
            plane = 2 * (at.z // 2) + (at.z + dz) % 2
            target = 2 * (parity * 2 + column) + at.c
            mine = jnp.logical_and(
                parity == at.y, jnp.logical_and(column == at.x, plane == at.z)
            )
            for k, w in enumerate((wq_ref, wk_ref, wv_ref)):
                send_or_copy(
                    w.at[:, lanes(column)],
                    wqkv.at[lanes(at.b), pl.ds(k * 128, 128)],
                    w_send.at[0],
                    w_recv.at[0],
                    (target, plane),
                    mine if dx == 0 and dz == 0 else None,
                )

    pltpu.make_async_copy(small_ref, smalls.at[flat], misc_recv.at[0]).start()

    def spread(step, carry):
        other = (flat + step) % 32
        remote(
            small_ref,
            smalls.at[flat],
            misc_send.at[0],
            misc_recv.at[0],
            (other // 4, other % 4),
        ).start()
        return carry

    lax.fori_loop(1, 32, spread, 0)

    col = wo.at[pl.ds(pl.multiple_of(at.z * 256, 256), 256), lanes(at.b)]
    pltpu.make_async_copy(wout_ref, col, o_recv.at[0]).start()
    for dz in range(1, 4):
        remote(
            wout_ref, col, o_send.at[0], o_recv.at[0], (at.b, (at.z + dz) % 4)
        ).start()

    for dz in (0, 1, 3, 2):
        block = xs.at[slot_rows(at.q * 4 + (at.z - dz + 4) % 4)]
        wait_bytes(block, z_recv.at[dz])
        for r in (1, 2, 3):
            remote(block, block, p_send.at[r, dz], p_recv.at[r, dz], at.peer(r)).start()

    wait_bytes(wqkv.at[pl.ds(0, 512)], w_recv.at[0])
    for r in range(4):
        part = wqkv.at[lanes(2 * at.chip(r) + at.c)]
        remote(part, part, w_send.at[1], w_recv.at[1], at.sibling()).start()

    wait_bytes(smalls, misc_recv.at[0])
    for b in range(8):
        total = smalls[4 * b].astype(F32)
        for z in range(1, 4):
            total += smalls[4 * b + z].astype(F32)
        par[:, 128 * b : 128 * b + 128] = total[0:8]
    for h in range(4):
        bins[0:1, 128 * h : 128 * h + 128] = smalls[8 * h + at.b].astype(F32)[8:9]
    pair = 4 * (at.z // 2) + at.q
    bias_q = par[0:1, lanes(pair)]
    bias_v = par[1:2, lanes(pair)]
    wait_bytes(wqkv.at[pl.ds(0, 512)], w_recv.at[1])

    for r in range(4):
        chip = at.chip(r)
        if r:
            for dz in (0, 1, 3, 2):
                wait_bytes(xs.at[slot_rows(0)], p_recv.at[r, dz])
        rows = chip_rows(chip)
        proj[...] = dot_nn(xs[rows], wqkv[...])
        queries[rows] = (proj[:, 0:128] + bias_q).astype(BF16)
        own_rows = chip_rows(at.c * 4 + chip)
        keys_all[own_rows] = proj[:, 128:256].astype(BF16)
        values_all[own_rows] = (proj[:, 256:384] + bias_v).astype(BF16)
        for k, ref in enumerate((keys_all, values_all)):
            view = ref.at[own_rows]
            remote(view, view, k_send.at[k, r], k_recv.at[k, r], at.sibling()).start()

    whole = wo.at[:, lanes(at.b)]
    wait_bytes(whole, o_recv.at[0])
    for r in (1, 2, 3):
        remote(whole, whole, o_send.at[r], o_recv.at[r], at.peer(r)).start()
    remote(whole, whole, o_send.at[4], o_recv.at[4], at.sibling()).start()
    push_weights(at, win_ref, wi, misc_send.at[1], misc_recv.at[1])

    for r in range(4):
        for k, ref in enumerate((keys_all, values_all)):
            wait_bytes(ref.at[pl.ds(0, 256)], k_recv.at[k, r])

    sequence = parity

    def attend(step, carry):
        chip = (at.q + 1 + step) % 4
        rows = chip_rows(chip)
        outs = []
        logs = []
        for h in range(2):
            q = (queries[rows].astype(F32) * head_mask(h) * HEAD_DIM**-0.5).astype(BF16)
            scores[...] = contract_cols(q, keys_all[...])
            top = jnp.max(scores[...], axis=-1, keepdims=True)
            weights = jnp.exp(scores[...] - top)
            total = jnp.sum(weights, axis=-1, keepdims=True)
            outs.append(dot_nn(weights.astype(BF16), values_all[...]) / total)
            logs.append(top + jnp.log(total))
        first = head_mask(0) > 0.5
        merged = jnp.where(first, outs[0], outs[1])
        mixed[rows] = merged
        log_sums[rows] = jnp.where(first, logs[0], logs[1])
        att_send[rows] = merged.astype(BF16)
        for k in range(4):
            plane = (at.z + 1 + k) % 4
            send_or_copy(
                att_send.at[slot_rows(chip * 4 + plane)],
                att.at[slot_rows(sequence), lanes(pair)],
                misc_send.at[2],
                misc_recv.at[2],
                (2 * chip + at.c, plane),
                step == 3 if k == 3 else None,
            )
        return carry

    lax.fori_loop(0, 4, attend, 0)

    for r in (1, 2, 3):
        part = wo.at[:, lanes(2 * at.chip(r) + at.c)]
        wait_bytes(part, o_recv.at[r])
        remote(part, part, o_send.at[4 + r], o_recv.at[4 + r], at.sibling()).start()
    for r in range(4):
        wait_bytes(whole, o_recv.at[4 + r])
    wait_bytes(wi, misc_recv.at[1])
    wait_bytes(att, misc_recv.at[2])

    for dz in range(1, 4):
        wait_bytes(xs.at[slot_rows(0)], z_send.at[dz])
    for r in (1, 2, 3):
        for dz in range(4):
            wait_bytes(xs.at[slot_rows(0)], p_send.at[r, dz])
    away = jnp.logical_not(parity == at.y)

    @pl.when(away)
    def _():
        wait_bytes(wqkv.at[pl.ds(0, 512)], w_send.at[0])

    @pl.when(jnp.logical_not(away))
    def _():
        wait_bytes(wqkv.at[pl.ds(0, 384)], w_send.at[0])

    wait_bytes(wqkv.at[pl.ds(0, 512)], w_send.at[1])
    wait_bytes(smalls.at[pl.ds(0, 31)], misc_send.at[0])
    wait_bytes(wo.at[pl.ds(0, 768), pl.ds(0, 128)], o_send.at[0])
    for r in range(1, 8):
        wait_bytes(whole, o_send.at[r])
    for r in range(4):
        for k in range(2):
            wait_bytes(keys_all.at[pl.ds(0, 256)], k_send.at[k, r])
    wait_bytes(wi.at[pl.ds(0, 992)], misc_send.at[1])
    wait_bytes(att_send.at[pl.ds(0, 960)], misc_send.at[2])


def grads_kernel(
    xs,
    wqkv,
    queries,
    keys_all,
    values_all,
    mixed,
    log_sums,
    da_ref,
    d1_ref,
    att,
    db_ref,
    pg_ref,
    gbin_ref,
    gin_ref,
    gtok_ref,
    gq_ref,
    gk_ref,
    gv_ref,
    gout_ref,
    gwin_ref,
    small_ref,
    q_turned,
    da_turned,
    s_buf,
    p_buf,
    d_buf,
    dq,
    dk_turned,
    dv_turned,
    dk,
    dv,
    sib_k,
    sib_v,
    dqkv,
    terms,
    x_out,
    x_in,
    x_sum,
    x_own,
    z_out,
    z_in,
    w_sib_out,
    w_sib_in,
    w_out,
    w_in,
    sib_out,
    sib_in,
    peer_out,
    peer_in,
    o_out,
    o_in,
    vec,
    notes,
    notes_in,
    grecv,
    kv_send,
    kv_recv,
    x_send,
    x_recv,
    z_send,
    z_recv,
    ws_send,
    ws_recv,
    send,
    recv,
    send_sib,
    recv_sib,
    o_send,
    o_recv,
    misc_send,
    misc_recv,
):
    at = Place()
    flat = at.b * 4 + at.z
    parity = at.z % 2
    pair = 4 * (at.z // 2) + at.q
    greet_all(at)

    push_grads(at, gin_ref, grecv, misc_send.at[0], misc_recv.at[0])

    out_scatter = Exchange(at, send, recv, send_sib, recv_sib)
    for r in range(4):
        terms[r] = contract_rows(db_ref[:, chip_rows(at.chip(r))], att[...])
        out_scatter.scatter_put(terms, sib_out, sib_in, r)

    q_turned[...] = queries[...].astype(F32).T.astype(BF16)
    da_turned[...] = da_ref[...].astype(F32).T.astype(BF16)
    dk_turned[...] = jnp.zeros_like(dk_turned)
    dv_turned[...] = jnp.zeros_like(dv_turned)

    def attend(step, carry):
        rows = chip_rows(step)
        parts = []
        for h in range(2):
            mask = head_mask(h)
            grad = da_ref[rows].astype(F32) * mask
            delta = jnp.sum(grad * mixed[rows], axis=-1, keepdims=True)
            q = (queries[rows].astype(F32) * mask * HEAD_DIM**-0.5).astype(BF16)
            s_buf[...] = contract_cols(q, keys_all[...])
            d_buf[...] = contract_cols(grad.astype(BF16), values_all[...])
            logs = log_sums[rows][:, h * HEAD_DIM : h * HEAD_DIM + 1]
            probs = jnp.exp(s_buf[...] - logs)
            p_buf[...] = probs.astype(BF16)
            low = (probs * (d_buf[...] - delta)).astype(BF16)
            band = pl.ds(h * HEAD_DIM, HEAD_DIM)
            dv_turned[band] += dot_nn(da_turned[band, rows], p_buf[...])
            dk_turned[band] += dot_nn(q_turned[band, rows], low)
            parts.append(dot_nn(low, keys_all[...]))
        dq[rows] = jnp.where(head_mask(0) > 0.5, parts[0], parts[1]) * HEAD_DIM**-0.5
        return carry

    lax.fori_loop(0, 4, attend, 0)
    for r in range(4):
        out_scatter.scatter_pass(terms, sib_in, peer_out, peer_in, r)

    dk[...] = dk_turned[...].T * HEAD_DIM**-0.5
    dv[...] = dv_turned[...].T
    other = core_rows(1 - at.c)
    mine = core_rows(at.c)
    for k, (ref, into) in enumerate(((dk, sib_k), (dv, sib_v))):
        remote(ref.at[other], into, kv_send.at[k], kv_recv.at[k], at.sibling()).start()
    low = dq[...].astype(BF16)
    dqkv[:, 0:128] = low
    vec[...] = pg_ref[...]
    vec[0:1, lanes(pair)] = jnp.sum(low.astype(F32), axis=0, keepdims=True)
    wait_bytes(sib_k, kv_recv.at[0])
    dqkv[:, 128:256] = (dk[mine] + sib_k[...]).astype(BF16)
    wait_bytes(sib_v, kv_recv.at[1])
    low = (dv[mine] + sib_v[...]).astype(BF16)
    dqkv[:, 256:384] = low
    vec[1:2, lanes(pair)] = jnp.sum(low.astype(F32), axis=0, keepdims=True)

    for r in (3, 1, 2, 0):
        part = contract_cols(dqkv[chip_rows(at.chip(r))], wqkv[...])
        if r:
            x_out[r] = part.astype(BF16)
            remote(x_out.at[r], x_in.at[r], x_send.at[r], x_recv.at[r], at.peer(r)).start()
        else:
            x_sum[...] = part

    for d in range(32):
        notes[d, 0:8] = vec[:, 128 * (d // 4) : 128 * (d // 4) + 128]
        notes[d, 8:16] = jnp.zeros((8, 128), F32)
    for h in range(4):
        notes[8 * h + at.b, 8:9] = gbin_ref[0:1, 128 * h : 128 * h + 128]
    pltpu.make_async_copy(notes.at[flat], notes_in.at[flat], misc_recv.at[1]).start()

    def spread(step, carry):
        to = (flat + step) % 32
        remote(
            notes.at[to],
            notes_in.at[flat],
            misc_send.at[1],
            misc_recv.at[1],
            (to // 4, to % 4),
        ).start()
        return carry

    lax.fori_loop(1, 32, spread, 0)

    def features(b):
        return contract_rows(xs[:, lanes(b)], dqkv[...])

    for r in range(4):
        w_sib_out[r] = features(2 * at.chip(r) + 1 - at.c)
        remote(
            w_sib_out.at[r], w_sib_in.at[r], ws_send.at[r], ws_recv.at[r], at.sibling()
        ).start()
    plane_w = 2 * (at.z // 2) + at.y
    for r in range(4):
        total = features(2 * at.chip(r) + at.c)
        wait_bytes(w_sib_in.at[r], ws_recv.at[r])
        w_out[r] = (total + w_sib_in[r]).astype(BF16)
        send_or_copy(
            w_out.at[r],
            w_in.at[parity, at.x],
            misc_send.at[2],
            misc_recv.at[2],
            at.peer(r)[:1] + (plane_w,),
            plane_w == at.z if r == 0 else None,
        )

    out_scatter.scatter_arrive(peer_in)

    def out_rows(rows):
        own = pl.ds(pl.multiple_of(at.c * 128 + rows.start, 32), 32)
        total = (
            terms[0, own]
            + peer_in[1, rows].astype(F32)
            + peer_in[2, rows].astype(F32)
            + peer_in[3, rows].astype(F32)
        )
        o_out[rows] = total.astype(BF16)

    by_rows(128, 32, out_rows)
    wide = pl.ds(pl.multiple_of(at.z * 256, 256), 256)
    pltpu.make_async_copy(o_out.at[:, wide], o_in.at[0], o_recv).start()
    for dz in range(1, 4):
        plane = (at.z + dz) % 4
        remote(
            o_out.at[:, pl.ds(pl.multiple_of(plane * 256, 256), 256)],
            o_in.at[dz],
            o_send,
            o_recv,
            (at.b, plane),
        ).start()

    for r in (1, 2, 3):
        wait_bytes(x_in.at[r], x_recv.at[r])
    for dz in (2, 1, 3, 0):
        plane = (at.z + dz) % 4
        rows = slot_rows(plane)
        total = (
            x_sum[rows]
            + x_in[1, rows].astype(F32)
            + x_in[2, rows].astype(F32)
            + x_in[3, rows].astype(F32)
        )
        if dz:
            z_out[dz] = total.astype(BF16)
            remote(
                z_out.at[dz], z_in.at[dz], z_send.at[dz], z_recv.at[dz], (at.b, plane)
            ).start()
        else:
            x_own[...] = total
    for dz in (1, 2, 3):
        wait_bytes(z_in.at[dz], z_recv.at[dz])
    same = slot_rows(parity)
    gtok_ref[same] = (d1_ref[same] + x_own[...] + z_in[2].astype(F32)).astype(BF16)
    cross = slot_rows(1 - parity)
    gtok_ref[cross] = (d1_ref[cross] + z_in[1].astype(F32) + z_in[3].astype(F32)).astype(BF16)

    wait_bytes(o_in, o_recv)
    gout_ref[...] = (
        o_in[0].astype(F32) + o_in[1].astype(F32) + o_in[2].astype(F32) + o_in[3].astype(F32)
    )
    wait_bytes(w_in, misc_recv.at[2])
    for x in range(2):
        total = w_in[0, x].astype(F32) + w_in[1, x].astype(F32)
        for k, ref in enumerate((gq_ref, gk_ref, gv_ref)):
            ref[:, 128 * x : 128 * x + 128] = total[:, 128 * k : 128 * k + 128]
    wait_bytes(notes_in, misc_recv.at[1])
    total = notes_in[0]
    for d in range(1, 32):
        total += notes_in[d]
    small_ref[...] = total
    take_grads(grecv, gwin_ref, misc_recv.at[0])

    for k in range(2):
        wait_bytes(sib_k, kv_send.at[k])
    out_scatter.scatter_end(sib_out, peer_out)
    wait_bytes(o_in.at[pl.ds(0, 3)], o_send)
    for r in range(4):
        wait_bytes(w_sib_out.at[r], ws_send.at[r])
        if r:
            wait_bytes(x_out.at[r], x_send.at[r])
            wait_bytes(z_out.at[r], z_send.at[r])
    wait_bytes(xs.at[pl.ds(0, 496)], misc_send.at[0])
    wait_bytes(notes.at[pl.ds(0, 31)], misc_send.at[1])

    @pl.when(plane_w == at.z)
    def _():
        wait_bytes(w_out.at[pl.ds(0, 3)], misc_send.at[2])

    @pl.when(plane_w != at.z)
    def _():
        wait_bytes(w_out, misc_send.at[2])


def run_kernel(body, shapes, scratch, ident, args):
    return pl.pallas_call(
        body,
        out_shape=[jax.ShapeDtypeStruct(s, t) for s, t in shapes],
        in_specs=[vmem()] * len(args),
        out_specs=[vmem()] * len(shapes),
        scratch_shapes=scratch,
        compiler_params=pltpu.CompilerParams(
            collective_id=ident, has_side_effects=True, vmem_limit_bytes=VMEM_LIMIT
        ),
    )(*args)


def run_attend(*args):
    shapes = (
        ((1024, 1024), BF16),
        ((1024, 384), BF16),
        ((1024, 128), BF16),
        ((2048, 128), BF16),
        ((2048, 128), BF16),
        ((1024, 128), F32),
        ((1024, 128), F32),
        ((128, 1024), BF16),
        ((1024, 1024), BF16),
        ((8, 1024), F32),
        ((1, 512), F32),
        ((1024, 512), BF16),
    )
    scratch = [
        pltpu.VMEM((32, 16, 128), BF16),
        pltpu.VMEM((256, 384), F32),
        pltpu.VMEM((256, 2048), F32),
        pltpu.VMEM((1024, 128), BF16),
        DMA((4,)),
        DMA((4,)),
        DMA((4, 4)),
        DMA((4, 4)),
        DMA((2,)),
        DMA((2,)),
        DMA((8,)),
        DMA((8,)),
        DMA((2, 4)),
        DMA((2, 4)),
        DMA((3,)),
        DMA((3,)),
    ]
    return run_kernel(attend_kernel, shapes, scratch, 1, args)


def run_ffn(*args):
    shapes = (
        ((128, 1024), BF16),
        ((128, 1024), F32),
        ((128, 1024), BF16),
        ((1024, 128), BF16),
        ((8, 128, 512), BF16),
        ((128, 1024), F32),
        ((8, 1024), F32),
        ((1, 512), F32),
    )
    scratch = [
        pltpu.VMEM((1024, 512), BF16),
        pltpu.VMEM((128, 1024), F32),
        pltpu.VMEM((128, 1024), F32),
        pltpu.VMEM((128, 128), F32),
        pltpu.VMEM((128, 1024), F32),
        pltpu.VMEM((4, 256, 1024), BF16),
        pltpu.VMEM((4, 256, 1024), BF16),
        pltpu.VMEM((4, 256, 512), BF16),
        pltpu.VMEM((4, 256, 512), F32),
        pltpu.VMEM((256, 512), F32),
        pltpu.VMEM((4, 256, 1024), F32),
        pltpu.VMEM((2, 4, 128, 1024), BF16),
        pltpu.VMEM((2, 4, 128, 1024), BF16),
        pltpu.VMEM((2, 4, 128, 1024), BF16),
        pltpu.VMEM((2, 4, 128, 1024), BF16),
        pltpu.VMEM((8, 128, 512), BF16),
        pltpu.VMEM((4, 128, 1024), BF16),
        pltpu.VMEM((128, 1024), BF16),
        DMA((4, 4)),
        DMA((4, 4)),
        DMA((4, 4)),
        DMA((4, 4)),
        DMA,
        DMA,
        DMA,
        DMA,
        DMA,
        DMA,
    ]
    return run_kernel(ffn_kernel, shapes, scratch, 2, args)


def run_grads(*args):
    shapes = (
        ((128, 1024), BF16),
        ((128, 256), F32),
        ((128, 256), F32),
        ((128, 256), F32),
        ((128, 256), F32),
        ((128, 1024), F32),
        ((16, 128), F32),
    )
    scratch = [
        pltpu.VMEM((128, 1024), BF16),
        pltpu.VMEM((128, 1024), BF16),
        pltpu.VMEM((256, 2048), F32),
        pltpu.VMEM((256, 2048), BF16),
        pltpu.VMEM((256, 2048), F32),
        pltpu.VMEM((1024, 128), F32),
        pltpu.VMEM((128, 2048), F32),
        pltpu.VMEM((128, 2048), F32),
        pltpu.VMEM((2048, 128), F32),
        pltpu.VMEM((2048, 128), F32),
        pltpu.VMEM((1024, 128), F32),
        pltpu.VMEM((1024, 128), F32),
        pltpu.VMEM((1024, 384), BF16),
        pltpu.VMEM((4, 256, 1024), F32),
        pltpu.VMEM((4, 256, 1024), BF16),
        pltpu.VMEM((4, 256, 1024), BF16),
        pltpu.VMEM((256, 1024), F32),
        pltpu.VMEM((64, 1024), F32),
        pltpu.VMEM((4, 64, 1024), BF16),
        pltpu.VMEM((4, 64, 1024), BF16),
        pltpu.VMEM((4, 128, 384), F32),
        pltpu.VMEM((4, 128, 384), F32),
        pltpu.VMEM((4, 128, 384), BF16),
        pltpu.VMEM((2, 2, 128, 384), BF16),
        pltpu.VMEM((4, 128, 1024), BF16),
        pltpu.VMEM((4, 128, 1024), BF16),
        pltpu.VMEM((4, 128, 1024), BF16),
        pltpu.VMEM((4, 128, 1024), BF16),
        pltpu.VMEM((128, 1024), BF16),
        pltpu.VMEM((4, 128, 256), BF16),
        pltpu.VMEM((8, 1024), F32),
        pltpu.VMEM((32, 16, 128), F32),
        pltpu.VMEM((32, 16, 128), F32),
        pltpu.VMEM((4, 128, 1024), BF16),
        DMA((2,)),
        DMA((2,)),
        DMA((4,)),
        DMA((4,)),
        DMA((4,)),
        DMA((4,)),
        DMA((4,)),
        DMA((4,)),
        DMA((4,)),
        DMA((4,)),
        DMA((4,)),
        DMA((4,)),
        DMA,
        DMA,
        DMA((3,)),
        DMA((3,)),
    ]
    return run_kernel(grads_kernel, shapes, scratch, 3, args)


def fast_device(
    tokens,
    w_query,
    w_key,
    w_value,
    w_out,
    b_query,
    b_value,
    b_out,
    norm1_gain,
    norm1_shift,
    w_in,
    w_back,
    b_in,
    b_back,
    norm2_gain,
    norm2_shift,
    cotangent,
):
    head_id = lax.axis_index("head")
    token_shape = tokens.shape
    model_dim = tokens.shape[2]
    x = tokens.reshape(-1, model_dim)
    vectors = jnp.stack(
        (b_query, b_value, b_out, norm1_gain, norm1_shift, b_back, norm2_gain, norm2_shift)
    )
    spread = jnp.where(
        lax.broadcasted_iota(jnp.int32, (1, 128), 1) // 32 == head_id,
        jnp.tile(vectors, (1, 4)),
        jnp.zeros((), BF16),
    )
    small = jnp.concatenate((spread, b_in[None], jnp.zeros((7, 128), BF16)), axis=0)
    xs, wqkv, queries, keys_all, values_all, mixed, log_sums, att, wo, par, bins, wi = run_attend(
        x, w_query, w_key, w_value, w_out, small, w_in
    )
    output, d_first, d_branch, da, g_in, gw_back, pg, gbin = run_ffn(
        x, att, wo, cotangent.reshape(-1, model_dim), par, bins, wi, w_back
    )
    grad_tokens, gq, gk, gv, gout, gw_in, notes = run_grads(
        xs,
        wqkv,
        queries,
        keys_all,
        values_all,
        mixed,
        log_sums,
        da,
        d_first,
        att,
        d_branch,
        pg,
        gbin,
        g_in,
    )
    own = lax.dynamic_slice(notes, (0, head_id * 32), (8, 32))
    return (
        output.reshape(token_shape),
        grad_tokens.reshape(token_shape),
        gq,
        gk,
        gv,
        gout.T,
        own[0],
        own[1],
        own[2],
        own[3],
        own[4],
        gw_in,
        gw_back,
        notes[8],
        own[5],
        own[6],
        own[7],
    )


def solution(mesh):
    in_specs = (
        P(None, ("blk", "head"), None),
        P("blk", "head"),
        P("blk", "head"),
        P("blk", "head"),
        P("head", "blk"),
        P(("blk", "head")),
        P(("blk", "head")),
        P(("blk", "head")),
        P(("blk", "head")),
        P(("blk", "head")),
        P("blk", "head"),
        P("blk", "head"),
        P(("blk", "head")),
        P(("blk", "head")),
        P(("blk", "head")),
        P(("blk", "head")),
        P(None, ("blk", "head"), None),
    )
    out_specs = (
        P(None, ("blk", "head"), None),
        P(None, ("blk", "head"), None),
        P("blk", "head"),
        P("blk", "head"),
        P("blk", "head"),
        P("head", "blk"),
        P(("blk", "head")),
        P(("blk", "head")),
        P(("blk", "head")),
        P(("blk", "head")),
        P(("blk", "head")),
        P("blk", "head"),
        P("blk", "head"),
        P(("blk", "head")),
        P(("blk", "head")),
        P(("blk", "head")),
        P(("blk", "head")),
    )
    sizes = (mesh.shape["blk"], mesh.shape["head"])
    body = fast_device if sizes == (8, 4) else per_device
    return jax.shard_map(
        body, mesh=mesh, in_specs=in_specs, out_specs=out_specs, check_vma=False
    )
```

```python
import functools
import math

import jax
import jax.numpy as jnp
from jax import lax
from jax.experimental import pallas as pl
from jax.experimental.pallas import tpu as pltpu
from jax.sharding import PartitionSpec as P

HEAD_DIM = 64


NORM_EPS = 1e-05


def layer_norm(summed, gain, shift):
    centre = jnp.mean(summed, axis=-1, keepdims=True)
    centred = summed - centre
    spread = jnp.mean(centred * centred, axis=-1, keepdims=True)
    return centred * lax.rsqrt(spread + NORM_EPS) * gain + shift


def gelu_exact(inputs):
    return jax.nn.gelu(inputs, approximate=False)


def split_heads(packed):
    return packed.reshape(packed.shape[0], packed.shape[1], -1, HEAD_DIM)


def contract_rows(left, right):
    return lax.dot_general(
        left, right, (((0,), (0,)), ((), ())), preferred_element_type=jnp.float32
    )


def contract_cols(left, right):
    return lax.dot_general(
        left, right, (((1,), (1,)), ((), ())), preferred_element_type=jnp.float32
    )


def score_block(queries4, keys4):
    return jnp.einsum(
        "sqge,skge->sqgk", queries4, keys4, preferred_element_type=jnp.float32
    ) * HEAD_DIM ** (-0.5)


def score_grads(queries4, keys4, values4, grads4, log_sums, deltas):
    probs = jnp.exp(score_block(queries4, keys4) - log_sums[..., None])
    d_probs = jnp.einsum("sqge,skge->sqgk", grads4, values4, preferred_element_type=jnp.float32)
    d_scores = (probs * (d_probs - deltas[..., None])).astype(jnp.bfloat16)
    return (probs.astype(jnp.bfloat16), d_scores)


def token_rows(local):
    return lax.all_gather(local, "head", axis=1, tiled=True)


def token_partials(terms):
    return lax.psum_scatter(
        terms.astype(jnp.bfloat16), "head", scatter_dimension=1, tiled=True
    ).astype(jnp.float32)


def place_part(part, full_len, start):
    return lax.dynamic_update_slice_in_dim(jnp.zeros((full_len,), jnp.float32), part, start, 0)


def per_device(
    tokens,
    w_query,
    w_key,
    w_value,
    w_out,
    b_query,
    b_value,
    b_out,
    norm1_gain,
    norm1_shift,
    w_in,
    w_back,
    b_in,
    b_back,
    norm2_gain,
    norm2_shift,
    cotangent,
):
    f32 = jnp.float32
    bf16 = jnp.bfloat16
    score_scale = HEAD_DIM ** (-0.5)
    bq_full, bv_full, bo_full, gain_one, shift_one, bin_full, bback_full, gain_two, shift_two = (
        lax.all_gather(b_query, ("blk", "head"), axis=0, tiled=True),
        lax.all_gather(b_value, ("blk", "head"), axis=0, tiled=True),
        lax.all_gather(b_out, ("blk", "head"), axis=0, tiled=True),
        lax.all_gather(norm1_gain, ("blk", "head"), axis=0, tiled=True),
        lax.all_gather(norm1_shift, ("blk", "head"), axis=0, tiled=True),
        lax.all_gather(b_in, ("blk", "head"), axis=0, tiled=True),
        lax.all_gather(b_back, ("blk", "head"), axis=0, tiled=True),
        lax.all_gather(norm2_gain, ("blk", "head"), axis=0, tiled=True),
        lax.all_gather(norm2_shift, ("blk", "head"), axis=0, tiled=True),
    )
    attn_cols, out_rows, ffn_cols = (
        lax.all_gather(jnp.stack((w_query, w_key, w_value)), "blk", axis=1, tiled=True),
        lax.all_gather(w_out, "blk", axis=1, tiled=True),
        lax.all_gather(jnp.stack((w_in, w_back)), "blk", axis=1, tiled=True),
    )
    seq_count, local_len, model_dim = tokens.shape
    token_shape = (seq_count, local_len, model_dim)
    head_id = lax.axis_index("head")
    width_part = attn_cols.shape[2]
    bq_part = lax.dynamic_slice_in_dim(bq_full, head_id * width_part, width_part).astype(f32)
    bv_part = lax.dynamic_slice_in_dim(bv_full, head_id * width_part, width_part).astype(f32)
    wide_rows = token_rows(tokens)
    wide_len = wide_rows.shape[1]
    wide_flat = wide_rows.reshape(-1, model_dim)
    head_shape = (seq_count, wide_len, width_part)
    wide_shape = (seq_count, wide_len, model_dim)
    query_heads = (
        (jnp.dot(wide_flat, attn_cols[0], preferred_element_type=f32) + bq_part)
        .astype(bf16)
        .reshape(head_shape)
    )
    key_heads = (
        jnp.dot(wide_flat, attn_cols[1], preferred_element_type=f32)
        .astype(bf16)
        .reshape(head_shape)
    )
    value_heads = (
        (jnp.dot(wide_flat, attn_cols[2], preferred_element_type=f32) + bv_part)
        .astype(bf16)
        .reshape(head_shape)
    )
    query4 = split_heads(query_heads)
    key4 = split_heads(key_heads)
    value4 = split_heads(value_heads)
    stat_shape = query4.shape[:3]
    pieces = (
        lax.all_gather(key_heads, "blk", axis=1, tiled=True),
        lax.all_gather(value_heads, "blk", axis=1, tiled=True),
    )
    maxima = jnp.full(stat_shape, -1e30, f32)
    scores = score_block(query4, split_heads(pieces[0]))
    new_max = jnp.maximum(maxima, jnp.max(scores, axis=-1))
    weights = jnp.exp(scores - new_max[..., None])
    totals = jnp.sum(weights, axis=-1)
    summed = jnp.einsum(
        "sqgk,skge->sqge", weights.astype(bf16), split_heads(pieces[1]), preferred_element_type=f32
    )
    maxima, totals, summed = (new_max, totals, summed)
    log_sums = maxima + jnp.log(totals)
    attended4 = summed / totals[..., None]
    attended_heads = attended4.reshape(head_shape).astype(bf16)
    attended_flat = attended_heads.reshape(-1, width_part)
    branch_terms = jnp.dot(attended_flat, out_rows, preferred_element_type=f32).reshape(wide_shape)
    branch = token_partials(branch_terms).reshape(-1, model_dim) + bo_full.astype(f32)
    flat_rows = tokens.reshape(-1, model_dim)
    normed, norm1_pull = jax.vjp(
        layer_norm, flat_rows.astype(f32) + branch, gain_one.astype(f32), shift_one.astype(f32)
    )
    normed_low = normed.astype(bf16)
    ffn_full = lax.all_gather(ffn_cols, "head", axis=2, tiled=True)
    pre_act = jnp.dot(normed_low, ffn_full[0], preferred_element_type=f32) + bin_full.astype(f32)
    hidden_act, gelu_pull = jax.vjp(gelu_exact, pre_act)
    hidden_low = hidden_act.astype(bf16)
    ffn_out = contract_cols(hidden_low, ffn_full[1]) + bback_full.astype(f32)
    final, norm2_pull = jax.vjp(
        layer_norm, normed + ffn_out, gain_two.astype(f32), shift_two.astype(f32)
    )
    output = final.astype(bf16).reshape(token_shape)
    d_second, grad_norm2_gain, grad_norm2_shift = norm2_pull(
        cotangent.reshape(-1, model_dim).astype(f32)
    )
    d_ffn = d_second.astype(bf16)
    grad_b_back = jnp.sum(d_ffn.astype(f32), axis=0)
    grad_back_whole = contract_rows(d_ffn, hidden_low)
    d_hidden = jnp.dot(d_ffn, ffn_full[1], preferred_element_type=f32)
    d_pre = gelu_pull(d_hidden)[0].astype(bf16)
    grad_b_in = jnp.sum(d_pre.astype(f32), axis=0)
    grad_in_whole = contract_rows(normed_low, d_pre)
    ffn_grad_parts = lax.psum_scatter(
        jnp.stack((grad_in_whole, grad_back_whole)).astype(jnp.bfloat16),
        "head",
        scatter_dimension=2,
        tiled=True,
    ).astype(jnp.float32)
    d_normed = d_second + contract_cols(d_pre, ffn_full[0])
    d_first, grad_norm1_gain, grad_norm1_shift = norm1_pull(d_normed)
    d_branch = d_first.astype(bf16)
    grad_b_out = jnp.sum(d_branch.astype(f32), axis=0)
    wide_dbranch = token_rows(d_branch.reshape(token_shape)).reshape(-1, model_dim)
    grad_out_part = contract_rows(attended_flat, wide_dbranch)
    grad_heads = contract_cols(wide_dbranch, out_rows).astype(bf16).reshape(head_shape)
    grads4 = split_heads(grad_heads)
    deltas = jnp.sum(grads4.astype(f32) * attended4, axis=-1)
    row_stats = (
        lax.all_gather(log_sums, "blk", axis=1, tiled=True),
        lax.all_gather(deltas, "blk", axis=1, tiled=True),
    )
    pieces = (
        lax.all_gather(key_heads, "blk", axis=1, tiled=True),
        lax.all_gather(value_heads, "blk", axis=1, tiled=True),
        lax.all_gather(query_heads, "blk", axis=1, tiled=True),
        lax.all_gather(grad_heads, "blk", axis=1, tiled=True),
    )
    piece_keys = split_heads(pieces[0])
    piece_values = split_heads(pieces[1])
    piece_queries = split_heads(pieces[2])
    piece_grads = split_heads(pieces[3])
    piece_sums = row_stats[0]
    piece_deltas = row_stats[1]
    own_probs, own_scores = score_grads(query4, piece_keys, piece_values, grads4, log_sums, deltas)
    d_query = score_scale * jnp.einsum(
        "sqgk,skge->sqge", own_scores, piece_keys, preferred_element_type=f32
    )
    probs_low, d_scores = score_grads(
        piece_queries, key4, value4, piece_grads, piece_sums, piece_deltas
    )
    key_acc = score_scale * jnp.einsum(
        "sqgk,sqge->skge", d_scores, piece_queries, preferred_element_type=f32
    )
    value_acc = jnp.einsum("sqgk,sqge->skge", probs_low, piece_grads, preferred_element_type=f32)
    d_query_low = d_query.reshape(-1, width_part).astype(bf16)
    d_key_low = key_acc.reshape(-1, width_part).astype(bf16)
    d_value_low = value_acc.reshape(-1, width_part).astype(bf16)
    grad_b_query = place_part(
        jnp.sum(d_query_low.astype(f32), axis=0), model_dim, head_id * width_part
    )
    grad_b_value = place_part(
        jnp.sum(d_value_low.astype(f32), axis=0), model_dim, head_id * width_part
    )
    attn_grad_parts = jnp.stack(
        (
            contract_rows(wide_flat, d_query_low),
            contract_rows(wide_flat, d_key_low),
            contract_rows(wide_flat, d_value_low),
        )
    )
    token_terms = (
        contract_cols(d_query_low, attn_cols[0])
        + contract_cols(d_key_low, attn_cols[1])
        + contract_cols(d_value_low, attn_cols[2])
    )
    d_tokens = d_first + token_partials(token_terms.reshape(wide_shape)).reshape(-1, model_dim)
    grad_tokens = d_tokens.astype(bf16).reshape(token_shape)
    attn_sums, grad_w_out, ffn_sums = (
        lax.psum_scatter(attn_grad_parts, "blk", scatter_dimension=1, tiled=True),
        lax.psum_scatter(grad_out_part, "blk", scatter_dimension=1, tiled=True),
        lax.psum_scatter(ffn_grad_parts, "blk", scatter_dimension=1, tiled=True),
    )
    (
        grad_b_query,
        grad_b_value,
        grad_b_out,
        grad_norm1_gain,
        grad_norm1_shift,
        grad_b_in,
        grad_b_back,
        grad_norm2_gain,
        grad_norm2_shift,
    ) = (
        lax.psum_scatter(grad_b_query, ("blk", "head"), scatter_dimension=0, tiled=True),
        lax.psum_scatter(grad_b_value, ("blk", "head"), scatter_dimension=0, tiled=True),
        lax.psum_scatter(grad_b_out, ("blk", "head"), scatter_dimension=0, tiled=True),
        lax.psum_scatter(grad_norm1_gain, ("blk", "head"), scatter_dimension=0, tiled=True),
        lax.psum_scatter(grad_norm1_shift, ("blk", "head"), scatter_dimension=0, tiled=True),
        lax.psum_scatter(grad_b_in, ("blk", "head"), scatter_dimension=0, tiled=True),
        lax.psum_scatter(grad_b_back, ("blk", "head"), scatter_dimension=0, tiled=True),
        lax.psum_scatter(grad_norm2_gain, ("blk", "head"), scatter_dimension=0, tiled=True),
        lax.psum_scatter(grad_norm2_shift, ("blk", "head"), scatter_dimension=0, tiled=True),
    )
    return (
        output,
        grad_tokens,
        attn_sums[0],
        attn_sums[1],
        attn_sums[2],
        grad_w_out,
        grad_b_query,
        grad_b_value,
        grad_b_out,
        grad_norm1_gain,
        grad_norm1_shift,
        ffn_sums[0],
        ffn_sums[1],
        grad_b_in,
        grad_b_back,
        grad_norm2_gain,
        grad_norm2_shift,
    )


MESH = pl.DeviceIdType.MESH
F32 = jnp.float32
BF16 = jnp.bfloat16
VMEM_LIMIT = 60 * 2**20


def dot_nn(left, right):
    return jnp.dot(left, right, preferred_element_type=F32)


class Place:
    def __init__(self):
        self.b = lax.axis_index("blk")
        self.z = lax.axis_index("head")
        self.y = self.b // 4
        self.x = (self.b // 2) % 2
        self.c = self.b % 2
        self.q = self.b // 2

    def chip(self, r):
        return ((self.y + r // 2) % 2) * 2 + (self.x + r % 2) % 2

    def peer(self, r):
        return (2 * self.chip(r) + self.c, self.z)

    def sibling(self):
        return (2 * self.q + 1 - self.c, self.z)


def remote(src, dst, send_sem, recv_sem, device):
    return pltpu.make_async_remote_copy(
        src_ref=src,
        dst_ref=dst,
        send_sem=send_sem,
        recv_sem=recv_sem,
        device_id=device,
        device_id_type=MESH,
    )


def wait_bytes(view, sem):
    pltpu.make_async_copy(view, view, sem).wait()


def greet_all(at):
    barrier = pltpu.get_barrier_semaphore()
    flat = at.b * 4 + at.z

    def greet(step, carry):
        other = (flat + step) % 32
        pl.semaphore_signal(
            barrier, inc=1, device_id=(other // 4, other % 4), device_id_type=MESH
        )
        return carry

    lax.fori_loop(1, 32, greet, 0)
    pl.semaphore_wait(barrier, 31)


def half(core):
    return pl.ds(pl.multiple_of(core * 128, 128), 128)


def lanes(index):
    return pl.ds(pl.multiple_of(index * 128, 128), 128)


def by_rows(count, size, step):
    def body(i, carry):
        step(pl.ds(pl.multiple_of(i * size, size), size))
        return carry

    lax.fori_loop(0, count // size, body, 0)


def row_sums(count, size, width, step):
    def body(i, carry):
        parts = step(pl.ds(pl.multiple_of(i * size, size), size))
        return tuple(
            kept + jnp.sum(part.reshape(size // 8, 8, width), axis=0)
            for kept, part in zip(carry, parts)
        )

    n = step.count
    sums = lax.fori_loop(
        0, count // size, body, tuple(jnp.zeros((8, width), F32) for _ in range(n))
    )
    return tuple(jnp.sum(s, axis=0, keepdims=True) for s in sums)


class Exchange:
    def __init__(self, at, send, recv, send_sib, recv_sib):
        self.at, self.send, self.recv = at, send, recv
        self.send_sib, self.recv_sib = send_sib, recv_sib

    def gather_start(self, slots):
        at = self.at
        mine = slots.at[at.q, half(at.c)]
        for r in (1, 2, 3):
            remote(mine, mine, self.send.at[r], self.recv.at[r], at.peer(r)).start()
        remote(mine, mine, self.send_sib.at[0], self.recv_sib.at[0], at.sibling()).start()

    def gather_step(self, slots, r):
        at = self.at
        chip = at.chip(r)
        block = slots.at[chip, half(at.c)]
        if r:
            wait_bytes(block, self.recv.at[r])
            remote(
                block, block, self.send_sib.at[r], self.recv_sib.at[r], at.sibling()
            ).start()
        wait_bytes(slots.at[chip, half(1 - at.c)], self.recv_sib.at[r])
        return chip

    def gather_end(self, slots):
        at = self.at
        for r in range(4):
            block = slots.at[at.chip(r), half(at.c)]
            if r:
                wait_bytes(slots.at[at.q, half(at.c)], self.send.at[r])
            wait_bytes(block, self.send_sib.at[r])

    def scatter_put(self, terms, out_sib, in_sib, r):
        at = self.at
        out_sib[r] = terms[r, half(1 - at.c)].astype(BF16)
        remote(
            out_sib.at[r], in_sib.at[r], self.send_sib.at[r], self.recv_sib.at[r], at.sibling()
        ).start()

    def scatter_pass(self, terms, in_sib, out, into, r):
        at = self.at
        wait_bytes(in_sib.at[r], self.recv_sib.at[r])
        total = terms[r, half(at.c)] + in_sib[r].astype(F32)
        if r:
            out[r] = total.astype(BF16)
            remote(out.at[r], into.at[r], self.send.at[r], self.recv.at[r], at.peer(r)).start()
        else:
            terms[0, half(at.c)] = total

    def scatter_arrive(self, into):
        for r in (1, 2, 3):
            wait_bytes(into.at[r], self.recv.at[r])

    def scatter_end(self, out_sib, out):
        for r in range(4):
            wait_bytes(out_sib.at[r], self.send_sib.at[r])
            if r:
                wait_bytes(out.at[r], self.send.at[r])


def norm_rows(values):
    centre = jnp.mean(values, axis=-1, keepdims=True)
    centred = values - centre
    spread = jnp.mean(centred * centred, axis=-1, keepdims=True)
    scale = lax.rsqrt(spread + NORM_EPS)
    return centred * scale, scale


def norm_back(grad, unit, scale):
    centre = jnp.mean(grad, axis=-1, keepdims=True)
    along = jnp.mean(grad * unit, axis=-1, keepdims=True)
    return (grad - centre - unit * along) * scale


def send_or_copy(src, dst, send_sem, recv_sem, device, own):
    def away():
        remote(src, dst, send_sem, recv_sem, device).start()

    if own is None:
        away()
        return
    pl.when(jnp.logical_not(own))(away)

    @pl.when(own)
    def _():
        pltpu.make_async_copy(src, dst, recv_sem).start()


class Column:
    def __init__(self, at, ref, sems):
        self.at, self.ref = at, ref
        self.up_send, self.up_recv, self.down_send, self.down_recv = sems

    def block(self, plane):
        return self.ref.at[:, lanes(plane)]

    def sides(self, hop, act, arriving):
        z = self.at.z
        if arriving:
            below, above = z - 1 - hop, z + 1 + hop
            pl.when(below >= 0)(lambda: act(self.block(below), 0))
            pl.when(above <= 3)(lambda: act(self.block(above), 1))
        else:
            up = jnp.logical_and(z >= hop, z < 3)
            down = jnp.logical_and(z + hop <= 3, z > 0)
            pl.when(up)(lambda: act(self.block(z - hop), 0))
            pl.when(down)(lambda: act(self.block(z + hop), 1))

    def send(self, hop):
        def act(block, side):
            send = (self.up_send, self.down_send)[side].at[hop]
            recv = (self.up_recv, self.down_recv)[side].at[hop]
            remote(block, block, send, recv, (self.at.b, self.at.z + 1 - 2 * side)).start()

        self.sides(hop, act, False)

    def arrive(self, hop):
        def act(block, side):
            wait_bytes(block, (self.up_recv, self.down_recv)[side].at[hop])

        self.sides(hop, act, True)

    def end(self):
        def wait(hop):
            def act(block, side):
                wait_bytes(block, (self.up_send, self.down_send)[side].at[hop])

            return act

        for hop in range(3):
            self.sides(hop, wait(hop), False)


def plane_weights(at, src, dst, send_sem, recv_sem):
    rows, cols = lanes(at.b), lanes(at.z)
    pltpu.make_async_copy(src.at[:, lanes(at.b)], dst.at[rows, cols], recv_sem).start()

    def push(step, carry):
        other = (at.b + step) % 8
        remote(
            src.at[:, lanes(other)], dst.at[rows, cols], send_sem, recv_sem, (other, at.z)
        ).start()
        return carry

    lax.fori_loop(1, 8, push, 0)


def column_grads(at, blocks, into, send_sem, recv_sem):
    for dz in (2, 1, 3):
        plane = (at.z + dz) % 4
        remote(
            blocks.at[:, :, lanes(plane)],
            into.at[dz],
            send_sem.at[dz],
            recv_sem.at[dz],
            (at.b, plane),
        ).start()


def plane_grads(at, blocks, into, sums, final, recv_sem, send_out, recv_out):
    for dz in (1, 3, 2):
        wait_bytes(into.at[dz], recv_sem.at[dz])

    def one(step, carry):
        other = (at.b + 1 + step) % 8
        sums[other] = (
            blocks[other, :, lanes(at.z)].astype(F32)
            + into[1, other].astype(F32)
            + into[2, other].astype(F32)
            + into[3, other].astype(F32)
        ).astype(BF16)
        send_or_copy(
            sums.at[other],
            final.at[:, lanes(at.b)],
            send_out,
            recv_out,
            (other, at.z),
            step == 7,
        )
        return carry

    lax.fori_loop(0, 8, one, 0)


def head_mask(h):
    lane = lax.broadcasted_iota(jnp.int32, (1, 128), 1)
    return jnp.where(lane // HEAD_DIM == h, 1.0, 0.0).astype(F32)


def slot_rows(index):
    return pl.ds(pl.multiple_of(index * 64, 64), 64)


def chip_rows(index):
    return pl.ds(pl.multiple_of(index * 256, 256), 256)


def core_rows(index):
    return pl.ds(pl.multiple_of(index * 1024, 1024), 1024)


INPUTS = ("x", "wq", "wk", "wv", "wout", "small", "win", "wback", "cot")

RESULTS = (
    ("out", (128, 1024), BF16),
    ("gtok", (128, 1024), BF16),
    ("w_in", (2, 2, 128, 384), BF16),
    ("o_in", (4, 128, 256), BF16),
    ("fin_in", (128, 1024), BF16),
    ("fin_back", (128, 1024), BF16),
    ("notes_in", (32, 16, 128), F32),
)

SCRATCH = (
    ("xs", (1024, 1024), BF16),
    ("wqkv", (1024, 384), BF16),
    ("queries", (1024, 128), BF16),
    ("keys_all", (2048, 128), BF16),
    ("values_all", (2048, 128), BF16),
    ("mixed", (1024, 128), F32),
    ("log_sums", (1024, 128), F32),
    ("att", (128, 1024), BF16),
    ("wo", (1024, 1024), BF16),
    ("par", (8, 1024), F32),
    ("bins", (1, 512), F32),
    ("wi", (1024, 512), BF16),
    ("wb", (1024, 512), BF16),
    ("smalls", (32, 16, 128), BF16),
    ("proj", (256, 384), F32),
    ("scores", (256, 2048), F32),
    ("d_buf", (256, 2048), F32),
    ("p_buf", (256, 2048), BF16),
    ("att_send", (1024, 128), BF16),
    ("n1", (128, 1024), F32),
    ("unit1", (128, 1024), F32),
    ("scale1", (128, 128), F32),
    ("d2", (128, 1024), F32),
    ("d1", (128, 1024), F32),
    ("db", (128, 1024), BF16),
    ("norm_slots", (4, 256, 1024), BF16),
    ("grad_slots", (4, 256, 1024), BF16),
    ("hid", (4, 256, 512), BF16),
    ("slope", (4, 256, 512), F32),
    ("pre", (256, 512), F32),
    ("terms", (4, 256, 1024), F32),
    ("sib_out", (2, 4, 128, 1024), BF16),
    ("sib_in", (2, 4, 128, 1024), BF16),
    ("peer_out", (2, 4, 128, 1024), BF16),
    ("peer_in", (2, 4, 128, 1024), BF16),
    ("g_back", (8, 128, 512), BF16),
    ("g_in", (8, 128, 512), BF16),
    ("zg_back", (4, 8, 128, 128), BF16),
    ("zg_in", (4, 8, 128, 128), BF16),
    ("gs_back", (8, 128, 128), BF16),
    ("gs_in", (8, 128, 128), BF16),
    ("da_send", (128, 1024), BF16),
    ("da", (1024, 128), BF16),
    ("q_turned", (128, 1024), BF16),
    ("da_turned", (128, 1024), BF16),
    ("dq", (1024, 128), F32),
    ("dk_turned", (128, 2048), F32),
    ("dv_turned", (128, 2048), F32),
    ("out_k", (1024, 128), F32),
    ("out_v", (1024, 128), F32),
    ("sib_k", (1024, 128), F32),
    ("sib_v", (1024, 128), F32),
    ("dqkv", (1024, 384), BF16),
    ("x_in", (4, 256, 1024), BF16),
    ("x_sum", (256, 1024), F32),
    ("x_own", (64, 1024), F32),
    ("z_out", (4, 64, 1024), BF16),
    ("z_in", (4, 64, 1024), BF16),
    ("w_sib_out", (4, 128, 384), F32),
    ("w_sib_in", (4, 128, 384), F32),
    ("w_out", (4, 128, 384), BF16),
    ("o_out", (128, 1024), BF16),
    ("vec", (8, 1024), F32),
    ("gbin", (1, 512), F32),
    ("notes", (32, 16, 128), F32),
)

SEMAPHORES = (
    ("z", (4,)),
    ("p", (4, 4)),
    ("w", (2,)),
    ("o", (8,)),
    ("kv", (2, 4)),
    ("misc", (12,)),
    ("col", (4, 3)),
    ("ex", (5, 4)),
    ("ex_sib", (5, 4)),
    ("zg", (2, 4)),
    ("kv2", (2,)),
    ("dx", (4, 4)),
    ("dz", (4,)),
    ("ws", (4,)),
)


class Refs:
    pass


def layer_kernel(*refs):
    v = Refs()
    names = list(INPUTS) + [n for n, _, _ in RESULTS] + [n for n, _, _ in SCRATCH]
    for n, _ in SEMAPHORES:
        names += ["s_" + n, "r_" + n]
    for name, ref in zip(names, refs):
        setattr(v, name, ref)
    at = Place()
    at.flat = at.b * 4 + at.z
    at.place = at.q * 4 + at.z
    at.parity = at.z % 2
    at.pair = 4 * (at.z // 2) + at.q
    col_in = Column(at, v.wi, [s.at[0] for s in (v.s_col, v.r_col)] + [s.at[1] for s in (v.s_col, v.r_col)])
    col_back = Column(at, v.wb, [s.at[2] for s in (v.s_col, v.r_col)] + [s.at[3] for s in (v.s_col, v.r_col)])
    exchanges = [
        Exchange(at, v.s_ex.at[i], v.r_ex.at[i], v.s_ex_sib.at[i], v.r_ex_sib.at[i])
        for i in range(5)
    ]
    greet_all(at)
    attend_phase(at, v, col_in, col_back)
    ffn_phase(at, v, col_in, col_back, exchanges)
    grads_phase(at, v, exchanges[0], exchanges[4])
    end_phase(at, v, col_in, col_back, exchanges)


def attend_phase(at, v, col_in, col_back):
    xs, wqkv, wo = v.xs, v.wqkv, v.wo
    parity, pair = at.parity, at.pair

    for dz in (1, 3, 2):
        plane = (at.z + dz) % 4
        remote(
            v.x.at[slot_rows(plane % 2)],
            xs.at[slot_rows(at.place)],
            v.s_z.at[dz],
            v.r_z.at[dz],
            (at.b, plane),
        ).start()
    pltpu.make_async_copy(
        v.x.at[slot_rows(parity)], xs.at[slot_rows(at.place)], v.r_z.at[0]
    ).start()
    plane_weights(at, v.win, v.wi, v.s_misc.at[0], v.r_misc.at[0])

    for dx in range(2):
        for dz in range(2):
            column = (at.x + dx) % 2
            plane = 2 * (at.z // 2) + (at.z + dz) % 2
            target = 2 * (parity * 2 + column) + at.c
            mine = jnp.logical_and(
                parity == at.y, jnp.logical_and(column == at.x, plane == at.z)
            )
            for k, w in enumerate((v.wq, v.wk, v.wv)):
                send_or_copy(
                    w.at[:, lanes(column)],
                    wqkv.at[lanes(at.b), pl.ds(k * 128, 128)],
                    v.s_w.at[0],
                    v.r_w.at[0],
                    (target, plane),
                    mine if dx == 0 and dz == 0 else None,
                )

    pltpu.make_async_copy(v.small, v.smalls.at[at.flat], v.r_misc.at[1]).start()

    def spread(step, carry):
        other = (at.flat + step) % 32
        remote(
            v.small,
            v.smalls.at[at.flat],
            v.s_misc.at[1],
            v.r_misc.at[1],
            (other // 4, other % 4),
        ).start()
        return carry

    lax.fori_loop(1, 32, spread, 0)

    part = wo.at[pl.ds(pl.multiple_of(at.z * 256, 256), 256), lanes(at.b)]
    pltpu.make_async_copy(v.wout, part, v.r_o.at[0]).start()
    for dz in range(1, 4):
        remote(v.wout, part, v.s_o.at[0], v.r_o.at[0], (at.b, (at.z + dz) % 4)).start()

    for dz in (0, 1, 3, 2):
        block = xs.at[slot_rows(at.q * 4 + (at.z - dz + 4) % 4)]
        wait_bytes(block, v.r_z.at[dz])
        for r in (1, 2, 3):
            remote(block, block, v.s_p.at[r, dz], v.r_p.at[r, dz], at.peer(r)).start()

    wait_bytes(v.wi.at[:, pl.ds(0, 128)], v.r_misc.at[0])
    col_in.send(0)

    wait_bytes(wqkv.at[pl.ds(0, 512)], v.r_w.at[0])
    for r in range(4):
        part = wqkv.at[lanes(2 * at.chip(r) + at.c)]
        remote(part, part, v.s_w.at[1], v.r_w.at[1], at.sibling()).start()

    wait_bytes(v.smalls, v.r_misc.at[1])
    for b in range(8):
        total = v.smalls[4 * b].astype(F32)
        for z in range(1, 4):
            total += v.smalls[4 * b + z].astype(F32)
        v.par[:, 128 * b : 128 * b + 128] = total[0:8]
    for h in range(4):
        v.bins[0:1, 128 * h : 128 * h + 128] = v.smalls[8 * h + at.b].astype(F32)[8:9]
    bias_q = v.par[0:1, lanes(pair)]
    bias_v = v.par[1:2, lanes(pair)]
    wait_bytes(wqkv.at[pl.ds(0, 512)], v.r_w.at[1])

    for r in range(4):
        chip = at.chip(r)
        if r:
            for dz in (0, 1, 3, 2):
                wait_bytes(xs.at[slot_rows(0)], v.r_p.at[r, dz])
        rows = chip_rows(chip)
        v.proj[...] = dot_nn(xs[rows], wqkv[...])
        v.queries[rows] = (v.proj[:, 0:128] + bias_q).astype(BF16)
        own_rows = chip_rows(at.c * 4 + chip)
        v.keys_all[own_rows] = v.proj[:, 128:256].astype(BF16)
        v.values_all[own_rows] = (v.proj[:, 256:384] + bias_v).astype(BF16)
        for k, ref in enumerate((v.keys_all, v.values_all)):
            view = ref.at[own_rows]
            remote(view, view, v.s_kv.at[k, r], v.r_kv.at[k, r], at.sibling()).start()
        if r == 1:
            col_in.arrive(0)
            col_in.send(1)
            plane_weights(at, v.wback, v.wb, v.s_misc.at[2], v.r_misc.at[2])

    whole = wo.at[:, lanes(at.b)]
    wait_bytes(whole, v.r_o.at[0])
    for r in (1, 2, 3):
        remote(whole, whole, v.s_o.at[r], v.r_o.at[r], at.peer(r)).start()
    remote(whole, whole, v.s_o.at[4], v.r_o.at[4], at.sibling()).start()
    col_in.arrive(1)
    col_in.send(2)
    wait_bytes(v.wb.at[:, pl.ds(0, 128)], v.r_misc.at[2])
    col_back.send(0)

    for r in range(4):
        for k, ref in enumerate((v.keys_all, v.values_all)):
            wait_bytes(ref.at[pl.ds(0, 256)], v.r_kv.at[k, r])

    scores = v.scores

    def attend(step, carry):
        chip = (at.q + 1 + step) % 4
        rows = chip_rows(chip)
        outs = []
        logs = []
        for h in range(2):
            q = (v.queries[rows].astype(F32) * head_mask(h) * HEAD_DIM**-0.5).astype(BF16)
            scores[...] = contract_cols(q, v.keys_all[...])
            top = jnp.max(scores[...], axis=-1, keepdims=True)
            weights = jnp.exp(scores[...] - top)
            total = jnp.sum(weights, axis=-1, keepdims=True)
            outs.append(dot_nn(weights.astype(BF16), v.values_all[...]) / total)
            logs.append(top + jnp.log(total))
        first = head_mask(0) > 0.5
        merged = jnp.where(first, outs[0], outs[1])
        v.mixed[rows] = merged
        v.log_sums[rows] = jnp.where(first, logs[0], logs[1])
        v.att_send[rows] = merged.astype(BF16)
        for k in range(4):
            plane = (at.z + 1 + k) % 4
            send_or_copy(
                v.att_send.at[slot_rows(chip * 4 + plane)],
                v.att.at[slot_rows(parity), lanes(pair)],
                v.s_misc.at[3],
                v.r_misc.at[3],
                (2 * chip + at.c, plane),
                step == 3 if k == 3 else None,
            )
        return carry

    lax.fori_loop(0, 4, attend, 0)

    col_back.arrive(0)
    col_back.send(1)
    for r in (1, 2, 3):
        part = wo.at[:, lanes(2 * at.chip(r) + at.c)]
        wait_bytes(part, v.r_o.at[r])
        remote(part, part, v.s_o.at[4 + r], v.r_o.at[4 + r], at.sibling()).start()
    for r in range(4):
        wait_bytes(whole, v.r_o.at[4 + r])
    wait_bytes(v.att, v.r_misc.at[3])


def ffn_phase(at, v, col_in, col_back, exchanges):
    n1, terms = v.n1, v.terms
    sib_out, sib_in, peer_out, peer_in = v.sib_out, v.sib_in, v.peer_out, v.peer_in
    gather, scatter, gather2, scatter2 = exchanges[:4]

    def param(i):
        return v.par[i : i + 1, :]

    n1[...] = dot_nn(v.att[...], v.wo[...])

    def first_norm(rows):
        unit, scale = norm_rows(v.x[rows].astype(F32) + n1[rows] + param(2))
        v.unit1[rows] = unit
        v.scale1[rows] = jnp.broadcast_to(scale, (32, 128))
        n1[rows] = unit * param(3) + param(4)

    by_rows(128, 32, first_norm)
    v.norm_slots[at.q, half(at.c)] = n1[...].astype(BF16)
    gather.gather_start(v.norm_slots)

    col_in.arrive(2)
    col_back.arrive(1)
    col_back.send(2)
    col_back.arrive(2)

    for r in range(4):
        chip = gather.gather_step(v.norm_slots, r)
        v.pre[...] = dot_nn(v.norm_slots[chip], v.wi[...])

        def activate(rows, r=r):
            u = v.pre[rows] + v.bins[...]
            cdf = 0.5 * (1.0 + lax.erf(u * math.sqrt(0.5)))
            bell = jnp.exp(-0.5 * u * u) * (1.0 / math.sqrt(2.0 * math.pi))
            v.hid[r, rows] = (u * cdf).astype(BF16)
            v.slope[r, rows] = cdf + u * bell

        by_rows(256, 32, activate)
        terms[r] = contract_cols(v.hid[r], v.wb[...])
        scatter.scatter_put(terms, sib_out.at[0], sib_in.at[0], r)
        if r:
            scatter.scatter_pass(terms, sib_in.at[0], peer_out.at[0], peer_in.at[0], r - 1)
    scatter.scatter_pass(terms, sib_in.at[0], peer_out.at[0], peer_in.at[0], 3)
    scatter.scatter_arrive(peer_in.at[0])

    base = pl.multiple_of(at.c * 128, 128)

    def second_norm(rows):
        own = pl.ds(pl.multiple_of(base + rows.start, 32), 32)
        total = (
            terms[0, own]
            + peer_in[0, 1, rows].astype(F32)
            + peer_in[0, 2, rows].astype(F32)
            + peer_in[0, 3, rows].astype(F32)
        )
        unit, scale = norm_rows(n1[rows] + total + param(5))
        v.out[rows] = (unit * param(6) + param(7)).astype(BF16)
        g = v.cot[rows].astype(F32)
        d = norm_back(g * param(6), unit, scale)
        v.d2[rows] = d
        low = d.astype(BF16)
        v.grad_slots[at.q, own] = low
        return g * unit, g, low.astype(F32)

    second_norm.count = 3
    sums = row_sums(128, 32, 1024, second_norm)
    v.vec[6:7, :] = sums[0]
    v.vec[7:8, :] = sums[1]
    v.vec[5:6, :] = sums[2]

    gather2.gather_start(v.grad_slots)
    gbin = jnp.zeros((1, 512), F32)
    for r in range(4):
        chip = gather2.gather_step(v.grad_slots, r)
        v.pre[...] = dot_nn(v.grad_slots[chip], v.wb[...])

        def deactivate(rows, r=r):
            low = (v.pre[rows] * v.slope[r, rows]).astype(BF16)
            v.pre[rows] = low.astype(F32)
            return (low.astype(F32),)

        deactivate.count = 1
        gbin = gbin + row_sums(256, 32, 512, deactivate)[0]
        v.slope[r] = v.pre[...]
        terms[r] = contract_cols(v.pre[...].astype(BF16), v.wi[...])
        if r == 0:
            scatter.scatter_end(sib_out.at[0], peer_out.at[0])
        scatter2.scatter_put(terms, sib_out.at[1], sib_in.at[1], r)
        if r:
            scatter2.scatter_pass(terms, sib_in.at[1], peer_out.at[1], peer_in.at[1], r - 1)
    scatter2.scatter_pass(terms, sib_in.at[1], peer_out.at[1], peer_in.at[1], 3)
    v.gbin[...] = gbin

    def weight_grad(slots, right, into):
        def one(step, carry):
            other = (at.b + step) % 8
            total = jnp.zeros((128, 512), F32)
            for r in range(4):
                total += contract_rows(slots[at.chip(r), :, lanes(other)], right(r))
            into[other] = total.astype(BF16)
            return carry

        lax.fori_loop(0, 8, one, 0)

    weight_grad(v.grad_slots, lambda r: v.hid[r], v.g_back)
    column_grads(at, v.g_back, v.zg_back, v.s_zg.at[0], v.r_zg.at[0])
    weight_grad(v.norm_slots, lambda r: v.slope[r].astype(BF16), v.g_in)

    scatter2.scatter_arrive(peer_in.at[1])

    def first_back(rows):
        own = pl.ds(pl.multiple_of(base + rows.start, 32), 32)
        total = (
            v.d2[rows]
            + terms[0, own]
            + peer_in[1, 1, rows].astype(F32)
            + peer_in[1, 2, rows].astype(F32)
            + peer_in[1, 3, rows].astype(F32)
        )
        unit = v.unit1[rows]
        d = norm_back(total * param(3), unit, v.scale1[rows][:, :1])
        v.d1[rows] = d
        low = d.astype(BF16)
        v.db[rows] = low
        return total * unit, total, low.astype(F32)

    first_back.count = 3
    sums = row_sums(128, 32, 1024, first_back)
    v.vec[3:4, :] = sums[0]
    v.vec[4:5, :] = sums[1]
    v.vec[2:3, :] = sums[2]
    v.vec[0:2, :] = jnp.zeros((2, 1024), F32)

    v.da_send[...] = contract_cols(v.db[...], v.wo[...]).astype(BF16)

    def give(step, carry):
        for k in range(4):
            chip = (at.q + 1 + step) % 4
            plane = (at.z + 1 + k) % 4
            pair = 4 * (plane // 2) + chip
            send_or_copy(
                v.da_send.at[slot_rows(plane % 2), lanes(pair)],
                v.da.at[slot_rows(at.place)],
                v.s_misc.at[4],
                v.r_misc.at[4],
                (2 * chip + at.c, plane),
                step == 3 if k == 3 else None,
            )
        return carry

    lax.fori_loop(0, 4, give, 0)


def grads_phase(at, v, gather, out_scatter):
    xs, wqkv, terms = v.xs, v.wqkv, v.terms
    parity, pair = at.parity, at.pair
    sib_out, sib_in = v.sib_out.at[0], v.sib_in.at[0]
    peer_out, peer_in = v.peer_out.at[0], v.peer_in.at[0]

    for r in range(4):
        terms[r] = contract_rows(v.db[:, chip_rows(at.chip(r))], v.att[...])
        out_scatter.scatter_put(terms, sib_out, sib_in, r)
        if r:
            out_scatter.scatter_pass(terms, sib_in, peer_out, peer_in, r - 1)
    out_scatter.scatter_pass(terms, sib_in, peer_out, peer_in, 3)

    v.q_turned[...] = v.queries[...].astype(F32).T.astype(BF16)
    v.dk_turned[...] = jnp.zeros_like(v.dk_turned)
    v.dv_turned[...] = jnp.zeros_like(v.dv_turned)
    wait_bytes(v.da, v.r_misc.at[4])
    column_grads(at, v.g_in, v.zg_in, v.s_zg.at[1], v.r_zg.at[1])
    v.da_turned[...] = v.da[...].astype(F32).T.astype(BF16)
    s_buf, d_buf, p_buf = v.scores, v.d_buf, v.p_buf

    def attend(step, carry):
        rows = chip_rows(step)
        parts = []
        for h in range(2):
            mask = head_mask(h)
            grad = v.da[rows].astype(F32) * mask
            delta = jnp.sum(grad * v.mixed[rows], axis=-1, keepdims=True)
            q = (v.queries[rows].astype(F32) * mask * HEAD_DIM**-0.5).astype(BF16)
            s_buf[...] = contract_cols(q, v.keys_all[...])
            d_buf[...] = contract_cols(grad.astype(BF16), v.values_all[...])
            logs = v.log_sums[rows][:, h * HEAD_DIM : h * HEAD_DIM + 1]
            probs = jnp.exp(s_buf[...] - logs)
            p_buf[...] = probs.astype(BF16)
            low = (probs * (d_buf[...] - delta)).astype(BF16)
            band = pl.ds(h * HEAD_DIM, HEAD_DIM)
            v.dv_turned[band] += dot_nn(v.da_turned[band, rows], p_buf[...])
            v.dk_turned[band] += dot_nn(v.q_turned[band, rows], low)
            parts.append(dot_nn(low, v.keys_all[...]))
        v.dq[rows] = jnp.where(head_mask(0) > 0.5, parts[0], parts[1]) * HEAD_DIM**-0.5
        return carry

    lax.fori_loop(0, 4, attend, 0)

    other = core_rows(1 - at.c)
    mine = core_rows(at.c)
    v.out_k[...] = v.dk_turned[:, other].T * HEAD_DIM**-0.5
    v.out_v[...] = v.dv_turned[:, other].T
    for k, (ref, into) in enumerate(((v.out_k, v.sib_k), (v.out_v, v.sib_v))):
        remote(ref, into, v.s_kv2.at[k], v.r_kv2.at[k], at.sibling()).start()
    dqkv = v.dqkv
    low = v.dq[...].astype(BF16)
    dqkv[:, 0:128] = low
    v.vec[0:1, lanes(pair)] = jnp.sum(low.astype(F32), axis=0, keepdims=True)
    own_k = v.dk_turned[:, mine].T * HEAD_DIM**-0.5
    wait_bytes(v.sib_k, v.r_kv2.at[0])
    dqkv[:, 128:256] = (own_k + v.sib_k[...]).astype(BF16)
    own_v = v.dv_turned[:, mine].T
    wait_bytes(v.sib_v, v.r_kv2.at[1])
    low = (own_v + v.sib_v[...]).astype(BF16)
    dqkv[:, 256:384] = low
    v.vec[1:2, lanes(pair)] = jnp.sum(low.astype(F32), axis=0, keepdims=True)

    gather.gather_end(v.norm_slots)
    x_out, x_in = v.norm_slots, v.x_in
    for r in (3, 1, 2, 0):
        part = contract_cols(dqkv[chip_rows(at.chip(r))], wqkv[...])
        if r:
            x_out[r] = part.astype(BF16)
        else:
            v.x_sum[...] = part
    for dz in (2, 1, 3, 0):
        rows = slot_rows((at.z + dz) % 4)
        for r in (3, 1, 2):
            remote(
                x_out.at[r, rows],
                x_in.at[r, rows],
                v.s_dx.at[r, dz],
                v.r_dx.at[r, dz],
                at.peer(r),
            ).start()

    notes = v.notes
    for d in range(32):
        notes[d, 0:8] = v.vec[:, 128 * (d // 4) : 128 * (d // 4) + 128]
        notes[d, 8:16] = jnp.zeros((8, 128), F32)
    for h in range(4):
        notes[8 * h + at.b, 8:9] = v.gbin[0:1, 128 * h : 128 * h + 128]
    pltpu.make_async_copy(notes.at[at.flat], v.notes_in.at[at.flat], v.r_misc.at[5]).start()

    def spread(step, carry):
        to = (at.flat + step) % 32
        remote(
            notes.at[to],
            v.notes_in.at[at.flat],
            v.s_misc.at[5],
            v.r_misc.at[5],
            (to // 4, to % 4),
        ).start()
        return carry

    lax.fori_loop(1, 32, spread, 0)

    def features(b):
        return contract_rows(xs[:, lanes(b)], dqkv[...])

    for r in range(4):
        v.w_sib_out[r] = features(2 * at.chip(r) + 1 - at.c)
        remote(
            v.w_sib_out.at[r], v.w_sib_in.at[r], v.s_ws.at[r], v.r_ws.at[r], at.sibling()
        ).start()
    plane_w = 2 * (at.z // 2) + at.y
    for r in range(4):
        total = features(2 * at.chip(r) + at.c)
        wait_bytes(v.w_sib_in.at[r], v.r_ws.at[r])
        v.w_out[r] = (total + v.w_sib_in[r]).astype(BF16)
        send_or_copy(
            v.w_out.at[r],
            v.w_in.at[parity, at.x],
            v.s_misc.at[6],
            v.r_misc.at[6],
            at.peer(r)[:1] + (plane_w,),
            plane_w == at.z if r == 0 else None,
        )

    plane_grads(
        at, v.g_back, v.zg_back, v.gs_back, v.fin_back, v.r_zg.at[0], v.s_misc.at[7], v.r_misc.at[7]
    )
    out_scatter.scatter_arrive(peer_in)

    def out_rows(rows):
        own = pl.ds(pl.multiple_of(at.c * 128 + rows.start, 32), 32)
        total = (
            terms[0, own]
            + peer_in[1, rows].astype(F32)
            + peer_in[2, rows].astype(F32)
            + peer_in[3, rows].astype(F32)
        )
        v.o_out[rows] = total.astype(BF16)

    by_rows(128, 32, out_rows)
    wide = pl.ds(pl.multiple_of(at.z * 256, 256), 256)
    pltpu.make_async_copy(v.o_out.at[:, wide], v.o_in.at[0], v.r_misc.at[8]).start()
    for dz in range(1, 4):
        plane = (at.z + dz) % 4
        remote(
            v.o_out.at[:, pl.ds(pl.multiple_of(plane * 256, 256), 256)],
            v.o_in.at[dz],
            v.s_misc.at[8],
            v.r_misc.at[8],
            (at.b, plane),
        ).start()

    z_out, z_in = v.z_out, v.z_in
    for dz in (2, 1, 3, 0):
        plane = (at.z + dz) % 4
        rows = slot_rows(plane)
        for r in (3, 1, 2):
            wait_bytes(x_in.at[r, rows], v.r_dx.at[r, dz])
        total = (
            v.x_sum[rows]
            + x_in[1, rows].astype(F32)
            + x_in[2, rows].astype(F32)
            + x_in[3, rows].astype(F32)
        )
        if dz:
            z_out[dz] = total.astype(BF16)
            remote(
                z_out.at[dz], z_in.at[dz], v.s_dz.at[dz], v.r_dz.at[dz], (at.b, plane)
            ).start()
        else:
            v.x_own[...] = total
    plane_grads(
        at, v.g_in, v.zg_in, v.gs_in, v.fin_in, v.r_zg.at[1], v.s_misc.at[9], v.r_misc.at[9]
    )
    for dz in (1, 2, 3):
        wait_bytes(z_in.at[dz], v.r_dz.at[dz])
    same = slot_rows(parity)
    v.gtok[same] = (v.d1[same] + v.x_own[...] + z_in[2].astype(F32)).astype(BF16)
    cross = slot_rows(1 - parity)
    v.gtok[cross] = (v.d1[cross] + z_in[1].astype(F32) + z_in[3].astype(F32)).astype(BF16)

    wait_bytes(v.o_in, v.r_misc.at[8])
    wait_bytes(v.w_in, v.r_misc.at[6])
    wait_bytes(v.notes_in, v.r_misc.at[5])
    wait_bytes(v.fin_back, v.r_misc.at[7])
    wait_bytes(v.fin_in, v.r_misc.at[9])


def end_phase(at, v, col_in, col_back, exchanges):
    gather, scatter, gather2, scatter2, out_scatter = exchanges
    slot = v.xs.at[slot_rows(0)]
    for dz in range(1, 4):
        wait_bytes(slot, v.s_z.at[dz])
    for r in (1, 2, 3):
        for dz in range(4):
            wait_bytes(slot, v.s_p.at[r, dz])
            wait_bytes(slot, v.s_dx.at[r, dz])
    near = at.parity == at.y

    @pl.when(jnp.logical_not(near))
    def _():
        wait_bytes(v.wqkv.at[pl.ds(0, 512)], v.s_w.at[0])

    @pl.when(near)
    def _():
        wait_bytes(v.wqkv.at[pl.ds(0, 384)], v.s_w.at[0])

    wait_bytes(v.wqkv.at[pl.ds(0, 512)], v.s_w.at[1])
    seven = v.wi.at[pl.ds(0, 896), pl.ds(0, 128)]
    for i in (0, 2, 7, 9):
        wait_bytes(seven, v.s_misc.at[i])
    wait_bytes(v.smalls.at[pl.ds(0, 31)], v.s_misc.at[1])
    wait_bytes(v.wo.at[pl.ds(0, 768), pl.ds(0, 128)], v.s_o.at[0])
    for r in range(1, 8):
        wait_bytes(v.wo.at[:, pl.ds(0, 128)], v.s_o.at[r])
    for r in range(4):
        for k in range(2):
            wait_bytes(v.keys_all.at[pl.ds(0, 256)], v.s_kv.at[k, r])
    for i in (3, 4):
        wait_bytes(v.att_send.at[pl.ds(0, 960)], v.s_misc.at[i])
    col_in.end()
    col_back.end()
    for dz in (1, 2, 3):
        for k in range(2):
            wait_bytes(v.zg_in.at[dz], v.s_zg.at[k, dz])
        wait_bytes(v.z_out.at[dz], v.s_dz.at[dz])
    for k in range(2):
        wait_bytes(v.sib_k, v.s_kv2.at[k])
    wait_bytes(v.notes.at[pl.ds(0, 31)], v.s_misc.at[5])
    for r in range(4):
        wait_bytes(v.w_sib_out.at[r], v.s_ws.at[r])
    plane_w = 2 * (at.z // 2) + at.y

    @pl.when(plane_w == at.z)
    def _():
        wait_bytes(v.w_out.at[pl.ds(0, 3)], v.s_misc.at[6])

    @pl.when(plane_w != at.z)
    def _():
        wait_bytes(v.w_out, v.s_misc.at[6])

    wait_bytes(v.o_in.at[pl.ds(0, 3)], v.s_misc.at[8])
    gather2.gather_end(v.grad_slots)
    scatter2.scatter_end(v.sib_out.at[1], v.peer_out.at[1])
    out_scatter.scatter_end(v.sib_out.at[0], v.peer_out.at[0])


def finish_kernel(
    place_ref,
    out_in,
    gtok_in,
    w_in,
    o_in,
    fin_in,
    fin_back,
    notes_in,
    out_ref,
    gtok_ref,
    gq_ref,
    gk_ref,
    gv_ref,
    gout_ref,
    gwin_ref,
    gwback_ref,
    small_ref,
    bin_ref,
):
    out_ref[...] = out_in[...]
    gtok_ref[...] = gtok_in[...]
    for x in range(2):
        total = w_in[0, x].astype(F32) + w_in[1, x].astype(F32)
        for k, ref in enumerate((gq_ref, gk_ref, gv_ref)):
            ref[:, 128 * x : 128 * x + 128] = total[:, 128 * k : 128 * k + 128]
    gout_ref[...] = (
        o_in[0].astype(F32) + o_in[1].astype(F32) + o_in[2].astype(F32) + o_in[3].astype(F32)
    ).T
    gwin_ref[...] = fin_in[...].astype(F32)
    gwback_ref[...] = fin_back[...].astype(F32)
    total = notes_in[0]
    for d in range(1, 32):
        total += notes_in[d]
    z = place_ref[0]
    part = jnp.zeros((8, 32), F32)
    for k in range(4):
        part += jnp.where(z == k, total[0:8, 32 * k : 32 * k + 32], 0.0)
    small_ref[...] = part
    bin_ref[...] = total[8:9, :]


def vmem():
    return pl.BlockSpec(memory_space=pltpu.VMEM)


def run_layer(*args):
    scratch = [pltpu.VMEM(s, t) for _, s, t in SCRATCH]
    for _, shape in SEMAPHORES:
        scratch += [DMA(shape), DMA(shape)]
    return pl.pallas_call(
        layer_kernel,
        out_shape=[jax.ShapeDtypeStruct(s, t) for _, s, t in RESULTS],
        in_specs=[vmem()] * len(args),
        out_specs=[vmem()] * len(RESULTS),
        scratch_shapes=scratch,
        compiler_params=pltpu.CompilerParams(
            collective_id=1, has_side_effects=True, vmem_limit_bytes=VMEM_LIMIT
        ),
    )(*args)


def run_finish(*args):
    shapes = (
        ((128, 1024), BF16),
        ((128, 1024), BF16),
        ((128, 256), F32),
        ((128, 256), F32),
        ((128, 256), F32),
        ((256, 128), F32),
        ((128, 1024), F32),
        ((128, 1024), F32),
        ((8, 32), F32),
        ((1, 128), F32),
    )
    return pl.pallas_call(
        finish_kernel,
        out_shape=[jax.ShapeDtypeStruct(s, t) for s, t in shapes],
        in_specs=[pl.BlockSpec(memory_space=pltpu.SMEM)] + [vmem()] * (len(args) - 1),
        out_specs=[vmem()] * len(shapes),
        compiler_params=pltpu.CompilerParams(vmem_limit_bytes=32 * 2**20),
    )(*args)


DMA = pltpu.SemaphoreType.DMA


def fast_device(
    tokens,
    w_query,
    w_key,
    w_value,
    w_out,
    b_query,
    b_value,
    b_out,
    norm1_gain,
    norm1_shift,
    w_in,
    w_back,
    b_in,
    b_back,
    norm2_gain,
    norm2_shift,
    cotangent,
):
    head_id = lax.axis_index("head")
    token_shape = tokens.shape
    model_dim = tokens.shape[2]
    x = tokens.reshape(-1, model_dim)
    vectors = jnp.stack(
        (b_query, b_value, b_out, norm1_gain, norm1_shift, b_back, norm2_gain, norm2_shift)
    )
    spread = jnp.where(
        lax.broadcasted_iota(jnp.int32, (1, 128), 1) // 32 == head_id,
        jnp.tile(vectors, (1, 4)),
        jnp.zeros((), BF16),
    )
    small = jnp.concatenate((spread, b_in[None], jnp.zeros((7, 128), BF16)), axis=0)
    results = run_layer(
        x, w_query, w_key, w_value, w_out, small, w_in, w_back, cotangent.reshape(-1, model_dim)
    )
    output, grad_tokens, gq, gk, gv, gout, gw_in, gw_back, own, gb_in = run_finish(
        head_id.astype(jnp.int32).reshape(1), *results
    )
    return (
        output.reshape(token_shape),
        grad_tokens.reshape(token_shape),
        gq,
        gk,
        gv,
        gout,
        own[0],
        own[1],
        own[2],
        own[3],
        own[4],
        gw_in,
        gw_back,
        gb_in.reshape(-1),
        own[5],
        own[6],
        own[7],
    )


def solution(mesh):
    in_specs = (
        P(None, ("blk", "head"), None),
        P("blk", "head"),
        P("blk", "head"),
        P("blk", "head"),
        P("head", "blk"),
        P(("blk", "head")),
        P(("blk", "head")),
        P(("blk", "head")),
        P(("blk", "head")),
        P(("blk", "head")),
        P("blk", "head"),
        P("blk", "head"),
        P(("blk", "head")),
        P(("blk", "head")),
        P(("blk", "head")),
        P(("blk", "head")),
        P(None, ("blk", "head"), None),
    )
    out_specs = (
        P(None, ("blk", "head"), None),
        P(None, ("blk", "head"), None),
        P("blk", "head"),
        P("blk", "head"),
        P("blk", "head"),
        P("head", "blk"),
        P(("blk", "head")),
        P(("blk", "head")),
        P(("blk", "head")),
        P(("blk", "head")),
        P(("blk", "head")),
        P("blk", "head"),
        P("blk", "head"),
        P(("blk", "head")),
        P(("blk", "head")),
        P(("blk", "head")),
        P(("blk", "head")),
    )
    sizes = (mesh.shape["blk"], mesh.shape["head"])
    body = fast_device if sizes == (8, 4) else per_device
    return jax.shard_map(
        body, mesh=mesh, in_specs=in_specs, out_specs=out_specs, check_vma=False
    )
```

```python
import functools
import math

import jax
import jax.numpy as jnp
from jax import lax
from jax.experimental import pallas as pl
from jax.experimental.pallas import tpu as pltpu
from jax.sharding import PartitionSpec as P

HEAD_DIM = 64


NORM_EPS = 1e-05


def layer_norm(summed, gain, shift):
    centre = jnp.mean(summed, axis=-1, keepdims=True)
    centred = summed - centre
    spread = jnp.mean(centred * centred, axis=-1, keepdims=True)
    return centred * lax.rsqrt(spread + NORM_EPS) * gain + shift


def gelu_exact(inputs):
    return jax.nn.gelu(inputs, approximate=False)


def split_heads(packed):
    return packed.reshape(packed.shape[0], packed.shape[1], -1, HEAD_DIM)


def contract_rows(left, right):
    return lax.dot_general(
        left, right, (((0,), (0,)), ((), ())), preferred_element_type=jnp.float32
    )


def contract_cols(left, right):
    return lax.dot_general(
        left, right, (((1,), (1,)), ((), ())), preferred_element_type=jnp.float32
    )


def score_block(queries4, keys4):
    return jnp.einsum(
        "sqge,skge->sqgk", queries4, keys4, preferred_element_type=jnp.float32
    ) * HEAD_DIM ** (-0.5)


def score_grads(queries4, keys4, values4, grads4, log_sums, deltas):
    probs = jnp.exp(score_block(queries4, keys4) - log_sums[..., None])
    d_probs = jnp.einsum("sqge,skge->sqgk", grads4, values4, preferred_element_type=jnp.float32)
    d_scores = (probs * (d_probs - deltas[..., None])).astype(jnp.bfloat16)
    return (probs.astype(jnp.bfloat16), d_scores)


def token_rows(local):
    return lax.all_gather(local, "head", axis=1, tiled=True)


def token_partials(terms):
    return lax.psum_scatter(
        terms.astype(jnp.bfloat16), "head", scatter_dimension=1, tiled=True
    ).astype(jnp.float32)


def place_part(part, full_len, start):
    return lax.dynamic_update_slice_in_dim(jnp.zeros((full_len,), jnp.float32), part, start, 0)


def per_device(
    tokens,
    w_query,
    w_key,
    w_value,
    w_out,
    b_query,
    b_value,
    b_out,
    norm1_gain,
    norm1_shift,
    w_in,
    w_back,
    b_in,
    b_back,
    norm2_gain,
    norm2_shift,
    cotangent,
):
    f32 = jnp.float32
    bf16 = jnp.bfloat16
    score_scale = HEAD_DIM ** (-0.5)
    bq_full, bv_full, bo_full, gain_one, shift_one, bin_full, bback_full, gain_two, shift_two = (
        lax.all_gather(b_query, ("blk", "head"), axis=0, tiled=True),
        lax.all_gather(b_value, ("blk", "head"), axis=0, tiled=True),
        lax.all_gather(b_out, ("blk", "head"), axis=0, tiled=True),
        lax.all_gather(norm1_gain, ("blk", "head"), axis=0, tiled=True),
        lax.all_gather(norm1_shift, ("blk", "head"), axis=0, tiled=True),
        lax.all_gather(b_in, ("blk", "head"), axis=0, tiled=True),
        lax.all_gather(b_back, ("blk", "head"), axis=0, tiled=True),
        lax.all_gather(norm2_gain, ("blk", "head"), axis=0, tiled=True),
        lax.all_gather(norm2_shift, ("blk", "head"), axis=0, tiled=True),
    )
    attn_cols, out_rows, ffn_cols = (
        lax.all_gather(jnp.stack((w_query, w_key, w_value)), "blk", axis=1, tiled=True),
        lax.all_gather(w_out, "blk", axis=1, tiled=True),
        lax.all_gather(jnp.stack((w_in, w_back)), "blk", axis=1, tiled=True),
    )
    seq_count, local_len, model_dim = tokens.shape
    token_shape = (seq_count, local_len, model_dim)
    head_id = lax.axis_index("head")
    width_part = attn_cols.shape[2]
    bq_part = lax.dynamic_slice_in_dim(bq_full, head_id * width_part, width_part).astype(f32)
    bv_part = lax.dynamic_slice_in_dim(bv_full, head_id * width_part, width_part).astype(f32)
    wide_rows = token_rows(tokens)
    wide_len = wide_rows.shape[1]
    wide_flat = wide_rows.reshape(-1, model_dim)
    head_shape = (seq_count, wide_len, width_part)
    wide_shape = (seq_count, wide_len, model_dim)
    query_heads = (
        (jnp.dot(wide_flat, attn_cols[0], preferred_element_type=f32) + bq_part)
        .astype(bf16)
        .reshape(head_shape)
    )
    key_heads = (
        jnp.dot(wide_flat, attn_cols[1], preferred_element_type=f32)
        .astype(bf16)
        .reshape(head_shape)
    )
    value_heads = (
        (jnp.dot(wide_flat, attn_cols[2], preferred_element_type=f32) + bv_part)
        .astype(bf16)
        .reshape(head_shape)
    )
    query4 = split_heads(query_heads)
    key4 = split_heads(key_heads)
    value4 = split_heads(value_heads)
    stat_shape = query4.shape[:3]
    pieces = (
        lax.all_gather(key_heads, "blk", axis=1, tiled=True),
        lax.all_gather(value_heads, "blk", axis=1, tiled=True),
    )
    maxima = jnp.full(stat_shape, -1e30, f32)
    scores = score_block(query4, split_heads(pieces[0]))
    new_max = jnp.maximum(maxima, jnp.max(scores, axis=-1))
    weights = jnp.exp(scores - new_max[..., None])
    totals = jnp.sum(weights, axis=-1)
    summed = jnp.einsum(
        "sqgk,skge->sqge", weights.astype(bf16), split_heads(pieces[1]), preferred_element_type=f32
    )
    maxima, totals, summed = (new_max, totals, summed)
    log_sums = maxima + jnp.log(totals)
    attended4 = summed / totals[..., None]
    attended_heads = attended4.reshape(head_shape).astype(bf16)
    attended_flat = attended_heads.reshape(-1, width_part)
    branch_terms = jnp.dot(attended_flat, out_rows, preferred_element_type=f32).reshape(wide_shape)
    branch = token_partials(branch_terms).reshape(-1, model_dim) + bo_full.astype(f32)
    flat_rows = tokens.reshape(-1, model_dim)
    normed, norm1_pull = jax.vjp(
        layer_norm, flat_rows.astype(f32) + branch, gain_one.astype(f32), shift_one.astype(f32)
    )
    normed_low = normed.astype(bf16)
    ffn_full = lax.all_gather(ffn_cols, "head", axis=2, tiled=True)
    pre_act = jnp.dot(normed_low, ffn_full[0], preferred_element_type=f32) + bin_full.astype(f32)
    hidden_act, gelu_pull = jax.vjp(gelu_exact, pre_act)
    hidden_low = hidden_act.astype(bf16)
    ffn_out = contract_cols(hidden_low, ffn_full[1]) + bback_full.astype(f32)
    final, norm2_pull = jax.vjp(
        layer_norm, normed + ffn_out, gain_two.astype(f32), shift_two.astype(f32)
    )
    output = final.astype(bf16).reshape(token_shape)
    d_second, grad_norm2_gain, grad_norm2_shift = norm2_pull(
        cotangent.reshape(-1, model_dim).astype(f32)
    )
    d_ffn = d_second.astype(bf16)
    grad_b_back = jnp.sum(d_ffn.astype(f32), axis=0)
    grad_back_whole = contract_rows(d_ffn, hidden_low)
    d_hidden = jnp.dot(d_ffn, ffn_full[1], preferred_element_type=f32)
    d_pre = gelu_pull(d_hidden)[0].astype(bf16)
    grad_b_in = jnp.sum(d_pre.astype(f32), axis=0)
    grad_in_whole = contract_rows(normed_low, d_pre)
    ffn_grad_parts = lax.psum_scatter(
        jnp.stack((grad_in_whole, grad_back_whole)).astype(jnp.bfloat16),
        "head",
        scatter_dimension=2,
        tiled=True,
    ).astype(jnp.float32)
    d_normed = d_second + contract_cols(d_pre, ffn_full[0])
    d_first, grad_norm1_gain, grad_norm1_shift = norm1_pull(d_normed)
    d_branch = d_first.astype(bf16)
    grad_b_out = jnp.sum(d_branch.astype(f32), axis=0)
    wide_dbranch = token_rows(d_branch.reshape(token_shape)).reshape(-1, model_dim)
    grad_out_part = contract_rows(attended_flat, wide_dbranch)
    grad_heads = contract_cols(wide_dbranch, out_rows).astype(bf16).reshape(head_shape)
    grads4 = split_heads(grad_heads)
    deltas = jnp.sum(grads4.astype(f32) * attended4, axis=-1)
    row_stats = (
        lax.all_gather(log_sums, "blk", axis=1, tiled=True),
        lax.all_gather(deltas, "blk", axis=1, tiled=True),
    )
    pieces = (
        lax.all_gather(key_heads, "blk", axis=1, tiled=True),
        lax.all_gather(value_heads, "blk", axis=1, tiled=True),
        lax.all_gather(query_heads, "blk", axis=1, tiled=True),
        lax.all_gather(grad_heads, "blk", axis=1, tiled=True),
    )
    piece_keys = split_heads(pieces[0])
    piece_values = split_heads(pieces[1])
    piece_queries = split_heads(pieces[2])
    piece_grads = split_heads(pieces[3])
    piece_sums = row_stats[0]
    piece_deltas = row_stats[1]
    own_probs, own_scores = score_grads(query4, piece_keys, piece_values, grads4, log_sums, deltas)
    d_query = score_scale * jnp.einsum(
        "sqgk,skge->sqge", own_scores, piece_keys, preferred_element_type=f32
    )
    probs_low, d_scores = score_grads(
        piece_queries, key4, value4, piece_grads, piece_sums, piece_deltas
    )
    key_acc = score_scale * jnp.einsum(
        "sqgk,sqge->skge", d_scores, piece_queries, preferred_element_type=f32
    )
    value_acc = jnp.einsum("sqgk,sqge->skge", probs_low, piece_grads, preferred_element_type=f32)
    d_query_low = d_query.reshape(-1, width_part).astype(bf16)
    d_key_low = key_acc.reshape(-1, width_part).astype(bf16)
    d_value_low = value_acc.reshape(-1, width_part).astype(bf16)
    grad_b_query = place_part(
        jnp.sum(d_query_low.astype(f32), axis=0), model_dim, head_id * width_part
    )
    grad_b_value = place_part(
        jnp.sum(d_value_low.astype(f32), axis=0), model_dim, head_id * width_part
    )
    attn_grad_parts = jnp.stack(
        (
            contract_rows(wide_flat, d_query_low),
            contract_rows(wide_flat, d_key_low),
            contract_rows(wide_flat, d_value_low),
        )
    )
    token_terms = (
        contract_cols(d_query_low, attn_cols[0])
        + contract_cols(d_key_low, attn_cols[1])
        + contract_cols(d_value_low, attn_cols[2])
    )
    d_tokens = d_first + token_partials(token_terms.reshape(wide_shape)).reshape(-1, model_dim)
    grad_tokens = d_tokens.astype(bf16).reshape(token_shape)
    attn_sums, grad_w_out, ffn_sums = (
        lax.psum_scatter(attn_grad_parts, "blk", scatter_dimension=1, tiled=True),
        lax.psum_scatter(grad_out_part, "blk", scatter_dimension=1, tiled=True),
        lax.psum_scatter(ffn_grad_parts, "blk", scatter_dimension=1, tiled=True),
    )
    (
        grad_b_query,
        grad_b_value,
        grad_b_out,
        grad_norm1_gain,
        grad_norm1_shift,
        grad_b_in,
        grad_b_back,
        grad_norm2_gain,
        grad_norm2_shift,
    ) = (
        lax.psum_scatter(grad_b_query, ("blk", "head"), scatter_dimension=0, tiled=True),
        lax.psum_scatter(grad_b_value, ("blk", "head"), scatter_dimension=0, tiled=True),
        lax.psum_scatter(grad_b_out, ("blk", "head"), scatter_dimension=0, tiled=True),
        lax.psum_scatter(grad_norm1_gain, ("blk", "head"), scatter_dimension=0, tiled=True),
        lax.psum_scatter(grad_norm1_shift, ("blk", "head"), scatter_dimension=0, tiled=True),
        lax.psum_scatter(grad_b_in, ("blk", "head"), scatter_dimension=0, tiled=True),
        lax.psum_scatter(grad_b_back, ("blk", "head"), scatter_dimension=0, tiled=True),
        lax.psum_scatter(grad_norm2_gain, ("blk", "head"), scatter_dimension=0, tiled=True),
        lax.psum_scatter(grad_norm2_shift, ("blk", "head"), scatter_dimension=0, tiled=True),
    )
    return (
        output,
        grad_tokens,
        attn_sums[0],
        attn_sums[1],
        attn_sums[2],
        grad_w_out,
        grad_b_query,
        grad_b_value,
        grad_b_out,
        grad_norm1_gain,
        grad_norm1_shift,
        ffn_sums[0],
        ffn_sums[1],
        grad_b_in,
        grad_b_back,
        grad_norm2_gain,
        grad_norm2_shift,
    )


MESH = pl.DeviceIdType.MESH
F32 = jnp.float32
BF16 = jnp.bfloat16
VMEM_LIMIT = 62 * 2**20


def dot_nn(left, right):
    return jnp.dot(left, right, preferred_element_type=F32)


class Place:
    def __init__(self):
        self.b = lax.axis_index("blk")
        self.z = lax.axis_index("head")
        self.y = self.b // 4
        self.x = (self.b // 2) % 2
        self.c = self.b % 2
        self.q = self.b // 2

    def chip(self, r):
        return ((self.y + r // 2) % 2) * 2 + (self.x + r % 2) % 2

    def peer(self, r):
        return (2 * self.chip(r) + self.c, self.z)

    def sibling(self):
        return (2 * self.q + 1 - self.c, self.z)


def remote(src, dst, send_sem, recv_sem, device):
    return pltpu.make_async_remote_copy(
        src_ref=src,
        dst_ref=dst,
        send_sem=send_sem,
        recv_sem=recv_sem,
        device_id=device,
        device_id_type=MESH,
    )


def wait_bytes(view, sem):
    pltpu.make_async_copy(view, view, sem).wait()


def greet_all(at):
    barrier = pltpu.get_barrier_semaphore()
    flat = at.b * 4 + at.z

    def greet(step, carry):
        other = (flat + step) % 32
        pl.semaphore_signal(
            barrier, inc=1, device_id=(other // 4, other % 4), device_id_type=MESH
        )
        return carry

    lax.fori_loop(1, 32, greet, 0)
    pl.semaphore_wait(barrier, 31)


def half(core):
    return pl.ds(pl.multiple_of(core * 128, 128), 128)


def lanes(index):
    return pl.ds(pl.multiple_of(index * 128, 128), 128)


def by_rows(count, size, step):
    def body(i, carry):
        step(pl.ds(pl.multiple_of(i * size, size), size))
        return carry

    lax.fori_loop(0, count // size, body, 0)


class Spread:
    def __init__(self, at, block, part, send, recv):
        self.at, self.block, self.part = at, block, part
        self.send, self.recv = send, recv

    def start(self):
        mine = self.block(0)
        for i in (0, 1):
            for r, k in ((1, i), (2, 1 - i)):
                piece = self.part(mine, k)
                remote(piece, piece, self.send.at[r, k], self.recv.at[r, k], self.at.peer(r)).start()

    def relay(self):
        for r, k in ((1, 0), (2, 1)):
            piece = self.part(self.block(r), k)
            wait_bytes(piece, self.recv.at[r, k])
            remote(piece, piece, self.send.at[0, k], self.recv.at[0, k], self.at.peer(3 - r)).start()

    def rest(self, r):
        block = self.block(r)
        for row, k in {1: ((1, 1),), 2: ((2, 0),), 3: ((0, 0), (0, 1))}[r]:
            wait_bytes(self.part(block, k), self.recv.at[row, k])

    def end(self):
        mine = self.block(0)
        for row in range(3):
            for k in range(2):
                wait_bytes(self.part(mine, k), self.send.at[row, k])


def part_rows(h, core):
    return pl.ds(pl.multiple_of(h * 128 + core * 64, 64), 64)


class Gather:
    def __init__(self, at, slots, h, send, recv, send_sib, recv_sib):
        self.at, self.slots, self.h = at, slots, h
        self.send_sib, self.recv_sib = send_sib, recv_sib

        def part(block, k):
            return block.at[pl.ds(k * 32, 32)]

        self.spread = Spread(
            at, lambda r: slots.at[at.chip(r), part_rows(h, at.c)], part, send, recv
        )

    def to_sibling(self, r):
        block = self.spread.block(r)
        remote(
            block, block, self.send_sib.at[r], self.recv_sib.at[r], self.at.sibling()
        ).start()

    def start(self):
        self.spread.start()
        self.to_sibling(0)

    def relay(self):
        self.spread.relay()

    def step(self, r):
        at = self.at
        if r:
            self.spread.rest(r)
            self.to_sibling(r)
        wait_bytes(self.slots.at[at.chip(r), part_rows(self.h, 1 - at.c)], self.recv_sib.at[r])
        return at.chip(r)

    def end(self):
        self.spread.end()
        for r in range(4):
            wait_bytes(self.spread.block(r), self.send_sib.at[r])


class Exchange:
    def __init__(self, at, buffers, rows, send, recv, send_sib, recv_sib):
        self.at, self.send, self.recv = at, send, recv
        self.send_sib, self.recv_sib = send_sib, recv_sib
        self.sib_out, self.sib_in, self.out, self.into = buffers
        self.rows = rows

    def put(self, r, theirs):
        mine = self.sib_out.at[r, self.rows]
        mine[...] = theirs.astype(BF16)
        remote(
            mine,
            self.sib_in.at[r, self.rows],
            self.send_sib.at[r],
            self.recv_sib.at[r],
            self.at.sibling(),
        ).start()

    def add(self, r, mine):
        wait_bytes(self.sib_in.at[r, self.rows], self.recv_sib.at[r])
        total = mine + self.sib_in[r, self.rows].astype(F32)
        if r == 0:
            return total
        held = self.out.at[r, self.rows]
        held[...] = total.astype(BF16)
        remote(
            held, self.into.at[r, self.rows], self.send.at[r], self.recv.at[r], self.at.peer(r)
        ).start()

    def arrive(self):
        for r in (1, 2, 3):
            wait_bytes(self.into.at[r, self.rows], self.recv.at[r])

    def end(self):
        for r in range(4):
            wait_bytes(self.sib_out.at[r, self.rows], self.send_sib.at[r])
            if r:
                wait_bytes(self.out.at[r, self.rows], self.send.at[r])


def norm_rows(values):
    centre = jnp.mean(values, axis=-1, keepdims=True)
    centred = values - centre
    spread = jnp.mean(centred * centred, axis=-1, keepdims=True)
    scale = lax.rsqrt(spread + NORM_EPS)
    return centred * scale, scale


def norm_back(grad, unit, scale):
    centre = jnp.mean(grad, axis=-1, keepdims=True)
    along = jnp.mean(grad * unit, axis=-1, keepdims=True)
    return (grad - centre - unit * along) * scale


def send_or_copy(src, dst, send_sem, recv_sem, device, own):
    def away():
        remote(src, dst, send_sem, recv_sem, device).start()

    if own is None:
        away()
        return
    pl.when(jnp.logical_not(own))(away)

    @pl.when(own)
    def _():
        pltpu.make_async_copy(src, dst, recv_sem).start()


class Column:
    def __init__(self, at, ref, sems):
        self.at, self.ref = at, ref
        self.up_send, self.up_recv, self.down_send, self.down_recv = sems

    def block(self, plane):
        return self.ref.at[:, lanes(plane)]

    def sides(self, hop, act, arriving):
        z = self.at.z
        if arriving:
            below, above = z - 1 - hop, z + 1 + hop
            pl.when(below >= 0)(lambda: act(self.block(below), 0))
            pl.when(above <= 3)(lambda: act(self.block(above), 1))
        else:
            up = jnp.logical_and(z >= hop, z < 3)
            down = jnp.logical_and(z + hop <= 3, z > 0)
            pl.when(up)(lambda: act(self.block(z - hop), 0))
            pl.when(down)(lambda: act(self.block(z + hop), 1))

    def send(self, hop):
        def act(block, side):
            send = (self.up_send, self.down_send)[side].at[hop]
            recv = (self.up_recv, self.down_recv)[side].at[hop]
            remote(block, block, send, recv, (self.at.b, self.at.z + 1 - 2 * side)).start()

        self.sides(hop, act, False)

    def arrive(self, hop):
        def act(block, side):
            wait_bytes(block, (self.up_recv, self.down_recv)[side].at[hop])

        self.sides(hop, act, True)

    def end(self):
        def wait(hop):
            def act(block, side):
                wait_bytes(block, (self.up_send, self.down_send)[side].at[hop])

            return act

        for hop in range(3):
            self.sides(hop, wait(hop), False)


def plane_weights(at, src, dst, send_sem, recv_sem):
    rows, cols = lanes(at.b), lanes(at.z)
    pltpu.make_async_copy(src.at[:, lanes(at.b)], dst.at[rows, cols], recv_sem).start()

    def push(step, carry):
        other = (at.b + step) % 8
        remote(
            src.at[:, lanes(other)], dst.at[rows, cols], send_sem, recv_sem, (other, at.z)
        ).start()
        return carry

    lax.fori_loop(1, 8, push, 0)


class ColumnSum:
    def __init__(self, at, blocks, passing, send, recv):
        self.at, self.blocks, self.passing = at, blocks, passing
        self.send_sem, self.recv_sem = send, recv

    def plane(self, side, i):
        return i if side else 3 - i

    def hop(self, side):
        return 3 - self.at.z if side else self.at.z

    def next(self, side):
        return (self.at.b, self.at.z + 1 - 2 * side)

    def begin(self, which):
        for side in range(2):

            @pl.when(self.hop(side) == 0)
            def _(side=side):
                for i in which:
                    remote(
                        self.blocks.at[:, :, pl.ds(128 * self.plane(side, i), 128)],
                        self.passing.at[side, i],
                        self.send_sem.at[side, i],
                        self.recv_sem.at[side, i],
                        self.next(side),
                    ).start()

    def relay(self, hop, i):
        for side in range(2):

            @pl.when(self.hop(side) == hop)
            def _(side=side):
                held = self.passing.at[side, i]
                wait_bytes(held, self.recv_sem.at[side, i])
                cols = pl.ds(128 * self.plane(side, i), 128)
                for b in range(8):
                    self.passing[side, i, b] = (
                        self.passing[side, i, b].astype(F32)
                        + self.blocks[b, :, cols].astype(F32)
                    ).astype(BF16)
                remote(
                    held,
                    held,
                    self.send_sem.at[side, i],
                    self.recv_sem.at[side, i],
                    self.next(side),
                ).start()

    def finish(self, sums, final, send_out, recv_out):
        at = self.at
        own = lanes(at.z)
        for b in range(8):
            sums[b] = self.blocks[b, :, own]
        for side in range(2):
            for hop in range(1, 4):
                i = 3 - hop

                @pl.when(self.hop(side) == hop)
                def _(side=side, i=i):
                    wait_bytes(self.passing.at[side, i], self.recv_sem.at[side, i])
                    for b in range(8):
                        sums[b] = (
                            sums[b].astype(F32) + self.passing[side, i, b].astype(F32)
                        ).astype(BF16)

        def one(step, carry):
            other = (at.b + 1 + step) % 8
            send_or_copy(
                sums.at[other],
                final.at[:, lanes(at.b)],
                send_out,
                recv_out,
                (other, at.z),
                step == 7,
            )
            return carry

        lax.fori_loop(0, 8, one, 0)

    def end(self):
        for side in range(2):
            for i in range(3):

                @pl.when(self.hop(side) < 3 - i)
                def _(side=side, i=i):
                    wait_bytes(self.passing.at[side, i], self.send_sem.at[side, i])


def head_mask(h):
    lane = lax.broadcasted_iota(jnp.int32, (1, 128), 1)
    return jnp.where(lane // HEAD_DIM == h, 1.0, 0.0).astype(F32)


def slot_rows(index):
    return pl.ds(pl.multiple_of(index * 64, 64), 64)


def chip_rows(index):
    return pl.ds(pl.multiple_of(index * 256, 256), 256)


def core_rows(index):
    return pl.ds(pl.multiple_of(index * 1024, 1024), 1024)


class Inputs:
    x = wq = wk = wv = wout = small = win = wback = cot = None


def entries(table):
    return [(n, e) for n, e in vars(table).items() if n[0] != "_"]


class Results:
    out = ((128, 1024), BF16)
    gtok = ((128, 1024), BF16)
    w_in = ((2, 2, 128, 384), BF16)
    o_in = ((4, 128, 256), BF16)
    fin_in = ((128, 1024), BF16)
    fin_back = ((128, 1024), BF16)
    notes_in = ((4, 16, 128), F32)


class Scratch:
    xs = ((1024, 1024), BF16)
    wqkv = ((1024, 384), BF16)
    w_near = ((3, 128, 256), BF16)
    queries = ((1024, 128), BF16)
    keys_all = ((2048, 128), BF16)
    values_all = ((2048, 128), BF16)
    mixed = ((1024, 128), F32)
    log_sums = ((1024, 128), F32)
    att = ((128, 1024), BF16)
    wo = ((1024, 1024), BF16)
    par = ((8, 1024), F32)
    bins = ((1, 512), F32)
    wi = ((1024, 512), BF16)
    wb = ((1024, 512), BF16)
    smalls = ((8, 16, 128), BF16)
    smalls_z = ((4, 16, 128), BF16)
    smalls_sum = ((16, 128), BF16)
    proj = ((256, 384), F32)
    scores = ((256, 2048), F32)
    d_buf = ((256, 2048), F32)
    p_buf = ((256, 2048), BF16)
    att_send = ((1024, 128), BF16)
    n1 = ((128, 1024), F32)
    unit1 = ((128, 1024), F32)
    scale1 = ((128, 128), F32)
    d2 = ((128, 1024), F32)
    d1 = ((128, 1024), F32)
    db = ((128, 1024), BF16)
    norm_slots = ((4, 256, 1024), BF16)
    grad_slots = ((4, 256, 1024), BF16)
    hid = ((4, 256, 512), BF16)
    slope = ((4, 256, 512), F32)
    low = ((4, 256, 512), BF16)
    pre = ((128, 512), F32)
    terms = ((4, 256, 1024), F32)
    sib_out = ((2, 4, 128, 1024), BF16)
    sib_in = ((2, 4, 128, 1024), BF16)
    peer_out = ((2, 4, 128, 1024), BF16)
    peer_in = ((2, 4, 128, 1024), BF16)
    g_back = ((8, 128, 512), BF16)
    g_in = ((8, 128, 512), BF16)
    pass_back = ((2, 3, 8, 128, 128), BF16)
    pass_in = ((2, 3, 8, 128, 128), BF16)
    gs_back = ((8, 128, 128), BF16)
    gs_in = ((8, 128, 128), BF16)
    da_send = ((128, 1024), BF16)
    da = ((1024, 128), BF16)
    q_turned = ((128, 1024), BF16)
    da_turned = ((128, 1024), BF16)
    dq = ((1024, 128), F32)
    dk_turned = ((128, 2048), F32)
    dv_turned = ((128, 2048), F32)
    out_k = ((1024, 128), F32)
    out_v = ((1024, 128), F32)
    sib_k = ((1024, 128), F32)
    sib_v = ((1024, 128), F32)
    dqkv = ((1024, 384), BF16)
    x_sum = ((256, 1024), F32)
    x_own = ((64, 1024), F32)
    z_out = ((4, 64, 1024), BF16)
    z_in = ((4, 64, 1024), BF16)
    w_sib_out = ((4, 128, 384), F32)
    w_sib_in = ((4, 128, 384), F32)
    w_out = ((4, 128, 384), BF16)
    o_out = ((128, 1024), BF16)
    vec = ((8, 1024), F32)
    gbin = ((1, 512), F32)
    notes = ((8, 16, 128), F32)
    notes_p = ((8, 16, 128), F32)
    notes_sum = ((16, 128), F32)


class Semaphores:
    z = (4,)
    p = (4, 3, 2)
    wo = (3, 2)
    w = (3,)
    o = (5,)
    kv = (2, 4)
    misc = (12,)
    col = (4, 3)
    ga = (4, 3, 2)
    ga_sib = (4, 4)
    ex = (5, 4)
    ex_sib = (5, 4)
    zg = (2, 2, 3)
    kv2 = (2,)
    dx = (4, 3, 2)
    da = (4,)
    dz = (4,)
    ws = (4,)


class Refs:
    pass


def layer_kernel(*refs):
    v = Refs()
    names = [n for table in (Inputs, Results, Scratch) for n, _ in entries(table)]
    for n, _ in entries(Semaphores):
        names += ["s_" + n, "r_" + n]
    for name, ref in zip(names, refs):
        setattr(v, name, ref)
    at = Place()
    at.flat = at.b * 4 + at.z
    at.place = at.q * 4 + at.z
    at.parity = at.z % 2
    at.pair = 4 * (at.z // 2) + at.q
    col_in = Column(at, v.wi, [s.at[0] for s in (v.s_col, v.r_col)] + [s.at[1] for s in (v.s_col, v.r_col)])
    col_back = Column(at, v.wb, [s.at[2] for s in (v.s_col, v.r_col)] + [s.at[3] for s in (v.s_col, v.r_col)])
    gathers = [
        [
            Gather(at, slots, h, *[t.at[2 * i + h] for t in (v.s_ga, v.r_ga, v.s_ga_sib, v.r_ga_sib)])
            for h in range(2)
        ]
        for i, slots in enumerate((v.norm_slots, v.grad_slots))
    ]

    def exchange(i, side, rows):
        buffers = [t.at[side] for t in (v.sib_out, v.sib_in, v.peer_out, v.peer_in)]
        sems = [t.at[i] for t in (v.s_ex, v.r_ex, v.s_ex_sib, v.r_ex_sib)]
        return Exchange(at, buffers, rows, *sems)

    scatters = [
        [exchange(2 * i + h, i, pl.ds(64 * h, 64)) for h in range(2)] for i in range(2)
    ]
    out_scatter = exchange(4, 0, pl.ds(0, 128))
    upper = at.z // 2
    at.planes = (at.z, at.z + 1 - 2 * at.parity, 2 - upper, 3 - 3 * upper)
    rows_spread = [
        Spread(
            at,
            lambda r, plane=plane: v.xs.at[slot_rows(at.chip(r) * 4 + plane)],
            lambda block, k: block.at[pl.ds(k * 32, 32)],
            v.s_p.at[i],
            v.r_p.at[i],
        )
        for i, plane in enumerate(at.planes)
    ]
    wo_spread = Spread(
        at,
        lambda r: v.wo.at[:, lanes(2 * at.chip(r) + at.c)],
        lambda block, k: block.at[pl.ds(k * 512, 512)],
        v.s_wo,
        v.r_wo,
    )
    sum_in = ColumnSum(at, v.g_in, v.pass_in, v.s_zg.at[0], v.r_zg.at[0])
    sum_back = ColumnSum(at, v.g_back, v.pass_back, v.s_zg.at[1], v.r_zg.at[1])
    greet_all(at)
    attend_phase(at, v, col_in, col_back, rows_spread, wo_spread)
    ffn_phase(at, v, col_in, col_back, gathers, scatters, sum_back, sum_in)
    grads_phase(at, v, gathers[0], scatters, out_scatter, sum_in, sum_back)
    ends = rows_spread + [wo_spread, sum_in, sum_back] + scatters[1] + [out_scatter]
    end_phase(at, v, col_in, col_back, ends)


def attend_phase(at, v, col_in, col_back, rows_spread, wo_spread):
    xs, wqkv, wo = v.xs, v.wqkv, v.wo
    parity, pair = at.parity, at.pair

    pltpu.make_async_copy(v.small, v.smalls_z.at[at.z], v.r_misc.at[1]).start()
    for dz in range(1, 4):
        remote(
            v.small,
            v.smalls_z.at[at.z],
            v.s_misc.at[1],
            v.r_misc.at[1],
            (at.b, (at.z + dz) % 4),
        ).start()

    pltpu.make_async_copy(
        v.x.at[slot_rows(parity)], xs.at[slot_rows(at.place)], v.r_z.at[at.z]
    ).start()
    weights = (v.wq, v.wk, v.wv)
    for i in (1, 2, 3):
        plane = at.planes[i]
        remote(
            v.x.at[slot_rows(plane % 2)],
            xs.at[slot_rows(at.place)],
            v.s_z.at[i],
            v.r_z.at[at.z],
            (at.b, plane),
        ).start()
        if i == 1:
            for k, w in enumerate(weights):
                remote(
                    w, v.w_near.at[k], v.s_w.at[2], v.r_w.at[2], (at.b, at.planes[1])
                ).start()

    part = wo.at[pl.ds(pl.multiple_of(at.z * 256, 256), 256), lanes(at.b)]
    pltpu.make_async_copy(v.wout, part, v.r_o.at[4]).start()
    for i in (1, 2, 3):
        remote(v.wout, part, v.s_o.at[4], v.r_o.at[4], (at.b, at.planes[i])).start()

    def to_pairs(sources, group):
        for dx in range(2):
            column = (at.x + dx) % 2
            for k, w in enumerate(sources):
                send_or_copy(
                    w.at[:, lanes(column)],
                    wqkv.at[lanes(at.b), pl.ds(k * 128, 128)],
                    v.s_w.at[0],
                    v.r_w.at[0],
                    (2 * (group * 2 + column) + at.c, at.z),
                    None if dx else group == at.y,
                )

    for i in range(4):
        wait_bytes(rows_spread[i].block(0), v.r_z.at[at.planes[i]])
        rows_spread[i].start()
        if i == 0:
            to_pairs(weights, parity)
            wait_bytes(v.smalls_z, v.r_misc.at[1])
            total = v.smalls_z[0].astype(F32)
            for z in range(1, 4):
                total += v.smalls_z[z].astype(F32)
            v.smalls_sum[...] = total.astype(BF16)
            mine = v.smalls.at[at.b]
            pltpu.make_async_copy(v.smalls_sum, mine, v.r_misc.at[10]).start()

            def spread(step, carry):
                remote(
                    v.smalls_sum,
                    mine,
                    v.s_misc.at[10],
                    v.r_misc.at[10],
                    ((at.b + step) % 8, at.z),
                ).start()
                return carry

            lax.fori_loop(1, 8, spread, 0)
        if i == 1:
            plane_weights(at, v.win, v.wi, v.s_misc.at[0], v.r_misc.at[0])
            wait_bytes(v.w_near, v.r_w.at[2])
            to_pairs([v.w_near.at[k] for k in range(3)], 1 - parity)
        if i:
            rows_spread[i - 1].relay()
    wait_bytes(v.wi.at[:, pl.ds(0, 128)], v.r_misc.at[0])
    col_in.send(0)

    wait_bytes(wqkv.at[pl.ds(0, 512)], v.r_w.at[0])
    for r in range(4):
        part = wqkv.at[lanes(2 * at.chip(r) + at.c)]
        remote(part, part, v.s_w.at[1], v.r_w.at[1], at.sibling()).start()
    rows_spread[3].relay()

    wait_bytes(v.smalls, v.r_misc.at[10])
    for b in range(8):
        v.par[:, 128 * b : 128 * b + 128] = v.smalls[b].astype(F32)[0:8]
    row = lax.broadcasted_iota(jnp.int32, (8, 128), 0)
    for h in range(4):
        rows = v.smalls[2 * h + at.b // 4].astype(F32)[8:16]
        rows = jnp.where(row == at.b % 4, rows, 0.0)
        v.bins[0:1, 128 * h : 128 * h + 128] = jnp.sum(rows, axis=0, keepdims=True)
    bias_q = v.par[0:1, lanes(pair)]
    bias_v = v.par[1:2, lanes(pair)]
    wait_bytes(wqkv.at[pl.ds(0, 512)], v.r_w.at[1])

    whole = wo_spread.block(0)
    wait_bytes(whole, v.r_o.at[4])
    wo_spread.start()
    remote(whole, whole, v.s_o.at[0], v.r_o.at[0], at.sibling()).start()
    plane_weights(at, v.wback, v.wb, v.s_misc.at[2], v.r_misc.at[2])

    for r in range(4):
        chip = at.chip(r)
        if r:
            for i in range(4):
                rows_spread[i].rest(r)
        rows = chip_rows(chip)
        v.proj[...] = dot_nn(xs[rows], wqkv[...])
        v.queries[rows] = (v.proj[:, 0:128] + bias_q).astype(BF16)
        own_rows = chip_rows(at.c * 4 + chip)
        v.keys_all[own_rows] = v.proj[:, 128:256].astype(BF16)
        v.values_all[own_rows] = (v.proj[:, 256:384] + bias_v).astype(BF16)
        for k, ref in enumerate((v.keys_all, v.values_all)):
            view = ref.at[own_rows]
            remote(view, view, v.s_kv.at[k, r], v.r_kv.at[k, r], at.sibling()).start()

    for r in range(4):
        for k, ref in enumerate((v.keys_all, v.values_all)):
            wait_bytes(ref.at[pl.ds(0, 256)], v.r_kv.at[k, r])

    col_in.arrive(0)
    col_in.send(1)
    scores = v.scores

    def attend(step, carry):
        chip = (at.q + 1 + step) % 4
        rows = chip_rows(chip)
        outs = []
        logs = []
        for h in range(2):
            q = (v.queries[rows].astype(F32) * head_mask(h) * HEAD_DIM**-0.5).astype(BF16)
            scores[...] = contract_cols(q, v.keys_all[...])
            top = jnp.max(scores[...], axis=-1, keepdims=True)
            weights = jnp.exp(scores[...] - top)
            total = jnp.sum(weights, axis=-1, keepdims=True)
            outs.append(dot_nn(weights.astype(BF16), v.values_all[...]) / total)
            logs.append(top + jnp.log(total))
        first = head_mask(0) > 0.5
        merged = jnp.where(first, outs[0], outs[1])
        v.mixed[rows] = merged
        v.log_sums[rows] = jnp.where(first, logs[0], logs[1])
        v.att_send[rows] = merged.astype(BF16)
        for k in range(4):
            plane = (at.z + 1 + k) % 4
            send_or_copy(
                v.att_send.at[slot_rows(chip * 4 + plane)],
                v.att.at[slot_rows(parity), lanes(pair)],
                v.s_misc.at[3],
                v.r_misc.at[3],
                (2 * chip + at.c, plane),
                step == 3 if k == 3 else None,
            )

        @pl.when(step == 0)
        def _():
            wo_spread.relay()

        @pl.when(step == 2)
        def _():
            col_in.arrive(1)
            col_in.send(2)

        return carry

    lax.fori_loop(0, 4, attend, 0)

    wait_bytes(v.wb.at[:, pl.ds(0, 128)], v.r_misc.at[2])
    col_back.send(0)
    for r in (1, 2, 3):
        wo_spread.rest(r)
        part = wo_spread.block(r)
        remote(part, part, v.s_o.at[r], v.r_o.at[r], at.sibling()).start()
    for r in range(4):
        wait_bytes(whole, v.r_o.at[r])
    wait_bytes(v.att, v.r_misc.at[3])


def ffn_phase(at, v, col_in, col_back, gathers, scatters, sum_back, sum_in):
    n1, terms, peer_in = v.n1, v.terms, v.peer_in

    def param(i):
        return v.par[i : i + 1, :]

    def local(h, i):
        return pl.ds(64 * h + 32 * i, 32)

    def chip_part(h, i):
        return pl.ds(pl.multiple_of(h * 128 + at.c * 64 + 32 * i, 32), 32)

    n1[...] = dot_nn(v.att[...], v.wo[...])
    for h in range(2):
        for i in range(2):
            rows = local(h, i)
            unit, scale = norm_rows(v.x[rows].astype(F32) + n1[rows] + param(2))
            v.unit1[rows] = unit
            v.scale1[rows] = jnp.broadcast_to(scale, (32, 128))
            normed = unit * param(3) + param(4)
            n1[rows] = normed
            v.norm_slots[at.q, chip_part(h, i)] = normed.astype(BF16)
        gathers[0][h].start()

    for h in range(2):
        gathers[0][h].relay()
    col_back.arrive(0)
    col_back.send(1)
    col_in.arrive(2)

    for n, (h, r) in enumerate(((0, 0), (1, 0), (0, 1), (0, 2), (0, 3), (1, 1), (1, 2), (1, 3))):
        chip = gathers[0][h].step(r)
        v.pre[...] = dot_nn(v.norm_slots[chip, pl.ds(128 * h, 128)], v.wi[...])

        def activate(i, carry, r=r, h=h):
            rows = pl.ds(pl.multiple_of(i * 32, 32), 32)
            into = pl.ds(pl.multiple_of(128 * h + i * 32, 32), 32)
            u = v.pre[rows] + v.bins[...]
            cdf = 0.5 * (1.0 + lax.erf(u * math.sqrt(0.5)))
            bell = jnp.exp(-0.5 * u * u) * (1.0 / math.sqrt(2.0 * math.pi))
            v.hid[r, into] = (u * cdf).astype(BF16)
            v.slope[r, into] = cdf + u * bell
            return carry

        lax.fori_loop(0, 4, activate, 0)
        if n == 4:
            col_back.arrive(1)
            col_back.send(2)
    col_back.arrive(2)

    def to_plane(scatter, done, h, r, product):
        terms[r, pl.ds(128 * h, 128)] = product
        scatter[h].put(r, terms[r, part_rows(h, 1 - at.c)])
        done.append((h, r))
        if len(done) > 3:
            pass_on(scatter, *done[-4])

    def pass_on(scatter, h, r):
        total = scatter[h].add(r, terms[r, part_rows(h, at.c)])
        if r == 0:
            terms[0, part_rows(h, at.c)] = total

    done = []
    for h in range(2):
        for r in (3, 1, 2, 0):
            product = contract_cols(v.hid[r, pl.ds(128 * h, 128)], v.wb[...])
            to_plane(scatters[0], done, h, r, product)
    for one in done[-3:]:
        pass_on(scatters[0], *one)

    def peers(side, rows):
        return (
            peer_in[side, 1, rows].astype(F32)
            + peer_in[side, 2, rows].astype(F32)
            + peer_in[side, 3, rows].astype(F32)
        )

    def column_sums(parts, sums):
        return tuple(
            kept + jnp.sum(part.reshape(4, 8, 1024), axis=0) for kept, part in zip(sums, parts)
        )

    gbin = [jnp.zeros((8, 512), F32)]
    done = []

    def hidden_grad(h, r):
        chip = gathers[1][h].step(r)
        v.pre[...] = dot_nn(v.grad_slots[chip, pl.ds(128 * h, 128)], v.wb[...])

        def deactivate(i, carry):
            rows = pl.ds(pl.multiple_of(i * 32, 32), 32)
            into = pl.ds(pl.multiple_of(128 * h + i * 32, 32), 32)
            low = (v.pre[rows] * v.slope[r, into]).astype(BF16)
            v.low[r, into] = low
            return carry + jnp.sum(low.astype(F32).reshape(4, 8, 512), axis=0)

        gbin[0] = lax.fori_loop(0, 4, deactivate, gbin[0])
        product = contract_cols(v.low[r, pl.ds(128 * h, 128)], v.wi[...])
        to_plane(scatters[1], done, h, r, product)

    sums = tuple(jnp.zeros((8, 1024), F32) for _ in range(3))
    for h in range(2):
        scatters[0][h].arrive()
        for i in range(2):
            rows = local(h, i)
            total = terms[0, chip_part(h, i)] + peers(0, rows)
            unit, scale = norm_rows(n1[rows] + total + param(5))
            v.out[rows] = (unit * param(6) + param(7)).astype(BF16)
            g = v.cot[rows].astype(F32)
            d = norm_back(g * param(6), unit, scale)
            v.d2[rows] = d
            low = d.astype(BF16)
            v.grad_slots[at.q, chip_part(h, i)] = low
            sums = column_sums((g * unit, g, low.astype(F32)), sums)
        gathers[1][h].start()
        if h == 0:
            hidden_grad(0, 0)
            gathers[1][0].relay()
    for row, total in zip((6, 7, 5), sums):
        v.vec[row : row + 1, :] = jnp.sum(total, axis=0, keepdims=True)

    hidden_grad(0, 1)
    hidden_grad(0, 2)
    gathers[1][1].relay()
    for h, r in ((0, 3), (1, 0), (1, 1), (1, 2), (1, 3)):
        hidden_grad(h, r)
    for one in done[-3:]:
        pass_on(scatters[1], *one)
    v.gbin[...] = jnp.sum(gbin[0], axis=0, keepdims=True)

    def weight_grad(slots, right, into):
        def one(step, carry):
            other = (at.q + step) % 4
            total = jnp.zeros((256, 512), F32)
            for r in range(4):
                total += contract_rows(slots[at.chip(r), :, chip_rows(other)], right(r))
            into[2 * other] = total[0:128].astype(BF16)
            into[2 * other + 1] = total[128:256].astype(BF16)
            return carry

        lax.fori_loop(0, 4, one, 0)

    sums = tuple(jnp.zeros((8, 1024), F32) for _ in range(3))
    for h in range(2):
        if h == 0:
            weight_grad(v.grad_slots, lambda r: v.hid[r], v.g_back)
            for gather in gathers[1]:
                gather.end()
            sum_back.begin((0,))
        else:
            weight_grad(v.norm_slots, lambda r: v.low[r], v.g_in)
        scatters[1][h].arrive()
        for i in range(2):
            rows = local(h, i)
            total = v.d2[rows] + terms[0, chip_part(h, i)] + peers(1, rows)
            unit = v.unit1[rows]
            d = norm_back(total * param(3), unit, v.scale1[rows][:, :1])
            v.d1[rows] = d
            low = d.astype(BF16)
            v.db[rows] = low
            sums = column_sums((total * unit, total, low.astype(F32)), sums)
        rows = pl.ds(64 * h, 64)
        v.da_send[rows] = contract_cols(v.db[rows], v.wo[...]).astype(BF16)
        for r in range(4):
            chip = at.chip(r)
            for plane in (h, h + 2):
                pair = 2 * (plane - h) + chip
                send_or_copy(
                    v.da_send.at[rows, lanes(pair)],
                    v.da.at[slot_rows(at.place)],
                    v.s_misc.at[4],
                    v.r_da.at[r],
                    (2 * chip + at.c, plane),
                    None if r else at.z == plane,
                )

    for row, total in zip((3, 4, 2), sums):
        v.vec[row : row + 1, :] = jnp.sum(total, axis=0, keepdims=True)
    v.vec[0:2, :] = jnp.zeros((2, 1024), F32)
    sum_back.begin((1, 2))
    sum_in.begin((0, 1, 2))


def grads_phase(at, v, gathers, scatters, out_scatter, sum_in, sum_back):
    xs, wqkv, terms = v.xs, v.wqkv, v.terms
    parity, pair = at.parity, at.pair

    for h in range(2):
        scatters[0][h].end()
    for r in range(4):
        for core in (1 - at.c, at.c):
            part = contract_rows(v.db[:, lanes(2 * at.chip(r) + core)], v.att[...])
            if core is at.c:
                terms[r, 0:128] = part
            else:
                out_scatter.put(r, part)

    v.q_turned[...] = v.queries[...].astype(F32).T.astype(BF16)
    v.dk_turned[...] = jnp.zeros_like(v.dk_turned)
    v.dv_turned[...] = jnp.zeros_like(v.dv_turned)
    wait_bytes(v.da.at[chip_rows(at.q)], v.r_da.at[0])
    s_buf, d_buf, p_buf = v.scores, v.d_buf, v.p_buf

    def attend(step, carry):
        chip = ((at.y + step // 2) % 2) * 2 + (at.x + step % 2) % 2
        rows = chip_rows(chip)

        @pl.when(step > 0)
        def _():
            wait_bytes(v.da.at[rows], v.r_da.at[step])

        v.da_turned[:, rows] = v.da[rows].astype(F32).T.astype(BF16)
        parts = []
        for h in range(2):
            mask = head_mask(h)
            grad = v.da[rows].astype(F32) * mask
            delta = jnp.sum(grad * v.mixed[rows], axis=-1, keepdims=True)
            q = (v.queries[rows].astype(F32) * mask * HEAD_DIM**-0.5).astype(BF16)
            s_buf[...] = contract_cols(q, v.keys_all[...])
            d_buf[...] = contract_cols(grad.astype(BF16), v.values_all[...])
            logs = v.log_sums[rows][:, h * HEAD_DIM : h * HEAD_DIM + 1]
            probs = jnp.exp(s_buf[...] - logs)
            p_buf[...] = probs.astype(BF16)
            low = (probs * (d_buf[...] - delta)).astype(BF16)
            band = pl.ds(h * HEAD_DIM, HEAD_DIM)
            v.dv_turned[band] += dot_nn(v.da_turned[band, rows], p_buf[...])
            v.dk_turned[band] += dot_nn(v.q_turned[band, rows], low)
            parts.append(dot_nn(low, v.keys_all[...]))
        v.dq[rows] = jnp.where(head_mask(0) > 0.5, parts[0], parts[1]) * HEAD_DIM**-0.5

        @pl.when(step == 0)
        def _():
            for r in (3, 1, 2):
                out_scatter.add(r, terms[r, 0:128])
            terms[0, 0:128] = out_scatter.add(0, terms[0, 0:128])
            sum_back.relay(1, 0)

        @pl.when(step == 1)
        def _():
            sum_back.relay(1, 1)

        @pl.when(step == 3)
        def _():
            sum_back.relay(2, 0)

        return carry

    lax.fori_loop(0, 4, attend, 0)

    other = core_rows(1 - at.c)
    mine = core_rows(at.c)
    v.out_k[...] = v.dk_turned[:, other].T * HEAD_DIM**-0.5
    v.out_v[...] = v.dv_turned[:, other].T
    for k, (ref, into) in enumerate(((v.out_k, v.sib_k), (v.out_v, v.sib_v))):
        remote(ref, into, v.s_kv2.at[k], v.r_kv2.at[k], at.sibling()).start()
    dqkv = v.dqkv
    low = v.dq[...].astype(BF16)
    dqkv[:, 0:128] = low
    v.vec[0:1, lanes(pair)] = jnp.sum(low.astype(F32), axis=0, keepdims=True)
    own_k = v.dk_turned[:, mine].T * HEAD_DIM**-0.5
    wait_bytes(v.sib_k, v.r_kv2.at[0])
    dqkv[:, 128:256] = (own_k + v.sib_k[...]).astype(BF16)
    own_v = v.dv_turned[:, mine].T
    wait_bytes(v.sib_v, v.r_kv2.at[1])
    low = (own_v + v.sib_v[...]).astype(BF16)
    dqkv[:, 256:384] = low
    v.vec[1:2, lanes(pair)] = jnp.sum(low.astype(F32), axis=0, keepdims=True)

    notes = v.notes
    for b in range(8):
        notes[b, 0:8] = v.vec[:, 128 * b : 128 * b + 128]
        notes[b, 8:16] = jnp.zeros((8, 128), F32)
    row = lax.broadcasted_iota(jnp.int32, (8, 128), 0)
    for h in range(4):
        notes[2 * h + at.b // 4, 8:16] = jnp.where(
            row == at.b % 4, v.gbin[0:1, 128 * h : 128 * h + 128], 0.0
        )
    pltpu.make_async_copy(notes.at[at.b], v.notes_p.at[at.b], v.r_misc.at[5]).start()

    def spread(step, carry):
        to = (at.b + step) % 8
        remote(
            notes.at[to], v.notes_p.at[at.b], v.s_misc.at[5], v.r_misc.at[5], (to, at.z)
        ).start()
        return carry

    lax.fori_loop(1, 8, spread, 0)

    for gather in gathers:
        gather.end()
    x_out, x_in, x_via = v.norm_slots, v.grad_slots.at[0:2], v.grad_slots.at[2:4]
    for r in (3, 1, 2, 0):
        part = contract_cols(dqkv[chip_rows(at.chip(r))], wqkv[...])
        if r:
            x_out[r] = part.astype(BF16)
        else:
            v.x_sum[...] = part
    def piece(dz, k):
        return pl.ds(pl.multiple_of(((at.z + dz) % 4) * 64 + 32 * k, 32), 32)

    order = (2, 1, 3, 0)

    def send_dx(dz, via):
        for r, k in ((1, 0), (2, 1)):
            rows = piece(dz, k)
            remote(
                x_out.at[3 if via else r, rows],
                x_via.at[r - 1, rows] if via else x_in.at[r - 1, rows],
                v.s_dx.at[dz, 0 if via else r, k],
                v.r_dx.at[dz, 0 if via else r, k],
                at.peer(r),
            ).start()

    for dz in order:
        send_dx(dz, True)

    def relay_dx(dz):
        for r, k in ((2, 0), (1, 1)):
            rows = piece(dz, k)
            wait_bytes(x_via.at[k, rows], v.r_dx.at[dz, 0, k])
            x_out[r, rows] = (
                x_out[r, rows].astype(F32) + x_via[k, rows].astype(F32)
            ).astype(BF16)
            remote(
                x_out.at[r, rows],
                x_in.at[r - 1, rows],
                v.s_dx.at[dz, r, k],
                v.r_dx.at[dz, r, k],
                at.peer(r),
            ).start()

    out_scatter.arrive()
    peer_in = v.peer_in.at[0]

    def out_rows(rows):
        total = (
            terms[0, rows]
            + peer_in[1, rows].astype(F32)
            + peer_in[2, rows].astype(F32)
            + peer_in[3, rows].astype(F32)
        )
        v.o_out[rows] = total.astype(BF16)

    by_rows(128, 32, out_rows)
    wide = pl.ds(pl.multiple_of(at.z * 256, 256), 256)
    pltpu.make_async_copy(v.o_out.at[:, wide], v.o_in.at[0], v.r_misc.at[8]).start()
    for dz in range(1, 4):
        plane = (at.z + dz) % 4
        remote(
            v.o_out.at[:, pl.ds(pl.multiple_of(plane * 256, 256), 256)],
            v.o_in.at[dz],
            v.s_misc.at[8],
            v.r_misc.at[8],
            (at.b, plane),
        ).start()

    def features(b):
        return contract_rows(xs[:, lanes(b)], dqkv[...])

    for r in range(4):
        v.w_sib_out[r] = features(2 * at.chip(r) + 1 - at.c)
        remote(
            v.w_sib_out.at[r], v.w_sib_in.at[r], v.s_ws.at[r], v.r_ws.at[r], at.sibling()
        ).start()
    for dz in order:
        send_dx(dz, False)
        relay_dx(dz)
    sum_in.relay(1, 0)
    sum_back.finish(v.gs_back, v.fin_back, v.s_misc.at[7], v.r_misc.at[7])
    plane_w = 2 * (at.z // 2) + at.y
    for r in range(4):
        total = features(2 * at.chip(r) + at.c)
        wait_bytes(v.w_sib_in.at[r], v.r_ws.at[r])
        v.w_out[r] = (total + v.w_sib_in[r]).astype(BF16)
        send_or_copy(
            v.w_out.at[r],
            v.w_in.at[parity, at.x],
            v.s_misc.at[6],
            v.r_misc.at[6],
            at.peer(r)[:1] + (plane_w,),
            plane_w == at.z if r == 0 else None,
        )

    sum_in.relay(1, 1)
    wait_bytes(v.notes_p, v.r_misc.at[5])
    total = v.notes_p[0]
    for b in range(1, 8):
        total += v.notes_p[b]
    v.notes_sum[...] = total
    mine = v.notes_in.at[at.z]
    pltpu.make_async_copy(v.notes_sum, mine, v.r_misc.at[11]).start()
    for dz in range(1, 4):
        remote(
            v.notes_sum, mine, v.s_misc.at[11], v.r_misc.at[11], (at.b, (at.z + dz) % 4)
        ).start()

    z_out, z_in = v.z_out, v.z_in
    for dz in order:
        plane = (at.z + dz) % 4
        rows = slot_rows(plane)
        for r in (1, 2):
            for k in range(2):
                wait_bytes(x_in.at[r - 1, piece(dz, k)], v.r_dx.at[dz, r, k])
        total = v.x_sum[rows] + x_in[0, rows].astype(F32) + x_in[1, rows].astype(F32)
        if dz:
            z_out[dz] = total.astype(BF16)
            remote(
                z_out.at[dz], z_in.at[dz], v.s_dz.at[dz], v.r_dz.at[dz], (at.b, plane)
            ).start()
        else:
            v.x_own[...] = total
        if dz == 1:
            sum_in.relay(2, 0)
    sum_in.finish(v.gs_in, v.fin_in, v.s_misc.at[9], v.r_misc.at[9])
    for dz in (1, 2, 3):
        wait_bytes(z_in.at[dz], v.r_dz.at[dz])
    same = slot_rows(parity)
    v.gtok[same] = (v.d1[same] + v.x_own[...] + z_in[2].astype(F32)).astype(BF16)
    cross = slot_rows(1 - parity)
    v.gtok[cross] = (v.d1[cross] + z_in[1].astype(F32) + z_in[3].astype(F32)).astype(BF16)

    wait_bytes(v.o_in, v.r_misc.at[8])
    wait_bytes(v.w_in, v.r_misc.at[6])
    wait_bytes(v.notes_in, v.r_misc.at[11])
    wait_bytes(v.fin_back, v.r_misc.at[7])
    wait_bytes(v.fin_in, v.r_misc.at[9])


def end_phase(at, v, col_in, col_back, ends):
    for one in ends:
        one.end()
    slot = v.xs.at[slot_rows(0)]
    for dz in range(1, 4):
        wait_bytes(slot, v.s_z.at[dz])
    for dz in range(4):
        for r in range(3):
            for k in range(2):
                wait_bytes(v.grad_slots.at[0, pl.ds(0, 32)], v.s_dx.at[dz, r, k])
    wait_bytes(v.wqkv.at[pl.ds(0, 384)], v.s_w.at[0])
    wait_bytes(v.wqkv.at[pl.ds(0, 512)], v.s_w.at[1])
    wait_bytes(v.w_near, v.s_w.at[2])
    seven = v.wi.at[pl.ds(0, 896), pl.ds(0, 128)]
    for i in (0, 2, 7, 9):
        wait_bytes(seven, v.s_misc.at[i])
    wait_bytes(v.smalls.at[pl.ds(0, 3)], v.s_misc.at[1])
    wait_bytes(v.smalls.at[pl.ds(0, 7)], v.s_misc.at[10])
    wait_bytes(v.wo.at[pl.ds(0, 768), pl.ds(0, 128)], v.s_o.at[4])
    for r in range(4):
        wait_bytes(v.wo.at[:, pl.ds(0, 128)], v.s_o.at[r])
    for r in range(4):
        for k in range(2):
            wait_bytes(v.keys_all.at[pl.ds(0, 256)], v.s_kv.at[k, r])
    for i in (3, 4):
        wait_bytes(v.att_send.at[pl.ds(0, 960)], v.s_misc.at[i])
    col_in.end()
    col_back.end()
    for dz in (1, 2, 3):
        wait_bytes(v.z_out.at[dz], v.s_dz.at[dz])
    for k in range(2):
        wait_bytes(v.sib_k, v.s_kv2.at[k])
    wait_bytes(v.notes.at[pl.ds(0, 7)], v.s_misc.at[5])
    wait_bytes(v.notes.at[pl.ds(0, 3)], v.s_misc.at[11])
    for r in range(4):
        wait_bytes(v.w_sib_out.at[r], v.s_ws.at[r])
    plane_w = 2 * (at.z // 2) + at.y

    @pl.when(plane_w == at.z)
    def _():
        wait_bytes(v.w_out.at[pl.ds(0, 3)], v.s_misc.at[6])

    @pl.when(plane_w != at.z)
    def _():
        wait_bytes(v.w_out, v.s_misc.at[6])

    wait_bytes(v.o_in.at[pl.ds(0, 3)], v.s_misc.at[8])


def finish_kernel(
    place_ref,
    out_in,
    gtok_in,
    w_in,
    o_in,
    fin_in,
    fin_back,
    notes_in,
    out_ref,
    gtok_ref,
    gq_ref,
    gk_ref,
    gv_ref,
    gout_ref,
    gwin_ref,
    gwback_ref,
    small_ref,
    bin_ref,
):
    out_ref[...] = out_in[...]
    gtok_ref[...] = gtok_in[...]
    for x in range(2):
        total = w_in[0, x].astype(F32) + w_in[1, x].astype(F32)
        for k, ref in enumerate((gq_ref, gk_ref, gv_ref)):
            ref[:, 128 * x : 128 * x + 128] = total[:, 128 * k : 128 * k + 128]
    gout_ref[...] = (
        o_in[0].astype(F32) + o_in[1].astype(F32) + o_in[2].astype(F32) + o_in[3].astype(F32)
    ).T
    gwin_ref[...] = fin_in[...].astype(F32)
    gwback_ref[...] = fin_back[...].astype(F32)
    total = notes_in[0] + notes_in[1] + notes_in[2] + notes_in[3]
    z = place_ref[0]
    part = jnp.zeros((8, 32), F32)
    units = jnp.zeros((1, 128), F32)
    for k in range(4):
        part += jnp.where(z == k, total[0:8, 32 * k : 32 * k + 32], 0.0)
        units += jnp.where(z == k, total[8 + k : 9 + k], 0.0)
    small_ref[...] = part
    bin_ref[...] = units


def vmem():
    return pl.BlockSpec(memory_space=pltpu.VMEM)


def run_layer(*args):
    results = [e for _, e in entries(Results)]
    scratch = [pltpu.VMEM(s, t) for _, (s, t) in entries(Scratch)]
    for _, shape in entries(Semaphores):
        scratch += [DMA(shape), DMA(shape)]
    return pl.pallas_call(
        layer_kernel,
        out_shape=[jax.ShapeDtypeStruct(s, t) for s, t in results],
        in_specs=[vmem()] * len(args),
        out_specs=[vmem()] * len(results),
        scratch_shapes=scratch,
        compiler_params=pltpu.CompilerParams(
            collective_id=1, has_side_effects=True, vmem_limit_bytes=VMEM_LIMIT
        ),
    )(*args)


def run_finish(*args):
    shapes = (
        ((128, 1024), BF16),
        ((128, 1024), BF16),
        ((128, 256), F32),
        ((128, 256), F32),
        ((128, 256), F32),
        ((256, 128), F32),
        ((128, 1024), F32),
        ((128, 1024), F32),
        ((8, 32), F32),
        ((1, 128), F32),
    )
    return pl.pallas_call(
        finish_kernel,
        out_shape=[jax.ShapeDtypeStruct(s, t) for s, t in shapes],
        in_specs=[pl.BlockSpec(memory_space=pltpu.SMEM)] + [vmem()] * (len(args) - 1),
        out_specs=[vmem()] * len(shapes),
        compiler_params=pltpu.CompilerParams(vmem_limit_bytes=VMEM_LIMIT),
    )(*args)


DMA = pltpu.SemaphoreType.DMA


def fast_device(
    tokens,
    w_query,
    w_key,
    w_value,
    w_out,
    b_query,
    b_value,
    b_out,
    norm1_gain,
    norm1_shift,
    w_in,
    w_back,
    b_in,
    b_back,
    norm2_gain,
    norm2_shift,
    cotangent,
):
    head_id = lax.axis_index("head")
    token_shape = tokens.shape
    model_dim = tokens.shape[2]
    x = tokens.reshape(-1, model_dim)
    vectors = jnp.stack(
        (b_query, b_value, b_out, norm1_gain, norm1_shift, b_back, norm2_gain, norm2_shift)
    )
    spread = jnp.where(
        lax.broadcasted_iota(jnp.int32, (1, 128), 1) // 32 == head_id,
        jnp.tile(vectors, (1, 4)),
        jnp.zeros((), BF16),
    )
    units = jnp.where(
        lax.broadcasted_iota(jnp.int32, (8, 1), 0) == head_id, b_in[None], jnp.zeros((), BF16)
    )
    small = jnp.concatenate((spread, units), axis=0)
    results = run_layer(
        x, w_query, w_key, w_value, w_out, small, w_in, w_back, cotangent.reshape(-1, model_dim)
    )
    output, grad_tokens, gq, gk, gv, gout, gw_in, gw_back, own, gb_in = run_finish(
        head_id.astype(jnp.int32).reshape(1), *results
    )
    return (
        output.reshape(token_shape),
        grad_tokens.reshape(token_shape),
        gq,
        gk,
        gv,
        gout,
        own[0],
        own[1],
        own[2],
        own[3],
        own[4],
        gw_in,
        gw_back,
        gb_in.reshape(-1),
        own[5],
        own[6],
        own[7],
    )


def solution(mesh):
    in_specs = (
        P(None, ("blk", "head"), None),
        P("blk", "head"),
        P("blk", "head"),
        P("blk", "head"),
        P("head", "blk"),
        P(("blk", "head")),
        P(("blk", "head")),
        P(("blk", "head")),
        P(("blk", "head")),
        P(("blk", "head")),
        P("blk", "head"),
        P("blk", "head"),
        P(("blk", "head")),
        P(("blk", "head")),
        P(("blk", "head")),
        P(("blk", "head")),
        P(None, ("blk", "head"), None),
    )
    out_specs = (
        P(None, ("blk", "head"), None),
        P(None, ("blk", "head"), None),
        P("blk", "head"),
        P("blk", "head"),
        P("blk", "head"),
        P("head", "blk"),
        P(("blk", "head")),
        P(("blk", "head")),
        P(("blk", "head")),
        P(("blk", "head")),
        P(("blk", "head")),
        P("blk", "head"),
        P("blk", "head"),
        P(("blk", "head")),
        P(("blk", "head")),
        P(("blk", "head")),
        P(("blk", "head")),
    )
    sizes = (mesh.shape["blk"], mesh.shape["head"])
    body = fast_device if sizes == (8, 4) else per_device
    return jax.shard_map(
        body, mesh=mesh, in_specs=in_specs, out_specs=out_specs, check_vma=False
    )
```

```python
import functools
import math

import jax
import jax.numpy as jnp
from jax import lax
from jax.experimental import pallas as pl
from jax.experimental.pallas import tpu as pltpu
from jax.sharding import PartitionSpec as P

HEAD_DIM = 64


NORM_EPS = 1e-05


def layer_norm(summed, gain, shift):
    centre = jnp.mean(summed, axis=-1, keepdims=True)
    centred = summed - centre
    spread = jnp.mean(centred * centred, axis=-1, keepdims=True)
    return centred * lax.rsqrt(spread + NORM_EPS) * gain + shift


def gelu_exact(inputs):
    return jax.nn.gelu(inputs, approximate=False)


def split_heads(packed):
    return packed.reshape(packed.shape[0], packed.shape[1], -1, HEAD_DIM)


def contract_rows(left, right):
    return lax.dot_general(
        left, right, (((0,), (0,)), ((), ())), preferred_element_type=jnp.float32
    )


def contract_cols(left, right):
    return lax.dot_general(
        left, right, (((1,), (1,)), ((), ())), preferred_element_type=jnp.float32
    )


def score_block(queries4, keys4):
    return jnp.einsum(
        "sqge,skge->sqgk", queries4, keys4, preferred_element_type=jnp.float32
    ) * HEAD_DIM ** (-0.5)


def score_grads(queries4, keys4, values4, grads4, log_sums, deltas):
    probs = jnp.exp(score_block(queries4, keys4) - log_sums[..., None])
    d_probs = jnp.einsum("sqge,skge->sqgk", grads4, values4, preferred_element_type=jnp.float32)
    d_scores = (probs * (d_probs - deltas[..., None])).astype(jnp.bfloat16)
    return (probs.astype(jnp.bfloat16), d_scores)


def token_rows(local):
    return lax.all_gather(local, "head", axis=1, tiled=True)


def token_partials(terms):
    return lax.psum_scatter(
        terms.astype(jnp.bfloat16), "head", scatter_dimension=1, tiled=True
    ).astype(jnp.float32)


def place_part(part, full_len, start):
    return lax.dynamic_update_slice_in_dim(jnp.zeros((full_len,), jnp.float32), part, start, 0)


def per_device(
    tokens,
    w_query,
    w_key,
    w_value,
    w_out,
    b_query,
    b_value,
    b_out,
    norm1_gain,
    norm1_shift,
    w_in,
    w_back,
    b_in,
    b_back,
    norm2_gain,
    norm2_shift,
    cotangent,
):
    f32 = jnp.float32
    bf16 = jnp.bfloat16
    score_scale = HEAD_DIM ** (-0.5)
    bq_full, bv_full, bo_full, gain_one, shift_one, bin_full, bback_full, gain_two, shift_two = (
        lax.all_gather(b_query, ("blk", "head"), axis=0, tiled=True),
        lax.all_gather(b_value, ("blk", "head"), axis=0, tiled=True),
        lax.all_gather(b_out, ("blk", "head"), axis=0, tiled=True),
        lax.all_gather(norm1_gain, ("blk", "head"), axis=0, tiled=True),
        lax.all_gather(norm1_shift, ("blk", "head"), axis=0, tiled=True),
        lax.all_gather(b_in, ("blk", "head"), axis=0, tiled=True),
        lax.all_gather(b_back, ("blk", "head"), axis=0, tiled=True),
        lax.all_gather(norm2_gain, ("blk", "head"), axis=0, tiled=True),
        lax.all_gather(norm2_shift, ("blk", "head"), axis=0, tiled=True),
    )
    attn_cols, out_rows, ffn_cols = (
        lax.all_gather(jnp.stack((w_query, w_key, w_value)), "blk", axis=1, tiled=True),
        lax.all_gather(w_out, "blk", axis=1, tiled=True),
        lax.all_gather(jnp.stack((w_in, w_back)), "blk", axis=1, tiled=True),
    )
    seq_count, local_len, model_dim = tokens.shape
    token_shape = (seq_count, local_len, model_dim)
    head_id = lax.axis_index("head")
    width_part = attn_cols.shape[2]
    bq_part = lax.dynamic_slice_in_dim(bq_full, head_id * width_part, width_part).astype(f32)
    bv_part = lax.dynamic_slice_in_dim(bv_full, head_id * width_part, width_part).astype(f32)
    wide_rows = token_rows(tokens)
    wide_len = wide_rows.shape[1]
    wide_flat = wide_rows.reshape(-1, model_dim)
    head_shape = (seq_count, wide_len, width_part)
    wide_shape = (seq_count, wide_len, model_dim)
    query_heads = (
        (jnp.dot(wide_flat, attn_cols[0], preferred_element_type=f32) + bq_part)
        .astype(bf16)
        .reshape(head_shape)
    )
    key_heads = (
        jnp.dot(wide_flat, attn_cols[1], preferred_element_type=f32)
        .astype(bf16)
        .reshape(head_shape)
    )
    value_heads = (
        (jnp.dot(wide_flat, attn_cols[2], preferred_element_type=f32) + bv_part)
        .astype(bf16)
        .reshape(head_shape)
    )
    query4 = split_heads(query_heads)
    key4 = split_heads(key_heads)
    value4 = split_heads(value_heads)
    stat_shape = query4.shape[:3]
    pieces = (
        lax.all_gather(key_heads, "blk", axis=1, tiled=True),
        lax.all_gather(value_heads, "blk", axis=1, tiled=True),
    )
    maxima = jnp.full(stat_shape, -1e30, f32)
    scores = score_block(query4, split_heads(pieces[0]))
    new_max = jnp.maximum(maxima, jnp.max(scores, axis=-1))
    weights = jnp.exp(scores - new_max[..., None])
    totals = jnp.sum(weights, axis=-1)
    summed = jnp.einsum(
        "sqgk,skge->sqge", weights.astype(bf16), split_heads(pieces[1]), preferred_element_type=f32
    )
    maxima, totals, summed = (new_max, totals, summed)
    log_sums = maxima + jnp.log(totals)
    attended4 = summed / totals[..., None]
    attended_heads = attended4.reshape(head_shape).astype(bf16)
    attended_flat = attended_heads.reshape(-1, width_part)
    branch_terms = jnp.dot(attended_flat, out_rows, preferred_element_type=f32).reshape(wide_shape)
    branch = token_partials(branch_terms).reshape(-1, model_dim) + bo_full.astype(f32)
    flat_rows = tokens.reshape(-1, model_dim)
    normed, norm1_pull = jax.vjp(
        layer_norm, flat_rows.astype(f32) + branch, gain_one.astype(f32), shift_one.astype(f32)
    )
    normed_low = normed.astype(bf16)
    ffn_full = lax.all_gather(ffn_cols, "head", axis=2, tiled=True)
    pre_act = jnp.dot(normed_low, ffn_full[0], preferred_element_type=f32) + bin_full.astype(f32)
    hidden_act, gelu_pull = jax.vjp(gelu_exact, pre_act)
    hidden_low = hidden_act.astype(bf16)
    ffn_out = contract_cols(hidden_low, ffn_full[1]) + bback_full.astype(f32)
    final, norm2_pull = jax.vjp(
        layer_norm, normed + ffn_out, gain_two.astype(f32), shift_two.astype(f32)
    )
    output = final.astype(bf16).reshape(token_shape)
    d_second, grad_norm2_gain, grad_norm2_shift = norm2_pull(
        cotangent.reshape(-1, model_dim).astype(f32)
    )
    d_ffn = d_second.astype(bf16)
    grad_b_back = jnp.sum(d_ffn.astype(f32), axis=0)
    grad_back_whole = contract_rows(d_ffn, hidden_low)
    d_hidden = jnp.dot(d_ffn, ffn_full[1], preferred_element_type=f32)
    d_pre = gelu_pull(d_hidden)[0].astype(bf16)
    grad_b_in = jnp.sum(d_pre.astype(f32), axis=0)
    grad_in_whole = contract_rows(normed_low, d_pre)
    ffn_grad_parts = lax.psum_scatter(
        jnp.stack((grad_in_whole, grad_back_whole)).astype(jnp.bfloat16),
        "head",
        scatter_dimension=2,
        tiled=True,
    ).astype(jnp.float32)
    d_normed = d_second + contract_cols(d_pre, ffn_full[0])
    d_first, grad_norm1_gain, grad_norm1_shift = norm1_pull(d_normed)
    d_branch = d_first.astype(bf16)
    grad_b_out = jnp.sum(d_branch.astype(f32), axis=0)
    wide_dbranch = token_rows(d_branch.reshape(token_shape)).reshape(-1, model_dim)
    grad_out_part = contract_rows(attended_flat, wide_dbranch)
    grad_heads = contract_cols(wide_dbranch, out_rows).astype(bf16).reshape(head_shape)
    grads4 = split_heads(grad_heads)
    deltas = jnp.sum(grads4.astype(f32) * attended4, axis=-1)
    row_stats = (
        lax.all_gather(log_sums, "blk", axis=1, tiled=True),
        lax.all_gather(deltas, "blk", axis=1, tiled=True),
    )
    pieces = (
        lax.all_gather(key_heads, "blk", axis=1, tiled=True),
        lax.all_gather(value_heads, "blk", axis=1, tiled=True),
        lax.all_gather(query_heads, "blk", axis=1, tiled=True),
        lax.all_gather(grad_heads, "blk", axis=1, tiled=True),
    )
    piece_keys = split_heads(pieces[0])
    piece_values = split_heads(pieces[1])
    piece_queries = split_heads(pieces[2])
    piece_grads = split_heads(pieces[3])
    piece_sums = row_stats[0]
    piece_deltas = row_stats[1]
    own_probs, own_scores = score_grads(query4, piece_keys, piece_values, grads4, log_sums, deltas)
    d_query = score_scale * jnp.einsum(
        "sqgk,skge->sqge", own_scores, piece_keys, preferred_element_type=f32
    )
    probs_low, d_scores = score_grads(
        piece_queries, key4, value4, piece_grads, piece_sums, piece_deltas
    )
    key_acc = score_scale * jnp.einsum(
        "sqgk,sqge->skge", d_scores, piece_queries, preferred_element_type=f32
    )
    value_acc = jnp.einsum("sqgk,sqge->skge", probs_low, piece_grads, preferred_element_type=f32)
    d_query_low = d_query.reshape(-1, width_part).astype(bf16)
    d_key_low = key_acc.reshape(-1, width_part).astype(bf16)
    d_value_low = value_acc.reshape(-1, width_part).astype(bf16)
    grad_b_query = place_part(
        jnp.sum(d_query_low.astype(f32), axis=0), model_dim, head_id * width_part
    )
    grad_b_value = place_part(
        jnp.sum(d_value_low.astype(f32), axis=0), model_dim, head_id * width_part
    )
    attn_grad_parts = jnp.stack(
        (
            contract_rows(wide_flat, d_query_low),
            contract_rows(wide_flat, d_key_low),
            contract_rows(wide_flat, d_value_low),
        )
    )
    token_terms = (
        contract_cols(d_query_low, attn_cols[0])
        + contract_cols(d_key_low, attn_cols[1])
        + contract_cols(d_value_low, attn_cols[2])
    )
    d_tokens = d_first + token_partials(token_terms.reshape(wide_shape)).reshape(-1, model_dim)
    grad_tokens = d_tokens.astype(bf16).reshape(token_shape)
    attn_sums, grad_w_out, ffn_sums = (
        lax.psum_scatter(attn_grad_parts, "blk", scatter_dimension=1, tiled=True),
        lax.psum_scatter(grad_out_part, "blk", scatter_dimension=1, tiled=True),
        lax.psum_scatter(ffn_grad_parts, "blk", scatter_dimension=1, tiled=True),
    )
    (
        grad_b_query,
        grad_b_value,
        grad_b_out,
        grad_norm1_gain,
        grad_norm1_shift,
        grad_b_in,
        grad_b_back,
        grad_norm2_gain,
        grad_norm2_shift,
    ) = (
        lax.psum_scatter(grad_b_query, ("blk", "head"), scatter_dimension=0, tiled=True),
        lax.psum_scatter(grad_b_value, ("blk", "head"), scatter_dimension=0, tiled=True),
        lax.psum_scatter(grad_b_out, ("blk", "head"), scatter_dimension=0, tiled=True),
        lax.psum_scatter(grad_norm1_gain, ("blk", "head"), scatter_dimension=0, tiled=True),
        lax.psum_scatter(grad_norm1_shift, ("blk", "head"), scatter_dimension=0, tiled=True),
        lax.psum_scatter(grad_b_in, ("blk", "head"), scatter_dimension=0, tiled=True),
        lax.psum_scatter(grad_b_back, ("blk", "head"), scatter_dimension=0, tiled=True),
        lax.psum_scatter(grad_norm2_gain, ("blk", "head"), scatter_dimension=0, tiled=True),
        lax.psum_scatter(grad_norm2_shift, ("blk", "head"), scatter_dimension=0, tiled=True),
    )
    return (
        output,
        grad_tokens,
        attn_sums[0],
        attn_sums[1],
        attn_sums[2],
        grad_w_out,
        grad_b_query,
        grad_b_value,
        grad_b_out,
        grad_norm1_gain,
        grad_norm1_shift,
        ffn_sums[0],
        ffn_sums[1],
        grad_b_in,
        grad_b_back,
        grad_norm2_gain,
        grad_norm2_shift,
    )


MESH = pl.DeviceIdType.MESH
F32 = jnp.float32
BF16 = jnp.bfloat16
VMEM_LIMIT = 62 * 2**20


def dot_nn(left, right):
    return jnp.dot(left, right, preferred_element_type=F32)


class Place:
    def __init__(self):
        self.b = lax.axis_index("blk")
        self.z = lax.axis_index("head")
        self.y = self.b // 4
        self.x = (self.b // 2) % 2
        self.c = self.b % 2
        self.q = self.b // 2

    def chip(self, r):
        return ((self.y + r // 2) % 2) * 2 + (self.x + r % 2) % 2

    def peer(self, r):
        return (2 * self.chip(r) + self.c, self.z)

    def sibling(self):
        return (2 * self.q + 1 - self.c, self.z)


def remote(src, dst, send_sem, recv_sem, device):
    return pltpu.make_async_remote_copy(
        src_ref=src,
        dst_ref=dst,
        send_sem=send_sem,
        recv_sem=recv_sem,
        device_id=device,
        device_id_type=MESH,
    )


def wait_bytes(view, sem):
    pltpu.make_async_copy(view, view, sem).wait()


def greet_all(at):
    barrier = pltpu.get_barrier_semaphore()
    flat = at.b * 4 + at.z

    def greet(step, carry):
        other = (flat + step) % 32
        pl.semaphore_signal(
            barrier, inc=1, device_id=(other // 4, other % 4), device_id_type=MESH
        )
        return carry

    lax.fori_loop(1, 32, greet, 0)
    pl.semaphore_wait(barrier, 31)


def half(core):
    return pl.ds(pl.multiple_of(core * 128, 128), 128)


def lanes(index):
    return pl.ds(pl.multiple_of(index * 128, 128), 128)


def by_rows(count, size, step):
    def body(i, carry):
        step(pl.ds(pl.multiple_of(i * size, size), size))
        return carry

    lax.fori_loop(0, count // size, body, 0)


class Spread:
    def __init__(self, at, block, part, send, recv):
        self.at, self.block, self.part = at, block, part
        self.send, self.recv = send, recv

    def start(self):
        mine = self.block(0)
        for i in (0, 1):
            for r, k in ((1, i), (2, 1 - i)):
                piece = self.part(mine, k)
                remote(piece, piece, self.send, self.recv.at[r, k], self.at.peer(r)).start()

    def relay(self):
        for r, k in ((1, 0), (2, 1)):
            piece = self.part(self.block(r), k)
            wait_bytes(piece, self.recv.at[r, k])
            remote(piece, piece, self.send, self.recv.at[0, k], self.at.peer(3 - r)).start()

    def rest(self, r):
        block = self.block(r)
        for row, k in {1: ((1, 1),), 2: ((2, 0),), 3: ((0, 0), (0, 1))}[r]:
            wait_bytes(self.part(block, k), self.recv.at[row, k])


def part_rows(h, core):
    return pl.ds(pl.multiple_of(h * 128 + core * 64, 64), 64)


class Gather:
    def __init__(self, at, slots, h, send, recv, recv_sib):
        self.at, self.slots, self.h = at, slots, h
        self.send, self.recv_sib = send, recv_sib

        def part(block, k):
            return block.at[pl.ds(k * 32, 32)]

        self.spread = Spread(
            at, lambda r: slots.at[at.chip(r), part_rows(h, at.c)], part, send, recv
        )

    def to_sibling(self, r):
        block = self.spread.block(r)
        remote(block, block, self.send, self.recv_sib.at[r], self.at.sibling()).start()

    def start(self):
        self.spread.start()
        self.to_sibling(0)

    def relay(self):
        self.spread.relay()

    def forward(self, r):
        self.spread.rest(r)
        self.to_sibling(r)

    def ready(self, r):
        at = self.at
        wait_bytes(self.slots.at[at.chip(r), part_rows(self.h, 1 - at.c)], self.recv_sib.at[r])
        return at.chip(r)


class Exchange:
    def __init__(self, at, buffers, rows, send, recv, recv_sib):
        self.at, self.send, self.recv, self.recv_sib = at, send, recv, recv_sib
        self.sib_out, self.sib_in, self.out, self.into = buffers
        self.rows = rows

    def put(self, r, theirs):
        mine = self.sib_out.at[r, self.rows]
        mine[...] = theirs.astype(BF16)
        remote(
            mine,
            self.sib_in.at[r, self.rows],
            self.send,
            self.recv_sib.at[r],
            self.at.sibling(),
        ).start()

    def add(self, r, mine):
        wait_bytes(self.sib_in.at[r, self.rows], self.recv_sib.at[r])
        total = mine + self.sib_in[r, self.rows].astype(F32)
        if r == 0:
            return total
        held = self.out.at[r, self.rows]
        held[...] = total.astype(BF16)
        remote(
            held, self.into.at[r, self.rows], self.send, self.recv.at[r], self.at.peer(r)
        ).start()

    def arrive(self):
        for r in (1, 2, 3):
            wait_bytes(self.into.at[r, self.rows], self.recv.at[r])


def norm_rows(values):
    centre = jnp.mean(values, axis=-1, keepdims=True)
    centred = values - centre
    spread = jnp.mean(centred * centred, axis=-1, keepdims=True)
    scale = lax.rsqrt(spread + NORM_EPS)
    return centred * scale, scale


def norm_back(grad, unit, scale):
    centre = jnp.mean(grad, axis=-1, keepdims=True)
    along = jnp.mean(grad * unit, axis=-1, keepdims=True)
    return (grad - centre - unit * along) * scale


def send_or_copy(src, dst, send_sem, recv_sem, device, own):
    def away():
        remote(src, dst, send_sem, recv_sem, device).start()

    if own is None:
        away()
        return
    pl.when(jnp.logical_not(own))(away)

    @pl.when(own)
    def _():
        pltpu.make_async_copy(src, dst, recv_sem).start()


class Column:
    def __init__(self, at, ref, sems):
        self.at, self.ref = at, ref
        self.up_send, self.up_recv, self.down_send, self.down_recv = sems

    def block(self, plane):
        return self.ref.at[:, lanes(plane)]

    def sides(self, hop, act, arriving):
        z = self.at.z
        if arriving:
            below, above = z - 1 - hop, z + 1 + hop
            pl.when(below >= 0)(lambda: act(self.block(below), 0))
            pl.when(above <= 3)(lambda: act(self.block(above), 1))
        else:
            up = jnp.logical_and(z >= hop, z < 3)
            down = jnp.logical_and(z + hop <= 3, z > 0)
            pl.when(up)(lambda: act(self.block(z - hop), 0))
            pl.when(down)(lambda: act(self.block(z + hop), 1))

    def send(self, hop):
        def act(block, side):
            send = (self.up_send, self.down_send)[side].at[hop]
            recv = (self.up_recv, self.down_recv)[side].at[hop]
            remote(block, block, send, recv, (self.at.b, self.at.z + 1 - 2 * side)).start()

        self.sides(hop, act, False)

    def arrive(self, hop):
        def act(block, side):
            wait_bytes(block, (self.up_recv, self.down_recv)[side].at[hop])

        self.sides(hop, act, True)

    def end(self):
        def wait(hop):
            def act(block, side):
                wait_bytes(block, (self.up_send, self.down_send)[side].at[hop])

            return act

        for hop in range(3):
            self.sides(hop, wait(hop), False)


def plane_weights(at, src, dst, send_sem, recv_sem):
    rows, cols = lanes(at.b), lanes(at.z)
    pltpu.make_async_copy(src.at[:, lanes(at.b)], dst.at[rows, cols], recv_sem).start()

    def push(step, carry):
        other = (at.b + step) % 8
        remote(
            src.at[:, lanes(other)], dst.at[rows, cols], send_sem, recv_sem, (other, at.z)
        ).start()
        return carry

    lax.fori_loop(1, 8, push, 0)


class ColumnSum:
    def __init__(self, at, blocks, passing, send, recv):
        self.at, self.blocks, self.passing = at, blocks, passing
        self.send_sem, self.recv_sem = send, recv

    def plane(self, side, i):
        return i if side else 3 - i

    def hop(self, side):
        return 3 - self.at.z if side else self.at.z

    def next(self, side):
        return (self.at.b, self.at.z + 1 - 2 * side)

    def begin(self, which):
        for side in range(2):

            @pl.when(self.hop(side) == 0)
            def _(side=side):
                for i in which:
                    remote(
                        self.blocks.at[:, :, pl.ds(128 * self.plane(side, i), 128)],
                        self.passing.at[side, i],
                        self.send_sem.at[side, i],
                        self.recv_sem.at[side, i],
                        self.next(side),
                    ).start()

    def relay(self, hop, i):
        for side in range(2):

            @pl.when(self.hop(side) == hop)
            def _(side=side):
                held = self.passing.at[side, i]
                wait_bytes(held, self.recv_sem.at[side, i])
                cols = pl.ds(128 * self.plane(side, i), 128)
                for b in range(8):
                    self.passing[side, i, b] = (
                        self.passing[side, i, b].astype(F32)
                        + self.blocks[b, :, cols].astype(F32)
                    ).astype(BF16)
                remote(
                    held,
                    held,
                    self.send_sem.at[side, i],
                    self.recv_sem.at[side, i],
                    self.next(side),
                ).start()

    def finish(self, sums, final, send_out, recv_out):
        at = self.at
        own = lanes(at.z)
        for b in range(8):
            sums[b] = self.blocks[b, :, own]
        for side in range(2):
            for hop in range(1, 4):
                i = 3 - hop

                @pl.when(self.hop(side) == hop)
                def _(side=side, i=i):
                    wait_bytes(self.passing.at[side, i], self.recv_sem.at[side, i])
                    for b in range(8):
                        sums[b] = (
                            sums[b].astype(F32) + self.passing[side, i, b].astype(F32)
                        ).astype(BF16)

        def one(step, carry):
            other = (at.b + 1 + step) % 8
            send_or_copy(
                sums.at[other],
                final.at[:, lanes(at.b)],
                send_out,
                recv_out,
                (other, at.z),
                step == 7,
            )
            return carry

        lax.fori_loop(0, 8, one, 0)

    def end(self):
        for side in range(2):
            for i in range(3):

                @pl.when(self.hop(side) < 3 - i)
                def _(side=side, i=i):
                    wait_bytes(self.passing.at[side, i], self.send_sem.at[side, i])


def head_mask(h):
    lane = lax.broadcasted_iota(jnp.int32, (1, 128), 1)
    return jnp.where(lane // HEAD_DIM == h, 1.0, 0.0).astype(F32)


def slot_rows(index):
    return pl.ds(pl.multiple_of(index * 64, 64), 64)


def chip_rows(index):
    return pl.ds(pl.multiple_of(index * 256, 256), 256)


def core_rows(index):
    return pl.ds(pl.multiple_of(index * 1024, 1024), 1024)


class Inputs:
    small = x_hbm = cot_hbm = wq = wk = wv = wout = win = wback = None


def entries(table):
    return [(n, e) for n, e in vars(table).items() if n[0] != "_"]


class Results:
    out = ((128, 1024), BF16)
    gtok = ((128, 1024), BF16)
    w_in = ((2, 2, 128, 384), BF16)
    o_in = ((4, 128, 256), BF16)
    fin_in = ((128, 1024), BF16)
    fin_back = ((128, 1024), BF16)
    notes_in = ((4, 16, 128), F32)


class Scratch:
    out_here = ((128, 1024), BF16)
    gtok_here = ((128, 1024), BF16)
    x = ((128, 1024), BF16)
    cot = ((128, 1024), BF16)
    xs = ((1024, 1024), BF16)
    wqkv = ((1024, 384), BF16)
    w_near = ((3, 128, 256), BF16)
    queries = ((1024, 128), BF16)
    keys_all = ((2048, 128), BF16)
    values_all = ((2048, 128), BF16)
    mixed = ((1024, 128), F32)
    log_sums = ((1024, 128), F32)
    att = ((128, 1024), BF16)
    wo = ((1024, 1024), BF16)
    par = ((8, 1024), F32)
    bins = ((1, 512), F32)
    wi = ((1024, 512), BF16)
    wb = ((1024, 512), BF16)
    smalls = ((8, 16, 128), BF16)
    smalls_z = ((4, 16, 128), BF16)
    smalls_sum = ((16, 128), BF16)
    proj = ((256, 384), F32)
    scores = ((256, 2048), F32)
    d_buf = ((256, 2048), F32)
    p_buf = ((256, 2048), BF16)
    att_send = ((1024, 128), BF16)
    n1 = ((128, 1024), F32)
    unit1 = ((128, 1024), F32)
    scale1 = ((128, 128), F32)
    d2 = ((128, 1024), F32)
    d1 = ((128, 1024), F32)
    db = ((128, 1024), BF16)
    norm_slots = ((4, 256, 1024), BF16)
    grad_slots = ((4, 256, 1024), BF16)
    hid = ((4, 256, 512), BF16)
    slope = ((4, 256, 512), F32)
    low = ((4, 256, 512), BF16)
    pre = ((128, 512), F32)
    terms = ((4, 256, 1024), F32)
    sib_out = ((2, 4, 128, 1024), BF16)
    sib_in = ((2, 4, 128, 1024), BF16)
    peer_out = ((2, 4, 128, 1024), BF16)
    peer_in = ((2, 4, 128, 1024), BF16)
    g_back = ((8, 128, 512), BF16)
    g_in = ((8, 128, 512), BF16)
    pass_back = ((2, 3, 8, 128, 128), BF16)
    pass_in = ((2, 3, 8, 128, 128), BF16)
    gs_back = ((8, 128, 128), BF16)
    gs_in = ((8, 128, 128), BF16)
    da_send = ((128, 1024), BF16)
    da = ((1024, 128), BF16)
    q_turned = ((128, 1024), BF16)
    da_turned = ((128, 1024), BF16)
    dq = ((1024, 128), F32)
    dk_turned = ((128, 2048), F32)
    dv_turned = ((128, 2048), F32)
    out_k = ((1024, 128), F32)
    out_v = ((1024, 128), F32)
    sib_k = ((1024, 128), F32)
    sib_v = ((1024, 128), F32)
    dqkv = ((1024, 384), BF16)
    x_sum = ((256, 1024), F32)
    x_own = ((64, 1024), F32)
    z_out = ((4, 64, 1024), BF16)
    z_in = ((4, 64, 1024), BF16)
    w_sib_out = ((4, 128, 384), F32)
    w_sib_in = ((4, 128, 384), F32)
    w_out = ((4, 128, 384), BF16)
    o_out = ((128, 1024), BF16)
    vec = ((8, 1024), F32)
    gbin = ((1, 512), F32)
    notes = ((8, 16, 128), F32)
    notes_p = ((8, 16, 128), F32)
    notes_sum = ((16, 128), F32)


class Arrivals:
    z = (4,)
    p = (4, 3, 2)
    wo = (3, 2)
    w = (3,)
    o = (5,)
    kv = (1,)
    misc = (12,)
    col = (4, 3)
    ga = (4, 3, 2)
    ga_sib = (4, 4)
    ex = (5, 4)
    ex_sib = (5, 4)
    zg = (2, 2, 3)
    kv2 = (2,)
    dx = (4, 3, 2)
    dz = (4,)
    ws = (4,)
    da = (4,)
    own = (4,)


class Departures:
    z = (1,)
    p = (1,)
    wo = (1,)
    w = (3,)
    o = (1,)
    kv = (1,)
    misc = (12,)
    col = (4, 3)
    ga = (2,)
    ex = (3,)
    zg = (2, 2, 3)
    kv2 = (1,)
    dx = (1,)
    dz = (1,)
    ws = (1,)


class Refs:
    pass


def layer_kernel(*refs):
    v = Refs()
    names = [n for table in (Inputs, Results, Scratch) for n, _ in entries(table)]
    names += ["r_" + n for n, _ in entries(Arrivals)] + ["s_" + n for n, _ in entries(Departures)]
    for name, ref in zip(names, refs):
        setattr(v, name, ref)
    at = Place()
    at.flat = at.b * 4 + at.z
    at.place = at.q * 4 + at.z
    at.parity = at.z % 2
    at.pair = 4 * (at.z // 2) + at.q
    col_in = Column(at, v.wi, [s.at[0] for s in (v.s_col, v.r_col)] + [s.at[1] for s in (v.s_col, v.r_col)])
    col_back = Column(at, v.wb, [s.at[2] for s in (v.s_col, v.r_col)] + [s.at[3] for s in (v.s_col, v.r_col)])
    gathers = [
        [
            Gather(at, slots, h, v.s_ga.at[i], v.r_ga.at[2 * i + h], v.r_ga_sib.at[2 * i + h])
            for h in range(2)
        ]
        for i, slots in enumerate((v.norm_slots, v.grad_slots))
    ]

    def exchange(i, side, rows):
        buffers = [t.at[side] for t in (v.sib_out, v.sib_in, v.peer_out, v.peer_in)]
        return Exchange(at, buffers, rows, v.s_ex.at[i // 2], v.r_ex.at[i], v.r_ex_sib.at[i])

    scatters = [
        [exchange(2 * i + h, i, pl.ds(64 * h, 64)) for h in range(2)] for i in range(2)
    ]
    out_scatter = exchange(4, 0, pl.ds(0, 128))
    upper = at.z // 2
    at.planes = (at.z, at.z + 1 - 2 * at.parity, 2 - upper, 3 - 3 * upper)
    rows_spread = [
        Spread(
            at,
            lambda r, plane=plane: v.xs.at[slot_rows(at.chip(r) * 4 + plane)],
            lambda block, k: block.at[pl.ds(k * 32, 32)],
            v.s_p.at[0],
            v.r_p.at[i],
        )
        for i, plane in enumerate(at.planes)
    ]
    wo_spread = Spread(
        at,
        lambda r: v.wo.at[:, lanes(2 * at.chip(r) + at.c)],
        lambda block, k: block.at[pl.ds(k * 512, 512)],
        v.s_wo.at[0],
        v.r_wo,
    )
    sum_in = ColumnSum(at, v.g_in, v.pass_in, v.s_zg.at[0], v.r_zg.at[0])
    sum_back = ColumnSum(at, v.g_back, v.pass_back, v.s_zg.at[1], v.r_zg.at[1])
    pltpu.make_async_copy(v.x_hbm, v.x, v.r_own.at[0]).start()
    pltpu.make_async_copy(v.cot_hbm, v.cot, v.r_own.at[1]).start()
    greet_all(at)
    wait_bytes(v.x, v.r_own.at[0])
    attend_phase(at, v, col_in, col_back, rows_spread, wo_spread)
    ffn_phase(at, v, col_in, col_back, gathers, scatters, sum_back, sum_in)
    grads_phase(at, v, out_scatter, sum_in, sum_back)
    end_phase(at, v, (sum_in, sum_back, col_in, col_back))


def attend_phase(at, v, col_in, col_back, rows_spread, wo_spread):
    xs, wqkv, wo = v.xs, v.wqkv, v.wo
    parity, pair = at.parity, at.pair

    pltpu.make_async_copy(v.small, v.smalls_z.at[at.z], v.r_misc.at[1]).start()
    for dz in range(1, 4):
        remote(
            v.small,
            v.smalls_z.at[at.z],
            v.s_misc.at[1],
            v.r_misc.at[1],
            (at.b, (at.z + dz) % 4),
        ).start()

    pltpu.make_async_copy(
        v.x.at[slot_rows(parity)], xs.at[slot_rows(at.place)], v.r_z.at[at.z]
    ).start()
    weights = (v.wq, v.wk, v.wv)
    for i in (1, 2, 3):
        plane = at.planes[i]
        remote(
            v.x.at[slot_rows(plane % 2)],
            xs.at[slot_rows(at.place)],
            v.s_z.at[0],
            v.r_z.at[at.z],
            (at.b, plane),
        ).start()
        if i == 1:
            for k, w in enumerate(weights):
                remote(
                    w, v.w_near.at[k], v.s_w.at[2], v.r_w.at[2], (at.b, at.planes[1])
                ).start()

    part = wo.at[pl.ds(pl.multiple_of(at.z * 256, 256), 256), lanes(at.b)]
    pltpu.make_async_copy(v.wout, part, v.r_o.at[4]).start()
    for i in (1, 2, 3):
        remote(v.wout, part, v.s_o.at[0], v.r_o.at[4], (at.b, at.planes[i])).start()

    def to_pairs(sources, group):
        for dx in range(2):
            column = (at.x + dx) % 2
            for k, w in enumerate(sources):
                send_or_copy(
                    w.at[:, lanes(column)],
                    wqkv.at[lanes(at.b), pl.ds(k * 128, 128)],
                    v.s_w.at[0],
                    v.r_w.at[0],
                    (2 * (group * 2 + column) + at.c, at.z),
                    None if dx else group == at.y,
                )

    for i in range(4):
        wait_bytes(rows_spread[i].block(0), v.r_z.at[at.planes[i]])
        rows_spread[i].start()
        if i == 0:
            to_pairs(weights, parity)
            wait_bytes(v.smalls_z, v.r_misc.at[1])
            total = v.smalls_z[0].astype(F32)
            for z in range(1, 4):
                total += v.smalls_z[z].astype(F32)
            v.smalls_sum[...] = total.astype(BF16)
            mine = v.smalls.at[at.b]
            pltpu.make_async_copy(v.smalls_sum, mine, v.r_misc.at[10]).start()

            def spread(step, carry):
                remote(
                    v.smalls_sum,
                    mine,
                    v.s_misc.at[10],
                    v.r_misc.at[10],
                    ((at.b + step) % 8, at.z),
                ).start()
                return carry

            lax.fori_loop(1, 8, spread, 0)
        if i == 1:
            plane_weights(at, v.win, v.wi, v.s_misc.at[0], v.r_misc.at[0])
            wait_bytes(v.w_near, v.r_w.at[2])
            to_pairs([v.w_near.at[k] for k in range(3)], 1 - parity)
        if i:
            rows_spread[i - 1].relay()
    wait_bytes(v.wi.at[:, pl.ds(0, 128)], v.r_misc.at[0])
    col_in.send(0)

    wait_bytes(wqkv.at[pl.ds(0, 512)], v.r_w.at[0])
    for r in range(4):
        part = wqkv.at[lanes(2 * at.chip(r) + at.c)]
        remote(part, part, v.s_w.at[1], v.r_w.at[1], at.sibling()).start()
    rows_spread[3].relay()

    wait_bytes(v.smalls, v.r_misc.at[10])
    for b in range(8):
        v.par[:, 128 * b : 128 * b + 128] = v.smalls[b].astype(F32)[0:8]
    row = lax.broadcasted_iota(jnp.int32, (8, 128), 0)
    for h in range(4):
        rows = v.smalls[2 * h + at.b // 4].astype(F32)[8:16]
        rows = jnp.where(row == at.b % 4, rows, 0.0)
        v.bins[0:1, 128 * h : 128 * h + 128] = jnp.sum(rows, axis=0, keepdims=True)
    bias_q = v.par[0:1, lanes(pair)]
    bias_v = v.par[1:2, lanes(pair)]
    wait_bytes(wqkv.at[pl.ds(0, 512)], v.r_w.at[1])

    whole = wo_spread.block(0)
    wait_bytes(whole, v.r_o.at[4])
    wo_spread.start()
    remote(whole, whole, v.s_o.at[0], v.r_o.at[0], at.sibling()).start()
    plane_weights(at, v.wback, v.wb, v.s_misc.at[2], v.r_misc.at[2])

    for r in range(4):
        chip = at.chip(r)
        if r:
            for i in range(4):
                rows_spread[i].rest(r)
        rows = chip_rows(chip)
        v.proj[...] = dot_nn(xs[rows], wqkv[...])
        v.queries[rows] = (v.proj[:, 0:128] + bias_q).astype(BF16)
        own_rows = chip_rows(at.c * 4 + chip)
        v.keys_all[own_rows] = v.proj[:, 128:256].astype(BF16)
        v.values_all[own_rows] = (v.proj[:, 256:384] + bias_v).astype(BF16)
        for k, ref in enumerate((v.keys_all, v.values_all)):
            view = ref.at[own_rows]
            remote(view, view, v.s_kv.at[0], v.r_kv.at[0], at.sibling()).start()

    wait_bytes(v.keys_all, v.r_kv.at[0])

    col_in.arrive(0)
    col_in.send(1)
    scores = v.scores

    def attend(step, carry):
        chip = (at.q + 1 + step) % 4
        rows = chip_rows(chip)
        outs = []
        logs = []
        for h in range(2):
            q = (v.queries[rows].astype(F32) * head_mask(h) * HEAD_DIM**-0.5).astype(BF16)
            scores[...] = contract_cols(q, v.keys_all[...])
            top = jnp.max(scores[...], axis=-1, keepdims=True)
            weights = jnp.exp(scores[...] - top)
            total = jnp.sum(weights, axis=-1, keepdims=True)
            outs.append(dot_nn(weights.astype(BF16), v.values_all[...]) / total)
            logs.append(top + jnp.log(total))
        first = head_mask(0) > 0.5
        merged = jnp.where(first, outs[0], outs[1])
        v.mixed[rows] = merged
        v.log_sums[rows] = jnp.where(first, logs[0], logs[1])
        v.att_send[rows] = merged.astype(BF16)
        for k in range(4):
            plane = (at.z + 1 + k) % 4
            send_or_copy(
                v.att_send.at[slot_rows(chip * 4 + plane)],
                v.att.at[slot_rows(parity), lanes(pair)],
                v.s_misc.at[3],
                v.r_misc.at[3],
                (2 * chip + at.c, plane),
                step == 3 if k == 3 else None,
            )

        @pl.when(step == 0)
        def _():
            wo_spread.relay()

        @pl.when(step == 2)
        def _():
            col_in.arrive(1)
            col_in.send(2)

        return carry

    lax.fori_loop(0, 4, attend, 0)

    wait_bytes(v.wb.at[:, pl.ds(0, 128)], v.r_misc.at[2])
    col_back.send(0)
    for r in (1, 2, 3):
        wo_spread.rest(r)
        part = wo_spread.block(r)
        remote(part, part, v.s_o.at[0], v.r_o.at[r], at.sibling()).start()
    for r in range(4):
        wait_bytes(whole, v.r_o.at[r])
    wait_bytes(v.att, v.r_misc.at[3])


def ffn_phase(at, v, col_in, col_back, gathers, scatters, sum_back, sum_in):
    n1, terms, peer_in = v.n1, v.terms, v.peer_in

    def param(i):
        return v.par[i : i + 1, :]

    def local(h, i):
        return pl.ds(64 * h + 32 * i, 32)

    def chip_part(h, i):
        return pl.ds(pl.multiple_of(h * 128 + at.c * 64 + 32 * i, 32), 32)

    wait_bytes(v.cot, v.r_own.at[1])
    n1[...] = dot_nn(v.att[...], v.wo[...])
    for h in range(2):
        for i in range(2):
            rows = local(h, i)
            unit, scale = norm_rows(v.x[rows].astype(F32) + n1[rows] + param(2))
            v.unit1[rows] = unit
            v.scale1[rows] = jnp.broadcast_to(scale, (32, 128))
            normed = unit * param(3) + param(4)
            n1[rows] = normed
            v.norm_slots[at.q, chip_part(h, i)] = normed.astype(BF16)
        gathers[0][h].start()

    def hidden(h, r):
        chip = gathers[0][h].ready(r)
        v.pre[...] = dot_nn(v.norm_slots[chip, pl.ds(128 * h, 128)], v.wi[...])

        def activate(i, carry):
            rows = pl.ds(pl.multiple_of(i * 32, 32), 32)
            into = pl.ds(pl.multiple_of(128 * h + i * 32, 32), 32)
            u = v.pre[rows] + v.bins[...]
            cdf = 0.5 * (1.0 + lax.erf(u * math.sqrt(0.5)))
            bell = jnp.exp(-0.5 * u * u) * (1.0 / math.sqrt(2.0 * math.pi))
            v.hid[r, into] = (u * cdf).astype(BF16)
            v.slope[r, into] = cdf + u * bell
            return carry

        lax.fori_loop(0, 4, activate, 0)

    def neighbours(gather):
        gather.relay()
        gather.forward(1)
        gather.forward(2)

    neighbours(gathers[0][0])
    gathers[0][1].relay()
    col_back.arrive(0)
    col_back.send(1)
    col_in.arrive(2)
    hidden(0, 0)
    gathers[0][1].forward(1)
    gathers[0][1].forward(2)
    hidden(1, 0)
    hidden(0, 1)
    hidden(0, 2)
    gathers[0][0].forward(3)
    hidden(1, 1)
    gathers[0][1].forward(3)
    col_back.arrive(1)
    col_back.send(2)
    hidden(1, 2)
    hidden(0, 3)
    hidden(1, 3)
    col_back.arrive(2)

    def to_plane(scatter, done, h, r, product):
        terms[r, pl.ds(128 * h, 128)] = product
        scatter[h].put(r, terms[r, part_rows(h, 1 - at.c)])
        done.append((h, r))
        if len(done) > 3:
            pass_on(scatter, *done[-4])

    def pass_on(scatter, h, r):
        total = scatter[h].add(r, terms[r, part_rows(h, at.c)])
        if r == 0:
            terms[0, part_rows(h, at.c)] = total

    done = []
    for h in range(2):
        for r in (3, 1, 2, 0):
            product = contract_cols(v.hid[r, pl.ds(128 * h, 128)], v.wb[...])
            to_plane(scatters[0], done, h, r, product)
    for one in done[-3:]:
        pass_on(scatters[0], *one)

    def peers(side, rows):
        return (
            peer_in[side, 1, rows].astype(F32)
            + peer_in[side, 2, rows].astype(F32)
            + peer_in[side, 3, rows].astype(F32)
        )

    def column_sums(parts, sums):
        return tuple(
            kept + jnp.sum(part.reshape(4, 8, 1024), axis=0) for kept, part in zip(sums, parts)
        )

    gbin = [jnp.zeros((8, 512), F32)]
    done = []

    def hidden_grad(h, r):
        chip = gathers[1][h].ready(r)
        v.pre[...] = dot_nn(v.grad_slots[chip, pl.ds(128 * h, 128)], v.wb[...])

        def deactivate(i, carry):
            rows = pl.ds(pl.multiple_of(i * 32, 32), 32)
            into = pl.ds(pl.multiple_of(128 * h + i * 32, 32), 32)
            low = (v.pre[rows] * v.slope[r, into]).astype(BF16)
            v.low[r, into] = low
            return carry + jnp.sum(low.astype(F32).reshape(4, 8, 512), axis=0)

        gbin[0] = lax.fori_loop(0, 4, deactivate, gbin[0])
        product = contract_cols(v.low[r, pl.ds(128 * h, 128)], v.wi[...])
        to_plane(scatters[1], done, h, r, product)

    sums = tuple(jnp.zeros((8, 1024), F32) for _ in range(3))
    for h in range(2):
        scatters[0][h].arrive()
        for i in range(2):
            rows = local(h, i)
            total = terms[0, chip_part(h, i)] + peers(0, rows)
            unit, scale = norm_rows(n1[rows] + total + param(5))
            v.out_here[rows] = (unit * param(6) + param(7)).astype(BF16)
            g = v.cot[rows].astype(F32)
            d = norm_back(g * param(6), unit, scale)
            v.d2[rows] = d
            low = d.astype(BF16)
            v.grad_slots[at.q, chip_part(h, i)] = low
            sums = column_sums((g * unit, g, low.astype(F32)), sums)
        gathers[1][h].start()
        if h == 0:
            hidden_grad(0, 0)
    pltpu.make_async_copy(v.out_here, v.out, v.r_own.at[2]).start()
    for row, total in zip((6, 7, 5), sums):
        v.vec[row : row + 1, :] = jnp.sum(total, axis=0, keepdims=True)

    def weight_grad(slots, right, into):
        def one(step, carry):
            other = (at.q + step) % 4
            total = jnp.zeros((256, 512), F32)
            for r in range(4):
                total += contract_rows(slots[at.chip(r), :, chip_rows(other)], right[r])
            into[2 * other] = total[0:128].astype(BF16)
            into[2 * other + 1] = total[128:256].astype(BF16)
            return carry

        lax.fori_loop(0, 4, one, 0)

    neighbours(gathers[1][0])
    hidden_grad(1, 0)
    hidden_grad(0, 1)
    neighbours(gathers[1][1])
    hidden_grad(0, 2)
    gathers[1][0].forward(3)
    hidden_grad(1, 1)
    hidden_grad(0, 3)
    gathers[1][1].forward(3)
    hidden_grad(1, 2)
    hidden_grad(1, 3)
    for one in done[-3:]:
        pass_on(scatters[1], *one)
    v.gbin[...] = jnp.sum(gbin[0], axis=0, keepdims=True)

    sums = tuple(jnp.zeros((8, 1024), F32) for _ in range(3))
    for h in range(2):
        if h == 0:
            weight_grad(v.grad_slots, v.hid, v.g_back)
            wait_bytes(v.xs.at[pl.ds(0, 896)], v.s_ga.at[1])
            sum_back.begin((0,))
        else:
            weight_grad(v.norm_slots, v.low, v.g_in)
        scatters[1][h].arrive()
        for i in range(2):
            rows = local(h, i)
            total = v.d2[rows] + terms[0, chip_part(h, i)] + peers(1, rows)
            unit = v.unit1[rows]
            d = norm_back(total * param(3), unit, v.scale1[rows][:, :1])
            v.d1[rows] = d
            low = d.astype(BF16)
            v.db[rows] = low
            sums = column_sums((total * unit, total, low.astype(F32)), sums)
        rows = pl.ds(64 * h, 64)
        v.da_send[rows] = contract_cols(v.db[rows], v.wo[...]).astype(BF16)
        for r in range(4):
            chip = at.chip(r)
            for plane in (h, h + 2):
                pair = 2 * (plane - h) + chip
                send_or_copy(
                    v.da_send.at[rows, lanes(pair)],
                    v.da.at[slot_rows(at.place)],
                    v.s_misc.at[4],
                    v.r_da.at[r],
                    (2 * chip + at.c, plane),
                    None if r else at.z == plane,
                )

    for row, total in zip((3, 4, 2), sums):
        v.vec[row : row + 1, :] = jnp.sum(total, axis=0, keepdims=True)
    v.vec[0:2, :] = jnp.zeros((2, 1024), F32)
    for i in range(3):
        if i:
            sum_back.begin((i,))
        sum_in.begin((i,))


def grads_phase(at, v, out_scatter, sum_in, sum_back):
    xs, wqkv, terms = v.xs, v.wqkv, v.terms
    parity, pair = at.parity, at.pair

    wait_bytes(xs.at[pl.ds(0, 896)], v.s_ex.at[0])
    for r in (3, 1, 2, 0):
        for core in (1 - at.c, at.c):
            part = contract_rows(v.db[:, lanes(2 * at.chip(r) + core)], v.att[...])
            if core is at.c:
                terms[r, 0:128] = part
            else:
                out_scatter.put(r, part)

    v.q_turned[...] = v.queries[...].astype(F32).T.astype(BF16)
    v.dk_turned[...] = jnp.zeros_like(v.dk_turned)
    v.dv_turned[...] = jnp.zeros_like(v.dv_turned)
    for r in (3, 1, 2):
        out_scatter.add(r, terms[r, 0:128])
    terms[0, 0:128] = out_scatter.add(0, terms[0, 0:128])
    wait_bytes(v.da.at[chip_rows(at.q)], v.r_da.at[0])
    s_buf, d_buf, p_buf = v.scores, v.d_buf, v.p_buf

    def attend(step, carry):
        chip = ((at.y + step // 2) % 2) * 2 + (at.x + step % 2) % 2
        rows = chip_rows(chip)

        @pl.when(step > 0)
        def _():
            wait_bytes(v.da.at[rows], v.r_da.at[step])

        v.da_turned[:, rows] = v.da[rows].astype(F32).T.astype(BF16)
        parts = []
        for h in range(2):
            mask = head_mask(h)
            grad = v.da[rows].astype(F32) * mask
            delta = jnp.sum(grad * v.mixed[rows], axis=-1, keepdims=True)
            q = (v.queries[rows].astype(F32) * mask * HEAD_DIM**-0.5).astype(BF16)
            s_buf[...] = contract_cols(q, v.keys_all[...])
            d_buf[...] = contract_cols(grad.astype(BF16), v.values_all[...])
            logs = v.log_sums[rows][:, h * HEAD_DIM : h * HEAD_DIM + 1]
            probs = jnp.exp(s_buf[...] - logs)
            p_buf[...] = probs.astype(BF16)
            low = (probs * (d_buf[...] - delta)).astype(BF16)
            band = pl.ds(h * HEAD_DIM, HEAD_DIM)
            v.dv_turned[band] += dot_nn(v.da_turned[band, rows], p_buf[...])
            v.dk_turned[band] += dot_nn(v.q_turned[band, rows], low)
            parts.append(dot_nn(low, v.keys_all[...]))
        v.dq[rows] = jnp.where(head_mask(0) > 0.5, parts[0], parts[1]) * HEAD_DIM**-0.5

        @pl.when(step == 1)
        def _():
            sum_back.relay(1, 0)

        @pl.when(step == 2)
        def _():
            sum_in.relay(1, 0)

        return carry

    lax.fori_loop(0, 4, attend, 0)

    other = core_rows(1 - at.c)
    mine = core_rows(at.c)
    v.out_k[...] = v.dk_turned[:, other].T * HEAD_DIM**-0.5
    v.out_v[...] = v.dv_turned[:, other].T
    for k, (ref, into) in enumerate(((v.out_k, v.sib_k), (v.out_v, v.sib_v))):
        remote(ref, into, v.s_kv2.at[0], v.r_kv2.at[k], at.sibling()).start()
    dqkv = v.dqkv
    low = v.dq[...].astype(BF16)
    dqkv[:, 0:128] = low
    v.vec[0:1, lanes(pair)] = jnp.sum(low.astype(F32), axis=0, keepdims=True)
    out_scatter.arrive()
    peer_in = v.peer_in.at[0]

    def out_rows(rows):
        total = (
            terms[0, rows]
            + peer_in[1, rows].astype(F32)
            + peer_in[2, rows].astype(F32)
            + peer_in[3, rows].astype(F32)
        )
        v.o_out[rows] = total.astype(BF16)

    by_rows(128, 32, out_rows)
    wide = pl.ds(pl.multiple_of(at.z * 256, 256), 256)
    pltpu.make_async_copy(v.o_out.at[:, wide], v.o_in.at[0], v.r_misc.at[8]).start()
    for dz in range(1, 4):
        plane = (at.z + dz) % 4
        remote(
            v.o_out.at[:, pl.ds(pl.multiple_of(plane * 256, 256), 256)],
            v.o_in.at[dz],
            v.s_misc.at[8],
            v.r_misc.at[8],
            (at.b, plane),
        ).start()

    sum_back.relay(1, 1)
    sum_back.relay(2, 0)
    own_k = v.dk_turned[:, mine].T * HEAD_DIM**-0.5
    wait_bytes(v.sib_k, v.r_kv2.at[0])
    dqkv[:, 128:256] = (own_k + v.sib_k[...]).astype(BF16)
    own_v = v.dv_turned[:, mine].T
    wait_bytes(v.sib_v, v.r_kv2.at[1])
    low = (own_v + v.sib_v[...]).astype(BF16)
    dqkv[:, 256:384] = low
    v.vec[1:2, lanes(pair)] = jnp.sum(low.astype(F32), axis=0, keepdims=True)

    notes = v.notes
    for b in range(8):
        notes[b, 0:8] = v.vec[:, 128 * b : 128 * b + 128]
        notes[b, 8:16] = jnp.zeros((8, 128), F32)
    row = lax.broadcasted_iota(jnp.int32, (8, 128), 0)
    for h in range(4):
        notes[2 * h + at.b // 4, 8:16] = jnp.where(
            row == at.b % 4, v.gbin[0:1, 128 * h : 128 * h + 128], 0.0
        )
    pltpu.make_async_copy(notes.at[at.b], v.notes_p.at[at.b], v.r_misc.at[5]).start()

    def spread(step, carry):
        to = (at.b + step) % 8
        remote(
            notes.at[to], v.notes_p.at[at.b], v.s_misc.at[5], v.r_misc.at[5], (to, at.z)
        ).start()
        return carry

    lax.fori_loop(1, 8, spread, 0)

    wait_bytes(xs.at[pl.ds(0, 896)], v.s_ga.at[0])
    x_out, x_in, x_via = v.norm_slots, v.grad_slots.at[0:2], v.grad_slots.at[2:4]
    for r in (3, 1, 2, 0):
        part = contract_cols(dqkv[chip_rows(at.chip(r))], wqkv[...])
        if r:
            x_out[r] = part.astype(BF16)
        else:
            v.x_sum[...] = part
    def piece(dz, k):
        return pl.ds(pl.multiple_of(((at.z + dz) % 4) * 64 + 32 * k, 32), 32)

    order = (2, 1, 3, 0)

    def send_dx(dz, via):
        for r, k in ((1, 0), (2, 1)):
            rows = piece(dz, k)
            remote(
                x_out.at[3 if via else r, rows],
                x_via.at[r - 1, rows] if via else x_in.at[r - 1, rows],
                v.s_dx.at[0],
                v.r_dx.at[dz, 0 if via else r, k],
                at.peer(r),
            ).start()

    def relay_dx(dz):
        for r, k in ((2, 0), (1, 1)):
            rows = piece(dz, k)
            wait_bytes(x_via.at[k, rows], v.r_dx.at[dz, 0, k])
            x_out[r, rows] = (
                x_out[r, rows].astype(F32) + x_via[k, rows].astype(F32)
            ).astype(BF16)
            remote(
                x_out.at[r, rows],
                x_in.at[r - 1, rows],
                v.s_dx.at[0],
                v.r_dx.at[dz, r, k],
                at.peer(r),
            ).start()

    z_out, z_in = v.z_out, v.z_in
    def column_dx(dz):
        plane = (at.z + dz) % 4
        rows = slot_rows(plane)
        for r in (1, 2):
            for k in range(2):
                wait_bytes(x_in.at[r - 1, piece(dz, k)], v.r_dx.at[dz, r, k])
        total = v.x_sum[rows] + x_in[0, rows].astype(F32) + x_in[1, rows].astype(F32)
        if dz:
            z_out[dz] = total.astype(BF16)
            remote(
                z_out.at[dz], z_in.at[dz], v.s_dz.at[0], v.r_dz.at[dz], (at.b, plane)
            ).start()
        else:
            v.x_own[...] = total

    def begin_dx(dz):
        send_dx(dz, True)
        send_dx(dz, False)

    begin_dx(2)
    begin_dx(1)
    def features(b):
        return contract_rows(xs[:, lanes(b)], dqkv[...])

    for r in range(4):
        v.w_sib_out[r] = features(2 * at.chip(r) + 1 - at.c)
        remote(
            v.w_sib_out.at[r], v.w_sib_in.at[r], v.s_ws.at[0], v.r_ws.at[r], at.sibling()
        ).start()
    relay_dx(2)
    begin_dx(3)
    sum_in.relay(1, 1)
    sum_in.relay(2, 0)
    relay_dx(1)
    begin_dx(0)
    column_dx(2)
    relay_dx(3)
    column_dx(1)
    relay_dx(0)
    plane_w = 2 * (at.z // 2) + at.y
    for r in range(4):
        total = features(2 * at.chip(r) + at.c)
        wait_bytes(v.w_sib_in.at[r], v.r_ws.at[r])
        v.w_out[r] = (total + v.w_sib_in[r]).astype(BF16)
        send_or_copy(
            v.w_out.at[r],
            v.w_in.at[parity, at.x],
            v.s_misc.at[6],
            v.r_misc.at[6],
            at.peer(r)[:1] + (plane_w,),
            plane_w == at.z if r == 0 else None,
        )

    column_dx(3)
    sum_back.finish(v.gs_back, v.fin_back, v.s_misc.at[7], v.r_misc.at[7])
    sum_in.finish(v.gs_in, v.fin_in, v.s_misc.at[9], v.r_misc.at[9])
    wait_bytes(v.notes_p, v.r_misc.at[5])
    total = v.notes_p[0]
    for b in range(1, 8):
        total += v.notes_p[b]
    v.notes_sum[...] = total
    mine = v.notes_in.at[at.z]
    pltpu.make_async_copy(v.notes_sum, mine, v.r_misc.at[11]).start()
    for dz in range(1, 4):
        remote(
            v.notes_sum, mine, v.s_misc.at[11], v.r_misc.at[11], (at.b, (at.z + dz) % 4)
        ).start()

    column_dx(0)
    for dz in (1, 2, 3):
        wait_bytes(z_in.at[dz], v.r_dz.at[dz])
    same = slot_rows(parity)
    v.gtok_here[same] = (v.d1[same] + v.x_own[...] + z_in[2].astype(F32)).astype(BF16)
    cross = slot_rows(1 - parity)
    v.gtok_here[cross] = (v.d1[cross] + z_in[1].astype(F32) + z_in[3].astype(F32)).astype(BF16)

    pltpu.make_async_copy(v.gtok_here, v.gtok, v.r_own.at[3]).start()
    wait_bytes(v.o_in, v.r_misc.at[8])
    wait_bytes(v.w_in, v.r_misc.at[6])
    wait_bytes(v.notes_in, v.r_misc.at[11])
    wait_bytes(v.fin_back, v.r_misc.at[7])
    wait_bytes(v.fin_in, v.r_misc.at[9])


def end_phase(at, v, ends):
    wait_bytes(v.out_here, v.r_own.at[2])
    for one in ends:
        one.end()

    def rows(n):
        return v.xs.at[pl.ds(0, n)]

    wait_bytes(rows(192), v.s_z.at[0])
    wait_bytes(rows(768), v.s_p.at[0])
    wait_bytes(rows(384), v.s_wo.at[0])
    wait_bytes(rows(608), v.s_o.at[0])
    wait_bytes(rows(256), v.s_kv.at[0])
    for i in (1, 2):
        wait_bytes(rows(896), v.s_ex.at[i])
    wait_bytes(rows(768), v.s_dx.at[0])
    wait_bytes(rows(192), v.s_dz.at[0])
    wait_bytes(v.w_sib_out, v.s_ws.at[0])
    wait_bytes(rows(512), v.s_kv2.at[0])
    wait_bytes(v.wqkv.at[pl.ds(0, 384)], v.s_w.at[0])
    wait_bytes(v.wqkv.at[pl.ds(0, 512)], v.s_w.at[1])
    wait_bytes(v.w_near, v.s_w.at[2])
    seven = v.wi.at[pl.ds(0, 896), pl.ds(0, 128)]
    for i in (0, 2, 7, 9):
        wait_bytes(seven, v.s_misc.at[i])
    wait_bytes(v.smalls.at[pl.ds(0, 3)], v.s_misc.at[1])
    wait_bytes(v.smalls.at[pl.ds(0, 7)], v.s_misc.at[10])
    for i in (3, 4):
        wait_bytes(v.att_send.at[pl.ds(0, 960)], v.s_misc.at[i])
    wait_bytes(v.notes.at[pl.ds(0, 7)], v.s_misc.at[5])
    wait_bytes(v.notes.at[pl.ds(0, 3)], v.s_misc.at[11])
    plane_w = 2 * (at.z // 2) + at.y

    @pl.when(plane_w == at.z)
    def _():
        wait_bytes(v.w_out.at[pl.ds(0, 3)], v.s_misc.at[6])

    @pl.when(plane_w != at.z)
    def _():
        wait_bytes(v.w_out, v.s_misc.at[6])

    wait_bytes(v.o_in.at[pl.ds(0, 3)], v.s_misc.at[8])
    wait_bytes(v.gtok_here, v.r_own.at[3])


def finish_kernel(
    place_ref,
    out_in,
    gtok_in,
    w_in,
    o_in,
    fin_in,
    fin_back,
    notes_in,
    out_ref,
    gtok_ref,
    gq_ref,
    gk_ref,
    gv_ref,
    gout_ref,
    gwin_ref,
    gwback_ref,
    small_ref,
    bin_ref,
):
    out_ref[...] = out_in[...]
    gtok_ref[...] = gtok_in[...]
    for x in range(2):
        total = w_in[0, x].astype(F32) + w_in[1, x].astype(F32)
        for k, ref in enumerate((gq_ref, gk_ref, gv_ref)):
            ref[:, 128 * x : 128 * x + 128] = total[:, 128 * k : 128 * k + 128]
    gout_ref[...] = (
        o_in[0].astype(F32) + o_in[1].astype(F32) + o_in[2].astype(F32) + o_in[3].astype(F32)
    ).T
    gwin_ref[...] = fin_in[...].astype(F32)
    gwback_ref[...] = fin_back[...].astype(F32)
    total = notes_in[0] + notes_in[1] + notes_in[2] + notes_in[3]
    z = place_ref[0]
    part = jnp.zeros((8, 32), F32)
    units = jnp.zeros((1, 128), F32)
    for k in range(4):
        part += jnp.where(z == k, total[0:8, 32 * k : 32 * k + 32], 0.0)
        units += jnp.where(z == k, total[8 + k : 9 + k], 0.0)
    small_ref[...] = part
    bin_ref[...] = units


def vmem():
    return pl.BlockSpec(memory_space=pltpu.VMEM)


def run_layer(*args):
    results = [e for _, e in entries(Results)]
    scratch = [pltpu.VMEM(s, t) for _, (s, t) in entries(Scratch)]
    for _, shape in entries(Arrivals) + entries(Departures):
        scratch.append(DMA(shape))
    return pl.pallas_call(
        layer_kernel,
        out_shape=[jax.ShapeDtypeStruct(s, t) for s, t in results],
        in_specs=[vmem()] + [pl.BlockSpec(memory_space=pl.ANY)] * (len(args) - 1),
        out_specs=[pl.BlockSpec(memory_space=pl.ANY)] * len(results),
        scratch_shapes=scratch,
        compiler_params=pltpu.CompilerParams(
            collective_id=1, has_side_effects=True, vmem_limit_bytes=VMEM_LIMIT
        ),
    )(*args)


def run_finish(*args):
    shapes = (
        ((128, 1024), BF16),
        ((128, 1024), BF16),
        ((128, 256), F32),
        ((128, 256), F32),
        ((128, 256), F32),
        ((256, 128), F32),
        ((128, 1024), F32),
        ((128, 1024), F32),
        ((8, 32), F32),
        ((1, 128), F32),
    )
    return pl.pallas_call(
        finish_kernel,
        out_shape=[jax.ShapeDtypeStruct(s, t) for s, t in shapes],
        in_specs=[pl.BlockSpec(memory_space=pltpu.SMEM)] + [vmem()] * (len(args) - 1),
        out_specs=[vmem()] * len(shapes),
        compiler_params=pltpu.CompilerParams(vmem_limit_bytes=VMEM_LIMIT),
    )(*args)


DMA = pltpu.SemaphoreType.DMA


def fast_device(
    tokens,
    w_query,
    w_key,
    w_value,
    w_out,
    b_query,
    b_value,
    b_out,
    norm1_gain,
    norm1_shift,
    w_in,
    w_back,
    b_in,
    b_back,
    norm2_gain,
    norm2_shift,
    cotangent,
):
    head_id = lax.axis_index("head")
    token_shape = tokens.shape
    model_dim = tokens.shape[2]
    x = tokens.reshape(-1, model_dim)
    vectors = jnp.stack(
        (b_query, b_value, b_out, norm1_gain, norm1_shift, b_back, norm2_gain, norm2_shift)
    )
    spread = jnp.where(
        lax.broadcasted_iota(jnp.int32, (1, 128), 1) // 32 == head_id,
        jnp.tile(vectors, (1, 4)),
        jnp.zeros((), BF16),
    )
    units = jnp.where(
        lax.broadcasted_iota(jnp.int32, (8, 1), 0) == head_id, b_in[None], jnp.zeros((), BF16)
    )
    small = jnp.concatenate((spread, units), axis=0)
    results = run_layer(
        small, x, cotangent.reshape(-1, model_dim), w_query, w_key, w_value, w_out, w_in, w_back
    )
    output, grad_tokens, gq, gk, gv, gout, gw_in, gw_back, own, gb_in = run_finish(
        head_id.astype(jnp.int32).reshape(1), *results
    )
    return (
        output.reshape(token_shape),
        grad_tokens.reshape(token_shape),
        gq,
        gk,
        gv,
        gout,
        own[0],
        own[1],
        own[2],
        own[3],
        own[4],
        gw_in,
        gw_back,
        gb_in.reshape(-1),
        own[5],
        own[6],
        own[7],
    )


def solution(mesh):
    in_specs = (
        P(None, ("blk", "head"), None),
        P("blk", "head"),
        P("blk", "head"),
        P("blk", "head"),
        P("head", "blk"),
        P(("blk", "head")),
        P(("blk", "head")),
        P(("blk", "head")),
        P(("blk", "head")),
        P(("blk", "head")),
        P("blk", "head"),
        P("blk", "head"),
        P(("blk", "head")),
        P(("blk", "head")),
        P(("blk", "head")),
        P(("blk", "head")),
        P(None, ("blk", "head"), None),
    )
    out_specs = (
        P(None, ("blk", "head"), None),
        P(None, ("blk", "head"), None),
        P("blk", "head"),
        P("blk", "head"),
        P("blk", "head"),
        P("head", "blk"),
        P(("blk", "head")),
        P(("blk", "head")),
        P(("blk", "head")),
        P(("blk", "head")),
        P(("blk", "head")),
        P("blk", "head"),
        P("blk", "head"),
        P(("blk", "head")),
        P(("blk", "head")),
        P(("blk", "head")),
        P(("blk", "head")),
    )
    sizes = (mesh.shape["blk"], mesh.shape["head"])
    body = fast_device if sizes == (8, 4) else per_device
    return jax.shard_map(
        body, mesh=mesh, in_specs=in_specs, out_specs=out_specs, check_vma=False
    )
```

```python
import functools
import math

import jax
import jax.numpy as jnp
from jax import lax
from jax.experimental import pallas as pl
from jax.experimental.pallas import tpu as pltpu
from jax.sharding import PartitionSpec as P

HEAD_DIM = 64


NORM_EPS = 1e-05


def layer_norm(summed, gain, shift):
    centre = jnp.mean(summed, axis=-1, keepdims=True)
    centred = summed - centre
    spread = jnp.mean(centred * centred, axis=-1, keepdims=True)
    return centred * lax.rsqrt(spread + NORM_EPS) * gain + shift


def gelu_exact(inputs):
    return jax.nn.gelu(inputs, approximate=False)


def split_heads(packed):
    return packed.reshape(packed.shape[0], packed.shape[1], -1, HEAD_DIM)


def contract_rows(left, right):
    return lax.dot_general(
        left, right, (((0,), (0,)), ((), ())), preferred_element_type=jnp.float32
    )


def contract_cols(left, right):
    return lax.dot_general(
        left, right, (((1,), (1,)), ((), ())), preferred_element_type=jnp.float32
    )


def score_block(queries4, keys4):
    return jnp.einsum(
        "sqge,skge->sqgk", queries4, keys4, preferred_element_type=jnp.float32
    ) * HEAD_DIM ** (-0.5)


def score_grads(queries4, keys4, values4, grads4, log_sums, deltas):
    probs = jnp.exp(score_block(queries4, keys4) - log_sums[..., None])
    d_probs = jnp.einsum("sqge,skge->sqgk", grads4, values4, preferred_element_type=jnp.float32)
    d_scores = (probs * (d_probs - deltas[..., None])).astype(jnp.bfloat16)
    return (probs.astype(jnp.bfloat16), d_scores)


def token_rows(local):
    return lax.all_gather(local, "head", axis=1, tiled=True)


def token_partials(terms):
    return lax.psum_scatter(
        terms.astype(jnp.bfloat16), "head", scatter_dimension=1, tiled=True
    ).astype(jnp.float32)


def place_part(part, full_len, start):
    return lax.dynamic_update_slice_in_dim(jnp.zeros((full_len,), jnp.float32), part, start, 0)


def per_device(
    tokens,
    w_query,
    w_key,
    w_value,
    w_out,
    b_query,
    b_value,
    b_out,
    norm1_gain,
    norm1_shift,
    w_in,
    w_back,
    b_in,
    b_back,
    norm2_gain,
    norm2_shift,
    cotangent,
):
    f32 = jnp.float32
    bf16 = jnp.bfloat16
    score_scale = HEAD_DIM ** (-0.5)
    bq_full, bv_full, bo_full, gain_one, shift_one, bin_full, bback_full, gain_two, shift_two = (
        lax.all_gather(b_query, ("blk", "head"), axis=0, tiled=True),
        lax.all_gather(b_value, ("blk", "head"), axis=0, tiled=True),
        lax.all_gather(b_out, ("blk", "head"), axis=0, tiled=True),
        lax.all_gather(norm1_gain, ("blk", "head"), axis=0, tiled=True),
        lax.all_gather(norm1_shift, ("blk", "head"), axis=0, tiled=True),
        lax.all_gather(b_in, ("blk", "head"), axis=0, tiled=True),
        lax.all_gather(b_back, ("blk", "head"), axis=0, tiled=True),
        lax.all_gather(norm2_gain, ("blk", "head"), axis=0, tiled=True),
        lax.all_gather(norm2_shift, ("blk", "head"), axis=0, tiled=True),
    )
    attn_cols, out_rows, ffn_cols = (
        lax.all_gather(jnp.stack((w_query, w_key, w_value)), "blk", axis=1, tiled=True),
        lax.all_gather(w_out, "blk", axis=1, tiled=True),
        lax.all_gather(jnp.stack((w_in, w_back)), "blk", axis=1, tiled=True),
    )
    seq_count, local_len, model_dim = tokens.shape
    token_shape = (seq_count, local_len, model_dim)
    head_id = lax.axis_index("head")
    width_part = attn_cols.shape[2]
    bq_part = lax.dynamic_slice_in_dim(bq_full, head_id * width_part, width_part).astype(f32)
    bv_part = lax.dynamic_slice_in_dim(bv_full, head_id * width_part, width_part).astype(f32)
    wide_rows = token_rows(tokens)
    wide_len = wide_rows.shape[1]
    wide_flat = wide_rows.reshape(-1, model_dim)
    head_shape = (seq_count, wide_len, width_part)
    wide_shape = (seq_count, wide_len, model_dim)
    query_heads = (
        (jnp.dot(wide_flat, attn_cols[0], preferred_element_type=f32) + bq_part)
        .astype(bf16)
        .reshape(head_shape)
    )
    key_heads = (
        jnp.dot(wide_flat, attn_cols[1], preferred_element_type=f32)
        .astype(bf16)
        .reshape(head_shape)
    )
    value_heads = (
        (jnp.dot(wide_flat, attn_cols[2], preferred_element_type=f32) + bv_part)
        .astype(bf16)
        .reshape(head_shape)
    )
    query4 = split_heads(query_heads)
    key4 = split_heads(key_heads)
    value4 = split_heads(value_heads)
    stat_shape = query4.shape[:3]
    pieces = (
        lax.all_gather(key_heads, "blk", axis=1, tiled=True),
        lax.all_gather(value_heads, "blk", axis=1, tiled=True),
    )
    maxima = jnp.full(stat_shape, -1e30, f32)
    scores = score_block(query4, split_heads(pieces[0]))
    new_max = jnp.maximum(maxima, jnp.max(scores, axis=-1))
    weights = jnp.exp(scores - new_max[..., None])
    totals = jnp.sum(weights, axis=-1)
    summed = jnp.einsum(
        "sqgk,skge->sqge", weights.astype(bf16), split_heads(pieces[1]), preferred_element_type=f32
    )
    maxima, totals, summed = (new_max, totals, summed)
    log_sums = maxima + jnp.log(totals)
    attended4 = summed / totals[..., None]
    attended_heads = attended4.reshape(head_shape).astype(bf16)
    attended_flat = attended_heads.reshape(-1, width_part)
    branch_terms = jnp.dot(attended_flat, out_rows, preferred_element_type=f32).reshape(wide_shape)
    branch = token_partials(branch_terms).reshape(-1, model_dim) + bo_full.astype(f32)
    flat_rows = tokens.reshape(-1, model_dim)
    normed, norm1_pull = jax.vjp(
        layer_norm, flat_rows.astype(f32) + branch, gain_one.astype(f32), shift_one.astype(f32)
    )
    normed_low = normed.astype(bf16)
    ffn_full = lax.all_gather(ffn_cols, "head", axis=2, tiled=True)
    pre_act = jnp.dot(normed_low, ffn_full[0], preferred_element_type=f32) + bin_full.astype(f32)
    hidden_act, gelu_pull = jax.vjp(gelu_exact, pre_act)
    hidden_low = hidden_act.astype(bf16)
    ffn_out = contract_cols(hidden_low, ffn_full[1]) + bback_full.astype(f32)
    final, norm2_pull = jax.vjp(
        layer_norm, normed + ffn_out, gain_two.astype(f32), shift_two.astype(f32)
    )
    output = final.astype(bf16).reshape(token_shape)
    d_second, grad_norm2_gain, grad_norm2_shift = norm2_pull(
        cotangent.reshape(-1, model_dim).astype(f32)
    )
    d_ffn = d_second.astype(bf16)
    grad_b_back = jnp.sum(d_ffn.astype(f32), axis=0)
    grad_back_whole = contract_rows(d_ffn, hidden_low)
    d_hidden = jnp.dot(d_ffn, ffn_full[1], preferred_element_type=f32)
    d_pre = gelu_pull(d_hidden)[0].astype(bf16)
    grad_b_in = jnp.sum(d_pre.astype(f32), axis=0)
    grad_in_whole = contract_rows(normed_low, d_pre)
    ffn_grad_parts = lax.psum_scatter(
        jnp.stack((grad_in_whole, grad_back_whole)).astype(jnp.bfloat16),
        "head",
        scatter_dimension=2,
        tiled=True,
    ).astype(jnp.float32)
    d_normed = d_second + contract_cols(d_pre, ffn_full[0])
    d_first, grad_norm1_gain, grad_norm1_shift = norm1_pull(d_normed)
    d_branch = d_first.astype(bf16)
    grad_b_out = jnp.sum(d_branch.astype(f32), axis=0)
    wide_dbranch = token_rows(d_branch.reshape(token_shape)).reshape(-1, model_dim)
    grad_out_part = contract_rows(attended_flat, wide_dbranch)
    grad_heads = contract_cols(wide_dbranch, out_rows).astype(bf16).reshape(head_shape)
    grads4 = split_heads(grad_heads)
    deltas = jnp.sum(grads4.astype(f32) * attended4, axis=-1)
    row_stats = (
        lax.all_gather(log_sums, "blk", axis=1, tiled=True),
        lax.all_gather(deltas, "blk", axis=1, tiled=True),
    )
    pieces = (
        lax.all_gather(key_heads, "blk", axis=1, tiled=True),
        lax.all_gather(value_heads, "blk", axis=1, tiled=True),
        lax.all_gather(query_heads, "blk", axis=1, tiled=True),
        lax.all_gather(grad_heads, "blk", axis=1, tiled=True),
    )
    piece_keys = split_heads(pieces[0])
    piece_values = split_heads(pieces[1])
    piece_queries = split_heads(pieces[2])
    piece_grads = split_heads(pieces[3])
    piece_sums = row_stats[0]
    piece_deltas = row_stats[1]
    own_probs, own_scores = score_grads(query4, piece_keys, piece_values, grads4, log_sums, deltas)
    d_query = score_scale * jnp.einsum(
        "sqgk,skge->sqge", own_scores, piece_keys, preferred_element_type=f32
    )
    probs_low, d_scores = score_grads(
        piece_queries, key4, value4, piece_grads, piece_sums, piece_deltas
    )
    key_acc = score_scale * jnp.einsum(
        "sqgk,sqge->skge", d_scores, piece_queries, preferred_element_type=f32
    )
    value_acc = jnp.einsum("sqgk,sqge->skge", probs_low, piece_grads, preferred_element_type=f32)
    d_query_low = d_query.reshape(-1, width_part).astype(bf16)
    d_key_low = key_acc.reshape(-1, width_part).astype(bf16)
    d_value_low = value_acc.reshape(-1, width_part).astype(bf16)
    grad_b_query = place_part(
        jnp.sum(d_query_low.astype(f32), axis=0), model_dim, head_id * width_part
    )
    grad_b_value = place_part(
        jnp.sum(d_value_low.astype(f32), axis=0), model_dim, head_id * width_part
    )
    attn_grad_parts = jnp.stack(
        (
            contract_rows(wide_flat, d_query_low),
            contract_rows(wide_flat, d_key_low),
            contract_rows(wide_flat, d_value_low),
        )
    )
    token_terms = (
        contract_cols(d_query_low, attn_cols[0])
        + contract_cols(d_key_low, attn_cols[1])
        + contract_cols(d_value_low, attn_cols[2])
    )
    d_tokens = d_first + token_partials(token_terms.reshape(wide_shape)).reshape(-1, model_dim)
    grad_tokens = d_tokens.astype(bf16).reshape(token_shape)
    attn_sums, grad_w_out, ffn_sums = (
        lax.psum_scatter(attn_grad_parts, "blk", scatter_dimension=1, tiled=True),
        lax.psum_scatter(grad_out_part, "blk", scatter_dimension=1, tiled=True),
        lax.psum_scatter(ffn_grad_parts, "blk", scatter_dimension=1, tiled=True),
    )
    (
        grad_b_query,
        grad_b_value,
        grad_b_out,
        grad_norm1_gain,
        grad_norm1_shift,
        grad_b_in,
        grad_b_back,
        grad_norm2_gain,
        grad_norm2_shift,
    ) = (
        lax.psum_scatter(grad_b_query, ("blk", "head"), scatter_dimension=0, tiled=True),
        lax.psum_scatter(grad_b_value, ("blk", "head"), scatter_dimension=0, tiled=True),
        lax.psum_scatter(grad_b_out, ("blk", "head"), scatter_dimension=0, tiled=True),
        lax.psum_scatter(grad_norm1_gain, ("blk", "head"), scatter_dimension=0, tiled=True),
        lax.psum_scatter(grad_norm1_shift, ("blk", "head"), scatter_dimension=0, tiled=True),
        lax.psum_scatter(grad_b_in, ("blk", "head"), scatter_dimension=0, tiled=True),
        lax.psum_scatter(grad_b_back, ("blk", "head"), scatter_dimension=0, tiled=True),
        lax.psum_scatter(grad_norm2_gain, ("blk", "head"), scatter_dimension=0, tiled=True),
        lax.psum_scatter(grad_norm2_shift, ("blk", "head"), scatter_dimension=0, tiled=True),
    )
    return (
        output,
        grad_tokens,
        attn_sums[0],
        attn_sums[1],
        attn_sums[2],
        grad_w_out,
        grad_b_query,
        grad_b_value,
        grad_b_out,
        grad_norm1_gain,
        grad_norm1_shift,
        ffn_sums[0],
        ffn_sums[1],
        grad_b_in,
        grad_b_back,
        grad_norm2_gain,
        grad_norm2_shift,
    )


MESH = pl.DeviceIdType.MESH
F32 = jnp.float32
BF16 = jnp.bfloat16
VMEM_LIMIT = 62 * 2**20


def dot_nn(left, right):
    return jnp.dot(left, right, preferred_element_type=F32)


class Place:
    def __init__(self):
        self.b = lax.axis_index("blk")
        self.z = lax.axis_index("head")
        self.y = self.b // 4
        self.x = (self.b // 2) % 2
        self.c = self.b % 2
        self.q = self.b // 2

    def chip(self, r):
        return ((self.y + r // 2) % 2) * 2 + (self.x + r % 2) % 2

    def peer(self, r):
        return (2 * self.chip(r) + self.c, self.z)

    def sibling(self):
        return (2 * self.q + 1 - self.c, self.z)


def remote(src, dst, send_sem, recv_sem, device):
    return pltpu.make_async_remote_copy(
        src_ref=src,
        dst_ref=dst,
        send_sem=send_sem,
        recv_sem=recv_sem,
        device_id=device,
        device_id_type=MESH,
    )


def wait_bytes(view, sem):
    pltpu.make_async_copy(view, view, sem).wait()


def greet_all(at):
    barrier = pltpu.get_barrier_semaphore()
    flat = at.b * 4 + at.z

    def greet(step, carry):
        other = (flat + step) % 32
        pl.semaphore_signal(
            barrier, inc=1, device_id=(other // 4, other % 4), device_id_type=MESH
        )
        return carry

    lax.fori_loop(1, 32, greet, 0)
    pl.semaphore_wait(barrier, 31)


def half(core):
    return pl.ds(pl.multiple_of(core * 128, 128), 128)


def lanes(index):
    return pl.ds(pl.multiple_of(index * 128, 128), 128)


def by_rows(count, size, step):
    def body(i, carry):
        step(pl.ds(pl.multiple_of(i * size, size), size))
        return carry

    lax.fori_loop(0, count // size, body, 0)


class Spread:
    def __init__(self, at, block, part, send, recv):
        self.at, self.block, self.part = at, block, part
        self.send, self.recv = send, recv

    def start(self):
        mine = self.block(0)
        for i in (0, 1):
            for r, k in ((1, i), (2, 1 - i)):
                piece = self.part(mine, k)
                remote(piece, piece, self.send, self.recv.at[r, k], self.at.peer(r)).start()

    def relay(self):
        for r, k in ((1, 0), (2, 1)):
            piece = self.part(self.block(r), k)
            wait_bytes(piece, self.recv.at[r, k])
            remote(piece, piece, self.send, self.recv.at[0, k], self.at.peer(3 - r)).start()

    def rest(self, r):
        block = self.block(r)
        for row, k in {1: ((1, 1),), 2: ((2, 0),), 3: ((0, 0), (0, 1))}[r]:
            wait_bytes(self.part(block, k), self.recv.at[row, k])


def part_rows(h, core):
    return pl.ds(pl.multiple_of(h * 128 + core * 64, 64), 64)


class Gather:
    def __init__(self, at, slots, h, send, recv, recv_sib):
        self.at, self.slots, self.h = at, slots, h
        self.send, self.recv_sib = send, recv_sib

        def part(block, k):
            return block.at[pl.ds(k * 32, 32)]

        self.spread = Spread(
            at, lambda r: slots.at[at.chip(r), part_rows(h, at.c)], part, send, recv
        )

    def to_sibling(self, r):
        block = self.spread.block(r)
        remote(block, block, self.send, self.recv_sib.at[r], self.at.sibling()).start()

    def start(self):
        self.spread.start()
        self.to_sibling(0)

    def relay(self):
        self.spread.relay()

    def forward(self, r):
        self.spread.rest(r)
        self.to_sibling(r)

    def ready(self, r):
        at = self.at
        wait_bytes(self.slots.at[at.chip(r), part_rows(self.h, 1 - at.c)], self.recv_sib.at[r])
        return at.chip(r)


class Exchange:
    def __init__(self, at, buffers, rows, send, recv, recv_sib):
        self.at, self.send, self.recv, self.recv_sib = at, send, recv, recv_sib
        self.sib_out, self.sib_in, self.out, self.into = buffers
        self.rows = rows

    def put(self, r, theirs):
        mine = self.sib_out.at[r, self.rows]
        mine[...] = theirs.astype(BF16)
        remote(
            mine,
            self.sib_in.at[r, self.rows],
            self.send,
            self.recv_sib.at[r],
            self.at.sibling(),
        ).start()

    def add(self, r, mine):
        wait_bytes(self.sib_in.at[r, self.rows], self.recv_sib.at[r])
        total = mine + self.sib_in[r, self.rows].astype(F32)
        if r == 0:
            return total
        held = self.out.at[r, self.rows]
        held[...] = total.astype(BF16)
        remote(
            held, self.into.at[r, self.rows], self.send, self.recv.at[r], self.at.peer(r)
        ).start()

    def arrive(self):
        for r in (1, 2, 3):
            wait_bytes(self.into.at[r, self.rows], self.recv.at[r])


def norm_rows(values):
    centre = jnp.mean(values, axis=-1, keepdims=True)
    centred = values - centre
    spread = jnp.mean(centred * centred, axis=-1, keepdims=True)
    scale = lax.rsqrt(spread + NORM_EPS)
    return centred * scale, scale


def norm_back(grad, unit, scale):
    centre = jnp.mean(grad, axis=-1, keepdims=True)
    along = jnp.mean(grad * unit, axis=-1, keepdims=True)
    return (grad - centre - unit * along) * scale


def send_or_copy(src, dst, send_sem, recv_sem, device, own):
    def away():
        remote(src, dst, send_sem, recv_sem, device).start()

    if own is None:
        away()
        return
    pl.when(jnp.logical_not(own))(away)

    @pl.when(own)
    def _():
        pltpu.make_async_copy(src, dst, recv_sem).start()


class Column:
    def __init__(self, at, ref, rows, sems):
        self.at, self.ref, self.rows = at, ref, rows
        self.up_send, self.up_recv, self.down_send, self.down_recv = sems

    def block(self, plane):
        return self.ref.at[self.rows, lanes(plane)]

    def sides(self, hop, act, arriving):
        z = self.at.z
        if arriving:
            below, above = z - 1 - hop, z + 1 + hop
            pl.when(below >= 0)(lambda: act(self.block(below), 0))
            pl.when(above <= 3)(lambda: act(self.block(above), 1))
        else:
            up = jnp.logical_and(z >= hop, z < 3)
            down = jnp.logical_and(z + hop <= 3, z > 0)
            pl.when(up)(lambda: act(self.block(z - hop), 0))
            pl.when(down)(lambda: act(self.block(z + hop), 1))

    def send(self, hop):
        def act(block, side):
            send = (self.up_send, self.down_send)[side].at[hop]
            recv = (self.up_recv, self.down_recv)[side].at[hop]
            remote(block, block, send, recv, (self.at.b, self.at.z + 1 - 2 * side)).start()

        self.sides(hop, act, False)

    def arrive(self, hop):
        def act(block, side):
            wait_bytes(block, (self.up_recv, self.down_recv)[side].at[hop])

        self.sides(hop, act, True)

    def end(self):
        def wait(hop):
            def act(block, side):
                wait_bytes(block, (self.up_send, self.down_send)[side].at[hop])

            return act

        for hop in range(3):
            self.sides(hop, wait(hop), False)


def plane_weights(at, src, dst, send_sem, recv_sem):
    rows, cols = lanes(at.b), lanes(at.z)
    pltpu.make_async_copy(src.at[:, lanes(at.b)], dst.at[rows, cols], recv_sem).start()

    def push(step, carry):
        other = (at.b + step) % 8
        remote(
            src.at[:, lanes(other)], dst.at[rows, cols], send_sem, recv_sem, (other, at.z)
        ).start()
        return carry

    lax.fori_loop(1, 8, push, 0)


class ColumnSum:
    def __init__(self, at, blocks, passing, send, recv):
        self.at, self.blocks, self.passing = at, blocks, passing
        self.send_sem, self.recv_sem = send, recv

    def plane(self, side, i):
        return i if side else 3 - i

    def hop(self, side):
        return 3 - self.at.z if side else self.at.z

    def next(self, side):
        return (self.at.b, self.at.z + 1 - 2 * side)

    def begin(self, which):
        for side in range(2):

            @pl.when(self.hop(side) == 0)
            def _(side=side):
                for i in which:
                    remote(
                        self.blocks.at[:, :, pl.ds(128 * self.plane(side, i), 128)],
                        self.passing.at[side, i],
                        self.send_sem.at[side, i],
                        self.recv_sem.at[side, i],
                        self.next(side),
                    ).start()

    def relay(self, hop, i):
        for side in range(2):

            @pl.when(self.hop(side) == hop)
            def _(side=side):
                held = self.passing.at[side, i]
                wait_bytes(held, self.recv_sem.at[side, i])
                cols = pl.ds(128 * self.plane(side, i), 128)
                for b in range(8):
                    self.passing[side, i, b] = (
                        self.passing[side, i, b].astype(F32)
                        + self.blocks[b, :, cols].astype(F32)
                    ).astype(BF16)
                remote(
                    held,
                    held,
                    self.send_sem.at[side, i],
                    self.recv_sem.at[side, i],
                    self.next(side),
                ).start()

    def finish(self, sums, final, send_out, recv_out):
        at = self.at
        own = lanes(at.z)
        for b in range(8):
            sums[b] = self.blocks[b, :, own]
        for side in range(2):
            for hop in range(1, 4):
                i = 3 - hop

                @pl.when(self.hop(side) == hop)
                def _(side=side, i=i):
                    wait_bytes(self.passing.at[side, i], self.recv_sem.at[side, i])
                    for b in range(8):
                        sums[b] = (
                            sums[b].astype(F32) + self.passing[side, i, b].astype(F32)
                        ).astype(BF16)

        def one(step, carry):
            other = (at.b + 1 + step) % 8
            send_or_copy(
                sums.at[other],
                final.at[:, lanes(at.b)],
                send_out,
                recv_out,
                (other, at.z),
                step == 7,
            )
            return carry

        lax.fori_loop(0, 8, one, 0)

    def end(self):
        for side in range(2):
            for i in range(3):

                @pl.when(self.hop(side) < 3 - i)
                def _(side=side, i=i):
                    wait_bytes(self.passing.at[side, i], self.send_sem.at[side, i])


def head_mask(h):
    lane = lax.broadcasted_iota(jnp.int32, (1, 128), 1)
    return jnp.where(lane // HEAD_DIM == h, 1.0, 0.0).astype(F32)


def slot_rows(index):
    return pl.ds(pl.multiple_of(index * 64, 64), 64)


def chip_rows(index):
    return pl.ds(pl.multiple_of(index * 256, 256), 256)


def core_rows(index):
    return pl.ds(pl.multiple_of(index * 1024, 1024), 1024)


class Inputs:
    small = x_hbm = cot_hbm = wq = wk = wv = wout = win = wback = None


def entries(table):
    return [(n, e) for n, e in vars(table).items() if n[0] != "_"]


class Results:
    out = ((128, 1024), BF16)
    gtok = ((128, 1024), BF16)
    w_in = ((2, 2, 128, 384), BF16)
    o_in = ((4, 128, 256), BF16)
    fin_in = ((128, 1024), BF16)
    fin_back = ((128, 1024), BF16)
    notes_in = ((4, 16, 128), F32)


class Scratch:
    small_here = ((16, 128), BF16)
    out_here = ((128, 1024), BF16)
    gtok_here = ((128, 1024), BF16)
    x = ((128, 1024), BF16)
    cot = ((128, 1024), BF16)
    xs = ((1024, 1024), BF16)
    wqkv = ((1024, 384), BF16)
    w_near = ((3, 128, 256), BF16)
    queries = ((1024, 128), BF16)
    keys_all = ((2048, 128), BF16)
    values_all = ((2048, 128), BF16)
    mixed = ((1024, 128), F32)
    log_sums = ((1024, 128), F32)
    att = ((128, 1024), BF16)
    wo = ((1024, 1024), BF16)
    par = ((8, 1024), F32)
    bins = ((1, 512), F32)
    wi = ((1024, 512), BF16)
    wb = ((1024, 512), BF16)
    smalls = ((8, 16, 128), BF16)
    smalls_z = ((4, 16, 128), BF16)
    smalls_sum = ((16, 128), BF16)
    proj = ((256, 384), F32)
    scores = ((256, 2048), F32)
    d_buf = ((256, 2048), F32)
    p_buf = ((256, 2048), BF16)
    att_send = ((1024, 128), BF16)
    n1 = ((128, 1024), F32)
    unit1 = ((128, 1024), F32)
    scale1 = ((128, 128), F32)
    d2 = ((128, 1024), F32)
    d1 = ((128, 1024), F32)
    db = ((128, 1024), BF16)
    norm_slots = ((4, 256, 1024), BF16)
    grad_slots = ((4, 256, 1024), BF16)
    hid = ((4, 256, 512), BF16)
    slope = ((4, 256, 512), F32)
    low = ((4, 256, 512), BF16)
    pre = ((128, 512), F32)
    terms = ((4, 256, 1024), F32)
    sib_out = ((2, 4, 128, 1024), BF16)
    sib_in = ((2, 4, 128, 1024), BF16)
    peer_out = ((2, 4, 128, 1024), BF16)
    peer_in = ((2, 4, 128, 1024), BF16)
    g_back = ((8, 128, 512), BF16)
    g_in = ((8, 128, 512), BF16)
    pass_back = ((2, 3, 8, 128, 128), BF16)
    pass_in = ((2, 3, 8, 128, 128), BF16)
    gs_back = ((8, 128, 128), BF16)
    gs_in = ((8, 128, 128), BF16)
    da_send = ((128, 1024), BF16)
    da = ((1024, 128), BF16)
    q_turned = ((128, 1024), BF16)
    da_turned = ((128, 1024), BF16)
    dq = ((1024, 128), F32)
    dk_turned = ((128, 2048), F32)
    dv_turned = ((128, 2048), F32)
    out_k = ((1024, 128), F32)
    out_v = ((1024, 128), F32)
    sib_k = ((1024, 128), F32)
    sib_v = ((1024, 128), F32)
    dqkv = ((1024, 384), BF16)
    x_sum = ((256, 1024), F32)
    x_own = ((64, 1024), F32)
    z_out = ((4, 64, 1024), BF16)
    z_in = ((4, 64, 1024), BF16)
    w_sib_out = ((4, 128, 384), F32)
    w_sib_in = ((4, 128, 384), F32)
    w_out = ((4, 128, 384), BF16)
    o_out = ((128, 1024), BF16)
    vec = ((8, 1024), F32)
    gbin = ((1, 512), F32)
    notes = ((8, 16, 128), F32)
    notes_p = ((8, 16, 128), F32)
    notes_sum = ((16, 128), F32)


class Arrivals:
    z = (4,)
    p = (4, 3, 2)
    wo = (3, 2)
    w = (3,)
    o = (5,)
    kv = (1,)
    misc = (12,)
    col = (6, 3)
    ga = (4, 3, 2)
    ga_sib = (4, 4)
    ex = (5, 4)
    ex_sib = (5, 4)
    zg = (2, 2, 3)
    kv2 = (2,)
    dx = (4, 3, 2)
    dz = (4,)
    ws = (4,)
    da = (4,)
    own = (4,)


class Departures:
    z = (1,)
    p = (1,)
    wo = (1,)
    w = (3,)
    o = (1,)
    kv = (1,)
    misc = (12,)
    col = (6, 3)
    ga = (2,)
    ex = (3,)
    zg = (2, 2, 3)
    kv2 = (1,)
    dx = (1,)
    dz = (1,)
    ws = (1,)


class Refs:
    pass


def layer_kernel(*refs):
    v = Refs()
    names = [n for table in (Inputs, Results, Scratch) for n, _ in entries(table)]
    names += ["r_" + n for n, _ in entries(Arrivals)] + ["s_" + n for n, _ in entries(Departures)]
    for name, ref in zip(names, refs):
        setattr(v, name, ref)
    at = Place()
    at.flat = at.b * 4 + at.z
    at.place = at.q * 4 + at.z
    at.parity = at.z % 2
    at.pair = 4 * (at.z // 2) + at.q
    def column(ref, rows, i):
        sems = [t.at[2 * i + k] for k in range(2) for t in (v.s_col, v.r_col)]
        return Column(at, ref, rows, sems)

    col_in = column(v.wi, pl.ds(0, 1024), 0)
    col_back = [column(v.wb, pl.ds(512 * k, 512), 1 + k) for k in range(2)]
    gathers = [
        [
            Gather(at, slots, h, v.s_ga.at[i], v.r_ga.at[2 * i + h], v.r_ga_sib.at[2 * i + h])
            for h in range(2)
        ]
        for i, slots in enumerate((v.norm_slots, v.grad_slots))
    ]

    def exchange(i, side, rows):
        buffers = [t.at[side] for t in (v.sib_out, v.sib_in, v.peer_out, v.peer_in)]
        return Exchange(at, buffers, rows, v.s_ex.at[i // 2], v.r_ex.at[i], v.r_ex_sib.at[i])

    scatters = [
        [exchange(2 * i + h, i, pl.ds(64 * h, 64)) for h in range(2)] for i in range(2)
    ]
    out_scatter = exchange(4, 0, pl.ds(0, 128))
    upper = at.z // 2
    at.planes = (at.z, at.z + 1 - 2 * at.parity, 2 - upper, 3 - 3 * upper)
    rows_spread = [
        Spread(
            at,
            lambda r, plane=plane: v.xs.at[slot_rows(at.chip(r) * 4 + plane)],
            lambda block, k: block.at[pl.ds(k * 32, 32)],
            v.s_p.at[0],
            v.r_p.at[i],
        )
        for i, plane in enumerate(at.planes)
    ]
    wo_spread = Spread(
        at,
        lambda r: v.wo.at[:, lanes(2 * at.chip(r) + at.c)],
        lambda block, k: block.at[pl.ds(k * 512, 512)],
        v.s_wo.at[0],
        v.r_wo,
    )
    sum_in = ColumnSum(at, v.g_in, v.pass_in, v.s_zg.at[0], v.r_zg.at[0])
    sum_back = ColumnSum(at, v.g_back, v.pass_back, v.s_zg.at[1], v.r_zg.at[1])
    place_small(at, v)
    pltpu.make_async_copy(v.x_hbm, v.x, v.r_own.at[0]).start()
    pltpu.make_async_copy(v.cot_hbm, v.cot, v.r_own.at[1]).start()
    greet_all(at)
    wait_bytes(v.x, v.r_own.at[0])
    attend_phase(at, v, col_in, col_back, rows_spread, wo_spread)
    ffn_phase(at, v, col_in, col_back, gathers, scatters, sum_back, sum_in)
    grads_phase(at, v, out_scatter, sum_in, sum_back)
    end_phase(at, v, (sum_in, sum_back, col_in, *col_back))


def place_small(at, v):
    def iota(shape, axis):
        return lax.broadcasted_iota(jnp.int32, shape, axis)

    spread = jnp.where(
        iota((8, 256), 1) // 32 == iota((8, 256), 0), v.small[0:1, 0:256], 0.0
    ).astype(BF16)
    lane = iota((256, 128), 1)
    source = iota((256, 128), 0) % 32 + 32 * at.z
    picked = jnp.where(lane == source, 1.0, 0.0).astype(BF16)
    top = dot_nn(spread, picked)
    units = jnp.where(iota((8, 128), 0) == at.z, v.small[0:1, 256:384], 0.0)
    v.small_here[...] = jnp.concatenate((top, units), axis=0).astype(BF16)


def attend_phase(at, v, col_in, col_back, rows_spread, wo_spread):
    xs, wqkv, wo = v.xs, v.wqkv, v.wo
    parity, pair = at.parity, at.pair

    pltpu.make_async_copy(v.small_here, v.smalls_z.at[at.z], v.r_misc.at[1]).start()
    for dz in range(1, 4):
        remote(
            v.small_here,
            v.smalls_z.at[at.z],
            v.s_misc.at[1],
            v.r_misc.at[1],
            (at.b, (at.z + dz) % 4),
        ).start()

    pltpu.make_async_copy(
        v.x.at[slot_rows(parity)], xs.at[slot_rows(at.place)], v.r_z.at[at.z]
    ).start()
    weights = (v.wq, v.wk, v.wv)
    for i in (1, 2, 3):
        plane = at.planes[i]
        remote(
            v.x.at[slot_rows(plane % 2)],
            xs.at[slot_rows(at.place)],
            v.s_z.at[0],
            v.r_z.at[at.z],
            (at.b, plane),
        ).start()
        if i == 1:
            for k, w in enumerate(weights):
                remote(
                    w, v.w_near.at[k], v.s_w.at[2], v.r_w.at[2], (at.b, at.planes[1])
                ).start()

    part = wo.at[pl.ds(pl.multiple_of(at.z * 256, 256), 256), lanes(at.b)]
    pltpu.make_async_copy(v.wout, part, v.r_o.at[4]).start()
    for i in (1, 2, 3):
        remote(v.wout, part, v.s_o.at[0], v.r_o.at[4], (at.b, at.planes[i])).start()

    def to_pairs(sources, group):
        for dx in range(2):
            column = (at.x + dx) % 2
            for k, w in enumerate(sources):
                send_or_copy(
                    w.at[:, lanes(column)],
                    wqkv.at[lanes(at.b), pl.ds(k * 128, 128)],
                    v.s_w.at[0],
                    v.r_w.at[0],
                    (2 * (group * 2 + column) + at.c, at.z),
                    None if dx else group == at.y,
                )

    for i in range(4):
        wait_bytes(rows_spread[i].block(0), v.r_z.at[at.planes[i]])
        rows_spread[i].start()
        if i == 0:
            to_pairs(weights, parity)
            wait_bytes(v.smalls_z, v.r_misc.at[1])
            total = v.smalls_z[0].astype(F32)
            for z in range(1, 4):
                total += v.smalls_z[z].astype(F32)
            v.smalls_sum[...] = total.astype(BF16)
            mine = v.smalls.at[at.b]
            pltpu.make_async_copy(v.smalls_sum, mine, v.r_misc.at[10]).start()

            def spread(step, carry):
                remote(
                    v.smalls_sum,
                    mine,
                    v.s_misc.at[10],
                    v.r_misc.at[10],
                    ((at.b + step) % 8, at.z),
                ).start()
                return carry

            lax.fori_loop(1, 8, spread, 0)
        if i == 1:
            plane_weights(at, v.win, v.wi, v.s_misc.at[0], v.r_misc.at[0])
            wait_bytes(v.w_near, v.r_w.at[2])
            to_pairs([v.w_near.at[k] for k in range(3)], 1 - parity)
        if i:
            rows_spread[i - 1].relay()
    wait_bytes(v.wi.at[:, pl.ds(0, 128)], v.r_misc.at[0])
    col_in.send(0)

    wait_bytes(wqkv.at[pl.ds(0, 512)], v.r_w.at[0])
    for r in range(4):
        part = wqkv.at[lanes(2 * at.chip(r) + at.c)]
        remote(part, part, v.s_w.at[1], v.r_w.at[1], at.sibling()).start()
    wait_bytes(v.smalls, v.r_misc.at[10])
    for b in range(8):
        v.par[:, 128 * b : 128 * b + 128] = v.smalls[b].astype(F32)[0:8]
    row = lax.broadcasted_iota(jnp.int32, (8, 128), 0)
    for h in range(4):
        rows = v.smalls[2 * h + at.b // 4].astype(F32)[8:16]
        rows = jnp.where(row == at.b % 4, rows, 0.0)
        v.bins[0:1, 128 * h : 128 * h + 128] = jnp.sum(rows, axis=0, keepdims=True)
    bias_q = v.par[0:1, lanes(pair)]
    bias_v = v.par[1:2, lanes(pair)]
    wait_bytes(wqkv.at[pl.ds(0, 512)], v.r_w.at[1])

    def project(r):
        chip = at.chip(r)
        if r:
            for i in range(4):
                rows_spread[i].rest(r)
        rows = chip_rows(chip)
        v.proj[...] = dot_nn(xs[rows], wqkv[...])
        v.queries[rows] = (v.proj[:, 0:128] + bias_q).astype(BF16)
        own_rows = chip_rows(at.c * 4 + chip)
        v.keys_all[own_rows] = v.proj[:, 128:256].astype(BF16)
        v.values_all[own_rows] = (v.proj[:, 256:384] + bias_v).astype(BF16)
        for k, ref in enumerate((v.keys_all, v.values_all)):
            view = ref.at[own_rows]
            remote(view, view, v.s_kv.at[0], v.r_kv.at[0], at.sibling()).start()

    project(0)
    rows_spread[3].relay()

    whole = wo_spread.block(0)
    wait_bytes(whole, v.r_o.at[4])
    wo_spread.start()
    remote(whole, whole, v.s_o.at[0], v.r_o.at[0], at.sibling()).start()
    plane_weights(at, v.wback, v.wb, v.s_misc.at[2], v.r_misc.at[2])

    for r in (1, 2, 3):
        project(r)

    wait_bytes(v.keys_all, v.r_kv.at[0])

    col_in.arrive(0)
    col_in.send(1)
    scores = v.scores

    def attend(step, carry):
        chip = (at.q + 1 + step) % 4
        rows = chip_rows(chip)
        outs = []
        logs = []
        for h in range(2):
            q = (v.queries[rows].astype(F32) * head_mask(h) * HEAD_DIM**-0.5).astype(BF16)
            scores[...] = contract_cols(q, v.keys_all[...])
            top = jnp.max(scores[...], axis=-1, keepdims=True)
            weights = jnp.exp(scores[...] - top)
            total = jnp.sum(weights, axis=-1, keepdims=True)
            outs.append(dot_nn(weights.astype(BF16), v.values_all[...]) / total)
            logs.append(top + jnp.log(total))
        first = head_mask(0) > 0.5
        merged = jnp.where(first, outs[0], outs[1])
        v.mixed[rows] = merged
        v.log_sums[rows] = jnp.where(first, logs[0], logs[1])
        v.att_send[rows] = merged.astype(BF16)
        for k in range(4):
            plane = (at.z + 1 + k) % 4
            send_or_copy(
                v.att_send.at[slot_rows(chip * 4 + plane)],
                v.att.at[slot_rows(parity), lanes(pair)],
                v.s_misc.at[3],
                v.r_misc.at[3],
                (2 * chip + at.c, plane),
                step == 3 if k == 3 else None,
            )

        @pl.when(step == 0)
        def _():
            wo_spread.relay()

        @pl.when(step == 2)
        def _():
            col_in.arrive(1)
            col_in.send(2)

        return carry

    lax.fori_loop(0, 4, attend, 0)

    wait_bytes(v.wb.at[:, pl.ds(0, 128)], v.r_misc.at[2])
    for half_back in col_back:
        half_back.send(0)
    for r in (1, 2, 3):
        wo_spread.rest(r)
        part = wo_spread.block(r)
        remote(part, part, v.s_o.at[0], v.r_o.at[r], at.sibling()).start()
    for r in range(4):
        wait_bytes(whole, v.r_o.at[r])
    wait_bytes(v.att, v.r_misc.at[3])


def ffn_phase(at, v, col_in, col_back, gathers, scatters, sum_back, sum_in):
    n1, terms, peer_in = v.n1, v.terms, v.peer_in

    def param(i):
        return v.par[i : i + 1, :]

    def local(h, i):
        return pl.ds(64 * h + 32 * i, 32)

    def chip_part(h, i):
        return pl.ds(pl.multiple_of(h * 128 + at.c * 64 + 32 * i, 32), 32)

    wait_bytes(v.cot, v.r_own.at[1])
    n1[...] = dot_nn(v.att[...], v.wo[...])
    for h in range(2):
        for i in range(2):
            rows = local(h, i)
            unit, scale = norm_rows(v.x[rows].astype(F32) + n1[rows] + param(2))
            v.unit1[rows] = unit
            v.scale1[rows] = jnp.broadcast_to(scale, (32, 128))
            normed = unit * param(3) + param(4)
            n1[rows] = normed
            v.norm_slots[at.q, chip_part(h, i)] = normed.astype(BF16)
        gathers[0][h].start()

    def hidden(h, r):
        chip = gathers[0][h].ready(r)
        v.pre[...] = dot_nn(v.norm_slots[chip, pl.ds(128 * h, 128)], v.wi[...])

        def activate(i, carry):
            rows = pl.ds(pl.multiple_of(i * 32, 32), 32)
            into = pl.ds(pl.multiple_of(128 * h + i * 32, 32), 32)
            u = v.pre[rows] + v.bins[...]
            cdf = 0.5 * (1.0 + lax.erf(u * math.sqrt(0.5)))
            bell = jnp.exp(-0.5 * u * u) * (1.0 / math.sqrt(2.0 * math.pi))
            v.hid[r, into] = (u * cdf).astype(BF16)
            v.slope[r, into] = cdf + u * bell
            return carry

        lax.fori_loop(0, 4, activate, 0)

    def neighbours(gather):
        gather.relay()
        gather.forward(1)
        gather.forward(2)

    neighbours(gathers[0][0])
    gathers[0][1].relay()
    col_back[0].arrive(0)
    col_back[0].send(1)
    col_in.arrive(2)
    hidden(0, 0)
    gathers[0][1].forward(1)
    gathers[0][1].forward(2)
    col_back[1].arrive(0)
    col_back[1].send(1)
    hidden(1, 0)
    hidden(0, 1)
    hidden(0, 2)
    gathers[0][0].forward(3)
    hidden(1, 1)
    gathers[0][1].forward(3)
    hidden(1, 2)
    col_back[0].arrive(1)
    col_back[0].send(2)
    hidden(0, 3)
    hidden(1, 3)
    col_back[1].arrive(1)
    col_back[1].send(2)
    for half_back in col_back:
        half_back.arrive(2)

    def to_plane(scatter, done, h, r, product):
        terms[r, pl.ds(128 * h, 128)] = product
        scatter[h].put(r, terms[r, part_rows(h, 1 - at.c)])
        done.append((h, r))
        if len(done) > 3:
            pass_on(scatter, *done[-4])

    def pass_on(scatter, h, r):
        total = scatter[h].add(r, terms[r, part_rows(h, at.c)])
        if r == 0:
            terms[0, part_rows(h, at.c)] = total

    done = []
    for h in range(2):
        for r in (3, 1, 2, 0):
            product = contract_cols(v.hid[r, pl.ds(128 * h, 128)], v.wb[...])
            to_plane(scatters[0], done, h, r, product)
    for one in done[-3:]:
        pass_on(scatters[0], *one)

    def peers(side, rows):
        return (
            peer_in[side, 1, rows].astype(F32)
            + peer_in[side, 2, rows].astype(F32)
            + peer_in[side, 3, rows].astype(F32)
        )

    def column_sums(parts, sums):
        return tuple(
            kept + jnp.sum(part.reshape(4, 8, 1024), axis=0) for kept, part in zip(sums, parts)
        )

    gbin = [jnp.zeros((8, 512), F32)]
    done = []

    def hidden_grad(h, r):
        chip = gathers[1][h].ready(r)
        v.pre[...] = dot_nn(v.grad_slots[chip, pl.ds(128 * h, 128)], v.wb[...])

        def deactivate(i, carry):
            rows = pl.ds(pl.multiple_of(i * 32, 32), 32)
            into = pl.ds(pl.multiple_of(128 * h + i * 32, 32), 32)
            low = (v.pre[rows] * v.slope[r, into]).astype(BF16)
            v.low[r, into] = low
            return carry + jnp.sum(low.astype(F32).reshape(4, 8, 512), axis=0)

        gbin[0] = lax.fori_loop(0, 4, deactivate, gbin[0])
        product = contract_cols(v.low[r, pl.ds(128 * h, 128)], v.wi[...])
        to_plane(scatters[1], done, h, r, product)

    sums = tuple(jnp.zeros((8, 1024), F32) for _ in range(3))
    for h in range(2):
        scatters[0][h].arrive()
        for i in range(2):
            rows = local(h, i)
            total = terms[0, chip_part(h, i)] + peers(0, rows)
            unit, scale = norm_rows(n1[rows] + total + param(5))
            v.out_here[rows] = (unit * param(6) + param(7)).astype(BF16)
            g = v.cot[rows].astype(F32)
            d = norm_back(g * param(6), unit, scale)
            v.d2[rows] = d
            low = d.astype(BF16)
            v.grad_slots[at.q, chip_part(h, i)] = low
            sums = column_sums((g * unit, g, low.astype(F32)), sums)
        gathers[1][h].start()
        if h == 0:
            hidden_grad(0, 0)
    pltpu.make_async_copy(v.out_here, v.out, v.r_own.at[2]).start()
    for row, total in zip((6, 7, 5), sums):
        v.vec[row : row + 1, :] = jnp.sum(total, axis=0, keepdims=True)

    def weight_grad(slots, right, into):
        def one(step, carry):
            other = (at.q + step) % 4
            total = jnp.zeros((256, 512), F32)
            for r in range(4):
                total += contract_rows(slots[at.chip(r), :, chip_rows(other)], right[r])
            into[2 * other] = total[0:128].astype(BF16)
            into[2 * other + 1] = total[128:256].astype(BF16)
            return carry

        lax.fori_loop(0, 4, one, 0)

    neighbours(gathers[1][0])
    hidden_grad(1, 0)
    hidden_grad(0, 1)
    neighbours(gathers[1][1])
    hidden_grad(0, 2)
    gathers[1][0].forward(3)
    hidden_grad(1, 1)
    hidden_grad(0, 3)
    gathers[1][1].forward(3)
    hidden_grad(1, 2)
    hidden_grad(1, 3)
    for one in done[-3:]:
        pass_on(scatters[1], *one)
    v.gbin[...] = jnp.sum(gbin[0], axis=0, keepdims=True)

    sums = tuple(jnp.zeros((8, 1024), F32) for _ in range(3))
    for h in range(2):
        if h == 0:
            weight_grad(v.grad_slots, v.hid, v.g_back)
            wait_bytes(v.xs.at[pl.ds(0, 896)], v.s_ga.at[1])
            sum_back.begin((0,))
        else:
            weight_grad(v.norm_slots, v.low, v.g_in)
        scatters[1][h].arrive()
        for i in range(2):
            rows = local(h, i)
            total = v.d2[rows] + terms[0, chip_part(h, i)] + peers(1, rows)
            unit = v.unit1[rows]
            d = norm_back(total * param(3), unit, v.scale1[rows][:, :1])
            v.d1[rows] = d
            low = d.astype(BF16)
            v.db[rows] = low
            sums = column_sums((total * unit, total, low.astype(F32)), sums)
        rows = pl.ds(64 * h, 64)
        v.da_send[rows] = contract_cols(v.db[rows], v.wo[...]).astype(BF16)
        for r in range(4):
            chip = at.chip(r)
            for plane in (h, h + 2):
                pair = 2 * (plane - h) + chip
                send_or_copy(
                    v.da_send.at[rows, lanes(pair)],
                    v.da.at[slot_rows(at.place)],
                    v.s_misc.at[4],
                    v.r_da.at[r],
                    (2 * chip + at.c, plane),
                    None if r else at.z == plane,
                )

    for row, total in zip((3, 4, 2), sums):
        v.vec[row : row + 1, :] = jnp.sum(total, axis=0, keepdims=True)
    v.vec[0:2, :] = jnp.zeros((2, 1024), F32)
    for i in range(3):
        if i:
            sum_back.begin((i,))
        sum_in.begin((i,))


def grads_phase(at, v, out_scatter, sum_in, sum_back):
    xs, wqkv, terms = v.xs, v.wqkv, v.terms
    parity, pair = at.parity, at.pair

    wait_bytes(xs.at[pl.ds(0, 896)], v.s_ex.at[0])
    for r in (3, 1, 2, 0):
        for core in (1 - at.c, at.c):
            part = contract_rows(v.db[:, lanes(2 * at.chip(r) + core)], v.att[...])
            if core is at.c:
                terms[r, 0:128] = part
            else:
                out_scatter.put(r, part)

    v.q_turned[...] = v.queries[...].astype(F32).T.astype(BF16)
    v.dk_turned[...] = jnp.zeros_like(v.dk_turned)
    v.dv_turned[...] = jnp.zeros_like(v.dv_turned)
    for r in (3, 1, 2):
        out_scatter.add(r, terms[r, 0:128])
    terms[0, 0:128] = out_scatter.add(0, terms[0, 0:128])
    wait_bytes(v.da.at[chip_rows(at.q)], v.r_da.at[0])
    s_buf, d_buf, p_buf = v.scores, v.d_buf, v.p_buf

    def attend(step, carry):
        chip = ((at.y + step // 2) % 2) * 2 + (at.x + step % 2) % 2
        rows = chip_rows(chip)

        @pl.when(step > 0)
        def _():
            wait_bytes(v.da.at[rows], v.r_da.at[step])

        v.da_turned[:, rows] = v.da[rows].astype(F32).T.astype(BF16)
        parts = []
        for h in range(2):
            mask = head_mask(h)
            grad = v.da[rows].astype(F32) * mask
            delta = jnp.sum(grad * v.mixed[rows], axis=-1, keepdims=True)
            q = (v.queries[rows].astype(F32) * mask * HEAD_DIM**-0.5).astype(BF16)
            s_buf[...] = contract_cols(q, v.keys_all[...])
            d_buf[...] = contract_cols(grad.astype(BF16), v.values_all[...])
            logs = v.log_sums[rows][:, h * HEAD_DIM : h * HEAD_DIM + 1]
            probs = jnp.exp(s_buf[...] - logs)
            p_buf[...] = probs.astype(BF16)
            low = (probs * (d_buf[...] - delta)).astype(BF16)
            band = pl.ds(h * HEAD_DIM, HEAD_DIM)
            v.dv_turned[band] += dot_nn(v.da_turned[band, rows], p_buf[...])
            v.dk_turned[band] += dot_nn(v.q_turned[band, rows], low)
            parts.append(dot_nn(low, v.keys_all[...]))
        v.dq[rows] = jnp.where(head_mask(0) > 0.5, parts[0], parts[1]) * HEAD_DIM**-0.5

        @pl.when(step == 1)
        def _():
            sum_back.relay(1, 0)

        @pl.when(step == 2)
        def _():
            sum_in.relay(1, 0)

        return carry

    lax.fori_loop(0, 4, attend, 0)

    other = core_rows(1 - at.c)
    mine = core_rows(at.c)
    v.out_k[...] = v.dk_turned[:, other].T * HEAD_DIM**-0.5
    v.out_v[...] = v.dv_turned[:, other].T
    for k, (ref, into) in enumerate(((v.out_k, v.sib_k), (v.out_v, v.sib_v))):
        remote(ref, into, v.s_kv2.at[0], v.r_kv2.at[k], at.sibling()).start()
    dqkv = v.dqkv
    low = v.dq[...].astype(BF16)
    dqkv[:, 0:128] = low
    v.vec[0:1, lanes(pair)] = jnp.sum(low.astype(F32), axis=0, keepdims=True)
    out_scatter.arrive()
    peer_in = v.peer_in.at[0]

    def out_rows(rows):
        total = (
            terms[0, rows]
            + peer_in[1, rows].astype(F32)
            + peer_in[2, rows].astype(F32)
            + peer_in[3, rows].astype(F32)
        )
        v.o_out[rows] = total.astype(BF16)

    by_rows(128, 32, out_rows)
    wide = pl.ds(pl.multiple_of(at.z * 256, 256), 256)
    pltpu.make_async_copy(v.o_out.at[:, wide], v.o_in.at[0], v.r_misc.at[8]).start()
    for dz in range(1, 4):
        plane = (at.z + dz) % 4
        remote(
            v.o_out.at[:, pl.ds(pl.multiple_of(plane * 256, 256), 256)],
            v.o_in.at[dz],
            v.s_misc.at[8],
            v.r_misc.at[8],
            (at.b, plane),
        ).start()

    sum_back.relay(1, 1)
    sum_back.relay(2, 0)
    own_k = v.dk_turned[:, mine].T * HEAD_DIM**-0.5
    wait_bytes(v.sib_k, v.r_kv2.at[0])
    dqkv[:, 128:256] = (own_k + v.sib_k[...]).astype(BF16)
    own_v = v.dv_turned[:, mine].T
    wait_bytes(v.sib_v, v.r_kv2.at[1])
    low = (own_v + v.sib_v[...]).astype(BF16)
    dqkv[:, 256:384] = low
    v.vec[1:2, lanes(pair)] = jnp.sum(low.astype(F32), axis=0, keepdims=True)

    notes = v.notes
    for b in range(8):
        notes[b, 0:8] = v.vec[:, 128 * b : 128 * b + 128]
        notes[b, 8:16] = jnp.zeros((8, 128), F32)
    row = lax.broadcasted_iota(jnp.int32, (8, 128), 0)
    for h in range(4):
        notes[2 * h + at.b // 4, 8:16] = jnp.where(
            row == at.b % 4, v.gbin[0:1, 128 * h : 128 * h + 128], 0.0
        )
    pltpu.make_async_copy(notes.at[at.b], v.notes_p.at[at.b], v.r_misc.at[5]).start()

    def spread(step, carry):
        to = (at.b + step) % 8
        remote(
            notes.at[to], v.notes_p.at[at.b], v.s_misc.at[5], v.r_misc.at[5], (to, at.z)
        ).start()
        return carry

    lax.fori_loop(1, 8, spread, 0)

    wait_bytes(xs.at[pl.ds(0, 896)], v.s_ga.at[0])
    x_out, x_in, x_via = v.norm_slots, v.grad_slots.at[0:2], v.grad_slots.at[2:4]
    for r in (3, 1, 2, 0):
        part = contract_cols(dqkv[chip_rows(at.chip(r))], wqkv[...])
        if r:
            x_out[r] = part.astype(BF16)
        else:
            v.x_sum[...] = part
    def piece(dz, k):
        return pl.ds(pl.multiple_of(((at.z + dz) % 4) * 64 + 32 * k, 32), 32)

    order = (2, 1, 3, 0)

    def send_dx(dz, via):
        for r, k in ((1, 0), (2, 1)):
            rows = piece(dz, k)
            remote(
                x_out.at[3 if via else r, rows],
                x_via.at[r - 1, rows] if via else x_in.at[r - 1, rows],
                v.s_dx.at[0],
                v.r_dx.at[dz, 0 if via else r, k],
                at.peer(r),
            ).start()

    def relay_dx(dz):
        for r, k in ((2, 0), (1, 1)):
            rows = piece(dz, k)
            wait_bytes(x_via.at[k, rows], v.r_dx.at[dz, 0, k])
            x_out[r, rows] = (
                x_out[r, rows].astype(F32) + x_via[k, rows].astype(F32)
            ).astype(BF16)
            remote(
                x_out.at[r, rows],
                x_in.at[r - 1, rows],
                v.s_dx.at[0],
                v.r_dx.at[dz, r, k],
                at.peer(r),
            ).start()

    z_out, z_in = v.z_out, v.z_in
    def column_dx(dz):
        plane = (at.z + dz) % 4
        rows = slot_rows(plane)
        for r in (1, 2):
            for k in range(2):
                wait_bytes(x_in.at[r - 1, piece(dz, k)], v.r_dx.at[dz, r, k])
        total = v.x_sum[rows] + x_in[0, rows].astype(F32) + x_in[1, rows].astype(F32)
        if dz:
            z_out[dz] = total.astype(BF16)
            remote(
                z_out.at[dz], z_in.at[dz], v.s_dz.at[0], v.r_dz.at[dz], (at.b, plane)
            ).start()
        else:
            v.x_own[...] = total

    def begin_dx(dz):
        send_dx(dz, True)
        send_dx(dz, False)

    begin_dx(2)
    begin_dx(1)
    def features(b):
        return contract_rows(xs[:, lanes(b)], dqkv[...])

    for r in range(4):
        v.w_sib_out[r] = features(2 * at.chip(r) + 1 - at.c)
        remote(
            v.w_sib_out.at[r], v.w_sib_in.at[r], v.s_ws.at[0], v.r_ws.at[r], at.sibling()
        ).start()
    relay_dx(2)
    begin_dx(3)
    sum_in.relay(1, 1)
    sum_in.relay(2, 0)
    relay_dx(1)
    begin_dx(0)
    column_dx(2)
    relay_dx(3)
    column_dx(1)
    relay_dx(0)
    plane_w = 2 * (at.z // 2) + at.y
    for r in range(4):
        total = features(2 * at.chip(r) + at.c)
        wait_bytes(v.w_sib_in.at[r], v.r_ws.at[r])
        v.w_out[r] = (total + v.w_sib_in[r]).astype(BF16)
        send_or_copy(
            v.w_out.at[r],
            v.w_in.at[parity, at.x],
            v.s_misc.at[6],
            v.r_misc.at[6],
            at.peer(r)[:1] + (plane_w,),
            plane_w == at.z if r == 0 else None,
        )

    column_dx(3)
    sum_back.finish(v.gs_back, v.fin_back, v.s_misc.at[7], v.r_misc.at[7])
    sum_in.finish(v.gs_in, v.fin_in, v.s_misc.at[9], v.r_misc.at[9])
    wait_bytes(v.notes_p, v.r_misc.at[5])
    total = v.notes_p[0]
    for b in range(1, 8):
        total += v.notes_p[b]
    v.notes_sum[...] = total
    mine = v.notes_in.at[at.z]
    pltpu.make_async_copy(v.notes_sum, mine, v.r_misc.at[11]).start()
    for dz in range(1, 4):
        remote(
            v.notes_sum, mine, v.s_misc.at[11], v.r_misc.at[11], (at.b, (at.z + dz) % 4)
        ).start()

    column_dx(0)
    for dz in (1, 2, 3):
        wait_bytes(z_in.at[dz], v.r_dz.at[dz])
    same = slot_rows(parity)
    v.gtok_here[same] = (v.d1[same] + v.x_own[...] + z_in[2].astype(F32)).astype(BF16)
    cross = slot_rows(1 - parity)
    v.gtok_here[cross] = (v.d1[cross] + z_in[1].astype(F32) + z_in[3].astype(F32)).astype(BF16)

    pltpu.make_async_copy(v.gtok_here, v.gtok, v.r_own.at[3]).start()
    wait_bytes(v.o_in, v.r_misc.at[8])
    wait_bytes(v.w_in, v.r_misc.at[6])
    wait_bytes(v.notes_in, v.r_misc.at[11])
    wait_bytes(v.fin_back, v.r_misc.at[7])
    wait_bytes(v.fin_in, v.r_misc.at[9])


def end_phase(at, v, ends):
    wait_bytes(v.out_here, v.r_own.at[2])
    for one in ends:
        one.end()

    def rows(n):
        return v.xs.at[pl.ds(0, n)]

    wait_bytes(rows(192), v.s_z.at[0])
    wait_bytes(rows(768), v.s_p.at[0])
    wait_bytes(rows(384), v.s_wo.at[0])
    wait_bytes(rows(608), v.s_o.at[0])
    wait_bytes(rows(256), v.s_kv.at[0])
    for i in (1, 2):
        wait_bytes(rows(896), v.s_ex.at[i])
    wait_bytes(rows(768), v.s_dx.at[0])
    wait_bytes(rows(192), v.s_dz.at[0])
    wait_bytes(v.w_sib_out, v.s_ws.at[0])
    wait_bytes(rows(512), v.s_kv2.at[0])
    wait_bytes(v.wqkv.at[pl.ds(0, 384)], v.s_w.at[0])
    wait_bytes(v.wqkv.at[pl.ds(0, 512)], v.s_w.at[1])
    wait_bytes(v.w_near, v.s_w.at[2])
    seven = v.wi.at[pl.ds(0, 896), pl.ds(0, 128)]
    for i in (0, 2, 7, 9):
        wait_bytes(seven, v.s_misc.at[i])
    wait_bytes(v.smalls.at[pl.ds(0, 3)], v.s_misc.at[1])
    wait_bytes(v.smalls.at[pl.ds(0, 7)], v.s_misc.at[10])
    for i in (3, 4):
        wait_bytes(v.att_send.at[pl.ds(0, 960)], v.s_misc.at[i])
    wait_bytes(v.notes.at[pl.ds(0, 7)], v.s_misc.at[5])
    wait_bytes(v.notes.at[pl.ds(0, 3)], v.s_misc.at[11])
    plane_w = 2 * (at.z // 2) + at.y

    @pl.when(plane_w == at.z)
    def _():
        wait_bytes(v.w_out.at[pl.ds(0, 3)], v.s_misc.at[6])

    @pl.when(plane_w != at.z)
    def _():
        wait_bytes(v.w_out, v.s_misc.at[6])

    wait_bytes(v.o_in.at[pl.ds(0, 3)], v.s_misc.at[8])
    wait_bytes(v.gtok_here, v.r_own.at[3])


def finish_kernel(
    place_ref,
    out_in,
    gtok_in,
    w_in,
    o_in,
    fin_in,
    fin_back,
    notes_in,
    out_ref,
    gtok_ref,
    gq_ref,
    gk_ref,
    gv_ref,
    gout_ref,
    gwin_ref,
    gwback_ref,
    bin_ref,
    *vector_refs,
):
    out_ref[...] = out_in[...]
    gtok_ref[...] = gtok_in[...]
    for x in range(2):
        total = w_in[0, x].astype(F32) + w_in[1, x].astype(F32)
        for k, ref in enumerate((gq_ref, gk_ref, gv_ref)):
            ref[:, 128 * x : 128 * x + 128] = total[:, 128 * k : 128 * k + 128]
    gout_ref[...] = (
        o_in[0].astype(F32) + o_in[1].astype(F32) + o_in[2].astype(F32) + o_in[3].astype(F32)
    ).T
    gwin_ref[...] = fin_in[...].astype(F32)
    gwback_ref[...] = fin_back[...].astype(F32)
    total = notes_in[0] + notes_in[1] + notes_in[2] + notes_in[3]
    z = place_ref[0]
    part = jnp.zeros((8, 32), F32)
    units = jnp.zeros((1, 128), F32)
    for k in range(4):
        part += jnp.where(z == k, total[0:8, 32 * k : 32 * k + 32], 0.0)
        units += jnp.where(z == k, total[8 + k : 9 + k], 0.0)
    for j, ref in enumerate(vector_refs):
        ref[...] = part[j]
    bin_ref[...] = units[0]


def vmem():
    return pl.BlockSpec(memory_space=pltpu.VMEM)


def run_layer(*args):
    results = [e for _, e in entries(Results)]
    scratch = [pltpu.VMEM(s, t) for _, (s, t) in entries(Scratch)]
    for _, shape in entries(Arrivals) + entries(Departures):
        scratch.append(DMA(shape))
    return pl.pallas_call(
        layer_kernel,
        out_shape=[jax.ShapeDtypeStruct(s, t) for s, t in results],
        in_specs=[vmem()] + [pl.BlockSpec(memory_space=pl.ANY)] * (len(args) - 1),
        out_specs=[pl.BlockSpec(memory_space=pl.ANY)] * len(results),
        scratch_shapes=scratch,
        compiler_params=pltpu.CompilerParams(
            collective_id=1, has_side_effects=True, vmem_limit_bytes=VMEM_LIMIT
        ),
    )(*args)


def run_finish(*args):
    shapes = (
        ((128, 1024), BF16),
        ((128, 1024), BF16),
        ((128, 256), F32),
        ((128, 256), F32),
        ((128, 256), F32),
        ((256, 128), F32),
        ((128, 1024), F32),
        ((128, 1024), F32),
        ((128,), F32),
    ) + (((32,), F32),) * 8
    return pl.pallas_call(
        finish_kernel,
        out_shape=[jax.ShapeDtypeStruct(s, t) for s, t in shapes],
        in_specs=[pl.BlockSpec(memory_space=pltpu.SMEM)] + [vmem()] * (len(args) - 1),
        out_specs=[vmem()] * len(shapes),
        compiler_params=pltpu.CompilerParams(vmem_limit_bytes=VMEM_LIMIT),
    )(*args)


DMA = pltpu.SemaphoreType.DMA


def fast_device(
    tokens,
    w_query,
    w_key,
    w_value,
    w_out,
    b_query,
    b_value,
    b_out,
    norm1_gain,
    norm1_shift,
    w_in,
    w_back,
    b_in,
    b_back,
    norm2_gain,
    norm2_shift,
    cotangent,
):
    head_id = lax.axis_index("head")
    token_shape = tokens.shape
    model_dim = tokens.shape[2]
    x = tokens.reshape(-1, model_dim)
    vectors = (
        b_query,
        b_value,
        b_out,
        norm1_gain,
        norm1_shift,
        b_back,
        norm2_gain,
        norm2_shift,
        b_in,
    )
    small = jnp.concatenate(vectors).astype(F32).reshape(1, -1)
    results = run_layer(
        small, x, cotangent.reshape(-1, model_dim), w_query, w_key, w_value, w_out, w_in, w_back
    )
    output, grad_tokens, gq, gk, gv, gout, gw_in, gw_back, gb_in, *own = run_finish(
        head_id.astype(jnp.int32).reshape(1), *results
    )
    return (
        output.reshape(token_shape),
        grad_tokens.reshape(token_shape),
        gq,
        gk,
        gv,
        gout,
        own[0],
        own[1],
        own[2],
        own[3],
        own[4],
        gw_in,
        gw_back,
        gb_in,
        own[5],
        own[6],
        own[7],
    )


def solution(mesh):
    in_specs = (
        P(None, ("blk", "head"), None),
        P("blk", "head"),
        P("blk", "head"),
        P("blk", "head"),
        P("head", "blk"),
        P(("blk", "head")),
        P(("blk", "head")),
        P(("blk", "head")),
        P(("blk", "head")),
        P(("blk", "head")),
        P("blk", "head"),
        P("blk", "head"),
        P(("blk", "head")),
        P(("blk", "head")),
        P(("blk", "head")),
        P(("blk", "head")),
        P(None, ("blk", "head"), None),
    )
    out_specs = (
        P(None, ("blk", "head"), None),
        P(None, ("blk", "head"), None),
        P("blk", "head"),
        P("blk", "head"),
        P("blk", "head"),
        P("head", "blk"),
        P(("blk", "head")),
        P(("blk", "head")),
        P(("blk", "head")),
        P(("blk", "head")),
        P(("blk", "head")),
        P("blk", "head"),
        P("blk", "head"),
        P(("blk", "head")),
        P(("blk", "head")),
        P(("blk", "head")),
        P(("blk", "head")),
    )
    sizes = (mesh.shape["blk"], mesh.shape["head"])
    body = fast_device if sizes == (8, 4) else per_device
    return jax.shard_map(
        body, mesh=mesh, in_specs=in_specs, out_specs=out_specs, check_vma=False
    )
```

```python
import functools
import math

import jax
import jax.numpy as jnp
from jax import lax
from jax.experimental import pallas as pl
from jax.experimental.pallas import tpu as pltpu
from jax.sharding import PartitionSpec as P

HEAD_DIM = 64


NORM_EPS = 1e-05


def layer_norm(summed, gain, shift):
    centre = jnp.mean(summed, axis=-1, keepdims=True)
    centred = summed - centre
    spread = jnp.mean(centred * centred, axis=-1, keepdims=True)
    return centred * lax.rsqrt(spread + NORM_EPS) * gain + shift


def gelu_exact(inputs):
    return jax.nn.gelu(inputs, approximate=False)


def split_heads(packed):
    return packed.reshape(packed.shape[0], packed.shape[1], -1, HEAD_DIM)


def contract_rows(left, right):
    return lax.dot_general(
        left, right, (((0,), (0,)), ((), ())), preferred_element_type=jnp.float32
    )


def contract_cols(left, right):
    return lax.dot_general(
        left, right, (((1,), (1,)), ((), ())), preferred_element_type=jnp.float32
    )


def score_block(queries4, keys4):
    return jnp.einsum(
        "sqge,skge->sqgk", queries4, keys4, preferred_element_type=jnp.float32
    ) * HEAD_DIM ** (-0.5)


def score_grads(queries4, keys4, values4, grads4, log_sums, deltas):
    probs = jnp.exp(score_block(queries4, keys4) - log_sums[..., None])
    d_probs = jnp.einsum("sqge,skge->sqgk", grads4, values4, preferred_element_type=jnp.float32)
    d_scores = (probs * (d_probs - deltas[..., None])).astype(jnp.bfloat16)
    return (probs.astype(jnp.bfloat16), d_scores)


def token_rows(local):
    return lax.all_gather(local, "head", axis=1, tiled=True)


def token_partials(terms):
    return lax.psum_scatter(
        terms.astype(jnp.bfloat16), "head", scatter_dimension=1, tiled=True
    ).astype(jnp.float32)


def place_part(part, full_len, start):
    return lax.dynamic_update_slice_in_dim(jnp.zeros((full_len,), jnp.float32), part, start, 0)


def per_device(
    tokens,
    w_query,
    w_key,
    w_value,
    w_out,
    b_query,
    b_value,
    b_out,
    norm1_gain,
    norm1_shift,
    w_in,
    w_back,
    b_in,
    b_back,
    norm2_gain,
    norm2_shift,
    cotangent,
):
    f32 = jnp.float32
    bf16 = jnp.bfloat16
    score_scale = HEAD_DIM ** (-0.5)
    bq_full, bv_full, bo_full, gain_one, shift_one, bin_full, bback_full, gain_two, shift_two = (
        lax.all_gather(b_query, ("blk", "head"), axis=0, tiled=True),
        lax.all_gather(b_value, ("blk", "head"), axis=0, tiled=True),
        lax.all_gather(b_out, ("blk", "head"), axis=0, tiled=True),
        lax.all_gather(norm1_gain, ("blk", "head"), axis=0, tiled=True),
        lax.all_gather(norm1_shift, ("blk", "head"), axis=0, tiled=True),
        lax.all_gather(b_in, ("blk", "head"), axis=0, tiled=True),
        lax.all_gather(b_back, ("blk", "head"), axis=0, tiled=True),
        lax.all_gather(norm2_gain, ("blk", "head"), axis=0, tiled=True),
        lax.all_gather(norm2_shift, ("blk", "head"), axis=0, tiled=True),
    )
    attn_cols, out_rows, ffn_cols = (
        lax.all_gather(jnp.stack((w_query, w_key, w_value)), "blk", axis=1, tiled=True),
        lax.all_gather(w_out, "blk", axis=1, tiled=True),
        lax.all_gather(jnp.stack((w_in, w_back)), "blk", axis=1, tiled=True),
    )
    seq_count, local_len, model_dim = tokens.shape
    token_shape = (seq_count, local_len, model_dim)
    head_id = lax.axis_index("head")
    width_part = attn_cols.shape[2]
    bq_part = lax.dynamic_slice_in_dim(bq_full, head_id * width_part, width_part).astype(f32)
    bv_part = lax.dynamic_slice_in_dim(bv_full, head_id * width_part, width_part).astype(f32)
    wide_rows = token_rows(tokens)
    wide_len = wide_rows.shape[1]
    wide_flat = wide_rows.reshape(-1, model_dim)
    head_shape = (seq_count, wide_len, width_part)
    wide_shape = (seq_count, wide_len, model_dim)
    query_heads = (
        (jnp.dot(wide_flat, attn_cols[0], preferred_element_type=f32) + bq_part)
        .astype(bf16)
        .reshape(head_shape)
    )
    key_heads = (
        jnp.dot(wide_flat, attn_cols[1], preferred_element_type=f32)
        .astype(bf16)
        .reshape(head_shape)
    )
    value_heads = (
        (jnp.dot(wide_flat, attn_cols[2], preferred_element_type=f32) + bv_part)
        .astype(bf16)
        .reshape(head_shape)
    )
    query4 = split_heads(query_heads)
    key4 = split_heads(key_heads)
    value4 = split_heads(value_heads)
    stat_shape = query4.shape[:3]
    pieces = (
        lax.all_gather(key_heads, "blk", axis=1, tiled=True),
        lax.all_gather(value_heads, "blk", axis=1, tiled=True),
    )
    maxima = jnp.full(stat_shape, -1e30, f32)
    scores = score_block(query4, split_heads(pieces[0]))
    new_max = jnp.maximum(maxima, jnp.max(scores, axis=-1))
    weights = jnp.exp(scores - new_max[..., None])
    totals = jnp.sum(weights, axis=-1)
    summed = jnp.einsum(
        "sqgk,skge->sqge", weights.astype(bf16), split_heads(pieces[1]), preferred_element_type=f32
    )
    maxima, totals, summed = (new_max, totals, summed)
    log_sums = maxima + jnp.log(totals)
    attended4 = summed / totals[..., None]
    attended_heads = attended4.reshape(head_shape).astype(bf16)
    attended_flat = attended_heads.reshape(-1, width_part)
    branch_terms = jnp.dot(attended_flat, out_rows, preferred_element_type=f32).reshape(wide_shape)
    branch = token_partials(branch_terms).reshape(-1, model_dim) + bo_full.astype(f32)
    flat_rows = tokens.reshape(-1, model_dim)
    normed, norm1_pull = jax.vjp(
        layer_norm, flat_rows.astype(f32) + branch, gain_one.astype(f32), shift_one.astype(f32)
    )
    normed_low = normed.astype(bf16)
    ffn_full = lax.all_gather(ffn_cols, "head", axis=2, tiled=True)
    pre_act = jnp.dot(normed_low, ffn_full[0], preferred_element_type=f32) + bin_full.astype(f32)
    hidden_act, gelu_pull = jax.vjp(gelu_exact, pre_act)
    hidden_low = hidden_act.astype(bf16)
    ffn_out = contract_cols(hidden_low, ffn_full[1]) + bback_full.astype(f32)
    final, norm2_pull = jax.vjp(
        layer_norm, normed + ffn_out, gain_two.astype(f32), shift_two.astype(f32)
    )
    output = final.astype(bf16).reshape(token_shape)
    d_second, grad_norm2_gain, grad_norm2_shift = norm2_pull(
        cotangent.reshape(-1, model_dim).astype(f32)
    )
    d_ffn = d_second.astype(bf16)
    grad_b_back = jnp.sum(d_ffn.astype(f32), axis=0)
    grad_back_whole = contract_rows(d_ffn, hidden_low)
    d_hidden = jnp.dot(d_ffn, ffn_full[1], preferred_element_type=f32)
    d_pre = gelu_pull(d_hidden)[0].astype(bf16)
    grad_b_in = jnp.sum(d_pre.astype(f32), axis=0)
    grad_in_whole = contract_rows(normed_low, d_pre)
    ffn_grad_parts = lax.psum_scatter(
        jnp.stack((grad_in_whole, grad_back_whole)).astype(jnp.bfloat16),
        "head",
        scatter_dimension=2,
        tiled=True,
    ).astype(jnp.float32)
    d_normed = d_second + contract_cols(d_pre, ffn_full[0])
    d_first, grad_norm1_gain, grad_norm1_shift = norm1_pull(d_normed)
    d_branch = d_first.astype(bf16)
    grad_b_out = jnp.sum(d_branch.astype(f32), axis=0)
    wide_dbranch = token_rows(d_branch.reshape(token_shape)).reshape(-1, model_dim)
    grad_out_part = contract_rows(attended_flat, wide_dbranch)
    grad_heads = contract_cols(wide_dbranch, out_rows).astype(bf16).reshape(head_shape)
    grads4 = split_heads(grad_heads)
    deltas = jnp.sum(grads4.astype(f32) * attended4, axis=-1)
    row_stats = (
        lax.all_gather(log_sums, "blk", axis=1, tiled=True),
        lax.all_gather(deltas, "blk", axis=1, tiled=True),
    )
    pieces = (
        lax.all_gather(key_heads, "blk", axis=1, tiled=True),
        lax.all_gather(value_heads, "blk", axis=1, tiled=True),
        lax.all_gather(query_heads, "blk", axis=1, tiled=True),
        lax.all_gather(grad_heads, "blk", axis=1, tiled=True),
    )
    piece_keys = split_heads(pieces[0])
    piece_values = split_heads(pieces[1])
    piece_queries = split_heads(pieces[2])
    piece_grads = split_heads(pieces[3])
    piece_sums = row_stats[0]
    piece_deltas = row_stats[1]
    own_probs, own_scores = score_grads(query4, piece_keys, piece_values, grads4, log_sums, deltas)
    d_query = score_scale * jnp.einsum(
        "sqgk,skge->sqge", own_scores, piece_keys, preferred_element_type=f32
    )
    probs_low, d_scores = score_grads(
        piece_queries, key4, value4, piece_grads, piece_sums, piece_deltas
    )
    key_acc = score_scale * jnp.einsum(
        "sqgk,sqge->skge", d_scores, piece_queries, preferred_element_type=f32
    )
    value_acc = jnp.einsum("sqgk,sqge->skge", probs_low, piece_grads, preferred_element_type=f32)
    d_query_low = d_query.reshape(-1, width_part).astype(bf16)
    d_key_low = key_acc.reshape(-1, width_part).astype(bf16)
    d_value_low = value_acc.reshape(-1, width_part).astype(bf16)
    grad_b_query = place_part(
        jnp.sum(d_query_low.astype(f32), axis=0), model_dim, head_id * width_part
    )
    grad_b_value = place_part(
        jnp.sum(d_value_low.astype(f32), axis=0), model_dim, head_id * width_part
    )
    attn_grad_parts = jnp.stack(
        (
            contract_rows(wide_flat, d_query_low),
            contract_rows(wide_flat, d_key_low),
            contract_rows(wide_flat, d_value_low),
        )
    )
    token_terms = (
        contract_cols(d_query_low, attn_cols[0])
        + contract_cols(d_key_low, attn_cols[1])
        + contract_cols(d_value_low, attn_cols[2])
    )
    d_tokens = d_first + token_partials(token_terms.reshape(wide_shape)).reshape(-1, model_dim)
    grad_tokens = d_tokens.astype(bf16).reshape(token_shape)
    attn_sums, grad_w_out, ffn_sums = (
        lax.psum_scatter(attn_grad_parts, "blk", scatter_dimension=1, tiled=True),
        lax.psum_scatter(grad_out_part, "blk", scatter_dimension=1, tiled=True),
        lax.psum_scatter(ffn_grad_parts, "blk", scatter_dimension=1, tiled=True),
    )
    (
        grad_b_query,
        grad_b_value,
        grad_b_out,
        grad_norm1_gain,
        grad_norm1_shift,
        grad_b_in,
        grad_b_back,
        grad_norm2_gain,
        grad_norm2_shift,
    ) = (
        lax.psum_scatter(grad_b_query, ("blk", "head"), scatter_dimension=0, tiled=True),
        lax.psum_scatter(grad_b_value, ("blk", "head"), scatter_dimension=0, tiled=True),
        lax.psum_scatter(grad_b_out, ("blk", "head"), scatter_dimension=0, tiled=True),
        lax.psum_scatter(grad_norm1_gain, ("blk", "head"), scatter_dimension=0, tiled=True),
        lax.psum_scatter(grad_norm1_shift, ("blk", "head"), scatter_dimension=0, tiled=True),
        lax.psum_scatter(grad_b_in, ("blk", "head"), scatter_dimension=0, tiled=True),
        lax.psum_scatter(grad_b_back, ("blk", "head"), scatter_dimension=0, tiled=True),
        lax.psum_scatter(grad_norm2_gain, ("blk", "head"), scatter_dimension=0, tiled=True),
        lax.psum_scatter(grad_norm2_shift, ("blk", "head"), scatter_dimension=0, tiled=True),
    )
    return (
        output,
        grad_tokens,
        attn_sums[0],
        attn_sums[1],
        attn_sums[2],
        grad_w_out,
        grad_b_query,
        grad_b_value,
        grad_b_out,
        grad_norm1_gain,
        grad_norm1_shift,
        ffn_sums[0],
        ffn_sums[1],
        grad_b_in,
        grad_b_back,
        grad_norm2_gain,
        grad_norm2_shift,
    )


MESH = pl.DeviceIdType.MESH
F32 = jnp.float32
BF16 = jnp.bfloat16
VMEM_LIMIT = 62 * 2**20


def dot_nn(left, right):
    return jnp.dot(left, right, preferred_element_type=F32)


class Place:
    def __init__(self):
        self.b = lax.axis_index("blk")
        self.z = lax.axis_index("head")
        self.y = self.b // 4
        self.x = (self.b // 2) % 2
        self.c = self.b % 2
        self.q = self.b // 2

    def chip(self, r):
        return ((self.y + r // 2) % 2) * 2 + (self.x + r % 2) % 2

    def peer(self, r):
        return (2 * self.chip(r) + self.c, self.z)

    def sibling(self):
        return (2 * self.q + 1 - self.c, self.z)


def remote(src, dst, send_sem, recv_sem, device):
    return pltpu.make_async_remote_copy(
        src_ref=src,
        dst_ref=dst,
        send_sem=send_sem,
        recv_sem=recv_sem,
        device_id=device,
        device_id_type=MESH,
    )


def wait_bytes(view, sem):
    pltpu.make_async_copy(view, view, sem).wait()


def greet_all(at):
    barrier = pltpu.get_barrier_semaphore()
    flat = at.b * 4 + at.z

    def greet(step, carry):
        other = (flat + step) % 32
        pl.semaphore_signal(
            barrier, inc=1, device_id=(other // 4, other % 4), device_id_type=MESH
        )
        return carry

    lax.fori_loop(1, 32, greet, 0)
    pl.semaphore_wait(barrier, 31)


def half(core):
    return pl.ds(pl.multiple_of(core * 128, 128), 128)


def lanes(index):
    return pl.ds(pl.multiple_of(index * 128, 128), 128)


def by_rows(count, size, step):
    def body(i, carry):
        step(pl.ds(pl.multiple_of(i * size, size), size))
        return carry

    lax.fori_loop(0, count // size, body, 0)


class Spread:
    def __init__(self, at, block, part, send, recv):
        self.at, self.block, self.part = at, block, part
        self.send, self.recv = send, recv

    def start(self):
        mine = self.block(0)
        for i in (0, 1):
            for r, k in ((1, i), (2, 1 - i)):
                piece = self.part(mine, k)
                remote(piece, piece, self.send, self.recv.at[r, k], self.at.peer(r)).start()

    def relay(self):
        for r, k in ((1, 0), (2, 1)):
            piece = self.part(self.block(r), k)
            wait_bytes(piece, self.recv.at[r, k])
            remote(piece, piece, self.send, self.recv.at[0, k], self.at.peer(3 - r)).start()

    def rest(self, r):
        block = self.block(r)
        for row, k in {1: ((1, 1),), 2: ((2, 0),), 3: ((0, 0), (0, 1))}[r]:
            wait_bytes(self.part(block, k), self.recv.at[row, k])


def part_rows(h, core):
    return pl.ds(pl.multiple_of(h * 128 + core * 64, 64), 64)


class Gather:
    def __init__(self, at, slots, h, send, recv, recv_sib):
        self.at, self.slots, self.h = at, slots, h
        self.send, self.recv_sib = send, recv_sib

        def part(block, k):
            return block.at[pl.ds(k * 32, 32)]

        self.spread = Spread(
            at, lambda r: slots.at[at.chip(r), part_rows(h, at.c)], part, send, recv
        )

    def to_sibling(self, r):
        block = self.spread.block(r)
        remote(block, block, self.send, self.recv_sib.at[r], self.at.sibling()).start()

    def start(self):
        self.spread.start()
        self.to_sibling(0)

    def relay(self):
        self.spread.relay()

    def forward(self, r):
        self.spread.rest(r)
        self.to_sibling(r)

    def ready(self, r):
        at = self.at
        wait_bytes(self.slots.at[at.chip(r), part_rows(self.h, 1 - at.c)], self.recv_sib.at[r])
        return at.chip(r)


class Exchange:
    def __init__(self, at, buffers, rows, send, recv, recv_sib):
        self.at, self.send, self.recv, self.recv_sib = at, send, recv, recv_sib
        self.sib_out, self.sib_in, self.out, self.into = buffers
        self.rows = rows

    def put(self, r, theirs):
        mine = self.sib_out.at[r, self.rows]
        mine[...] = theirs.astype(BF16)
        remote(
            mine,
            self.sib_in.at[r, self.rows],
            self.send,
            self.recv_sib.at[r],
            self.at.sibling(),
        ).start()

    def add(self, r, mine):
        wait_bytes(self.sib_in.at[r, self.rows], self.recv_sib.at[r])
        total = mine + self.sib_in[r, self.rows].astype(F32)
        if r == 0:
            return total
        self.out[r, self.rows] = total.astype(BF16)
        if r == 3:
            for k in range(2):
                self.pass_half(3, k, 3, self.recv.at[3 * k], k + 1)
        else:
            self.pass_half(r, r - 1, r, self.recv.at[r], r)

    def half(self, k):
        size = self.rows.size // 2
        return pl.ds(self.rows.start + size * k, size)

    def pass_half(self, r, k, slot, recv, peer):
        rows = self.half(k)
        remote(
            self.out.at[r, rows], self.into.at[slot, rows], self.send, recv, self.at.peer(peer)
        ).start()

    def relay(self):
        for k in range(2):
            rows, r = self.half(k), 2 - k
            wait_bytes(self.into.at[3, rows], self.recv.at[3 * k])
            self.out[r, rows] = (
                self.out[r, rows].astype(F32) + self.into[3, rows].astype(F32)
            ).astype(BF16)
            self.pass_half(r, k, r, self.recv.at[r], r)

    def arrive(self):
        for r in (1, 2):
            wait_bytes(self.into.at[r, self.rows], self.recv.at[r])


def norm_rows(values):
    centre = jnp.mean(values, axis=-1, keepdims=True)
    centred = values - centre
    spread = jnp.mean(centred * centred, axis=-1, keepdims=True)
    scale = lax.rsqrt(spread + NORM_EPS)
    return centred * scale, scale


def norm_back(grad, unit, scale):
    centre = jnp.mean(grad, axis=-1, keepdims=True)
    along = jnp.mean(grad * unit, axis=-1, keepdims=True)
    return (grad - centre - unit * along) * scale


def send_or_copy(src, dst, send_sem, recv_sem, device, own):
    def away():
        remote(src, dst, send_sem, recv_sem, device).start()

    if own is None:
        away()
        return
    pl.when(jnp.logical_not(own))(away)

    @pl.when(own)
    def _():
        pltpu.make_async_copy(src, dst, recv_sem).start()


class Column:
    def __init__(self, at, ref, rows, sems):
        self.at, self.ref, self.rows = at, ref, rows
        self.up_send, self.up_recv, self.down_send, self.down_recv = sems

    def block(self, plane):
        return self.ref.at[self.rows, lanes(plane)]

    def sides(self, hop, act, arriving):
        z = self.at.z
        if arriving:
            below, above = z - 1 - hop, z + 1 + hop
            pl.when(below >= 0)(lambda: act(self.block(below), 0))
            pl.when(above <= 3)(lambda: act(self.block(above), 1))
        else:
            up = jnp.logical_and(z >= hop, z < 3)
            down = jnp.logical_and(z + hop <= 3, z > 0)
            pl.when(up)(lambda: act(self.block(z - hop), 0))
            pl.when(down)(lambda: act(self.block(z + hop), 1))

    def send(self, hop):
        def act(block, side):
            send = (self.up_send, self.down_send)[side].at[hop]
            recv = (self.up_recv, self.down_recv)[side].at[hop]
            remote(block, block, send, recv, (self.at.b, self.at.z + 1 - 2 * side)).start()

        self.sides(hop, act, False)

    def arrive(self, hop):
        def act(block, side):
            wait_bytes(block, (self.up_recv, self.down_recv)[side].at[hop])

        self.sides(hop, act, True)

    def end(self):
        def wait(hop):
            def act(block, side):
                wait_bytes(block, (self.up_send, self.down_send)[side].at[hop])

            return act

        for hop in range(3):
            self.sides(hop, wait(hop), False)


def plane_weights(at, src, dst, send_sem, recv_sem):
    rows, cols = lanes(at.b), lanes(at.z)
    pltpu.make_async_copy(src.at[:, lanes(at.b)], dst.at[rows, cols], recv_sem).start()

    def push(step, carry):
        other = (at.b + step) % 8
        remote(
            src.at[:, lanes(other)], dst.at[rows, cols], send_sem, recv_sem, (other, at.z)
        ).start()
        return carry

    lax.fori_loop(1, 8, push, 0)


class ColumnSum:
    def __init__(self, at, blocks, passing, send, recv):
        self.at, self.blocks, self.passing = at, blocks, passing
        self.send_sem, self.recv_sem = send, recv

    def plane(self, side, i):
        return i if side else 3 - i

    def hop(self, side):
        return 3 - self.at.z if side else self.at.z

    def next(self, side):
        return (self.at.b, self.at.z + 1 - 2 * side)

    def begin(self, which):
        for side in range(2):

            @pl.when(self.hop(side) == 0)
            def _(side=side):
                for i in which:
                    remote(
                        self.blocks.at[:, :, pl.ds(128 * self.plane(side, i), 128)],
                        self.passing.at[side, i],
                        self.send_sem.at[side, i],
                        self.recv_sem.at[side, i],
                        self.next(side),
                    ).start()

    def relay(self, hop, i):
        for side in range(2):

            @pl.when(self.hop(side) == hop)
            def _(side=side):
                held = self.passing.at[side, i]
                wait_bytes(held, self.recv_sem.at[side, i])
                cols = pl.ds(128 * self.plane(side, i), 128)
                for b in range(8):
                    self.passing[side, i, b] = (
                        self.passing[side, i, b].astype(F32)
                        + self.blocks[b, :, cols].astype(F32)
                    ).astype(BF16)
                remote(
                    held,
                    held,
                    self.send_sem.at[side, i],
                    self.recv_sem.at[side, i],
                    self.next(side),
                ).start()

    def finish(self, sums, final, send_out, recv_out):
        at = self.at
        own = lanes(at.z)
        for b in range(8):
            sums[b] = self.blocks[b, :, own]
        for side in range(2):
            for hop in range(1, 4):
                i = 3 - hop

                @pl.when(self.hop(side) == hop)
                def _(side=side, i=i):
                    wait_bytes(self.passing.at[side, i], self.recv_sem.at[side, i])
                    for b in range(8):
                        sums[b] = (
                            sums[b].astype(F32) + self.passing[side, i, b].astype(F32)
                        ).astype(BF16)

        def one(step, carry):
            other = (at.b + 1 + step) % 8
            send_or_copy(
                sums.at[other],
                final.at[:, lanes(at.b)],
                send_out,
                recv_out,
                (other, at.z),
                step == 7,
            )
            return carry

        lax.fori_loop(0, 8, one, 0)

    def end(self):
        for side in range(2):
            for i in range(3):

                @pl.when(self.hop(side) < 3 - i)
                def _(side=side, i=i):
                    wait_bytes(self.passing.at[side, i], self.send_sem.at[side, i])


def head_mask(h):
    lane = lax.broadcasted_iota(jnp.int32, (1, 128), 1)
    return jnp.where(lane // HEAD_DIM == h, 1.0, 0.0).astype(F32)


def slot_rows(index):
    return pl.ds(pl.multiple_of(index * 64, 64), 64)


def chip_rows(index):
    return pl.ds(pl.multiple_of(index * 256, 256), 256)


def core_rows(index):
    return pl.ds(pl.multiple_of(index * 1024, 1024), 1024)


class Inputs:
    small = x_hbm = cot_hbm = wq = wk = wv = wout = win = wback = None


def entries(table):
    return [(n, e) for n, e in vars(table).items() if n[0] != "_"]


class Results:
    out = ((128, 1024), BF16)
    gtok = ((128, 1024), BF16)
    w_in = ((2, 2, 128, 384), BF16)
    o_in = ((4, 128, 256), BF16)
    fin_in = ((128, 1024), BF16)
    fin_back = ((128, 1024), BF16)
    notes_in = ((4, 16, 128), F32)


class Scratch:
    small_here = ((16, 128), BF16)
    out_here = ((128, 1024), BF16)
    gtok_here = ((128, 1024), BF16)
    x = ((128, 1024), BF16)
    cot = ((128, 1024), BF16)
    xs = ((1024, 1024), BF16)
    wqkv = ((1024, 384), BF16)
    w_near = ((3, 128, 256), BF16)
    queries = ((1024, 128), BF16)
    keys_all = ((2048, 128), BF16)
    values_all = ((2048, 128), BF16)
    mixed = ((1024, 128), F32)
    log_sums = ((1024, 128), F32)
    att = ((128, 1024), BF16)
    wo = ((1024, 1024), BF16)
    par = ((8, 1024), F32)
    bins = ((1, 512), F32)
    wi = ((1024, 512), BF16)
    wb = ((1024, 512), BF16)
    smalls = ((8, 16, 128), BF16)
    smalls_z = ((4, 16, 128), BF16)
    smalls_sum = ((16, 128), BF16)
    proj = ((256, 384), F32)
    scores = ((256, 2048), F32)
    d_buf = ((256, 2048), F32)
    p_buf = ((256, 2048), BF16)
    att_send = ((1024, 128), BF16)
    n1 = ((128, 1024), F32)
    unit1 = ((128, 1024), F32)
    scale1 = ((128, 128), F32)
    d2 = ((128, 1024), F32)
    d1 = ((128, 1024), F32)
    db = ((128, 1024), BF16)
    norm_slots = ((4, 256, 1024), BF16)
    grad_slots = ((4, 256, 1024), BF16)
    hid = ((4, 256, 512), BF16)
    slope = ((4, 256, 512), F32)
    low = ((4, 256, 512), BF16)
    pre = ((128, 512), F32)
    terms = ((4, 256, 1024), F32)
    sib_out = ((2, 4, 128, 1024), BF16)
    sib_in = ((2, 4, 128, 1024), BF16)
    peer_out = ((2, 4, 128, 1024), BF16)
    peer_in = ((2, 4, 128, 1024), BF16)
    g_back = ((8, 128, 512), BF16)
    g_in = ((8, 128, 512), BF16)
    pass_back = ((2, 3, 8, 128, 128), BF16)
    pass_in = ((2, 3, 8, 128, 128), BF16)
    gs_back = ((8, 128, 128), BF16)
    gs_in = ((8, 128, 128), BF16)
    da_send = ((128, 1024), BF16)
    da = ((1024, 128), BF16)
    q_turned = ((128, 1024), BF16)
    da_turned = ((128, 1024), BF16)
    dq = ((1024, 128), F32)
    dk_turned = ((128, 2048), F32)
    dv_turned = ((128, 2048), F32)
    out_k = ((1024, 128), F32)
    out_v = ((1024, 128), F32)
    sib_k = ((1024, 128), F32)
    sib_v = ((1024, 128), F32)
    dqkv = ((1024, 384), BF16)
    x_sum = ((256, 1024), F32)
    x_own = ((64, 1024), F32)
    z_out = ((4, 64, 1024), BF16)
    z_in = ((4, 64, 1024), BF16)
    w_sib_out = ((4, 128, 384), F32)
    w_sib_in = ((4, 128, 384), F32)
    w_out = ((4, 128, 384), BF16)
    o_out = ((128, 1024), BF16)
    vec = ((8, 1024), F32)
    gbin = ((1, 512), F32)
    notes = ((8, 16, 128), F32)
    notes_p = ((8, 16, 128), F32)
    notes_sum = ((16, 128), F32)


class Arrivals:
    z = (4,)
    p = (4, 3, 2)
    wo = (3, 2)
    w = (3,)
    o = (5,)
    kv = (1,)
    misc = (12,)
    col = (6, 3)
    ga = (4, 3, 2)
    ga_sib = (4, 4)
    ex = (5, 4)
    ex_sib = (5, 4)
    zg = (2, 2, 3)
    kv2 = (2,)
    dx = (4, 3, 2)
    dz = (4,)
    ws = (4,)
    da = (4,)
    own = (4,)


class Departures:
    z = (1,)
    p = (1,)
    wo = (1,)
    w = (3,)
    o = (1,)
    kv = (1,)
    misc = (12,)
    col = (6, 3)
    ga = (2,)
    ex = (3,)
    zg = (2, 2, 3)
    kv2 = (1,)
    dx = (1,)
    dz = (1,)
    ws = (1,)


class Refs:
    pass


def layer_kernel(*refs):
    v = Refs()
    names = [n for table in (Inputs, Results, Scratch) for n, _ in entries(table)]
    names += ["r_" + n for n, _ in entries(Arrivals)] + ["s_" + n for n, _ in entries(Departures)]
    for name, ref in zip(names, refs):
        setattr(v, name, ref)
    at = Place()
    at.flat = at.b * 4 + at.z
    at.place = at.q * 4 + at.z
    at.parity = at.z % 2
    at.pair = 4 * (at.z // 2) + at.q
    def column(ref, rows, i):
        sems = [t.at[2 * i + k] for k in range(2) for t in (v.s_col, v.r_col)]
        return Column(at, ref, rows, sems)

    col_in = column(v.wi, pl.ds(0, 1024), 0)
    col_back = [column(v.wb, pl.ds(512 * k, 512), 1 + k) for k in range(2)]
    gathers = [
        [
            Gather(at, slots, h, v.s_ga.at[i], v.r_ga.at[2 * i + h], v.r_ga_sib.at[2 * i + h])
            for h in range(2)
        ]
        for i, slots in enumerate((v.norm_slots, v.grad_slots))
    ]

    def exchange(i, side, rows):
        buffers = [t.at[side] for t in (v.sib_out, v.sib_in, v.peer_out, v.peer_in)]
        return Exchange(at, buffers, rows, v.s_ex.at[i // 2], v.r_ex.at[i], v.r_ex_sib.at[i])

    scatters = [
        [exchange(2 * i + h, i, pl.ds(64 * h, 64)) for h in range(2)] for i in range(2)
    ]
    out_scatter = exchange(4, 0, pl.ds(0, 128))
    upper = at.z // 2
    at.planes = (at.z, at.z + 1 - 2 * at.parity, 2 - upper, 3 - 3 * upper)
    rows_spread = [
        Spread(
            at,
            lambda r, plane=plane: v.xs.at[slot_rows(at.chip(r) * 4 + plane)],
            lambda block, k: block.at[pl.ds(k * 32, 32)],
            v.s_p.at[0],
            v.r_p.at[i],
        )
        for i, plane in enumerate(at.planes)
    ]
    wo_spread = Spread(
        at,
        lambda r: v.wo.at[:, lanes(2 * at.chip(r) + at.c)],
        lambda block, k: block.at[pl.ds(k * 512, 512)],
        v.s_wo.at[0],
        v.r_wo,
    )
    sum_in = ColumnSum(at, v.g_in, v.pass_in, v.s_zg.at[0], v.r_zg.at[0])
    sum_back = ColumnSum(at, v.g_back, v.pass_back, v.s_zg.at[1], v.r_zg.at[1])
    place_small(at, v)
    pltpu.make_async_copy(v.x_hbm, v.x, v.r_own.at[0]).start()
    pltpu.make_async_copy(v.cot_hbm, v.cot, v.r_own.at[1]).start()
    greet_all(at)
    wait_bytes(v.x, v.r_own.at[0])
    attend_phase(at, v, col_in, col_back, rows_spread, wo_spread)
    ffn_phase(at, v, col_in, col_back, gathers, scatters, sum_back, sum_in)
    grads_phase(at, v, out_scatter, sum_in, sum_back)
    end_phase(at, v, (sum_in, sum_back, col_in, *col_back))


def place_small(at, v):
    def iota(shape, axis):
        return lax.broadcasted_iota(jnp.int32, shape, axis)

    spread = jnp.where(
        iota((8, 256), 1) // 32 == iota((8, 256), 0), v.small[0:1, 0:256], 0.0
    ).astype(BF16)
    lane = iota((256, 128), 1)
    source = iota((256, 128), 0) % 32 + 32 * at.z
    picked = jnp.where(lane == source, 1.0, 0.0).astype(BF16)
    top = dot_nn(spread, picked)
    units = jnp.where(iota((8, 128), 0) == at.z, v.small[0:1, 256:384], 0.0)
    v.small_here[...] = jnp.concatenate((top, units), axis=0).astype(BF16)


def attend_phase(at, v, col_in, col_back, rows_spread, wo_spread):
    xs, wqkv, wo = v.xs, v.wqkv, v.wo
    parity, pair = at.parity, at.pair

    pltpu.make_async_copy(v.small_here, v.smalls_z.at[at.z], v.r_misc.at[1]).start()
    for dz in range(1, 4):
        remote(
            v.small_here,
            v.smalls_z.at[at.z],
            v.s_misc.at[1],
            v.r_misc.at[1],
            (at.b, (at.z + dz) % 4),
        ).start()

    pltpu.make_async_copy(
        v.x.at[slot_rows(parity)], xs.at[slot_rows(at.place)], v.r_z.at[at.z]
    ).start()
    weights = (v.wq, v.wk, v.wv)
    for i in (1, 2, 3):
        plane = at.planes[i]
        remote(
            v.x.at[slot_rows(plane % 2)],
            xs.at[slot_rows(at.place)],
            v.s_z.at[0],
            v.r_z.at[at.z],
            (at.b, plane),
        ).start()
        if i == 1:
            for k, w in enumerate(weights):
                remote(
                    w, v.w_near.at[k], v.s_w.at[2], v.r_w.at[2], (at.b, at.planes[1])
                ).start()

    part = wo.at[pl.ds(pl.multiple_of(at.z * 256, 256), 256), lanes(at.b)]
    pltpu.make_async_copy(v.wout, part, v.r_o.at[4]).start()
    for i in (1, 2, 3):
        remote(v.wout, part, v.s_o.at[0], v.r_o.at[4], (at.b, at.planes[i])).start()

    def to_pairs(sources, group):
        for dx in range(2):
            column = (at.x + dx) % 2
            for k, w in enumerate(sources):
                send_or_copy(
                    w.at[:, lanes(column)],
                    wqkv.at[lanes(at.b), pl.ds(k * 128, 128)],
                    v.s_w.at[0],
                    v.r_w.at[0],
                    (2 * (group * 2 + column) + at.c, at.z),
                    None if dx else group == at.y,
                )

    for i in range(4):
        wait_bytes(rows_spread[i].block(0), v.r_z.at[at.planes[i]])
        rows_spread[i].start()
        if i == 0:
            to_pairs(weights, parity)
            wait_bytes(v.smalls_z, v.r_misc.at[1])
            total = v.smalls_z[0].astype(F32)
            for z in range(1, 4):
                total += v.smalls_z[z].astype(F32)
            v.smalls_sum[...] = total.astype(BF16)
            mine = v.smalls.at[at.b]
            pltpu.make_async_copy(v.smalls_sum, mine, v.r_misc.at[10]).start()

            def spread(step, carry):
                remote(
                    v.smalls_sum,
                    mine,
                    v.s_misc.at[10],
                    v.r_misc.at[10],
                    ((at.b + step) % 8, at.z),
                ).start()
                return carry

            lax.fori_loop(1, 8, spread, 0)
        if i == 1:
            plane_weights(at, v.win, v.wi, v.s_misc.at[0], v.r_misc.at[0])
            wait_bytes(v.w_near, v.r_w.at[2])
            to_pairs([v.w_near.at[k] for k in range(3)], 1 - parity)
        if i:
            rows_spread[i - 1].relay()
    wait_bytes(v.wi.at[:, pl.ds(0, 128)], v.r_misc.at[0])
    col_in.send(0)

    wait_bytes(wqkv.at[pl.ds(0, 512)], v.r_w.at[0])
    for r in range(4):
        part = wqkv.at[lanes(2 * at.chip(r) + at.c)]
        remote(part, part, v.s_w.at[1], v.r_w.at[1], at.sibling()).start()
    wait_bytes(v.smalls, v.r_misc.at[10])
    for b in range(8):
        v.par[:, 128 * b : 128 * b + 128] = v.smalls[b].astype(F32)[0:8]
    row = lax.broadcasted_iota(jnp.int32, (8, 128), 0)
    for h in range(4):
        rows = v.smalls[2 * h + at.b // 4].astype(F32)[8:16]
        rows = jnp.where(row == at.b % 4, rows, 0.0)
        v.bins[0:1, 128 * h : 128 * h + 128] = jnp.sum(rows, axis=0, keepdims=True)
    bias_q = v.par[0:1, lanes(pair)]
    bias_v = v.par[1:2, lanes(pair)]
    wait_bytes(wqkv.at[pl.ds(0, 512)], v.r_w.at[1])

    def project(r):
        chip = at.chip(r)
        if r:
            for i in range(4):
                rows_spread[i].rest(r)
        rows = chip_rows(chip)
        v.proj[...] = dot_nn(xs[rows], wqkv[...])
        v.queries[rows] = (v.proj[:, 0:128] + bias_q).astype(BF16)
        own_rows = chip_rows(at.c * 4 + chip)
        v.keys_all[own_rows] = v.proj[:, 128:256].astype(BF16)
        v.values_all[own_rows] = (v.proj[:, 256:384] + bias_v).astype(BF16)
        for k, ref in enumerate((v.keys_all, v.values_all)):
            view = ref.at[own_rows]
            remote(view, view, v.s_kv.at[0], v.r_kv.at[0], at.sibling()).start()

    project(0)
    rows_spread[3].relay()

    whole = wo_spread.block(0)
    wait_bytes(whole, v.r_o.at[4])
    wo_spread.start()
    remote(whole, whole, v.s_o.at[0], v.r_o.at[0], at.sibling()).start()
    plane_weights(at, v.wback, v.wb, v.s_misc.at[2], v.r_misc.at[2])

    for r in (1, 2, 3):
        project(r)

    wait_bytes(v.keys_all, v.r_kv.at[0])

    col_in.arrive(0)
    col_in.send(1)
    scores = v.scores

    def attend(step, carry):
        chip = (at.q + 1 + step) % 4
        rows = chip_rows(chip)
        outs = []
        logs = []
        for h in range(2):
            q = (v.queries[rows].astype(F32) * head_mask(h) * HEAD_DIM**-0.5).astype(BF16)
            scores[...] = contract_cols(q, v.keys_all[...])
            top = jnp.max(scores[...], axis=-1, keepdims=True)
            weights = jnp.exp(scores[...] - top)
            total = jnp.sum(weights, axis=-1, keepdims=True)
            outs.append(dot_nn(weights.astype(BF16), v.values_all[...]) / total)
            logs.append(top + jnp.log(total))
        first = head_mask(0) > 0.5
        merged = jnp.where(first, outs[0], outs[1])
        v.mixed[rows] = merged
        v.log_sums[rows] = jnp.where(first, logs[0], logs[1])
        v.att_send[rows] = merged.astype(BF16)
        for k in range(4):
            plane = (at.z + 1 + k) % 4
            send_or_copy(
                v.att_send.at[slot_rows(chip * 4 + plane)],
                v.att.at[slot_rows(parity), lanes(pair)],
                v.s_misc.at[3],
                v.r_misc.at[3],
                (2 * chip + at.c, plane),
                step == 3 if k == 3 else None,
            )

        @pl.when(step == 0)
        def _():
            wo_spread.relay()

        @pl.when(step == 2)
        def _():
            col_in.arrive(1)
            col_in.send(2)

        return carry

    lax.fori_loop(0, 4, attend, 0)

    wait_bytes(v.wb.at[:, pl.ds(0, 128)], v.r_misc.at[2])
    for half_back in col_back:
        half_back.send(0)
    for r in (1, 2, 3):
        wo_spread.rest(r)
        part = wo_spread.block(r)
        remote(part, part, v.s_o.at[0], v.r_o.at[r], at.sibling()).start()
    for r in range(4):
        wait_bytes(whole, v.r_o.at[r])
    wait_bytes(v.att, v.r_misc.at[3])


def ffn_phase(at, v, col_in, col_back, gathers, scatters, sum_back, sum_in):
    n1, terms, peer_in = v.n1, v.terms, v.peer_in

    def param(i):
        return v.par[i : i + 1, :]

    def local(h, i):
        return pl.ds(64 * h + 32 * i, 32)

    def chip_part(h, i):
        return pl.ds(pl.multiple_of(h * 128 + at.c * 64 + 32 * i, 32), 32)

    wait_bytes(v.cot, v.r_own.at[1])
    n1[...] = dot_nn(v.att[...], v.wo[...])
    for h in range(2):
        for i in range(2):
            rows = local(h, i)
            unit, scale = norm_rows(v.x[rows].astype(F32) + n1[rows] + param(2))
            v.unit1[rows] = unit
            v.scale1[rows] = jnp.broadcast_to(scale, (32, 128))
            normed = unit * param(3) + param(4)
            n1[rows] = normed
            v.norm_slots[at.q, chip_part(h, i)] = normed.astype(BF16)
        gathers[0][h].start()

    def hidden(h, r):
        chip = gathers[0][h].ready(r)
        v.pre[...] = dot_nn(v.norm_slots[chip, pl.ds(128 * h, 128)], v.wi[...])

        def activate(i, carry):
            rows = pl.ds(pl.multiple_of(i * 32, 32), 32)
            into = pl.ds(pl.multiple_of(128 * h + i * 32, 32), 32)
            u = v.pre[rows] + v.bins[...]
            cdf = 0.5 * (1.0 + lax.erf(u * math.sqrt(0.5)))
            bell = jnp.exp(-0.5 * u * u) * (1.0 / math.sqrt(2.0 * math.pi))
            v.hid[r, into] = (u * cdf).astype(BF16)
            v.slope[r, into] = cdf + u * bell
            return carry

        lax.fori_loop(0, 4, activate, 0)

    def neighbours(gather):
        gather.relay()
        gather.forward(1)
        gather.forward(2)

    neighbours(gathers[0][0])
    gathers[0][1].relay()
    col_back[0].arrive(0)
    col_back[0].send(1)
    col_in.arrive(2)
    hidden(0, 0)
    gathers[0][1].forward(1)
    gathers[0][1].forward(2)
    col_back[1].arrive(0)
    col_back[1].send(1)
    hidden(1, 0)
    hidden(0, 1)
    hidden(0, 2)
    gathers[0][0].forward(3)
    hidden(1, 1)
    gathers[0][1].forward(3)
    hidden(1, 2)
    col_back[0].arrive(1)
    col_back[0].send(2)
    hidden(0, 3)
    hidden(1, 3)
    col_back[1].arrive(1)
    col_back[1].send(2)
    for half_back in col_back:
        half_back.arrive(2)

    def to_plane(scatter, done, h, r, product):
        terms[r, pl.ds(128 * h, 128)] = product
        scatter[h].put(r, terms[r, part_rows(h, 1 - at.c)])
        done.append((h, r))
        if len(done) > 3:
            pass_on(scatter, *done[-4])

    def pass_on(scatter, h, r):
        total = scatter[h].add(r, terms[r, part_rows(h, at.c)])
        if r == 0:
            terms[0, part_rows(h, at.c)] = total

    done = []
    for h in range(2):
        for r in (3, 1, 2, 0):
            product = contract_cols(v.hid[r, pl.ds(128 * h, 128)], v.wb[...])
            to_plane(scatters[0], done, h, r, product)
    for one in done[-3:]:
        pass_on(scatters[0], *one)
    for h in range(2):
        scatters[0][h].relay()

    def peers(side, rows):
        return peer_in[side, 1, rows].astype(F32) + peer_in[side, 2, rows].astype(F32)

    def column_sums(parts, sums):
        return tuple(
            kept + jnp.sum(part.reshape(4, 8, 1024), axis=0) for kept, part in zip(sums, parts)
        )

    gbin = [jnp.zeros((8, 512), F32)]
    done = []

    def hidden_grad(h, r):
        chip = gathers[1][h].ready(r)
        v.pre[...] = dot_nn(v.grad_slots[chip, pl.ds(128 * h, 128)], v.wb[...])

        def deactivate(i, carry):
            rows = pl.ds(pl.multiple_of(i * 32, 32), 32)
            into = pl.ds(pl.multiple_of(128 * h + i * 32, 32), 32)
            low = (v.pre[rows] * v.slope[r, into]).astype(BF16)
            v.low[r, into] = low
            return carry + jnp.sum(low.astype(F32).reshape(4, 8, 512), axis=0)

        gbin[0] = lax.fori_loop(0, 4, deactivate, gbin[0])
        product = contract_cols(v.low[r, pl.ds(128 * h, 128)], v.wi[...])
        to_plane(scatters[1], done, h, r, product)

    sums = tuple(jnp.zeros((8, 1024), F32) for _ in range(3))
    for h in range(2):
        scatters[0][h].arrive()
        for i in range(2):
            rows = local(h, i)
            total = terms[0, chip_part(h, i)] + peers(0, rows)
            unit, scale = norm_rows(n1[rows] + total + param(5))
            v.out_here[rows] = (unit * param(6) + param(7)).astype(BF16)
            g = v.cot[rows].astype(F32)
            d = norm_back(g * param(6), unit, scale)
            v.d2[rows] = d
            low = d.astype(BF16)
            v.grad_slots[at.q, chip_part(h, i)] = low
            sums = column_sums((g * unit, g, low.astype(F32)), sums)
        gathers[1][h].start()
        if h == 0:
            hidden_grad(0, 0)
    pltpu.make_async_copy(v.out_here, v.out, v.r_own.at[2]).start()
    for row, total in zip((6, 7, 5), sums):
        v.vec[row : row + 1, :] = jnp.sum(total, axis=0, keepdims=True)

    def weight_grad(slots, right, into):
        def one(step, carry):
            other = (at.q + step) % 4
            total = jnp.zeros((256, 512), F32)
            for r in range(4):
                total += contract_rows(slots[at.chip(r), :, chip_rows(other)], right[r])
            into[2 * other] = total[0:128].astype(BF16)
            into[2 * other + 1] = total[128:256].astype(BF16)
            return carry

        lax.fori_loop(0, 4, one, 0)

    neighbours(gathers[1][0])
    hidden_grad(1, 0)
    hidden_grad(0, 1)
    neighbours(gathers[1][1])
    hidden_grad(0, 2)
    gathers[1][0].forward(3)
    hidden_grad(1, 1)
    hidden_grad(0, 3)
    gathers[1][1].forward(3)
    hidden_grad(1, 2)
    hidden_grad(1, 3)
    for one in done[-3:]:
        pass_on(scatters[1], *one)
    v.gbin[...] = jnp.sum(gbin[0], axis=0, keepdims=True)

    sums = tuple(jnp.zeros((8, 1024), F32) for _ in range(3))
    weight_grad(v.grad_slots, v.hid, v.g_back)
    wait_bytes(v.xs.at[pl.ds(0, 896)], v.s_ga.at[1])
    sum_back.begin((0,))
    scatters[1][0].relay()
    weight_grad(v.norm_slots, v.low, v.g_in)
    scatters[1][1].relay()
    for h in range(2):
        scatters[1][h].arrive()
        for i in range(2):
            rows = local(h, i)
            total = v.d2[rows] + terms[0, chip_part(h, i)] + peers(1, rows)
            unit = v.unit1[rows]
            d = norm_back(total * param(3), unit, v.scale1[rows][:, :1])
            v.d1[rows] = d
            low = d.astype(BF16)
            v.db[rows] = low
            sums = column_sums((total * unit, total, low.astype(F32)), sums)
        rows = pl.ds(64 * h, 64)
        v.da_send[rows] = contract_cols(v.db[rows], v.wo[...]).astype(BF16)
        for r in range(4):
            chip = at.chip(r)
            for plane in (h, h + 2):
                pair = 2 * (plane - h) + chip
                send_or_copy(
                    v.da_send.at[rows, lanes(pair)],
                    v.da.at[slot_rows(at.place)],
                    v.s_misc.at[4],
                    v.r_da.at[r],
                    (2 * chip + at.c, plane),
                    None if r else at.z == plane,
                )

    for row, total in zip((3, 4, 2), sums):
        v.vec[row : row + 1, :] = jnp.sum(total, axis=0, keepdims=True)
    v.vec[0:2, :] = jnp.zeros((2, 1024), F32)
    for i in range(3):
        if i:
            sum_back.begin((i,))
        sum_in.begin((i,))


def grads_phase(at, v, out_scatter, sum_in, sum_back):
    xs, wqkv, terms = v.xs, v.wqkv, v.terms
    parity, pair = at.parity, at.pair

    wait_bytes(xs.at[pl.ds(0, 896)], v.s_ex.at[0])
    for r in (3, 1, 2, 0):
        for core in (1 - at.c, at.c):
            part = contract_rows(v.db[:, lanes(2 * at.chip(r) + core)], v.att[...])
            if core is at.c:
                terms[r, 0:128] = part
            else:
                out_scatter.put(r, part)

    v.q_turned[...] = v.queries[...].astype(F32).T.astype(BF16)
    v.dk_turned[...] = jnp.zeros_like(v.dk_turned)
    v.dv_turned[...] = jnp.zeros_like(v.dv_turned)
    for r in (3, 1, 2):
        out_scatter.add(r, terms[r, 0:128])
    terms[0, 0:128] = out_scatter.add(0, terms[0, 0:128])
    wait_bytes(v.da.at[chip_rows(at.q)], v.r_da.at[0])
    s_buf, d_buf, p_buf = v.scores, v.d_buf, v.p_buf

    def attend(step, carry):
        chip = ((at.y + step // 2) % 2) * 2 + (at.x + step % 2) % 2
        rows = chip_rows(chip)

        @pl.when(step > 0)
        def _():
            wait_bytes(v.da.at[rows], v.r_da.at[step])

        v.da_turned[:, rows] = v.da[rows].astype(F32).T.astype(BF16)
        parts = []
        for h in range(2):
            mask = head_mask(h)
            grad = v.da[rows].astype(F32) * mask
            delta = jnp.sum(grad * v.mixed[rows], axis=-1, keepdims=True)
            q = (v.queries[rows].astype(F32) * mask * HEAD_DIM**-0.5).astype(BF16)
            s_buf[...] = contract_cols(q, v.keys_all[...])
            d_buf[...] = contract_cols(grad.astype(BF16), v.values_all[...])
            logs = v.log_sums[rows][:, h * HEAD_DIM : h * HEAD_DIM + 1]
            probs = jnp.exp(s_buf[...] - logs)
            p_buf[...] = probs.astype(BF16)
            low = (probs * (d_buf[...] - delta)).astype(BF16)
            band = pl.ds(h * HEAD_DIM, HEAD_DIM)
            v.dv_turned[band] += dot_nn(v.da_turned[band, rows], p_buf[...])
            v.dk_turned[band] += dot_nn(v.q_turned[band, rows], low)
            parts.append(dot_nn(low, v.keys_all[...]))
        v.dq[rows] = jnp.where(head_mask(0) > 0.5, parts[0], parts[1]) * HEAD_DIM**-0.5

        @pl.when(step == 1)
        def _():
            out_scatter.relay()
            sum_back.relay(1, 0)

        @pl.when(step == 2)
        def _():
            sum_in.relay(1, 0)

        return carry

    lax.fori_loop(0, 4, attend, 0)

    other = core_rows(1 - at.c)
    mine = core_rows(at.c)
    v.out_k[...] = v.dk_turned[:, other].T * HEAD_DIM**-0.5
    v.out_v[...] = v.dv_turned[:, other].T
    for k, (ref, into) in enumerate(((v.out_k, v.sib_k), (v.out_v, v.sib_v))):
        remote(ref, into, v.s_kv2.at[0], v.r_kv2.at[k], at.sibling()).start()
    dqkv = v.dqkv
    low = v.dq[...].astype(BF16)
    dqkv[:, 0:128] = low
    v.vec[0:1, lanes(pair)] = jnp.sum(low.astype(F32), axis=0, keepdims=True)
    out_scatter.arrive()
    peer_in = v.peer_in.at[0]

    def out_rows(rows):
        total = terms[0, rows] + peer_in[1, rows].astype(F32) + peer_in[2, rows].astype(F32)
        v.o_out[rows] = total.astype(BF16)

    by_rows(128, 32, out_rows)
    wide = pl.ds(pl.multiple_of(at.z * 256, 256), 256)
    pltpu.make_async_copy(v.o_out.at[:, wide], v.o_in.at[0], v.r_misc.at[8]).start()
    for dz in range(1, 4):
        plane = (at.z + dz) % 4
        remote(
            v.o_out.at[:, pl.ds(pl.multiple_of(plane * 256, 256), 256)],
            v.o_in.at[dz],
            v.s_misc.at[8],
            v.r_misc.at[8],
            (at.b, plane),
        ).start()

    sum_back.relay(1, 1)
    sum_back.relay(2, 0)
    own_k = v.dk_turned[:, mine].T * HEAD_DIM**-0.5
    wait_bytes(v.sib_k, v.r_kv2.at[0])
    dqkv[:, 128:256] = (own_k + v.sib_k[...]).astype(BF16)
    own_v = v.dv_turned[:, mine].T
    wait_bytes(v.sib_v, v.r_kv2.at[1])
    low = (own_v + v.sib_v[...]).astype(BF16)
    dqkv[:, 256:384] = low
    v.vec[1:2, lanes(pair)] = jnp.sum(low.astype(F32), axis=0, keepdims=True)

    notes = v.notes
    for b in range(8):
        notes[b, 0:8] = v.vec[:, 128 * b : 128 * b + 128]
        notes[b, 8:16] = jnp.zeros((8, 128), F32)
    row = lax.broadcasted_iota(jnp.int32, (8, 128), 0)
    for h in range(4):
        notes[2 * h + at.b // 4, 8:16] = jnp.where(
            row == at.b % 4, v.gbin[0:1, 128 * h : 128 * h + 128], 0.0
        )
    pltpu.make_async_copy(notes.at[at.b], v.notes_p.at[at.b], v.r_misc.at[5]).start()

    def spread(step, carry):
        to = (at.b + step) % 8
        remote(
            notes.at[to], v.notes_p.at[at.b], v.s_misc.at[5], v.r_misc.at[5], (to, at.z)
        ).start()
        return carry

    lax.fori_loop(1, 8, spread, 0)

    wait_bytes(xs.at[pl.ds(0, 896)], v.s_ga.at[0])
    x_out, x_in, x_via = v.norm_slots, v.grad_slots.at[0:2], v.grad_slots.at[2:4]
    for r in (3, 1, 2, 0):
        part = contract_cols(dqkv[chip_rows(at.chip(r))], wqkv[...])
        if r:
            x_out[r] = part.astype(BF16)
        else:
            v.x_sum[...] = part
    def piece(dz, k):
        return pl.ds(pl.multiple_of(((at.z + dz) % 4) * 64 + 32 * k, 32), 32)

    order = (2, 1, 3, 0)

    def send_dx(dz, via):
        for r, k in ((1, 0), (2, 1)):
            rows = piece(dz, k)
            remote(
                x_out.at[3 if via else r, rows],
                x_via.at[r - 1, rows] if via else x_in.at[r - 1, rows],
                v.s_dx.at[0],
                v.r_dx.at[dz, 0 if via else r, k],
                at.peer(r),
            ).start()

    def relay_dx(dz):
        for r, k in ((2, 0), (1, 1)):
            rows = piece(dz, k)
            wait_bytes(x_via.at[k, rows], v.r_dx.at[dz, 0, k])
            x_out[r, rows] = (
                x_out[r, rows].astype(F32) + x_via[k, rows].astype(F32)
            ).astype(BF16)
            remote(
                x_out.at[r, rows],
                x_in.at[r - 1, rows],
                v.s_dx.at[0],
                v.r_dx.at[dz, r, k],
                at.peer(r),
            ).start()

    z_out, z_in = v.z_out, v.z_in
    def column_dx(dz):
        plane = (at.z + dz) % 4
        rows = slot_rows(plane)
        for r in (1, 2):
            for k in range(2):
                wait_bytes(x_in.at[r - 1, piece(dz, k)], v.r_dx.at[dz, r, k])
        total = v.x_sum[rows] + x_in[0, rows].astype(F32) + x_in[1, rows].astype(F32)
        if dz:
            z_out[dz] = total.astype(BF16)
            remote(
                z_out.at[dz], z_in.at[dz], v.s_dz.at[0], v.r_dz.at[dz], (at.b, plane)
            ).start()
        else:
            v.x_own[...] = total

    def begin_dx(dz):
        send_dx(dz, True)
        send_dx(dz, False)

    begin_dx(2)
    begin_dx(1)
    def features(b):
        return contract_rows(xs[:, lanes(b)], dqkv[...])

    for r in range(4):
        v.w_sib_out[r] = features(2 * at.chip(r) + 1 - at.c)
        remote(
            v.w_sib_out.at[r], v.w_sib_in.at[r], v.s_ws.at[0], v.r_ws.at[r], at.sibling()
        ).start()
    relay_dx(2)
    begin_dx(3)
    sum_in.relay(1, 1)
    sum_in.relay(2, 0)
    relay_dx(1)
    begin_dx(0)
    column_dx(2)
    relay_dx(3)
    column_dx(1)
    relay_dx(0)
    plane_w = 2 * (at.z // 2) + at.y
    for r in range(4):
        total = features(2 * at.chip(r) + at.c)
        wait_bytes(v.w_sib_in.at[r], v.r_ws.at[r])
        v.w_out[r] = (total + v.w_sib_in[r]).astype(BF16)
        send_or_copy(
            v.w_out.at[r],
            v.w_in.at[parity, at.x],
            v.s_misc.at[6],
            v.r_misc.at[6],
            at.peer(r)[:1] + (plane_w,),
            plane_w == at.z if r == 0 else None,
        )

    column_dx(3)
    sum_back.finish(v.gs_back, v.fin_back, v.s_misc.at[7], v.r_misc.at[7])
    sum_in.finish(v.gs_in, v.fin_in, v.s_misc.at[9], v.r_misc.at[9])
    wait_bytes(v.notes_p, v.r_misc.at[5])
    total = v.notes_p[0]
    for b in range(1, 8):
        total += v.notes_p[b]
    v.notes_sum[...] = total
    mine = v.notes_in.at[at.z]
    pltpu.make_async_copy(v.notes_sum, mine, v.r_misc.at[11]).start()
    for dz in range(1, 4):
        remote(
            v.notes_sum, mine, v.s_misc.at[11], v.r_misc.at[11], (at.b, (at.z + dz) % 4)
        ).start()

    column_dx(0)
    for dz in (1, 2, 3):
        wait_bytes(z_in.at[dz], v.r_dz.at[dz])
    same = slot_rows(parity)
    v.gtok_here[same] = (v.d1[same] + v.x_own[...] + z_in[2].astype(F32)).astype(BF16)
    cross = slot_rows(1 - parity)
    v.gtok_here[cross] = (v.d1[cross] + z_in[1].astype(F32) + z_in[3].astype(F32)).astype(BF16)

    pltpu.make_async_copy(v.gtok_here, v.gtok, v.r_own.at[3]).start()
    wait_bytes(v.o_in, v.r_misc.at[8])
    wait_bytes(v.w_in, v.r_misc.at[6])
    wait_bytes(v.notes_in, v.r_misc.at[11])
    wait_bytes(v.fin_back, v.r_misc.at[7])
    wait_bytes(v.fin_in, v.r_misc.at[9])


def end_phase(at, v, ends):
    wait_bytes(v.out_here, v.r_own.at[2])
    for one in ends:
        one.end()

    def rows(n):
        return v.xs.at[pl.ds(0, n)]

    wait_bytes(rows(192), v.s_z.at[0])
    wait_bytes(rows(768), v.s_p.at[0])
    wait_bytes(rows(384), v.s_wo.at[0])
    wait_bytes(rows(608), v.s_o.at[0])
    wait_bytes(rows(256), v.s_kv.at[0])
    for i in (1, 2):
        wait_bytes(rows(896), v.s_ex.at[i])
    wait_bytes(rows(768), v.s_dx.at[0])
    wait_bytes(rows(192), v.s_dz.at[0])
    wait_bytes(v.w_sib_out, v.s_ws.at[0])
    wait_bytes(rows(512), v.s_kv2.at[0])
    wait_bytes(v.wqkv.at[pl.ds(0, 384)], v.s_w.at[0])
    wait_bytes(v.wqkv.at[pl.ds(0, 512)], v.s_w.at[1])
    wait_bytes(v.w_near, v.s_w.at[2])
    seven = v.wi.at[pl.ds(0, 896), pl.ds(0, 128)]
    for i in (0, 2, 7, 9):
        wait_bytes(seven, v.s_misc.at[i])
    wait_bytes(v.smalls.at[pl.ds(0, 3)], v.s_misc.at[1])
    wait_bytes(v.smalls.at[pl.ds(0, 7)], v.s_misc.at[10])
    for i in (3, 4):
        wait_bytes(v.att_send.at[pl.ds(0, 960)], v.s_misc.at[i])
    wait_bytes(v.notes.at[pl.ds(0, 7)], v.s_misc.at[5])
    wait_bytes(v.notes.at[pl.ds(0, 3)], v.s_misc.at[11])
    plane_w = 2 * (at.z // 2) + at.y

    @pl.when(plane_w == at.z)
    def _():
        wait_bytes(v.w_out.at[pl.ds(0, 3)], v.s_misc.at[6])

    @pl.when(plane_w != at.z)
    def _():
        wait_bytes(v.w_out, v.s_misc.at[6])

    wait_bytes(v.o_in.at[pl.ds(0, 3)], v.s_misc.at[8])
    wait_bytes(v.gtok_here, v.r_own.at[3])


def finish_kernel(
    place_ref,
    out_in,
    gtok_in,
    w_in,
    o_in,
    fin_in,
    fin_back,
    notes_in,
    out_ref,
    gtok_ref,
    gq_ref,
    gk_ref,
    gv_ref,
    gout_ref,
    gwin_ref,
    gwback_ref,
    bin_ref,
    *vector_refs,
):
    out_ref[...] = out_in[...]
    gtok_ref[...] = gtok_in[...]
    for x in range(2):
        total = w_in[0, x].astype(F32) + w_in[1, x].astype(F32)
        for k, ref in enumerate((gq_ref, gk_ref, gv_ref)):
            ref[:, 128 * x : 128 * x + 128] = total[:, 128 * k : 128 * k + 128]
    gout_ref[...] = (
        o_in[0].astype(F32) + o_in[1].astype(F32) + o_in[2].astype(F32) + o_in[3].astype(F32)
    ).T
    gwin_ref[...] = fin_in[...].astype(F32)
    gwback_ref[...] = fin_back[...].astype(F32)
    total = notes_in[0] + notes_in[1] + notes_in[2] + notes_in[3]
    z = place_ref[0]
    part = jnp.zeros((8, 32), F32)
    units = jnp.zeros((1, 128), F32)
    for k in range(4):
        part += jnp.where(z == k, total[0:8, 32 * k : 32 * k + 32], 0.0)
        units += jnp.where(z == k, total[8 + k : 9 + k], 0.0)
    for j, ref in enumerate(vector_refs):
        ref[...] = part[j]
    bin_ref[...] = units[0]


def vmem():
    return pl.BlockSpec(memory_space=pltpu.VMEM)


def run_layer(*args):
    results = [e for _, e in entries(Results)]
    scratch = [pltpu.VMEM(s, t) for _, (s, t) in entries(Scratch)]
    for _, shape in entries(Arrivals) + entries(Departures):
        scratch.append(DMA(shape))
    return pl.pallas_call(
        layer_kernel,
        out_shape=[jax.ShapeDtypeStruct(s, t) for s, t in results],
        in_specs=[vmem()] + [pl.BlockSpec(memory_space=pl.ANY)] * (len(args) - 1),
        out_specs=[pl.BlockSpec(memory_space=pl.ANY)] * len(results),
        scratch_shapes=scratch,
        compiler_params=pltpu.CompilerParams(
            collective_id=1, has_side_effects=True, vmem_limit_bytes=VMEM_LIMIT
        ),
    )(*args)


def run_finish(*args):
    shapes = (
        ((128, 1024), BF16),
        ((128, 1024), BF16),
        ((128, 256), F32),
        ((128, 256), F32),
        ((128, 256), F32),
        ((256, 128), F32),
        ((128, 1024), F32),
        ((128, 1024), F32),
        ((128,), F32),
    ) + (((32,), F32),) * 8
    return pl.pallas_call(
        finish_kernel,
        out_shape=[jax.ShapeDtypeStruct(s, t) for s, t in shapes],
        in_specs=[pl.BlockSpec(memory_space=pltpu.SMEM)] + [vmem()] * (len(args) - 1),
        out_specs=[vmem()] * len(shapes),
        compiler_params=pltpu.CompilerParams(vmem_limit_bytes=VMEM_LIMIT),
    )(*args)


DMA = pltpu.SemaphoreType.DMA


def fast_device(
    tokens,
    w_query,
    w_key,
    w_value,
    w_out,
    b_query,
    b_value,
    b_out,
    norm1_gain,
    norm1_shift,
    w_in,
    w_back,
    b_in,
    b_back,
    norm2_gain,
    norm2_shift,
    cotangent,
):
    head_id = lax.axis_index("head")
    token_shape = tokens.shape
    model_dim = tokens.shape[2]
    x = tokens.reshape(-1, model_dim)
    vectors = (
        b_query,
        b_value,
        b_out,
        norm1_gain,
        norm1_shift,
        b_back,
        norm2_gain,
        norm2_shift,
        b_in,
    )
    small = jnp.concatenate(vectors).astype(F32).reshape(1, -1)
    results = run_layer(
        small, x, cotangent.reshape(-1, model_dim), w_query, w_key, w_value, w_out, w_in, w_back
    )
    output, grad_tokens, gq, gk, gv, gout, gw_in, gw_back, gb_in, *own = run_finish(
        head_id.astype(jnp.int32).reshape(1), *results
    )
    return (
        output.reshape(token_shape),
        grad_tokens.reshape(token_shape),
        gq,
        gk,
        gv,
        gout,
        own[0],
        own[1],
        own[2],
        own[3],
        own[4],
        gw_in,
        gw_back,
        gb_in,
        own[5],
        own[6],
        own[7],
    )


def solution(mesh):
    in_specs = (
        P(None, ("blk", "head"), None),
        P("blk", "head"),
        P("blk", "head"),
        P("blk", "head"),
        P("head", "blk"),
        P(("blk", "head")),
        P(("blk", "head")),
        P(("blk", "head")),
        P(("blk", "head")),
        P(("blk", "head")),
        P("blk", "head"),
        P("blk", "head"),
        P(("blk", "head")),
        P(("blk", "head")),
        P(("blk", "head")),
        P(("blk", "head")),
        P(None, ("blk", "head"), None),
    )
    out_specs = (
        P(None, ("blk", "head"), None),
        P(None, ("blk", "head"), None),
        P("blk", "head"),
        P("blk", "head"),
        P("blk", "head"),
        P("head", "blk"),
        P(("blk", "head")),
        P(("blk", "head")),
        P(("blk", "head")),
        P(("blk", "head")),
        P(("blk", "head")),
        P("blk", "head"),
        P("blk", "head"),
        P(("blk", "head")),
        P(("blk", "head")),
        P(("blk", "head")),
        P(("blk", "head")),
    )
    sizes = (mesh.shape["blk"], mesh.shape["head"])
    body = fast_device if sizes == (8, 4) else per_device
    return jax.shard_map(
        body, mesh=mesh, in_specs=in_specs, out_specs=out_specs, check_vma=False
    )
```

```python
import functools
import math

import jax
import jax.numpy as jnp
from jax import lax
from jax.experimental import pallas as pl
from jax.experimental.pallas import tpu as pltpu
from jax.sharding import PartitionSpec as P

HEAD_DIM = 64


NORM_EPS = 1e-05


def layer_norm(summed, gain, shift):
    centre = jnp.mean(summed, axis=-1, keepdims=True)
    centred = summed - centre
    spread = jnp.mean(centred * centred, axis=-1, keepdims=True)
    return centred * lax.rsqrt(spread + NORM_EPS) * gain + shift


def gelu_exact(inputs):
    return jax.nn.gelu(inputs, approximate=False)


def split_heads(packed):
    return packed.reshape(packed.shape[0], packed.shape[1], -1, HEAD_DIM)


def contract_rows(left, right):
    return lax.dot_general(
        left, right, (((0,), (0,)), ((), ())), preferred_element_type=jnp.float32
    )


def contract_cols(left, right):
    return lax.dot_general(
        left, right, (((1,), (1,)), ((), ())), preferred_element_type=jnp.float32
    )


def score_block(queries4, keys4):
    return jnp.einsum(
        "sqge,skge->sqgk", queries4, keys4, preferred_element_type=jnp.float32
    ) * HEAD_DIM ** (-0.5)


def score_grads(queries4, keys4, values4, grads4, log_sums, deltas):
    probs = jnp.exp(score_block(queries4, keys4) - log_sums[..., None])
    d_probs = jnp.einsum("sqge,skge->sqgk", grads4, values4, preferred_element_type=jnp.float32)
    d_scores = (probs * (d_probs - deltas[..., None])).astype(jnp.bfloat16)
    return (probs.astype(jnp.bfloat16), d_scores)


def token_rows(local):
    return lax.all_gather(local, "head", axis=1, tiled=True)


def token_partials(terms):
    return lax.psum_scatter(
        terms.astype(jnp.bfloat16), "head", scatter_dimension=1, tiled=True
    ).astype(jnp.float32)


def place_part(part, full_len, start):
    return lax.dynamic_update_slice_in_dim(jnp.zeros((full_len,), jnp.float32), part, start, 0)


def per_device(
    tokens,
    w_query,
    w_key,
    w_value,
    w_out,
    b_query,
    b_value,
    b_out,
    norm1_gain,
    norm1_shift,
    w_in,
    w_back,
    b_in,
    b_back,
    norm2_gain,
    norm2_shift,
    cotangent,
):
    f32 = jnp.float32
    bf16 = jnp.bfloat16
    score_scale = HEAD_DIM ** (-0.5)
    bq_full, bv_full, bo_full, gain_one, shift_one, bin_full, bback_full, gain_two, shift_two = (
        lax.all_gather(b_query, ("blk", "head"), axis=0, tiled=True),
        lax.all_gather(b_value, ("blk", "head"), axis=0, tiled=True),
        lax.all_gather(b_out, ("blk", "head"), axis=0, tiled=True),
        lax.all_gather(norm1_gain, ("blk", "head"), axis=0, tiled=True),
        lax.all_gather(norm1_shift, ("blk", "head"), axis=0, tiled=True),
        lax.all_gather(b_in, ("blk", "head"), axis=0, tiled=True),
        lax.all_gather(b_back, ("blk", "head"), axis=0, tiled=True),
        lax.all_gather(norm2_gain, ("blk", "head"), axis=0, tiled=True),
        lax.all_gather(norm2_shift, ("blk", "head"), axis=0, tiled=True),
    )
    attn_cols, out_rows, ffn_cols = (
        lax.all_gather(jnp.stack((w_query, w_key, w_value)), "blk", axis=1, tiled=True),
        lax.all_gather(w_out, "blk", axis=1, tiled=True),
        lax.all_gather(jnp.stack((w_in, w_back)), "blk", axis=1, tiled=True),
    )
    seq_count, local_len, model_dim = tokens.shape
    token_shape = (seq_count, local_len, model_dim)
    head_id = lax.axis_index("head")
    width_part = attn_cols.shape[2]
    bq_part = lax.dynamic_slice_in_dim(bq_full, head_id * width_part, width_part).astype(f32)
    bv_part = lax.dynamic_slice_in_dim(bv_full, head_id * width_part, width_part).astype(f32)
    wide_rows = token_rows(tokens)
    wide_len = wide_rows.shape[1]
    wide_flat = wide_rows.reshape(-1, model_dim)
    head_shape = (seq_count, wide_len, width_part)
    wide_shape = (seq_count, wide_len, model_dim)
    query_heads = (
        (jnp.dot(wide_flat, attn_cols[0], preferred_element_type=f32) + bq_part)
        .astype(bf16)
        .reshape(head_shape)
    )
    key_heads = (
        jnp.dot(wide_flat, attn_cols[1], preferred_element_type=f32)
        .astype(bf16)
        .reshape(head_shape)
    )
    value_heads = (
        (jnp.dot(wide_flat, attn_cols[2], preferred_element_type=f32) + bv_part)
        .astype(bf16)
        .reshape(head_shape)
    )
    query4 = split_heads(query_heads)
    key4 = split_heads(key_heads)
    value4 = split_heads(value_heads)
    stat_shape = query4.shape[:3]
    pieces = (
        lax.all_gather(key_heads, "blk", axis=1, tiled=True),
        lax.all_gather(value_heads, "blk", axis=1, tiled=True),
    )
    maxima = jnp.full(stat_shape, -1e30, f32)
    scores = score_block(query4, split_heads(pieces[0]))
    new_max = jnp.maximum(maxima, jnp.max(scores, axis=-1))
    weights = jnp.exp(scores - new_max[..., None])
    totals = jnp.sum(weights, axis=-1)
    summed = jnp.einsum(
        "sqgk,skge->sqge", weights.astype(bf16), split_heads(pieces[1]), preferred_element_type=f32
    )
    maxima, totals, summed = (new_max, totals, summed)
    log_sums = maxima + jnp.log(totals)
    attended4 = summed / totals[..., None]
    attended_heads = attended4.reshape(head_shape).astype(bf16)
    attended_flat = attended_heads.reshape(-1, width_part)
    branch_terms = jnp.dot(attended_flat, out_rows, preferred_element_type=f32).reshape(wide_shape)
    branch = token_partials(branch_terms).reshape(-1, model_dim) + bo_full.astype(f32)
    flat_rows = tokens.reshape(-1, model_dim)
    normed, norm1_pull = jax.vjp(
        layer_norm, flat_rows.astype(f32) + branch, gain_one.astype(f32), shift_one.astype(f32)
    )
    normed_low = normed.astype(bf16)
    ffn_full = lax.all_gather(ffn_cols, "head", axis=2, tiled=True)
    pre_act = jnp.dot(normed_low, ffn_full[0], preferred_element_type=f32) + bin_full.astype(f32)
    hidden_act, gelu_pull = jax.vjp(gelu_exact, pre_act)
    hidden_low = hidden_act.astype(bf16)
    ffn_out = contract_cols(hidden_low, ffn_full[1]) + bback_full.astype(f32)
    final, norm2_pull = jax.vjp(
        layer_norm, normed + ffn_out, gain_two.astype(f32), shift_two.astype(f32)
    )
    output = final.astype(bf16).reshape(token_shape)
    d_second, grad_norm2_gain, grad_norm2_shift = norm2_pull(
        cotangent.reshape(-1, model_dim).astype(f32)
    )
    d_ffn = d_second.astype(bf16)
    grad_b_back = jnp.sum(d_ffn.astype(f32), axis=0)
    grad_back_whole = contract_rows(d_ffn, hidden_low)
    d_hidden = jnp.dot(d_ffn, ffn_full[1], preferred_element_type=f32)
    d_pre = gelu_pull(d_hidden)[0].astype(bf16)
    grad_b_in = jnp.sum(d_pre.astype(f32), axis=0)
    grad_in_whole = contract_rows(normed_low, d_pre)
    ffn_grad_parts = lax.psum_scatter(
        jnp.stack((grad_in_whole, grad_back_whole)).astype(jnp.bfloat16),
        "head",
        scatter_dimension=2,
        tiled=True,
    ).astype(jnp.float32)
    d_normed = d_second + contract_cols(d_pre, ffn_full[0])
    d_first, grad_norm1_gain, grad_norm1_shift = norm1_pull(d_normed)
    d_branch = d_first.astype(bf16)
    grad_b_out = jnp.sum(d_branch.astype(f32), axis=0)
    wide_dbranch = token_rows(d_branch.reshape(token_shape)).reshape(-1, model_dim)
    grad_out_part = contract_rows(attended_flat, wide_dbranch)
    grad_heads = contract_cols(wide_dbranch, out_rows).astype(bf16).reshape(head_shape)
    grads4 = split_heads(grad_heads)
    deltas = jnp.sum(grads4.astype(f32) * attended4, axis=-1)
    row_stats = (
        lax.all_gather(log_sums, "blk", axis=1, tiled=True),
        lax.all_gather(deltas, "blk", axis=1, tiled=True),
    )
    pieces = (
        lax.all_gather(key_heads, "blk", axis=1, tiled=True),
        lax.all_gather(value_heads, "blk", axis=1, tiled=True),
        lax.all_gather(query_heads, "blk", axis=1, tiled=True),
        lax.all_gather(grad_heads, "blk", axis=1, tiled=True),
    )
    piece_keys = split_heads(pieces[0])
    piece_values = split_heads(pieces[1])
    piece_queries = split_heads(pieces[2])
    piece_grads = split_heads(pieces[3])
    piece_sums = row_stats[0]
    piece_deltas = row_stats[1]
    own_probs, own_scores = score_grads(query4, piece_keys, piece_values, grads4, log_sums, deltas)
    d_query = score_scale * jnp.einsum(
        "sqgk,skge->sqge", own_scores, piece_keys, preferred_element_type=f32
    )
    probs_low, d_scores = score_grads(
        piece_queries, key4, value4, piece_grads, piece_sums, piece_deltas
    )
    key_acc = score_scale * jnp.einsum(
        "sqgk,sqge->skge", d_scores, piece_queries, preferred_element_type=f32
    )
    value_acc = jnp.einsum("sqgk,sqge->skge", probs_low, piece_grads, preferred_element_type=f32)
    d_query_low = d_query.reshape(-1, width_part).astype(bf16)
    d_key_low = key_acc.reshape(-1, width_part).astype(bf16)
    d_value_low = value_acc.reshape(-1, width_part).astype(bf16)
    grad_b_query = place_part(
        jnp.sum(d_query_low.astype(f32), axis=0), model_dim, head_id * width_part
    )
    grad_b_value = place_part(
        jnp.sum(d_value_low.astype(f32), axis=0), model_dim, head_id * width_part
    )
    attn_grad_parts = jnp.stack(
        (
            contract_rows(wide_flat, d_query_low),
            contract_rows(wide_flat, d_key_low),
            contract_rows(wide_flat, d_value_low),
        )
    )
    token_terms = (
        contract_cols(d_query_low, attn_cols[0])
        + contract_cols(d_key_low, attn_cols[1])
        + contract_cols(d_value_low, attn_cols[2])
    )
    d_tokens = d_first + token_partials(token_terms.reshape(wide_shape)).reshape(-1, model_dim)
    grad_tokens = d_tokens.astype(bf16).reshape(token_shape)
    attn_sums, grad_w_out, ffn_sums = (
        lax.psum_scatter(attn_grad_parts, "blk", scatter_dimension=1, tiled=True),
        lax.psum_scatter(grad_out_part, "blk", scatter_dimension=1, tiled=True),
        lax.psum_scatter(ffn_grad_parts, "blk", scatter_dimension=1, tiled=True),
    )
    (
        grad_b_query,
        grad_b_value,
        grad_b_out,
        grad_norm1_gain,
        grad_norm1_shift,
        grad_b_in,
        grad_b_back,
        grad_norm2_gain,
        grad_norm2_shift,
    ) = (
        lax.psum_scatter(grad_b_query, ("blk", "head"), scatter_dimension=0, tiled=True),
        lax.psum_scatter(grad_b_value, ("blk", "head"), scatter_dimension=0, tiled=True),
        lax.psum_scatter(grad_b_out, ("blk", "head"), scatter_dimension=0, tiled=True),
        lax.psum_scatter(grad_norm1_gain, ("blk", "head"), scatter_dimension=0, tiled=True),
        lax.psum_scatter(grad_norm1_shift, ("blk", "head"), scatter_dimension=0, tiled=True),
        lax.psum_scatter(grad_b_in, ("blk", "head"), scatter_dimension=0, tiled=True),
        lax.psum_scatter(grad_b_back, ("blk", "head"), scatter_dimension=0, tiled=True),
        lax.psum_scatter(grad_norm2_gain, ("blk", "head"), scatter_dimension=0, tiled=True),
        lax.psum_scatter(grad_norm2_shift, ("blk", "head"), scatter_dimension=0, tiled=True),
    )
    return (
        output,
        grad_tokens,
        attn_sums[0],
        attn_sums[1],
        attn_sums[2],
        grad_w_out,
        grad_b_query,
        grad_b_value,
        grad_b_out,
        grad_norm1_gain,
        grad_norm1_shift,
        ffn_sums[0],
        ffn_sums[1],
        grad_b_in,
        grad_b_back,
        grad_norm2_gain,
        grad_norm2_shift,
    )


MESH = pl.DeviceIdType.MESH
F32 = jnp.float32
BF16 = jnp.bfloat16
VMEM_LIMIT = 62 * 2**20


def dot_nn(left, right):
    return jnp.dot(left, right, preferred_element_type=F32)


class Place:
    def __init__(self):
        self.b = lax.axis_index("blk")
        self.z = lax.axis_index("head")
        self.y = self.b // 4
        self.x = (self.b // 2) % 2
        self.c = self.b % 2
        self.q = self.b // 2

    def chip(self, r):
        return ((self.y + r // 2) % 2) * 2 + (self.x + r % 2) % 2

    def peer(self, r):
        return (2 * self.chip(r) + self.c, self.z)

    def sibling(self):
        return (2 * self.q + 1 - self.c, self.z)


def remote(src, dst, send_sem, recv_sem, device):
    return pltpu.make_async_remote_copy(
        src_ref=src,
        dst_ref=dst,
        send_sem=send_sem,
        recv_sem=recv_sem,
        device_id=device,
        device_id_type=MESH,
    )


def wait_bytes(view, sem):
    pltpu.make_async_copy(view, view, sem).wait()


def greet_all(at):
    barrier = pltpu.get_barrier_semaphore()
    flat = at.b * 4 + at.z

    def greet(step, carry):
        other = (flat + step) % 32
        pl.semaphore_signal(
            barrier, inc=1, device_id=(other // 4, other % 4), device_id_type=MESH
        )
        return carry

    lax.fori_loop(1, 32, greet, 0)
    pl.semaphore_wait(barrier, 31)


def half(core):
    return pl.ds(pl.multiple_of(core * 128, 128), 128)


def lanes(index):
    return pl.ds(pl.multiple_of(index * 128, 128), 128)


def by_rows(count, size, step):
    def body(i, carry):
        step(pl.ds(pl.multiple_of(i * size, size), size))
        return carry

    lax.fori_loop(0, count // size, body, 0)


class Spread:
    def __init__(self, at, block, part, send, recv):
        self.at, self.block, self.part = at, block, part
        self.send, self.recv = send, recv

    def start(self):
        mine = self.block(0)
        for i in (0, 1):
            for r, k in ((1, i), (2, 1 - i)):
                piece = self.part(mine, k)
                remote(piece, piece, self.send, self.recv.at[r, k], self.at.peer(r)).start()

    def relay(self):
        for r, k in ((1, 0), (2, 1)):
            piece = self.part(self.block(r), k)
            wait_bytes(piece, self.recv.at[r, k])
            remote(piece, piece, self.send, self.recv.at[0, k], self.at.peer(3 - r)).start()

    def rest(self, r):
        block = self.block(r)
        for row, k in {1: ((1, 1),), 2: ((2, 0),), 3: ((0, 0), (0, 1))}[r]:
            wait_bytes(self.part(block, k), self.recv.at[row, k])


def part_rows(h, core):
    return pl.ds(pl.multiple_of(h * 128 + core * 64, 64), 64)


class Gather:
    def __init__(self, at, slots, h, send, recv, recv_sib):
        self.at, self.slots, self.h = at, slots, h
        self.send, self.recv_sib = send, recv_sib

        def part(block, k):
            return block.at[pl.ds(k * 32, 32)]

        self.spread = Spread(
            at, lambda r: slots.at[at.chip(r), part_rows(h, at.c)], part, send, recv
        )

    def to_sibling(self, r):
        block = self.spread.block(r)
        remote(block, block, self.send, self.recv_sib.at[r], self.at.sibling()).start()

    def start(self):
        self.spread.start()
        self.to_sibling(0)

    def relay(self):
        self.spread.relay()

    def forward(self, r):
        self.spread.rest(r)
        self.to_sibling(r)

    def ready(self, r):
        at = self.at
        wait_bytes(self.slots.at[at.chip(r), part_rows(self.h, 1 - at.c)], self.recv_sib.at[r])
        return at.chip(r)


class Exchange:
    def __init__(self, at, buffers, rows, send, recv, recv_sib):
        self.at, self.send, self.recv, self.recv_sib = at, send, recv, recv_sib
        self.sib_out, self.sib_in, self.out, self.into = buffers
        self.rows = rows

    def put(self, r, theirs):
        mine = self.sib_out.at[r, self.rows]
        mine[...] = theirs.astype(BF16)
        remote(
            mine,
            self.sib_in.at[r, self.rows],
            self.send,
            self.recv_sib.at[r],
            self.at.sibling(),
        ).start()

    def add(self, r, mine):
        wait_bytes(self.sib_in.at[r, self.rows], self.recv_sib.at[r])
        total = mine + self.sib_in[r, self.rows].astype(F32)
        if r == 0:
            return total
        self.out[r, self.rows] = total.astype(BF16)
        if r == 3:
            for k in range(2):
                self.pass_half(3, k, 3, self.recv.at[3 * k], k + 1)
        else:
            self.pass_half(r, r - 1, r, self.recv.at[r], r)

    def half(self, k):
        size = self.rows.size // 2
        return pl.ds(self.rows.start + size * k, size)

    def pass_half(self, r, k, slot, recv, peer):
        rows = self.half(k)
        remote(
            self.out.at[r, rows], self.into.at[slot, rows], self.send, recv, self.at.peer(peer)
        ).start()

    def relay(self):
        for k in range(2):
            rows, r = self.half(k), 2 - k
            wait_bytes(self.into.at[3, rows], self.recv.at[3 * k])
            self.out[r, rows] = (
                self.out[r, rows].astype(F32) + self.into[3, rows].astype(F32)
            ).astype(BF16)
            self.pass_half(r, k, r, self.recv.at[r], r)

    def arrive(self):
        for r in (1, 2):
            wait_bytes(self.into.at[r, self.rows], self.recv.at[r])


def norm_rows(values):
    centre = jnp.mean(values, axis=-1, keepdims=True)
    centred = values - centre
    spread = jnp.mean(centred * centred, axis=-1, keepdims=True)
    scale = lax.rsqrt(spread + NORM_EPS)
    return centred * scale, scale


def norm_back(grad, unit, scale):
    centre = jnp.mean(grad, axis=-1, keepdims=True)
    along = jnp.mean(grad * unit, axis=-1, keepdims=True)
    return (grad - centre - unit * along) * scale


def send_or_copy(src, dst, send_sem, recv_sem, device, own):
    def away():
        remote(src, dst, send_sem, recv_sem, device).start()

    if own is None:
        away()
        return
    pl.when(jnp.logical_not(own))(away)

    @pl.when(own)
    def _():
        pltpu.make_async_copy(src, dst, recv_sem).start()


class Column:
    def __init__(self, at, ref, rows, sems):
        self.at, self.ref, self.rows = at, ref, rows
        self.up_send, self.up_recv, self.down_send, self.down_recv = sems

    def block(self, plane):
        return self.ref.at[self.rows, lanes(plane)]

    def sides(self, hop, act, arriving):
        z = self.at.z
        if arriving:
            below, above = z - 1 - hop, z + 1 + hop
            pl.when(below >= 0)(lambda: act(self.block(below), 0))
            pl.when(above <= 3)(lambda: act(self.block(above), 1))
        else:
            up = jnp.logical_and(z >= hop, z < 3)
            down = jnp.logical_and(z + hop <= 3, z > 0)
            pl.when(up)(lambda: act(self.block(z - hop), 0))
            pl.when(down)(lambda: act(self.block(z + hop), 1))

    def send(self, hop):
        def act(block, side):
            send = (self.up_send, self.down_send)[side].at[hop]
            recv = (self.up_recv, self.down_recv)[side].at[hop]
            remote(block, block, send, recv, (self.at.b, self.at.z + 1 - 2 * side)).start()

        self.sides(hop, act, False)

    def arrive(self, hop):
        def act(block, side):
            wait_bytes(block, (self.up_recv, self.down_recv)[side].at[hop])

        self.sides(hop, act, True)

    def end(self):
        def wait(hop):
            def act(block, side):
                wait_bytes(block, (self.up_send, self.down_send)[side].at[hop])

            return act

        for hop in range(3):
            self.sides(hop, wait(hop), False)


def plane_weights(at, src, dst, send_sem, recv_sem):
    rows, cols = lanes(at.b), lanes(at.z)
    pltpu.make_async_copy(src.at[:, lanes(at.b)], dst.at[rows, cols], recv_sem).start()

    def push(step, carry):
        other = (at.b + step) % 8
        remote(
            src.at[:, lanes(other)], dst.at[rows, cols], send_sem, recv_sem, (other, at.z)
        ).start()
        return carry

    lax.fori_loop(1, 8, push, 0)


class ColumnSum:
    def __init__(self, at, blocks, passing, send, recv):
        self.at, self.blocks, self.passing = at, blocks, passing
        self.send_sem, self.recv_sem = send, recv

    def plane(self, side, i):
        return i if side else 3 - i

    def hop(self, side):
        return 3 - self.at.z if side else self.at.z

    def next(self, side):
        return (self.at.b, self.at.z + 1 - 2 * side)

    def begin(self, which):
        for side in range(2):

            @pl.when(self.hop(side) == 0)
            def _(side=side):
                for i in which:
                    remote(
                        self.blocks.at[:, :, pl.ds(128 * self.plane(side, i), 128)],
                        self.passing.at[side, i],
                        self.send_sem.at[side, i],
                        self.recv_sem.at[side, i],
                        self.next(side),
                    ).start()

    def relay(self, hop, i):
        for side in range(2):

            @pl.when(self.hop(side) == hop)
            def _(side=side):
                held = self.passing.at[side, i]
                wait_bytes(held, self.recv_sem.at[side, i])
                cols = pl.ds(128 * self.plane(side, i), 128)
                for b in range(8):
                    self.passing[side, i, b] = (
                        self.passing[side, i, b].astype(F32)
                        + self.blocks[b, :, cols].astype(F32)
                    ).astype(BF16)
                remote(
                    held,
                    held,
                    self.send_sem.at[side, i],
                    self.recv_sem.at[side, i],
                    self.next(side),
                ).start()

    def finish(self, sums, final, send_out, recv_out):
        at = self.at
        own = lanes(at.z)
        for b in range(8):
            sums[b] = self.blocks[b, :, own]
        for side in range(2):
            for hop in range(1, 4):
                i = 3 - hop

                @pl.when(self.hop(side) == hop)
                def _(side=side, i=i):
                    wait_bytes(self.passing.at[side, i], self.recv_sem.at[side, i])
                    for b in range(8):
                        sums[b] = (
                            sums[b].astype(F32) + self.passing[side, i, b].astype(F32)
                        ).astype(BF16)

        def one(step, carry):
            other = (at.b + 1 + step) % 8
            send_or_copy(
                sums.at[other],
                final.at[:, lanes(at.b)],
                send_out,
                recv_out,
                (other, at.z),
                step == 7,
            )
            return carry

        lax.fori_loop(0, 8, one, 0)

    def end(self):
        for side in range(2):
            for i in range(3):

                @pl.when(self.hop(side) < 3 - i)
                def _(side=side, i=i):
                    wait_bytes(self.passing.at[side, i], self.send_sem.at[side, i])


def head_mask(h):
    lane = lax.broadcasted_iota(jnp.int32, (1, 128), 1)
    return jnp.where(lane // HEAD_DIM == h, 1.0, 0.0).astype(F32)


def slot_rows(index):
    return pl.ds(pl.multiple_of(index * 64, 64), 64)


def chip_rows(index):
    return pl.ds(pl.multiple_of(index * 256, 256), 256)


def core_rows(index):
    return pl.ds(pl.multiple_of(index * 1024, 1024), 1024)


class Inputs:
    small = x_hbm = cot_hbm = wq = wk = wv = wout = win = wback = None


def entries(table):
    return [(n, e) for n, e in vars(table).items() if n[0] != "_"]


class Results:
    out = ((128, 1024), BF16)
    gtok = ((128, 1024), BF16)
    w_in = ((2, 2, 128, 384), BF16)
    o_in = ((4, 128, 256), BF16)
    fin_in = ((128, 1024), BF16)
    fin_back = ((128, 1024), BF16)
    notes_in = ((4, 16, 128), F32)


class Scratch:
    small_here = ((16, 128), BF16)
    out_here = ((128, 1024), BF16)
    gtok_here = ((128, 1024), BF16)
    x = ((128, 1024), BF16)
    cot = ((128, 1024), BF16)
    xs = ((1024, 1024), BF16)
    wqkv = ((1024, 384), BF16)
    w_near = ((3, 128, 256), BF16)
    queries = ((1024, 128), BF16)
    keys_all = ((2048, 128), BF16)
    values_all = ((2048, 128), BF16)
    mixed = ((1024, 128), F32)
    log_sums = ((1024, 128), F32)
    att = ((128, 1024), BF16)
    wo = ((1024, 1024), BF16)
    par = ((8, 1024), F32)
    bins = ((1, 512), F32)
    wi = ((1024, 512), BF16)
    wb = ((1024, 512), BF16)
    smalls = ((8, 16, 128), BF16)
    smalls_z = ((4, 16, 128), BF16)
    smalls_sum = ((16, 128), BF16)
    proj = ((256, 384), F32)
    scores = ((256, 2048), F32)
    d_buf = ((256, 2048), F32)
    p_buf = ((256, 2048), BF16)
    att_send = ((1024, 128), BF16)
    n1 = ((128, 1024), F32)
    unit1 = ((128, 1024), F32)
    scale1 = ((128, 128), F32)
    d2 = ((128, 1024), F32)
    d1 = ((128, 1024), F32)
    db = ((128, 1024), BF16)
    norm_slots = ((4, 256, 1024), BF16)
    grad_slots = ((4, 256, 1024), BF16)
    hid = ((4, 256, 512), BF16)
    slope = ((4, 256, 512), F32)
    low = ((4, 256, 512), BF16)
    pre = ((128, 512), F32)
    terms = ((4, 256, 1024), F32)
    sib_out = ((2, 4, 128, 1024), BF16)
    sib_in = ((2, 4, 128, 1024), BF16)
    peer_out = ((2, 4, 128, 1024), BF16)
    peer_in = ((2, 4, 128, 1024), BF16)
    g_back = ((8, 128, 512), BF16)
    g_in = ((8, 128, 512), BF16)
    pass_back = ((2, 3, 8, 128, 128), BF16)
    pass_in = ((2, 3, 8, 128, 128), BF16)
    gs_back = ((8, 128, 128), BF16)
    gs_in = ((8, 128, 128), BF16)
    da_send = ((128, 1024), BF16)
    da = ((1024, 128), BF16)
    q_turned = ((128, 1024), BF16)
    da_turned = ((128, 1024), BF16)
    dq = ((1024, 128), F32)
    dk_turned = ((128, 2048), F32)
    dv_turned = ((128, 2048), F32)
    out_k = ((1024, 128), F32)
    out_v = ((1024, 128), F32)
    sib_k = ((1024, 128), F32)
    sib_v = ((1024, 128), F32)
    dqkv = ((1024, 384), BF16)
    x_sum = ((256, 1024), F32)
    x_own = ((64, 1024), F32)
    z_out = ((4, 64, 1024), BF16)
    z_in = ((4, 64, 1024), BF16)
    w_sib_out = ((4, 128, 384), F32)
    w_sib_in = ((4, 128, 384), F32)
    w_out = ((4, 128, 384), BF16)
    o_out = ((128, 1024), BF16)
    vec = ((8, 1024), F32)
    gbin = ((1, 512), F32)
    notes = ((8, 16, 128), F32)
    notes_p = ((8, 16, 128), F32)
    notes_sum = ((16, 128), F32)


class Arrivals:
    z = (4,)
    p = (4, 3, 2)
    wo = (3, 2)
    w = (3,)
    o = (5,)
    kv = (1,)
    misc = (12,)
    col = (6, 3)
    ga = (4, 3, 2)
    ga_sib = (4, 4)
    ex = (5, 4)
    ex_sib = (5, 4)
    zg = (2, 2, 3)
    kv2 = (2,)
    dx = (4, 3, 2)
    dz = (4,)
    ws = (4,)
    da = (4,)
    own = (4,)


class Departures:
    z = (1,)
    p = (1,)
    wo = (1,)
    w = (3,)
    o = (1,)
    kv = (1,)
    misc = (12,)
    col = (6, 3)
    ga = (2,)
    ex = (3,)
    zg = (2, 2, 3)
    kv2 = (1,)
    dx = (1,)
    dz = (1,)
    ws = (1,)


class Refs:
    pass


def layer_kernel(*refs):
    v = Refs()
    names = [n for table in (Inputs, Results, Scratch) for n, _ in entries(table)]
    names += ["r_" + n for n, _ in entries(Arrivals)] + ["s_" + n for n, _ in entries(Departures)]
    for name, ref in zip(names, refs):
        setattr(v, name, ref)
    at = Place()
    at.flat = at.b * 4 + at.z
    at.place = at.q * 4 + at.z
    at.parity = at.z % 2
    at.pair = 4 * (at.z // 2) + at.q
    def column(ref, rows, i):
        sems = [t.at[2 * i + k] for k in range(2) for t in (v.s_col, v.r_col)]
        return Column(at, ref, rows, sems)

    col_in = column(v.wi, pl.ds(0, 1024), 0)
    col_back = [column(v.wb, pl.ds(512 * k, 512), 1 + k) for k in range(2)]
    gathers = [
        [
            Gather(at, slots, h, v.s_ga.at[i], v.r_ga.at[2 * i + h], v.r_ga_sib.at[2 * i + h])
            for h in range(2)
        ]
        for i, slots in enumerate((v.norm_slots, v.grad_slots))
    ]

    def exchange(i, side, rows):
        buffers = [t.at[side] for t in (v.sib_out, v.sib_in, v.peer_out, v.peer_in)]
        return Exchange(at, buffers, rows, v.s_ex.at[i // 2], v.r_ex.at[i], v.r_ex_sib.at[i])

    scatters = [
        [exchange(2 * i + h, i, pl.ds(64 * h, 64)) for h in range(2)] for i in range(2)
    ]
    out_scatter = exchange(4, 0, pl.ds(0, 128))
    upper = at.z // 2
    at.planes = (at.z, at.z + 1 - 2 * at.parity, 2 - upper, 3 - 3 * upper)
    rows_spread = [
        Spread(
            at,
            lambda r, plane=plane: v.xs.at[slot_rows(at.chip(r) * 4 + plane)],
            lambda block, k: block.at[pl.ds(k * 32, 32)],
            v.s_p.at[0],
            v.r_p.at[i],
        )
        for i, plane in enumerate(at.planes)
    ]
    wo_spread = Spread(
        at,
        lambda r: v.wo.at[:, lanes(2 * at.chip(r) + at.c)],
        lambda block, k: block.at[pl.ds(k * 512, 512)],
        v.s_wo.at[0],
        v.r_wo,
    )
    sum_in = ColumnSum(at, v.g_in, v.pass_in, v.s_zg.at[0], v.r_zg.at[0])
    sum_back = ColumnSum(at, v.g_back, v.pass_back, v.s_zg.at[1], v.r_zg.at[1])
    place_small(at, v)
    pltpu.make_async_copy(v.x_hbm, v.x, v.r_own.at[0]).start()
    pltpu.make_async_copy(v.cot_hbm, v.cot, v.r_own.at[1]).start()
    greet_all(at)
    wait_bytes(v.x, v.r_own.at[0])
    attend_phase(at, v, col_in, col_back, rows_spread, wo_spread)
    ffn_phase(at, v, col_in, col_back, gathers, scatters, sum_back, sum_in)
    grads_phase(at, v, out_scatter, sum_in, sum_back)
    end_phase(at, v, (sum_in, sum_back, col_in, *col_back))


def place_small(at, v):
    def iota(shape, axis):
        return lax.broadcasted_iota(jnp.int32, shape, axis)

    spread = jnp.where(
        iota((8, 256), 1) // 32 == iota((8, 256), 0), v.small[0:1, 0:256], 0.0
    ).astype(BF16)
    lane = iota((256, 128), 1)
    source = iota((256, 128), 0) % 32 + 32 * at.z
    picked = jnp.where(lane == source, 1.0, 0.0).astype(BF16)
    top = dot_nn(spread, picked)
    units = jnp.where(iota((8, 128), 0) == at.z, v.small[0:1, 256:384], 0.0)
    v.small_here[...] = jnp.concatenate((top, units), axis=0).astype(BF16)


def attend_phase(at, v, col_in, col_back, rows_spread, wo_spread):
    xs, wqkv, wo = v.xs, v.wqkv, v.wo
    parity, pair = at.parity, at.pair

    pltpu.make_async_copy(v.small_here, v.smalls_z.at[at.z], v.r_misc.at[1]).start()
    for dz in range(1, 4):
        remote(
            v.small_here,
            v.smalls_z.at[at.z],
            v.s_misc.at[1],
            v.r_misc.at[1],
            (at.b, (at.z + dz) % 4),
        ).start()

    pltpu.make_async_copy(
        v.x.at[slot_rows(parity)], xs.at[slot_rows(at.place)], v.r_z.at[at.z]
    ).start()
    weights = (v.wq, v.wk, v.wv)
    for i in (1, 2, 3):
        plane = at.planes[i]
        remote(
            v.x.at[slot_rows(plane % 2)],
            xs.at[slot_rows(at.place)],
            v.s_z.at[0],
            v.r_z.at[at.z],
            (at.b, plane),
        ).start()
        if i == 1:
            for k, w in enumerate(weights):
                remote(
                    w, v.w_near.at[k], v.s_w.at[2], v.r_w.at[2], (at.b, at.planes[1])
                ).start()

    part = wo.at[pl.ds(pl.multiple_of(at.z * 256, 256), 256), lanes(at.b)]
    pltpu.make_async_copy(v.wout, part, v.r_o.at[4]).start()
    for i in (1, 2, 3):
        remote(v.wout, part, v.s_o.at[0], v.r_o.at[4], (at.b, at.planes[i])).start()

    def to_pairs(sources, group):
        for dx in range(2):
            column = (at.x + dx) % 2
            for k, w in enumerate(sources):
                send_or_copy(
                    w.at[:, lanes(column)],
                    wqkv.at[lanes(at.b), pl.ds(k * 128, 128)],
                    v.s_w.at[0],
                    v.r_w.at[0],
                    (2 * (group * 2 + column) + at.c, at.z),
                    None if dx else group == at.y,
                )

    for i in range(4):
        wait_bytes(rows_spread[i].block(0), v.r_z.at[at.planes[i]])
        rows_spread[i].start()
        if i == 0:
            to_pairs(weights, parity)
            wait_bytes(v.smalls_z, v.r_misc.at[1])
            total = v.smalls_z[0].astype(F32)
            for z in range(1, 4):
                total += v.smalls_z[z].astype(F32)
            v.smalls_sum[...] = total.astype(BF16)
            mine = v.smalls.at[at.b]
            pltpu.make_async_copy(v.smalls_sum, mine, v.r_misc.at[10]).start()

            def spread(step, carry):
                remote(
                    v.smalls_sum,
                    mine,
                    v.s_misc.at[10],
                    v.r_misc.at[10],
                    ((at.b + step) % 8, at.z),
                ).start()
                return carry

            lax.fori_loop(1, 8, spread, 0)
        if i == 1:
            plane_weights(at, v.win, v.wi, v.s_misc.at[0], v.r_misc.at[0])
            wait_bytes(v.w_near, v.r_w.at[2])
            to_pairs([v.w_near.at[k] for k in range(3)], 1 - parity)
        if i == 3:
            wait_bytes(v.wi.at[:, pl.ds(0, 128)], v.r_misc.at[0])
            col_in.send(0)
        if i:
            rows_spread[i - 1].relay()

    wait_bytes(wqkv.at[pl.ds(0, 512)], v.r_w.at[0])
    for r in range(4):
        part = wqkv.at[lanes(2 * at.chip(r) + at.c)]
        remote(part, part, v.s_w.at[1], v.r_w.at[1], at.sibling()).start()
    wait_bytes(v.smalls, v.r_misc.at[10])
    for b in range(8):
        v.par[:, 128 * b : 128 * b + 128] = v.smalls[b].astype(F32)[0:8]
    row = lax.broadcasted_iota(jnp.int32, (8, 128), 0)
    for h in range(4):
        rows = v.smalls[2 * h + at.b // 4].astype(F32)[8:16]
        rows = jnp.where(row == at.b % 4, rows, 0.0)
        v.bins[0:1, 128 * h : 128 * h + 128] = jnp.sum(rows, axis=0, keepdims=True)
    bias_q = v.par[0:1, lanes(pair)]
    bias_v = v.par[1:2, lanes(pair)]
    wait_bytes(wqkv.at[pl.ds(0, 512)], v.r_w.at[1])

    def project(r):
        chip = at.chip(r)
        if r:
            for i in range(4):
                rows_spread[i].rest(r)
        rows = chip_rows(chip)
        v.proj[...] = dot_nn(xs[rows], wqkv[...])
        v.queries[rows] = (v.proj[:, 0:128] + bias_q).astype(BF16)
        own_rows = chip_rows(at.c * 4 + chip)
        v.keys_all[own_rows] = v.proj[:, 128:256].astype(BF16)
        v.values_all[own_rows] = (v.proj[:, 256:384] + bias_v).astype(BF16)
        for k, ref in enumerate((v.keys_all, v.values_all)):
            view = ref.at[own_rows]
            remote(view, view, v.s_kv.at[0], v.r_kv.at[0], at.sibling()).start()

    project(0)
    rows_spread[3].relay()

    whole = wo_spread.block(0)
    wait_bytes(whole, v.r_o.at[4])
    wo_spread.start()
    remote(whole, whole, v.s_o.at[0], v.r_o.at[0], at.sibling()).start()
    plane_weights(at, v.wback, v.wb, v.s_misc.at[2], v.r_misc.at[2])

    col_in.arrive(0)
    col_in.send(1)
    for r in (1, 2, 3):
        project(r)

    wait_bytes(v.keys_all, v.r_kv.at[0])

    scores = v.scores

    def attend(step, carry):
        chip = (at.q + 1 + step) % 4
        rows = chip_rows(chip)
        outs = []
        logs = []
        for h in range(2):
            q = (v.queries[rows].astype(F32) * head_mask(h) * HEAD_DIM**-0.5).astype(BF16)
            scores[...] = contract_cols(q, v.keys_all[...])
            top = jnp.max(scores[...], axis=-1, keepdims=True)
            weights = jnp.exp(scores[...] - top)
            total = jnp.sum(weights, axis=-1, keepdims=True)
            outs.append(dot_nn(weights.astype(BF16), v.values_all[...]) / total)
            logs.append(top + jnp.log(total))
        first = head_mask(0) > 0.5
        merged = jnp.where(first, outs[0], outs[1])
        v.mixed[rows] = merged
        v.log_sums[rows] = jnp.where(first, logs[0], logs[1])
        v.att_send[rows] = merged.astype(BF16)
        for k in range(4):
            plane = (at.z + 1 + k) % 4
            send_or_copy(
                v.att_send.at[slot_rows(chip * 4 + plane)],
                v.att.at[slot_rows(parity), lanes(pair)],
                v.s_misc.at[3],
                v.r_misc.at[3],
                (2 * chip + at.c, plane),
                step == 3 if k == 3 else None,
            )

        @pl.when(step == 0)
        def _():
            wo_spread.relay()
            col_in.arrive(1)
            col_in.send(2)

        return carry

    lax.fori_loop(0, 4, attend, 0)

    wait_bytes(v.wb.at[:, pl.ds(0, 128)], v.r_misc.at[2])
    for half_back in col_back:
        half_back.send(0)
    for r in (1, 2, 3):
        wo_spread.rest(r)
        part = wo_spread.block(r)
        remote(part, part, v.s_o.at[0], v.r_o.at[r], at.sibling()).start()
    for r in range(4):
        wait_bytes(whole, v.r_o.at[r])
    wait_bytes(v.att, v.r_misc.at[3])


def ffn_phase(at, v, col_in, col_back, gathers, scatters, sum_back, sum_in):
    n1, terms, peer_in = v.n1, v.terms, v.peer_in

    def param(i):
        return v.par[i : i + 1, :]

    def local(h, i):
        return pl.ds(64 * h + 32 * i, 32)

    def chip_part(h, i):
        return pl.ds(pl.multiple_of(h * 128 + at.c * 64 + 32 * i, 32), 32)

    wait_bytes(v.cot, v.r_own.at[1])
    n1[...] = dot_nn(v.att[...], v.wo[...])
    for h in range(2):
        for i in range(2):
            rows = local(h, i)
            unit, scale = norm_rows(v.x[rows].astype(F32) + n1[rows] + param(2))
            v.unit1[rows] = unit
            v.scale1[rows] = jnp.broadcast_to(scale, (32, 128))
            normed = unit * param(3) + param(4)
            n1[rows] = normed
            v.norm_slots[at.q, chip_part(h, i)] = normed.astype(BF16)
        gathers[0][h].start()

    def hidden(h, r):
        chip = gathers[0][h].ready(r)
        v.pre[...] = dot_nn(v.norm_slots[chip, pl.ds(128 * h, 128)], v.wi[...])

        def activate(i, carry):
            rows = pl.ds(pl.multiple_of(i * 32, 32), 32)
            into = pl.ds(pl.multiple_of(128 * h + i * 32, 32), 32)
            u = v.pre[rows] + v.bins[...]
            cdf = 0.5 * (1.0 + lax.erf(u * math.sqrt(0.5)))
            bell = jnp.exp(-0.5 * u * u) * (1.0 / math.sqrt(2.0 * math.pi))
            v.hid[r, into] = (u * cdf).astype(BF16)
            v.slope[r, into] = cdf + u * bell
            return carry

        lax.fori_loop(0, 4, activate, 0)

    def neighbours(gather):
        gather.relay()
        gather.forward(1)
        gather.forward(2)

    neighbours(gathers[0][0])
    for half_back in col_back:
        half_back.arrive(0)
        half_back.send(1)
    gathers[0][1].relay()
    col_in.arrive(2)
    hidden(0, 0)
    gathers[0][1].forward(1)
    gathers[0][1].forward(2)
    hidden(1, 0)
    hidden(0, 1)
    hidden(0, 2)
    col_back[0].arrive(1)
    col_back[0].send(2)
    gathers[0][0].forward(3)
    hidden(1, 1)
    gathers[0][1].forward(3)
    col_back[1].arrive(1)
    col_back[1].send(2)
    hidden(1, 2)
    hidden(0, 3)
    hidden(1, 3)
    for half_back in col_back:
        half_back.arrive(2)

    def to_plane(scatter, done, h, r, product):
        terms[r, pl.ds(128 * h, 128)] = product
        scatter[h].put(r, terms[r, part_rows(h, 1 - at.c)])
        done.append((h, r))
        if len(done) > 3:
            pass_on(scatter, *done[-4])

    def pass_on(scatter, h, r):
        total = scatter[h].add(r, terms[r, part_rows(h, at.c)])
        if r == 0:
            terms[0, part_rows(h, at.c)] = total

    done = []
    for h in range(2):
        for r in (3, 1, 2, 0):
            product = contract_cols(v.hid[r, pl.ds(128 * h, 128)], v.wb[...])
            to_plane(scatters[0], done, h, r, product)
    for one in done[-3:]:
        pass_on(scatters[0], *one)
    for h in range(2):
        scatters[0][h].relay()

    def peers(side, rows):
        return peer_in[side, 1, rows].astype(F32) + peer_in[side, 2, rows].astype(F32)

    def column_sums(parts, sums):
        return tuple(
            kept + jnp.sum(part.reshape(4, 8, 1024), axis=0) for kept, part in zip(sums, parts)
        )

    gbin = [jnp.zeros((8, 512), F32)]
    done = []

    def hidden_grad(h, r):
        chip = gathers[1][h].ready(r)
        v.pre[...] = dot_nn(v.grad_slots[chip, pl.ds(128 * h, 128)], v.wb[...])

        def deactivate(i, carry):
            rows = pl.ds(pl.multiple_of(i * 32, 32), 32)
            into = pl.ds(pl.multiple_of(128 * h + i * 32, 32), 32)
            low = (v.pre[rows] * v.slope[r, into]).astype(BF16)
            v.low[r, into] = low
            return carry + jnp.sum(low.astype(F32).reshape(4, 8, 512), axis=0)

        gbin[0] = lax.fori_loop(0, 4, deactivate, gbin[0])
        product = contract_cols(v.low[r, pl.ds(128 * h, 128)], v.wi[...])
        to_plane(scatters[1], done, h, r, product)

    sums = tuple(jnp.zeros((8, 1024), F32) for _ in range(3))
    for h in range(2):
        scatters[0][h].arrive()
        for i in range(2):
            rows = local(h, i)
            total = terms[0, chip_part(h, i)] + peers(0, rows)
            unit, scale = norm_rows(n1[rows] + total + param(5))
            v.out_here[rows] = (unit * param(6) + param(7)).astype(BF16)
            g = v.cot[rows].astype(F32)
            d = norm_back(g * param(6), unit, scale)
            v.d2[rows] = d
            low = d.astype(BF16)
            v.grad_slots[at.q, chip_part(h, i)] = low
            sums = column_sums((g * unit, g, low.astype(F32)), sums)
        gathers[1][h].start()
        if h == 0:
            hidden_grad(0, 0)
    pltpu.make_async_copy(v.out_here, v.out, v.r_own.at[2]).start()
    for row, total in zip((6, 7, 5), sums):
        v.vec[row : row + 1, :] = jnp.sum(total, axis=0, keepdims=True)

    def weight_grad(slots, right, into):
        def one(step, carry):
            other = (at.q + step) % 4
            total = jnp.zeros((256, 512), F32)
            for r in range(4):
                total += contract_rows(slots[at.chip(r), :, chip_rows(other)], right[r])
            into[2 * other] = total[0:128].astype(BF16)
            into[2 * other + 1] = total[128:256].astype(BF16)
            return carry

        lax.fori_loop(0, 4, one, 0)

    neighbours(gathers[1][0])
    hidden_grad(1, 0)
    hidden_grad(0, 1)
    neighbours(gathers[1][1])
    hidden_grad(0, 2)
    gathers[1][0].forward(3)
    hidden_grad(1, 1)
    hidden_grad(0, 3)
    gathers[1][1].forward(3)
    hidden_grad(1, 2)
    hidden_grad(1, 3)
    for one in done[-3:]:
        pass_on(scatters[1], *one)
    v.gbin[...] = jnp.sum(gbin[0], axis=0, keepdims=True)

    sums = tuple(jnp.zeros((8, 1024), F32) for _ in range(3))
    weight_grad(v.grad_slots, v.hid, v.g_back)
    wait_bytes(v.xs.at[pl.ds(0, 896)], v.s_ga.at[1])
    sum_back.begin((0,))
    scatters[1][0].relay()
    weight_grad(v.norm_slots, v.low, v.g_in)
    scatters[1][1].relay()
    for h in range(2):
        scatters[1][h].arrive()
        for i in range(2):
            rows = local(h, i)
            total = v.d2[rows] + terms[0, chip_part(h, i)] + peers(1, rows)
            unit = v.unit1[rows]
            d = norm_back(total * param(3), unit, v.scale1[rows][:, :1])
            v.d1[rows] = d
            low = d.astype(BF16)
            v.db[rows] = low
            sums = column_sums((total * unit, total, low.astype(F32)), sums)
        rows = pl.ds(64 * h, 64)
        v.da_send[rows] = contract_cols(v.db[rows], v.wo[...]).astype(BF16)
        for r in range(4):
            chip = at.chip(r)
            for plane in (h, h + 2):
                pair = 2 * (plane - h) + chip
                send_or_copy(
                    v.da_send.at[rows, lanes(pair)],
                    v.da.at[slot_rows(at.place)],
                    v.s_misc.at[4],
                    v.r_da.at[r],
                    (2 * chip + at.c, plane),
                    None if r else at.z == plane,
                )

    for row, total in zip((3, 4, 2), sums):
        v.vec[row : row + 1, :] = jnp.sum(total, axis=0, keepdims=True)
    v.vec[0:2, :] = jnp.zeros((2, 1024), F32)
    for i in range(3):
        if i:
            sum_back.begin((i,))
        sum_in.begin((i,))


def grads_phase(at, v, out_scatter, sum_in, sum_back):
    xs, wqkv, terms = v.xs, v.wqkv, v.terms
    parity, pair = at.parity, at.pair

    wait_bytes(xs.at[pl.ds(0, 896)], v.s_ex.at[0])
    for r in (3, 1, 2, 0):
        for core in (1 - at.c, at.c):
            part = contract_rows(v.db[:, lanes(2 * at.chip(r) + core)], v.att[...])
            if core is at.c:
                terms[r, 0:128] = part
            else:
                out_scatter.put(r, part)

    v.q_turned[...] = v.queries[...].astype(F32).T.astype(BF16)
    v.dk_turned[...] = jnp.zeros_like(v.dk_turned)
    v.dv_turned[...] = jnp.zeros_like(v.dv_turned)
    for r in (3, 1, 2):
        out_scatter.add(r, terms[r, 0:128])
    terms[0, 0:128] = out_scatter.add(0, terms[0, 0:128])
    sum_back.relay(1, 0)
    wait_bytes(v.da.at[chip_rows(at.q)], v.r_da.at[0])
    s_buf, d_buf, p_buf = v.scores, v.d_buf, v.p_buf

    def attend(step, carry):
        chip = ((at.y + step // 2) % 2) * 2 + (at.x + step % 2) % 2
        rows = chip_rows(chip)

        @pl.when(step > 0)
        def _():
            wait_bytes(v.da.at[rows], v.r_da.at[step])

        v.da_turned[:, rows] = v.da[rows].astype(F32).T.astype(BF16)
        parts = []
        for h in range(2):
            mask = head_mask(h)
            grad = v.da[rows].astype(F32) * mask
            delta = jnp.sum(grad * v.mixed[rows], axis=-1, keepdims=True)
            q = (v.queries[rows].astype(F32) * mask * HEAD_DIM**-0.5).astype(BF16)
            s_buf[...] = contract_cols(q, v.keys_all[...])
            d_buf[...] = contract_cols(grad.astype(BF16), v.values_all[...])
            logs = v.log_sums[rows][:, h * HEAD_DIM : h * HEAD_DIM + 1]
            probs = jnp.exp(s_buf[...] - logs)
            p_buf[...] = probs.astype(BF16)
            low = (probs * (d_buf[...] - delta)).astype(BF16)
            band = pl.ds(h * HEAD_DIM, HEAD_DIM)
            v.dv_turned[band] += dot_nn(v.da_turned[band, rows], p_buf[...])
            v.dk_turned[band] += dot_nn(v.q_turned[band, rows], low)
            parts.append(dot_nn(low, v.keys_all[...]))
        v.dq[rows] = jnp.where(head_mask(0) > 0.5, parts[0], parts[1]) * HEAD_DIM**-0.5

        @pl.when(step == 1)
        def _():
            out_scatter.relay()
            sum_back.relay(2, 0)
            sum_in.relay(1, 0)

        @pl.when(step == 3)
        def _():
            sum_back.relay(1, 1)

        return carry

    lax.fori_loop(0, 4, attend, 0)

    other = core_rows(1 - at.c)
    mine = core_rows(at.c)
    v.out_k[...] = v.dk_turned[:, other].T * HEAD_DIM**-0.5
    v.out_v[...] = v.dv_turned[:, other].T
    for k, (ref, into) in enumerate(((v.out_k, v.sib_k), (v.out_v, v.sib_v))):
        remote(ref, into, v.s_kv2.at[0], v.r_kv2.at[k], at.sibling()).start()
    dqkv = v.dqkv
    low = v.dq[...].astype(BF16)
    dqkv[:, 0:128] = low
    v.vec[0:1, lanes(pair)] = jnp.sum(low.astype(F32), axis=0, keepdims=True)
    out_scatter.arrive()
    peer_in = v.peer_in.at[0]

    def out_rows(rows):
        total = terms[0, rows] + peer_in[1, rows].astype(F32) + peer_in[2, rows].astype(F32)
        v.o_out[rows] = total.astype(BF16)

    by_rows(128, 32, out_rows)
    wide = pl.ds(pl.multiple_of(at.z * 256, 256), 256)
    pltpu.make_async_copy(v.o_out.at[:, wide], v.o_in.at[0], v.r_misc.at[8]).start()
    for dz in range(1, 4):
        plane = (at.z + dz) % 4
        remote(
            v.o_out.at[:, pl.ds(pl.multiple_of(plane * 256, 256), 256)],
            v.o_in.at[dz],
            v.s_misc.at[8],
            v.r_misc.at[8],
            (at.b, plane),
        ).start()

    own_k = v.dk_turned[:, mine].T * HEAD_DIM**-0.5
    wait_bytes(v.sib_k, v.r_kv2.at[0])
    dqkv[:, 128:256] = (own_k + v.sib_k[...]).astype(BF16)
    own_v = v.dv_turned[:, mine].T
    wait_bytes(v.sib_v, v.r_kv2.at[1])
    low = (own_v + v.sib_v[...]).astype(BF16)
    dqkv[:, 256:384] = low
    v.vec[1:2, lanes(pair)] = jnp.sum(low.astype(F32), axis=0, keepdims=True)

    notes = v.notes
    for b in range(8):
        notes[b, 0:8] = v.vec[:, 128 * b : 128 * b + 128]
        notes[b, 8:16] = jnp.zeros((8, 128), F32)
    row = lax.broadcasted_iota(jnp.int32, (8, 128), 0)
    for h in range(4):
        notes[2 * h + at.b // 4, 8:16] = jnp.where(
            row == at.b % 4, v.gbin[0:1, 128 * h : 128 * h + 128], 0.0
        )
    pltpu.make_async_copy(notes.at[at.b], v.notes_p.at[at.b], v.r_misc.at[5]).start()

    def spread(step, carry):
        to = (at.b + step) % 8
        remote(
            notes.at[to], v.notes_p.at[at.b], v.s_misc.at[5], v.r_misc.at[5], (to, at.z)
        ).start()
        return carry

    lax.fori_loop(1, 8, spread, 0)

    wait_bytes(xs.at[pl.ds(0, 896)], v.s_ga.at[0])
    x_out, x_in, x_via = v.norm_slots, v.grad_slots.at[0:2], v.grad_slots.at[2:4]
    for r in (3, 1, 2, 0):
        part = contract_cols(dqkv[chip_rows(at.chip(r))], wqkv[...])
        if r:
            x_out[r] = part.astype(BF16)
        else:
            v.x_sum[...] = part
    def piece(dz, k):
        return pl.ds(pl.multiple_of(((at.z + dz) % 4) * 64 + 32 * k, 32), 32)

    order = (2, 1, 3, 0)

    def send_dx(dz, via):
        for r, k in ((1, 0), (2, 1)):
            rows = piece(dz, k)
            remote(
                x_out.at[3 if via else r, rows],
                x_via.at[r - 1, rows] if via else x_in.at[r - 1, rows],
                v.s_dx.at[0],
                v.r_dx.at[dz, 0 if via else r, k],
                at.peer(r),
            ).start()

    def relay_dx(dz):
        for r, k in ((2, 0), (1, 1)):
            rows = piece(dz, k)
            wait_bytes(x_via.at[k, rows], v.r_dx.at[dz, 0, k])
            x_out[r, rows] = (
                x_out[r, rows].astype(F32) + x_via[k, rows].astype(F32)
            ).astype(BF16)
            remote(
                x_out.at[r, rows],
                x_in.at[r - 1, rows],
                v.s_dx.at[0],
                v.r_dx.at[dz, r, k],
                at.peer(r),
            ).start()

    z_out, z_in = v.z_out, v.z_in
    def column_dx(dz):
        plane = (at.z + dz) % 4
        rows = slot_rows(plane)
        for r in (1, 2):
            for k in range(2):
                wait_bytes(x_in.at[r - 1, piece(dz, k)], v.r_dx.at[dz, r, k])
        total = v.x_sum[rows] + x_in[0, rows].astype(F32) + x_in[1, rows].astype(F32)
        if dz:
            z_out[dz] = total.astype(BF16)
            remote(
                z_out.at[dz], z_in.at[dz], v.s_dz.at[0], v.r_dz.at[dz], (at.b, plane)
            ).start()
        else:
            v.x_own[...] = total

    def begin_dx(dz):
        send_dx(dz, True)
        send_dx(dz, False)

    begin_dx(2)
    begin_dx(1)
    def features(b):
        return contract_rows(xs[:, lanes(b)], dqkv[...])

    for r in range(4):
        v.w_sib_out[r] = features(2 * at.chip(r) + 1 - at.c)
        remote(
            v.w_sib_out.at[r], v.w_sib_in.at[r], v.s_ws.at[0], v.r_ws.at[r], at.sibling()
        ).start()
    relay_dx(2)
    begin_dx(3)
    sum_in.relay(1, 1)
    sum_in.relay(2, 0)
    relay_dx(1)
    begin_dx(0)
    column_dx(2)
    relay_dx(3)
    column_dx(1)
    relay_dx(0)
    column_dx(3)
    plane_w = 2 * (at.z // 2) + at.y
    for r in range(4):
        total = features(2 * at.chip(r) + at.c)
        wait_bytes(v.w_sib_in.at[r], v.r_ws.at[r])
        v.w_out[r] = (total + v.w_sib_in[r]).astype(BF16)
        send_or_copy(
            v.w_out.at[r],
            v.w_in.at[parity, at.x],
            v.s_misc.at[6],
            v.r_misc.at[6],
            at.peer(r)[:1] + (plane_w,),
            plane_w == at.z if r == 0 else None,
        )

    sum_back.finish(v.gs_back, v.fin_back, v.s_misc.at[7], v.r_misc.at[7])
    sum_in.finish(v.gs_in, v.fin_in, v.s_misc.at[9], v.r_misc.at[9])
    wait_bytes(v.notes_p, v.r_misc.at[5])
    total = v.notes_p[0]
    for b in range(1, 8):
        total += v.notes_p[b]
    v.notes_sum[...] = total
    mine = v.notes_in.at[at.z]
    pltpu.make_async_copy(v.notes_sum, mine, v.r_misc.at[11]).start()
    for dz in range(1, 4):
        remote(
            v.notes_sum, mine, v.s_misc.at[11], v.r_misc.at[11], (at.b, (at.z + dz) % 4)
        ).start()

    column_dx(0)
    for dz in (1, 2, 3):
        wait_bytes(z_in.at[dz], v.r_dz.at[dz])
    same = slot_rows(parity)
    v.gtok_here[same] = (v.d1[same] + v.x_own[...] + z_in[2].astype(F32)).astype(BF16)
    cross = slot_rows(1 - parity)
    v.gtok_here[cross] = (v.d1[cross] + z_in[1].astype(F32) + z_in[3].astype(F32)).astype(BF16)

    pltpu.make_async_copy(v.gtok_here, v.gtok, v.r_own.at[3]).start()
    wait_bytes(v.o_in, v.r_misc.at[8])
    wait_bytes(v.w_in, v.r_misc.at[6])
    wait_bytes(v.notes_in, v.r_misc.at[11])
    wait_bytes(v.fin_back, v.r_misc.at[7])
    wait_bytes(v.fin_in, v.r_misc.at[9])


def end_phase(at, v, ends):
    wait_bytes(v.out_here, v.r_own.at[2])
    for one in ends:
        one.end()

    def rows(n):
        return v.xs.at[pl.ds(0, n)]

    wait_bytes(rows(192), v.s_z.at[0])
    wait_bytes(rows(768), v.s_p.at[0])
    wait_bytes(rows(384), v.s_wo.at[0])
    wait_bytes(rows(608), v.s_o.at[0])
    wait_bytes(rows(256), v.s_kv.at[0])
    for i in (1, 2):
        wait_bytes(rows(896), v.s_ex.at[i])
    wait_bytes(rows(768), v.s_dx.at[0])
    wait_bytes(rows(192), v.s_dz.at[0])
    wait_bytes(v.w_sib_out, v.s_ws.at[0])
    wait_bytes(rows(512), v.s_kv2.at[0])
    wait_bytes(v.wqkv.at[pl.ds(0, 384)], v.s_w.at[0])
    wait_bytes(v.wqkv.at[pl.ds(0, 512)], v.s_w.at[1])
    wait_bytes(v.w_near, v.s_w.at[2])
    seven = v.wi.at[pl.ds(0, 896), pl.ds(0, 128)]
    for i in (0, 2, 7, 9):
        wait_bytes(seven, v.s_misc.at[i])
    wait_bytes(v.smalls.at[pl.ds(0, 3)], v.s_misc.at[1])
    wait_bytes(v.smalls.at[pl.ds(0, 7)], v.s_misc.at[10])
    for i in (3, 4):
        wait_bytes(v.att_send.at[pl.ds(0, 960)], v.s_misc.at[i])
    wait_bytes(v.notes.at[pl.ds(0, 7)], v.s_misc.at[5])
    wait_bytes(v.notes.at[pl.ds(0, 3)], v.s_misc.at[11])
    plane_w = 2 * (at.z // 2) + at.y

    @pl.when(plane_w == at.z)
    def _():
        wait_bytes(v.w_out.at[pl.ds(0, 3)], v.s_misc.at[6])

    @pl.when(plane_w != at.z)
    def _():
        wait_bytes(v.w_out, v.s_misc.at[6])

    wait_bytes(v.o_in.at[pl.ds(0, 3)], v.s_misc.at[8])
    wait_bytes(v.gtok_here, v.r_own.at[3])


def finish_kernel(
    place_ref,
    out_in,
    gtok_in,
    w_in,
    o_in,
    fin_in,
    fin_back,
    notes_in,
    out_ref,
    gtok_ref,
    gq_ref,
    gk_ref,
    gv_ref,
    gout_ref,
    gwin_ref,
    gwback_ref,
    bin_ref,
    *vector_refs,
):
    out_ref[...] = out_in[...]
    gtok_ref[...] = gtok_in[...]
    for x in range(2):
        total = w_in[0, x].astype(F32) + w_in[1, x].astype(F32)
        for k, ref in enumerate((gq_ref, gk_ref, gv_ref)):
            ref[:, 128 * x : 128 * x + 128] = total[:, 128 * k : 128 * k + 128]
    gout_ref[...] = (
        o_in[0].astype(F32) + o_in[1].astype(F32) + o_in[2].astype(F32) + o_in[3].astype(F32)
    ).T
    gwin_ref[...] = fin_in[...].astype(F32)
    gwback_ref[...] = fin_back[...].astype(F32)
    total = notes_in[0] + notes_in[1] + notes_in[2] + notes_in[3]
    z = place_ref[0]
    part = jnp.zeros((8, 32), F32)
    units = jnp.zeros((1, 128), F32)
    for k in range(4):
        part += jnp.where(z == k, total[0:8, 32 * k : 32 * k + 32], 0.0)
        units += jnp.where(z == k, total[8 + k : 9 + k], 0.0)
    for j, ref in enumerate(vector_refs):
        ref[...] = part[j]
    bin_ref[...] = units[0]


def vmem():
    return pl.BlockSpec(memory_space=pltpu.VMEM)


def run_layer(*args):
    results = [e for _, e in entries(Results)]
    scratch = [pltpu.VMEM(s, t) for _, (s, t) in entries(Scratch)]
    for _, shape in entries(Arrivals) + entries(Departures):
        scratch.append(DMA(shape))
    return pl.pallas_call(
        layer_kernel,
        out_shape=[jax.ShapeDtypeStruct(s, t) for s, t in results],
        in_specs=[vmem()] + [pl.BlockSpec(memory_space=pl.ANY)] * (len(args) - 1),
        out_specs=[pl.BlockSpec(memory_space=pl.ANY)] * len(results),
        scratch_shapes=scratch,
        compiler_params=pltpu.CompilerParams(
            collective_id=1, has_side_effects=True, vmem_limit_bytes=VMEM_LIMIT
        ),
    )(*args)


def run_finish(*args):
    shapes = (
        ((128, 1024), BF16),
        ((128, 1024), BF16),
        ((128, 256), F32),
        ((128, 256), F32),
        ((128, 256), F32),
        ((256, 128), F32),
        ((128, 1024), F32),
        ((128, 1024), F32),
        ((128,), F32),
    ) + (((32,), F32),) * 8
    return pl.pallas_call(
        finish_kernel,
        out_shape=[jax.ShapeDtypeStruct(s, t) for s, t in shapes],
        in_specs=[pl.BlockSpec(memory_space=pltpu.SMEM)] + [vmem()] * (len(args) - 1),
        out_specs=[vmem()] * len(shapes),
        compiler_params=pltpu.CompilerParams(vmem_limit_bytes=VMEM_LIMIT),
    )(*args)


DMA = pltpu.SemaphoreType.DMA


def fast_device(
    tokens,
    w_query,
    w_key,
    w_value,
    w_out,
    b_query,
    b_value,
    b_out,
    norm1_gain,
    norm1_shift,
    w_in,
    w_back,
    b_in,
    b_back,
    norm2_gain,
    norm2_shift,
    cotangent,
):
    head_id = lax.axis_index("head")
    token_shape = tokens.shape
    model_dim = tokens.shape[2]
    x = tokens.reshape(-1, model_dim)
    vectors = (
        b_query,
        b_value,
        b_out,
        norm1_gain,
        norm1_shift,
        b_back,
        norm2_gain,
        norm2_shift,
        b_in,
    )
    small = jnp.concatenate(vectors).astype(F32).reshape(1, -1)
    results = run_layer(
        small, x, cotangent.reshape(-1, model_dim), w_query, w_key, w_value, w_out, w_in, w_back
    )
    output, grad_tokens, gq, gk, gv, gout, gw_in, gw_back, gb_in, *own = run_finish(
        head_id.astype(jnp.int32).reshape(1), *results
    )
    return (
        output.reshape(token_shape),
        grad_tokens.reshape(token_shape),
        gq,
        gk,
        gv,
        gout,
        own[0],
        own[1],
        own[2],
        own[3],
        own[4],
        gw_in,
        gw_back,
        gb_in,
        own[5],
        own[6],
        own[7],
    )


def solution(mesh):
    in_specs = (
        P(None, ("blk", "head"), None),
        P("blk", "head"),
        P("blk", "head"),
        P("blk", "head"),
        P("head", "blk"),
        P(("blk", "head")),
        P(("blk", "head")),
        P(("blk", "head")),
        P(("blk", "head")),
        P(("blk", "head")),
        P("blk", "head"),
        P("blk", "head"),
        P(("blk", "head")),
        P(("blk", "head")),
        P(("blk", "head")),
        P(("blk", "head")),
        P(None, ("blk", "head"), None),
    )
    out_specs = (
        P(None, ("blk", "head"), None),
        P(None, ("blk", "head"), None),
        P("blk", "head"),
        P("blk", "head"),
        P("blk", "head"),
        P("head", "blk"),
        P(("blk", "head")),
        P(("blk", "head")),
        P(("blk", "head")),
        P(("blk", "head")),
        P(("blk", "head")),
        P("blk", "head"),
        P("blk", "head"),
        P(("blk", "head")),
        P(("blk", "head")),
        P(("blk", "head")),
        P(("blk", "head")),
    )
    sizes = (mesh.shape["blk"], mesh.shape["head"])
    body = fast_device if sizes == (8, 4) else per_device
    return jax.shard_map(
        body, mesh=mesh, in_specs=in_specs, out_specs=out_specs, check_vma=False
    )
```

```python
import functools
import math

import jax
import jax.numpy as jnp
from jax import lax
from jax.experimental import pallas as pl
from jax.experimental.pallas import tpu as pltpu
from jax.sharding import PartitionSpec as P

HEAD_DIM = 64


NORM_EPS = 1e-05


def layer_norm(summed, gain, shift):
    centre = jnp.mean(summed, axis=-1, keepdims=True)
    centred = summed - centre
    spread = jnp.mean(centred * centred, axis=-1, keepdims=True)
    return centred * lax.rsqrt(spread + NORM_EPS) * gain + shift


def gelu_exact(inputs):
    return jax.nn.gelu(inputs, approximate=False)


def split_heads(packed):
    return packed.reshape(packed.shape[0], packed.shape[1], -1, HEAD_DIM)


def contract_rows(left, right):
    return lax.dot_general(
        left, right, (((0,), (0,)), ((), ())), preferred_element_type=jnp.float32
    )


def contract_cols(left, right):
    return lax.dot_general(
        left, right, (((1,), (1,)), ((), ())), preferred_element_type=jnp.float32
    )


def score_block(queries4, keys4):
    return jnp.einsum(
        "sqge,skge->sqgk", queries4, keys4, preferred_element_type=jnp.float32
    ) * HEAD_DIM ** (-0.5)


def score_grads(queries4, keys4, values4, grads4, log_sums, deltas):
    probs = jnp.exp(score_block(queries4, keys4) - log_sums[..., None])
    d_probs = jnp.einsum("sqge,skge->sqgk", grads4, values4, preferred_element_type=jnp.float32)
    d_scores = (probs * (d_probs - deltas[..., None])).astype(jnp.bfloat16)
    return (probs.astype(jnp.bfloat16), d_scores)


def token_rows(local):
    return lax.all_gather(local, "head", axis=1, tiled=True)


def token_partials(terms):
    return lax.psum_scatter(
        terms.astype(jnp.bfloat16), "head", scatter_dimension=1, tiled=True
    ).astype(jnp.float32)


def place_part(part, full_len, start):
    return lax.dynamic_update_slice_in_dim(jnp.zeros((full_len,), jnp.float32), part, start, 0)


def per_device(
    tokens,
    w_query,
    w_key,
    w_value,
    w_out,
    b_query,
    b_value,
    b_out,
    norm1_gain,
    norm1_shift,
    w_in,
    w_back,
    b_in,
    b_back,
    norm2_gain,
    norm2_shift,
    cotangent,
):
    f32 = jnp.float32
    bf16 = jnp.bfloat16
    score_scale = HEAD_DIM ** (-0.5)
    bq_full, bv_full, bo_full, gain_one, shift_one, bin_full, bback_full, gain_two, shift_two = (
        lax.all_gather(b_query, ("blk", "head"), axis=0, tiled=True),
        lax.all_gather(b_value, ("blk", "head"), axis=0, tiled=True),
        lax.all_gather(b_out, ("blk", "head"), axis=0, tiled=True),
        lax.all_gather(norm1_gain, ("blk", "head"), axis=0, tiled=True),
        lax.all_gather(norm1_shift, ("blk", "head"), axis=0, tiled=True),
        lax.all_gather(b_in, ("blk", "head"), axis=0, tiled=True),
        lax.all_gather(b_back, ("blk", "head"), axis=0, tiled=True),
        lax.all_gather(norm2_gain, ("blk", "head"), axis=0, tiled=True),
        lax.all_gather(norm2_shift, ("blk", "head"), axis=0, tiled=True),
    )
    attn_cols, out_rows, ffn_cols = (
        lax.all_gather(jnp.stack((w_query, w_key, w_value)), "blk", axis=1, tiled=True),
        lax.all_gather(w_out, "blk", axis=1, tiled=True),
        lax.all_gather(jnp.stack((w_in, w_back)), "blk", axis=1, tiled=True),
    )
    seq_count, local_len, model_dim = tokens.shape
    token_shape = (seq_count, local_len, model_dim)
    head_id = lax.axis_index("head")
    width_part = attn_cols.shape[2]
    bq_part = lax.dynamic_slice_in_dim(bq_full, head_id * width_part, width_part).astype(f32)
    bv_part = lax.dynamic_slice_in_dim(bv_full, head_id * width_part, width_part).astype(f32)
    wide_rows = token_rows(tokens)
    wide_len = wide_rows.shape[1]
    wide_flat = wide_rows.reshape(-1, model_dim)
    head_shape = (seq_count, wide_len, width_part)
    wide_shape = (seq_count, wide_len, model_dim)
    query_heads = (
        (jnp.dot(wide_flat, attn_cols[0], preferred_element_type=f32) + bq_part)
        .astype(bf16)
        .reshape(head_shape)
    )
    key_heads = (
        jnp.dot(wide_flat, attn_cols[1], preferred_element_type=f32)
        .astype(bf16)
        .reshape(head_shape)
    )
    value_heads = (
        (jnp.dot(wide_flat, attn_cols[2], preferred_element_type=f32) + bv_part)
        .astype(bf16)
        .reshape(head_shape)
    )
    query4 = split_heads(query_heads)
    key4 = split_heads(key_heads)
    value4 = split_heads(value_heads)
    stat_shape = query4.shape[:3]
    pieces = (
        lax.all_gather(key_heads, "blk", axis=1, tiled=True),
        lax.all_gather(value_heads, "blk", axis=1, tiled=True),
    )
    maxima = jnp.full(stat_shape, -1e30, f32)
    scores = score_block(query4, split_heads(pieces[0]))
    new_max = jnp.maximum(maxima, jnp.max(scores, axis=-1))
    weights = jnp.exp(scores - new_max[..., None])
    totals = jnp.sum(weights, axis=-1)
    summed = jnp.einsum(
        "sqgk,skge->sqge", weights.astype(bf16), split_heads(pieces[1]), preferred_element_type=f32
    )
    maxima, totals, summed = (new_max, totals, summed)
    log_sums = maxima + jnp.log(totals)
    attended4 = summed / totals[..., None]
    attended_heads = attended4.reshape(head_shape).astype(bf16)
    attended_flat = attended_heads.reshape(-1, width_part)
    branch_terms = jnp.dot(attended_flat, out_rows, preferred_element_type=f32).reshape(wide_shape)
    branch = token_partials(branch_terms).reshape(-1, model_dim) + bo_full.astype(f32)
    flat_rows = tokens.reshape(-1, model_dim)
    normed, norm1_pull = jax.vjp(
        layer_norm, flat_rows.astype(f32) + branch, gain_one.astype(f32), shift_one.astype(f32)
    )
    normed_low = normed.astype(bf16)
    ffn_full = lax.all_gather(ffn_cols, "head", axis=2, tiled=True)
    pre_act = jnp.dot(normed_low, ffn_full[0], preferred_element_type=f32) + bin_full.astype(f32)
    hidden_act, gelu_pull = jax.vjp(gelu_exact, pre_act)
    hidden_low = hidden_act.astype(bf16)
    ffn_out = contract_cols(hidden_low, ffn_full[1]) + bback_full.astype(f32)
    final, norm2_pull = jax.vjp(
        layer_norm, normed + ffn_out, gain_two.astype(f32), shift_two.astype(f32)
    )
    output = final.astype(bf16).reshape(token_shape)
    d_second, grad_norm2_gain, grad_norm2_shift = norm2_pull(
        cotangent.reshape(-1, model_dim).astype(f32)
    )
    d_ffn = d_second.astype(bf16)
    grad_b_back = jnp.sum(d_ffn.astype(f32), axis=0)
    grad_back_whole = contract_rows(d_ffn, hidden_low)
    d_hidden = jnp.dot(d_ffn, ffn_full[1], preferred_element_type=f32)
    d_pre = gelu_pull(d_hidden)[0].astype(bf16)
    grad_b_in = jnp.sum(d_pre.astype(f32), axis=0)
    grad_in_whole = contract_rows(normed_low, d_pre)
    ffn_grad_parts = lax.psum_scatter(
        jnp.stack((grad_in_whole, grad_back_whole)).astype(jnp.bfloat16),
        "head",
        scatter_dimension=2,
        tiled=True,
    ).astype(jnp.float32)
    d_normed = d_second + contract_cols(d_pre, ffn_full[0])
    d_first, grad_norm1_gain, grad_norm1_shift = norm1_pull(d_normed)
    d_branch = d_first.astype(bf16)
    grad_b_out = jnp.sum(d_branch.astype(f32), axis=0)
    wide_dbranch = token_rows(d_branch.reshape(token_shape)).reshape(-1, model_dim)
    grad_out_part = contract_rows(attended_flat, wide_dbranch)
    grad_heads = contract_cols(wide_dbranch, out_rows).astype(bf16).reshape(head_shape)
    grads4 = split_heads(grad_heads)
    deltas = jnp.sum(grads4.astype(f32) * attended4, axis=-1)
    row_stats = (
        lax.all_gather(log_sums, "blk", axis=1, tiled=True),
        lax.all_gather(deltas, "blk", axis=1, tiled=True),
    )
    pieces = (
        lax.all_gather(key_heads, "blk", axis=1, tiled=True),
        lax.all_gather(value_heads, "blk", axis=1, tiled=True),
        lax.all_gather(query_heads, "blk", axis=1, tiled=True),
        lax.all_gather(grad_heads, "blk", axis=1, tiled=True),
    )
    piece_keys = split_heads(pieces[0])
    piece_values = split_heads(pieces[1])
    piece_queries = split_heads(pieces[2])
    piece_grads = split_heads(pieces[3])
    piece_sums = row_stats[0]
    piece_deltas = row_stats[1]
    own_probs, own_scores = score_grads(query4, piece_keys, piece_values, grads4, log_sums, deltas)
    d_query = score_scale * jnp.einsum(
        "sqgk,skge->sqge", own_scores, piece_keys, preferred_element_type=f32
    )
    probs_low, d_scores = score_grads(
        piece_queries, key4, value4, piece_grads, piece_sums, piece_deltas
    )
    key_acc = score_scale * jnp.einsum(
        "sqgk,sqge->skge", d_scores, piece_queries, preferred_element_type=f32
    )
    value_acc = jnp.einsum("sqgk,sqge->skge", probs_low, piece_grads, preferred_element_type=f32)
    d_query_low = d_query.reshape(-1, width_part).astype(bf16)
    d_key_low = key_acc.reshape(-1, width_part).astype(bf16)
    d_value_low = value_acc.reshape(-1, width_part).astype(bf16)
    grad_b_query = place_part(
        jnp.sum(d_query_low.astype(f32), axis=0), model_dim, head_id * width_part
    )
    grad_b_value = place_part(
        jnp.sum(d_value_low.astype(f32), axis=0), model_dim, head_id * width_part
    )
    attn_grad_parts = jnp.stack(
        (
            contract_rows(wide_flat, d_query_low),
            contract_rows(wide_flat, d_key_low),
            contract_rows(wide_flat, d_value_low),
        )
    )
    token_terms = (
        contract_cols(d_query_low, attn_cols[0])
        + contract_cols(d_key_low, attn_cols[1])
        + contract_cols(d_value_low, attn_cols[2])
    )
    d_tokens = d_first + token_partials(token_terms.reshape(wide_shape)).reshape(-1, model_dim)
    grad_tokens = d_tokens.astype(bf16).reshape(token_shape)
    attn_sums, grad_w_out, ffn_sums = (
        lax.psum_scatter(attn_grad_parts, "blk", scatter_dimension=1, tiled=True),
        lax.psum_scatter(grad_out_part, "blk", scatter_dimension=1, tiled=True),
        lax.psum_scatter(ffn_grad_parts, "blk", scatter_dimension=1, tiled=True),
    )
    (
        grad_b_query,
        grad_b_value,
        grad_b_out,
        grad_norm1_gain,
        grad_norm1_shift,
        grad_b_in,
        grad_b_back,
        grad_norm2_gain,
        grad_norm2_shift,
    ) = (
        lax.psum_scatter(grad_b_query, ("blk", "head"), scatter_dimension=0, tiled=True),
        lax.psum_scatter(grad_b_value, ("blk", "head"), scatter_dimension=0, tiled=True),
        lax.psum_scatter(grad_b_out, ("blk", "head"), scatter_dimension=0, tiled=True),
        lax.psum_scatter(grad_norm1_gain, ("blk", "head"), scatter_dimension=0, tiled=True),
        lax.psum_scatter(grad_norm1_shift, ("blk", "head"), scatter_dimension=0, tiled=True),
        lax.psum_scatter(grad_b_in, ("blk", "head"), scatter_dimension=0, tiled=True),
        lax.psum_scatter(grad_b_back, ("blk", "head"), scatter_dimension=0, tiled=True),
        lax.psum_scatter(grad_norm2_gain, ("blk", "head"), scatter_dimension=0, tiled=True),
        lax.psum_scatter(grad_norm2_shift, ("blk", "head"), scatter_dimension=0, tiled=True),
    )
    return (
        output,
        grad_tokens,
        attn_sums[0],
        attn_sums[1],
        attn_sums[2],
        grad_w_out,
        grad_b_query,
        grad_b_value,
        grad_b_out,
        grad_norm1_gain,
        grad_norm1_shift,
        ffn_sums[0],
        ffn_sums[1],
        grad_b_in,
        grad_b_back,
        grad_norm2_gain,
        grad_norm2_shift,
    )


MESH = pl.DeviceIdType.MESH
F32 = jnp.float32
BF16 = jnp.bfloat16
VMEM_LIMIT = 62 * 2**20


def dot_nn(left, right):
    return jnp.dot(left, right, preferred_element_type=F32)


class Place:
    def __init__(self):
        self.b = lax.axis_index("blk")
        self.z = lax.axis_index("head")
        self.y = self.b // 4
        self.x = (self.b // 2) % 2
        self.c = self.b % 2
        self.q = self.b // 2

    def chip(self, r):
        return ((self.y + r // 2) % 2) * 2 + (self.x + r % 2) % 2

    def peer(self, r):
        return (2 * self.chip(r) + self.c, self.z)

    def sibling(self):
        return (2 * self.q + 1 - self.c, self.z)


def remote(src, dst, send_sem, recv_sem, device):
    return pltpu.make_async_remote_copy(
        src_ref=src,
        dst_ref=dst,
        send_sem=send_sem,
        recv_sem=recv_sem,
        device_id=device,
        device_id_type=MESH,
    )


def wait_bytes(view, sem):
    pltpu.make_async_copy(view, view, sem).wait()


def greet_all(at):
    barrier = pltpu.get_barrier_semaphore()
    flat = at.b * 4 + at.z

    def greet(step, carry):
        other = (flat + step) % 32
        pl.semaphore_signal(
            barrier, inc=1, device_id=(other // 4, other % 4), device_id_type=MESH
        )
        return carry

    lax.fori_loop(1, 32, greet, 0)
    pl.semaphore_wait(barrier, 31)


def half(core):
    return pl.ds(pl.multiple_of(core * 128, 128), 128)


def lanes(index):
    return pl.ds(pl.multiple_of(index * 128, 128), 128)


def by_rows(count, size, step):
    def body(i, carry):
        step(pl.ds(pl.multiple_of(i * size, size), size))
        return carry

    lax.fori_loop(0, count // size, body, 0)


class Spread:
    def __init__(self, at, block, part, send, recv):
        self.at, self.block, self.part = at, block, part
        self.send, self.recv = send, recv

    def start(self):
        mine = self.block(0)
        for i in (0, 1):
            for r, k in ((1, i), (2, 1 - i)):
                piece = self.part(mine, k)
                remote(piece, piece, self.send, self.recv.at[r, k], self.at.peer(r)).start()

    def relay(self):
        for r, k in ((1, 0), (2, 1)):
            piece = self.part(self.block(r), k)
            wait_bytes(piece, self.recv.at[r, k])
            remote(piece, piece, self.send, self.recv.at[0, k], self.at.peer(3 - r)).start()

    def rest(self, r):
        block = self.block(r)
        for row, k in {1: ((1, 1),), 2: ((2, 0),), 3: ((0, 0), (0, 1))}[r]:
            wait_bytes(self.part(block, k), self.recv.at[row, k])


def part_rows(h, core):
    return pl.ds(pl.multiple_of(h * 128 + core * 64, 64), 64)


class Gather:
    def __init__(self, at, slots, h, send, recv, recv_sib):
        self.at, self.slots, self.h = at, slots, h
        self.send, self.recv_sib = send, recv_sib

        def part(block, k):
            return block.at[pl.ds(k * 32, 32)]

        self.spread = Spread(
            at, lambda r: slots.at[at.chip(r), part_rows(h, at.c)], part, send, recv
        )

    def to_sibling(self, r):
        block = self.spread.block(r)
        remote(block, block, self.send, self.recv_sib.at[r], self.at.sibling()).start()

    def start(self):
        self.spread.start()
        self.to_sibling(0)

    def relay(self):
        self.spread.relay()

    def forward(self, r):
        self.spread.rest(r)
        self.to_sibling(r)

    def ready(self, r):
        at = self.at
        wait_bytes(self.slots.at[at.chip(r), part_rows(self.h, 1 - at.c)], self.recv_sib.at[r])
        return at.chip(r)


class Exchange:
    def __init__(self, at, buffers, rows, send, recv, recv_sib):
        self.at, self.send, self.recv, self.recv_sib = at, send, recv, recv_sib
        self.sib_out, self.sib_in, self.out, self.into = buffers
        self.rows = rows

    def put(self, r, theirs):
        mine = self.sib_out.at[r, self.rows]
        mine[...] = theirs.astype(BF16)
        remote(
            mine,
            self.sib_in.at[r, self.rows],
            self.send,
            self.recv_sib.at[r],
            self.at.sibling(),
        ).start()

    def add(self, r, mine):
        wait_bytes(self.sib_in.at[r, self.rows], self.recv_sib.at[r])
        total = mine + self.sib_in[r, self.rows].astype(F32)
        if r == 0:
            return total
        self.out[r, self.rows] = total.astype(BF16)
        if r == 3:
            for k in range(2):
                self.pass_half(3, k, 3, self.recv.at[3 * k], k + 1)
        else:
            self.pass_half(r, r - 1, r, self.recv.at[r], r)

    def half(self, k):
        size = self.rows.size // 2
        return pl.ds(self.rows.start + size * k, size)

    def pass_half(self, r, k, slot, recv, peer):
        rows = self.half(k)
        remote(
            self.out.at[r, rows], self.into.at[slot, rows], self.send, recv, self.at.peer(peer)
        ).start()

    def relay(self):
        for k in range(2):
            rows, r = self.half(k), 2 - k
            wait_bytes(self.into.at[3, rows], self.recv.at[3 * k])
            self.out[r, rows] = (
                self.out[r, rows].astype(F32) + self.into[3, rows].astype(F32)
            ).astype(BF16)
            self.pass_half(r, k, r, self.recv.at[r], r)

    def arrive(self):
        for r in (1, 2):
            wait_bytes(self.into.at[r, self.rows], self.recv.at[r])


def norm_rows(values):
    centre = jnp.mean(values, axis=-1, keepdims=True)
    centred = values - centre
    spread = jnp.mean(centred * centred, axis=-1, keepdims=True)
    scale = lax.rsqrt(spread + NORM_EPS)
    return centred * scale, scale


def norm_back(grad, unit, scale):
    centre = jnp.mean(grad, axis=-1, keepdims=True)
    along = jnp.mean(grad * unit, axis=-1, keepdims=True)
    return (grad - centre - unit * along) * scale


def send_or_copy(src, dst, send_sem, recv_sem, device, own):
    def away():
        remote(src, dst, send_sem, recv_sem, device).start()

    if own is None:
        away()
        return
    pl.when(jnp.logical_not(own))(away)

    @pl.when(own)
    def _():
        pltpu.make_async_copy(src, dst, recv_sem).start()


class Column:
    def __init__(self, at, ref, rows, sems):
        self.at, self.ref, self.rows = at, ref, rows
        self.up_send, self.up_recv, self.down_send, self.down_recv = sems

    def block(self, plane):
        return self.ref.at[self.rows, lanes(plane)]

    def sides(self, hop, act, arriving):
        z = self.at.z
        if arriving:
            below, above = z - 1 - hop, z + 1 + hop
            pl.when(below >= 0)(lambda: act(self.block(below), 0))
            pl.when(above <= 3)(lambda: act(self.block(above), 1))
        else:
            up = jnp.logical_and(z >= hop, z < 3)
            down = jnp.logical_and(z + hop <= 3, z > 0)
            pl.when(up)(lambda: act(self.block(z - hop), 0))
            pl.when(down)(lambda: act(self.block(z + hop), 1))

    def send(self, hop):
        def act(block, side):
            send = (self.up_send, self.down_send)[side].at[hop]
            recv = (self.up_recv, self.down_recv)[side].at[hop]
            remote(block, block, send, recv, (self.at.b, self.at.z + 1 - 2 * side)).start()

        self.sides(hop, act, False)

    def arrive(self, hop):
        def act(block, side):
            wait_bytes(block, (self.up_recv, self.down_recv)[side].at[hop])

        self.sides(hop, act, True)

    def end(self):
        def wait(hop):
            def act(block, side):
                wait_bytes(block, (self.up_send, self.down_send)[side].at[hop])

            return act

        for hop in range(3):
            self.sides(hop, wait(hop), False)


def plane_weights(at, src, dst, send_sem, recv_sem):
    rows, cols = lanes(at.b), lanes(at.z)
    pltpu.make_async_copy(src.at[:, lanes(at.b)], dst.at[rows, cols], recv_sem).start()

    def push(step, carry):
        other = (at.b + step) % 8
        remote(
            src.at[:, lanes(other)], dst.at[rows, cols], send_sem, recv_sem, (other, at.z)
        ).start()
        return carry

    lax.fori_loop(1, 8, push, 0)


class ColumnSum:
    def __init__(self, at, blocks, passing, send, recv):
        self.at, self.blocks, self.passing = at, blocks, passing
        self.send_sem, self.recv_sem = send, recv

    def plane(self, side, i):
        return i if side else 3 - i

    def hop(self, side):
        return 3 - self.at.z if side else self.at.z

    def next(self, side):
        return (self.at.b, self.at.z + 1 - 2 * side)

    def begin(self, which):
        for side in range(2):

            @pl.when(self.hop(side) == 0)
            def _(side=side):
                for i in which:
                    remote(
                        self.blocks.at[:, :, pl.ds(128 * self.plane(side, i), 128)],
                        self.passing.at[side, i],
                        self.send_sem.at[side, i],
                        self.recv_sem.at[side, i],
                        self.next(side),
                    ).start()

    def relay(self, hop, i):
        for side in range(2):

            @pl.when(self.hop(side) == hop)
            def _(side=side):
                held = self.passing.at[side, i]
                wait_bytes(held, self.recv_sem.at[side, i])
                cols = pl.ds(128 * self.plane(side, i), 128)
                for b in range(8):
                    self.passing[side, i, b] = (
                        self.passing[side, i, b].astype(F32)
                        + self.blocks[b, :, cols].astype(F32)
                    ).astype(BF16)
                remote(
                    held,
                    held,
                    self.send_sem.at[side, i],
                    self.recv_sem.at[side, i],
                    self.next(side),
                ).start()

    def finish(self, sums, final, send_out, recv_out):
        at = self.at
        own = lanes(at.z)
        for b in range(8):
            sums[b] = self.blocks[b, :, own]
        for side in range(2):
            for hop in range(1, 4):
                i = 3 - hop

                @pl.when(self.hop(side) == hop)
                def _(side=side, i=i):
                    wait_bytes(self.passing.at[side, i], self.recv_sem.at[side, i])
                    for b in range(8):
                        sums[b] = (
                            sums[b].astype(F32) + self.passing[side, i, b].astype(F32)
                        ).astype(BF16)

        def one(step, carry):
            other = (at.b + 1 + step) % 8
            send_or_copy(
                sums.at[other],
                final.at[:, lanes(at.b)],
                send_out,
                recv_out,
                (other, at.z),
                step == 7,
            )
            return carry

        lax.fori_loop(0, 8, one, 0)

    def end(self):
        for side in range(2):
            for i in range(3):

                @pl.when(self.hop(side) < 3 - i)
                def _(side=side, i=i):
                    wait_bytes(self.passing.at[side, i], self.send_sem.at[side, i])


def head_mask(h):
    lane = lax.broadcasted_iota(jnp.int32, (1, 128), 1)
    return jnp.where(lane // HEAD_DIM == h, 1.0, 0.0).astype(F32)


def slot_rows(index):
    return pl.ds(pl.multiple_of(index * 64, 64), 64)


def chip_rows(index):
    return pl.ds(pl.multiple_of(index * 256, 256), 256)


def core_rows(index):
    return pl.ds(pl.multiple_of(index * 1024, 1024), 1024)


class Inputs:
    small = x_hbm = cot_hbm = wq = wk = wv = wout = win = wback = None


def entries(table):
    return [(n, e) for n, e in vars(table).items() if n[0] != "_"]


class Results:
    out = ((128, 1024), BF16)
    gtok = ((128, 1024), BF16)
    w_in = ((2, 2, 128, 384), BF16)
    o_in = ((4, 128, 256), BF16)
    fin_in = ((128, 1024), BF16)
    fin_back = ((128, 1024), BF16)
    notes_in = ((4, 16, 128), F32)


class Scratch:
    small_here = ((16, 128), BF16)
    out_here = ((128, 1024), BF16)
    gtok_here = ((128, 1024), BF16)
    x = ((128, 1024), BF16)
    cot = ((128, 1024), BF16)
    xs = ((1024, 1024), BF16)
    wqkv = ((1024, 384), BF16)
    w_near = ((3, 128, 256), BF16)
    queries = ((1024, 128), BF16)
    keys_all = ((2048, 128), BF16)
    values_all = ((2048, 128), BF16)
    mixed = ((1024, 128), F32)
    log_sums = ((1024, 128), F32)
    att = ((128, 1024), BF16)
    wo = ((1024, 1024), BF16)
    par = ((8, 1024), F32)
    bins = ((1, 512), F32)
    wi = ((1024, 512), BF16)
    wb = ((1024, 512), BF16)
    smalls = ((8, 16, 128), BF16)
    smalls_z = ((4, 16, 128), BF16)
    smalls_sum = ((16, 128), BF16)
    proj = ((256, 384), F32)
    scores = ((256, 2048), F32)
    d_buf = ((256, 2048), F32)
    p_buf = ((256, 2048), BF16)
    att_send = ((1024, 128), BF16)
    n1 = ((128, 1024), F32)
    unit1 = ((128, 1024), F32)
    scale1 = ((128, 128), F32)
    d2 = ((128, 1024), F32)
    d1 = ((128, 1024), F32)
    db = ((128, 1024), BF16)
    norm_slots = ((4, 256, 1024), BF16)
    grad_slots = ((4, 256, 1024), BF16)
    hid = ((4, 256, 512), BF16)
    slope = ((4, 256, 512), F32)
    low = ((4, 256, 512), BF16)
    pre = ((128, 512), F32)
    terms = ((4, 256, 1024), F32)
    sib_out = ((2, 4, 128, 1024), BF16)
    sib_in = ((2, 4, 128, 1024), BF16)
    peer_out = ((2, 4, 128, 1024), BF16)
    peer_in = ((2, 4, 128, 1024), BF16)
    g_back = ((8, 128, 512), BF16)
    g_in = ((8, 128, 512), BF16)
    pass_back = ((2, 3, 8, 128, 128), BF16)
    pass_in = ((2, 3, 8, 128, 128), BF16)
    gs_back = ((8, 128, 128), BF16)
    gs_in = ((8, 128, 128), BF16)
    da_send = ((128, 1024), BF16)
    da = ((1024, 128), BF16)
    q_turned = ((128, 1024), BF16)
    da_turned = ((128, 1024), BF16)
    dq = ((1024, 128), F32)
    dk_turned = ((128, 2048), F32)
    dv_turned = ((128, 2048), F32)
    out_k = ((1024, 128), F32)
    out_v = ((1024, 128), F32)
    sib_k = ((1024, 128), F32)
    sib_v = ((1024, 128), F32)
    dqkv = ((1024, 384), BF16)
    x_sum = ((256, 1024), F32)
    x_own = ((64, 1024), F32)
    z_out = ((4, 64, 1024), BF16)
    z_in = ((4, 64, 1024), BF16)
    w_sib_out = ((4, 128, 384), F32)
    w_sib_in = ((4, 128, 384), F32)
    w_out = ((4, 128, 384), BF16)
    o_out = ((128, 1024), BF16)
    vec = ((8, 1024), F32)
    gbin = ((1, 512), F32)
    notes = ((8, 16, 128), F32)
    notes_p = ((8, 16, 128), F32)
    notes_sum = ((16, 128), F32)


class Arrivals:
    z = (4,)
    p = (4, 3, 2)
    wo = (3, 2)
    w = (3,)
    o = (5,)
    kv = (1,)
    misc = (12,)
    col = (6, 3)
    ga = (4, 3, 2)
    ga_sib = (4, 4)
    ex = (5, 4)
    ex_sib = (5, 4)
    zg = (2, 2, 3)
    kv2 = (2,)
    dx = (4, 3, 2)
    dz = (4,)
    ws = (4,)
    da = (4,)
    own = (4,)


class Departures:
    z = (1,)
    p = (1,)
    wo = (1,)
    w = (3,)
    o = (1,)
    kv = (1,)
    misc = (12,)
    col = (6, 3)
    ga = (2,)
    ex = (3,)
    zg = (2, 2, 3)
    kv2 = (1,)
    dx = (1,)
    dz = (1,)
    ws = (1,)


class Refs:
    pass


def layer_kernel(*refs):
    v = Refs()
    names = [n for table in (Inputs, Results, Scratch) for n, _ in entries(table)]
    names += ["r_" + n for n, _ in entries(Arrivals)] + ["s_" + n for n, _ in entries(Departures)]
    for name, ref in zip(names, refs):
        setattr(v, name, ref)
    at = Place()
    at.flat = at.b * 4 + at.z
    at.place = at.q * 4 + at.z
    at.parity = at.z % 2
    at.pair = 4 * (at.z // 2) + at.q
    def column(ref, rows, i):
        sems = [t.at[2 * i + k] for k in range(2) for t in (v.s_col, v.r_col)]
        return Column(at, ref, rows, sems)

    col_in = column(v.wi, pl.ds(0, 1024), 0)
    col_back = [column(v.wb, pl.ds(512 * k, 512), 1 + k) for k in range(2)]
    gathers = [
        [
            Gather(at, slots, h, v.s_ga.at[i], v.r_ga.at[2 * i + h], v.r_ga_sib.at[2 * i + h])
            for h in range(2)
        ]
        for i, slots in enumerate((v.norm_slots, v.grad_slots))
    ]

    def exchange(i, side, rows):
        buffers = [t.at[side] for t in (v.sib_out, v.sib_in, v.peer_out, v.peer_in)]
        return Exchange(at, buffers, rows, v.s_ex.at[i // 2], v.r_ex.at[i], v.r_ex_sib.at[i])

    scatters = [
        [exchange(2 * i + h, i, pl.ds(64 * h, 64)) for h in range(2)] for i in range(2)
    ]
    out_scatter = exchange(4, 0, pl.ds(0, 128))
    upper = at.z // 2
    at.planes = (at.z, at.z + 1 - 2 * at.parity, 2 - upper, 3 - 3 * upper)
    rows_spread = [
        Spread(
            at,
            lambda r, plane=plane: v.xs.at[slot_rows(at.chip(r) * 4 + plane)],
            lambda block, k: block.at[pl.ds(k * 32, 32)],
            v.s_p.at[0],
            v.r_p.at[i],
        )
        for i, plane in enumerate(at.planes)
    ]
    wo_spread = Spread(
        at,
        lambda r: v.wo.at[:, lanes(2 * at.chip(r) + at.c)],
        lambda block, k: block.at[pl.ds(k * 512, 512)],
        v.s_wo.at[0],
        v.r_wo,
    )
    sum_in = ColumnSum(at, v.g_in, v.pass_in, v.s_zg.at[0], v.r_zg.at[0])
    sum_back = ColumnSum(at, v.g_back, v.pass_back, v.s_zg.at[1], v.r_zg.at[1])
    place_small(at, v)
    pltpu.make_async_copy(v.x_hbm, v.x, v.r_own.at[0]).start()
    pltpu.make_async_copy(v.cot_hbm, v.cot, v.r_own.at[1]).start()
    greet_all(at)
    wait_bytes(v.x, v.r_own.at[0])
    attend_phase(at, v, col_in, col_back, rows_spread, wo_spread)
    ffn_phase(at, v, col_in, col_back, gathers, scatters, sum_back, sum_in)
    grads_phase(at, v, out_scatter, sum_in, sum_back)
    end_phase(at, v, (sum_in, sum_back, col_in, *col_back))


def place_small(at, v):
    def iota(shape, axis):
        return lax.broadcasted_iota(jnp.int32, shape, axis)

    spread = jnp.where(
        iota((8, 256), 1) // 32 == iota((8, 256), 0), v.small[0:1, 0:256], 0.0
    ).astype(BF16)
    lane = iota((256, 128), 1)
    source = iota((256, 128), 0) % 32 + 32 * at.z
    picked = jnp.where(lane == source, 1.0, 0.0).astype(BF16)
    top = dot_nn(spread, picked)
    units = jnp.where(iota((8, 128), 0) == at.z, v.small[0:1, 256:384], 0.0)
    v.small_here[...] = jnp.concatenate((top, units), axis=0).astype(BF16)


def attend_phase(at, v, col_in, col_back, rows_spread, wo_spread):
    xs, wqkv, wo = v.xs, v.wqkv, v.wo
    parity, pair = at.parity, at.pair

    pltpu.make_async_copy(v.small_here, v.smalls_z.at[at.z], v.r_misc.at[1]).start()
    for dz in range(1, 4):
        remote(
            v.small_here,
            v.smalls_z.at[at.z],
            v.s_misc.at[1],
            v.r_misc.at[1],
            (at.b, (at.z + dz) % 4),
        ).start()

    pltpu.make_async_copy(
        v.x.at[slot_rows(parity)], xs.at[slot_rows(at.place)], v.r_z.at[at.z]
    ).start()
    weights = (v.wq, v.wk, v.wv)
    for i in (1, 2, 3):
        plane = at.planes[i]
        remote(
            v.x.at[slot_rows(plane % 2)],
            xs.at[slot_rows(at.place)],
            v.s_z.at[0],
            v.r_z.at[at.z],
            (at.b, plane),
        ).start()
        if i == 1:
            for k, w in enumerate(weights):
                remote(
                    w, v.w_near.at[k], v.s_w.at[2], v.r_w.at[2], (at.b, at.planes[1])
                ).start()

    part = wo.at[pl.ds(pl.multiple_of(at.z * 256, 256), 256), lanes(at.b)]
    pltpu.make_async_copy(v.wout, part, v.r_o.at[4]).start()
    for i in (1, 2, 3):
        remote(v.wout, part, v.s_o.at[0], v.r_o.at[4], (at.b, at.planes[i])).start()

    def to_pairs(sources, group):
        for dx in range(2):
            column = (at.x + dx) % 2
            for k, w in enumerate(sources):
                send_or_copy(
                    w.at[:, lanes(column)],
                    wqkv.at[lanes(at.b), pl.ds(k * 128, 128)],
                    v.s_w.at[0],
                    v.r_w.at[0],
                    (2 * (group * 2 + column) + at.c, at.z),
                    None if dx else group == at.y,
                )

    for i in range(4):
        wait_bytes(rows_spread[i].block(0), v.r_z.at[at.planes[i]])
        rows_spread[i].start()
        if i == 0:
            to_pairs(weights, parity)
            wait_bytes(v.smalls_z, v.r_misc.at[1])
            total = v.smalls_z[0].astype(F32)
            for z in range(1, 4):
                total += v.smalls_z[z].astype(F32)
            v.smalls_sum[...] = total.astype(BF16)
            mine = v.smalls.at[at.b]
            pltpu.make_async_copy(v.smalls_sum, mine, v.r_misc.at[10]).start()

            def spread(step, carry):
                remote(
                    v.smalls_sum,
                    mine,
                    v.s_misc.at[10],
                    v.r_misc.at[10],
                    ((at.b + step) % 8, at.z),
                ).start()
                return carry

            lax.fori_loop(1, 8, spread, 0)
        if i == 1:
            plane_weights(at, v.win, v.wi, v.s_misc.at[0], v.r_misc.at[0])
            wait_bytes(v.w_near, v.r_w.at[2])
            to_pairs([v.w_near.at[k] for k in range(3)], 1 - parity)
        if i == 3:
            wait_bytes(v.wi.at[:, pl.ds(0, 128)], v.r_misc.at[0])
            col_in.send(0)
        if i:
            rows_spread[i - 1].relay()

    wait_bytes(wqkv.at[pl.ds(0, 512)], v.r_w.at[0])
    for r in range(4):
        part = wqkv.at[lanes(2 * at.chip(r) + at.c)]
        remote(part, part, v.s_w.at[1], v.r_w.at[1], at.sibling()).start()
    wait_bytes(v.smalls, v.r_misc.at[10])
    for b in range(8):
        v.par[:, 128 * b : 128 * b + 128] = v.smalls[b].astype(F32)[0:8]
    row = lax.broadcasted_iota(jnp.int32, (8, 128), 0)
    for h in range(4):
        rows = v.smalls[2 * h + at.b // 4].astype(F32)[8:16]
        rows = jnp.where(row == at.b % 4, rows, 0.0)
        v.bins[0:1, 128 * h : 128 * h + 128] = jnp.sum(rows, axis=0, keepdims=True)
    bias_q = v.par[0:1, lanes(pair)]
    bias_v = v.par[1:2, lanes(pair)]
    wait_bytes(wqkv.at[pl.ds(0, 512)], v.r_w.at[1])

    def project(r):
        chip = at.chip(r)
        if r:
            for i in range(4):
                rows_spread[i].rest(r)
        rows = chip_rows(chip)
        v.proj[...] = dot_nn(xs[rows], wqkv[...])
        v.queries[rows] = (v.proj[:, 0:128] + bias_q).astype(BF16)
        own_rows = chip_rows(at.c * 4 + chip)
        v.keys_all[own_rows] = v.proj[:, 128:256].astype(BF16)
        v.values_all[own_rows] = (v.proj[:, 256:384] + bias_v).astype(BF16)
        for k, ref in enumerate((v.keys_all, v.values_all)):
            view = ref.at[own_rows]
            remote(view, view, v.s_kv.at[0], v.r_kv.at[0], at.sibling()).start()

    project(0)
    rows_spread[3].relay()

    whole = wo_spread.block(0)
    wait_bytes(whole, v.r_o.at[4])
    wo_spread.start()
    remote(whole, whole, v.s_o.at[0], v.r_o.at[0], at.sibling()).start()
    plane_weights(at, v.wback, v.wb, v.s_misc.at[2], v.r_misc.at[2])

    col_in.arrive(0)
    col_in.send(1)
    for r in (1, 2, 3):
        project(r)

    wait_bytes(v.keys_all, v.r_kv.at[0])

    scores = v.scores

    def attend(step, carry):
        chip = (at.q + 1 + step) % 4
        rows = chip_rows(chip)
        outs = []
        logs = []
        for h in range(2):
            q = (v.queries[rows].astype(F32) * head_mask(h) * HEAD_DIM**-0.5).astype(BF16)
            scores[...] = contract_cols(q, v.keys_all[...])
            top = jnp.max(scores[...], axis=-1, keepdims=True)
            weights = jnp.exp(scores[...] - top)
            total = jnp.sum(weights, axis=-1, keepdims=True)
            outs.append(dot_nn(weights.astype(BF16), v.values_all[...]) / total)
            logs.append(top + jnp.log(total))
        first = head_mask(0) > 0.5
        merged = jnp.where(first, outs[0], outs[1])
        v.mixed[rows] = merged
        v.log_sums[rows] = jnp.where(first, logs[0], logs[1])
        v.att_send[rows] = merged.astype(BF16)
        for k in range(4):
            plane = (at.z + 1 + k) % 4
            send_or_copy(
                v.att_send.at[slot_rows(chip * 4 + plane)],
                v.att.at[slot_rows(parity), lanes(pair)],
                v.s_misc.at[3],
                v.r_misc.at[3],
                (2 * chip + at.c, plane),
                step == 3 if k == 3 else None,
            )

        @pl.when(step == 0)
        def _():
            wo_spread.relay()
            col_in.arrive(1)
            col_in.send(2)

        return carry

    lax.fori_loop(0, 4, attend, 0)

    wait_bytes(v.wb.at[:, pl.ds(0, 128)], v.r_misc.at[2])
    for half_back in col_back:
        half_back.send(0)
    for r in (1, 2, 3):
        wo_spread.rest(r)
        part = wo_spread.block(r)
        remote(part, part, v.s_o.at[0], v.r_o.at[r], at.sibling()).start()
    for r in range(4):
        wait_bytes(whole, v.r_o.at[r])
    wait_bytes(v.att, v.r_misc.at[3])


def ffn_phase(at, v, col_in, col_back, gathers, scatters, sum_back, sum_in):
    n1, terms, peer_in = v.n1, v.terms, v.peer_in

    def param(i):
        return v.par[i : i + 1, :]

    def local(h, i):
        return pl.ds(64 * h + 32 * i, 32)

    def chip_part(h, i):
        return pl.ds(pl.multiple_of(h * 128 + at.c * 64 + 32 * i, 32), 32)

    wait_bytes(v.cot, v.r_own.at[1])
    n1[...] = dot_nn(v.att[...], v.wo[...])
    for h in range(2):
        for i in range(2):
            rows = local(h, i)
            unit, scale = norm_rows(v.x[rows].astype(F32) + n1[rows] + param(2))
            v.unit1[rows] = unit
            v.scale1[rows] = jnp.broadcast_to(scale, (32, 128))
            normed = unit * param(3) + param(4)
            n1[rows] = normed
            v.norm_slots[at.q, chip_part(h, i)] = normed.astype(BF16)
        gathers[0][h].start()

    def hidden(h, r):
        chip = gathers[0][h].ready(r)
        v.pre[...] = dot_nn(v.norm_slots[chip, pl.ds(128 * h, 128)], v.wi[...])

        def activate(i, carry):
            rows = pl.ds(pl.multiple_of(i * 32, 32), 32)
            into = pl.ds(pl.multiple_of(128 * h + i * 32, 32), 32)
            u = v.pre[rows] + v.bins[...]
            cdf = 0.5 * (1.0 + lax.erf(u * math.sqrt(0.5)))
            bell = jnp.exp(-0.5 * u * u) * (1.0 / math.sqrt(2.0 * math.pi))
            v.hid[r, into] = (u * cdf).astype(BF16)
            v.slope[r, into] = cdf + u * bell
            return carry

        lax.fori_loop(0, 4, activate, 0)

    def neighbours(gather):
        gather.relay()
        gather.forward(1)
        gather.forward(2)

    neighbours(gathers[0][0])
    for half_back in col_back:
        half_back.arrive(0)
        half_back.send(1)
    gathers[0][1].relay()
    col_in.arrive(2)
    hidden(0, 0)
    gathers[0][1].forward(1)
    gathers[0][1].forward(2)
    hidden(1, 0)
    hidden(0, 1)
    hidden(0, 2)
    col_back[0].arrive(1)
    col_back[0].send(2)
    gathers[0][0].forward(3)
    hidden(1, 1)
    gathers[0][1].forward(3)
    col_back[1].arrive(1)
    col_back[1].send(2)
    hidden(1, 2)
    hidden(0, 3)
    hidden(1, 3)
    for half_back in col_back:
        half_back.arrive(2)

    def to_plane(scatter, done, h, r, product):
        terms[r, pl.ds(128 * h, 128)] = product
        scatter[h].put(r, terms[r, part_rows(h, 1 - at.c)])
        done.append((h, r))
        if len(done) > 3:
            pass_on(scatter, *done[-4])

    def pass_on(scatter, h, r):
        total = scatter[h].add(r, terms[r, part_rows(h, at.c)])
        if r == 0:
            terms[0, part_rows(h, at.c)] = total

    done = []
    for h in range(2):
        for r in (3, 1, 2, 0):
            product = contract_cols(v.hid[r, pl.ds(128 * h, 128)], v.wb[...])
            to_plane(scatters[0], done, h, r, product)
    for one in done[-3:]:
        pass_on(scatters[0], *one)
    for h in range(2):
        scatters[0][h].relay()

    def peers(side, rows):
        return peer_in[side, 1, rows].astype(F32) + peer_in[side, 2, rows].astype(F32)

    def column_sums(parts, sums):
        return tuple(
            kept + jnp.sum(part.reshape(4, 8, 1024), axis=0) for kept, part in zip(sums, parts)
        )

    gbin = [jnp.zeros((8, 512), F32)]
    done = []

    def hidden_grad(h, r):
        chip = gathers[1][h].ready(r)
        v.pre[...] = dot_nn(v.grad_slots[chip, pl.ds(128 * h, 128)], v.wb[...])

        def deactivate(i, carry):
            rows = pl.ds(pl.multiple_of(i * 32, 32), 32)
            into = pl.ds(pl.multiple_of(128 * h + i * 32, 32), 32)
            low = (v.pre[rows] * v.slope[r, into]).astype(BF16)
            v.low[r, into] = low
            return carry + jnp.sum(low.astype(F32).reshape(4, 8, 512), axis=0)

        gbin[0] = lax.fori_loop(0, 4, deactivate, gbin[0])
        product = contract_cols(v.low[r, pl.ds(128 * h, 128)], v.wi[...])
        to_plane(scatters[1], done, h, r, product)

    sums = tuple(jnp.zeros((8, 1024), F32) for _ in range(3))
    for h in range(2):
        scatters[0][h].arrive()
        for i in range(2):
            rows = local(h, i)
            total = terms[0, chip_part(h, i)] + peers(0, rows)
            unit, scale = norm_rows(n1[rows] + total + param(5))
            v.out_here[rows] = (unit * param(6) + param(7)).astype(BF16)
            g = v.cot[rows].astype(F32)
            d = norm_back(g * param(6), unit, scale)
            v.d2[rows] = d
            low = d.astype(BF16)
            v.grad_slots[at.q, chip_part(h, i)] = low
            sums = column_sums((g * unit, g, low.astype(F32)), sums)
        gathers[1][h].start()
        if h == 0:
            hidden_grad(0, 0)
    pltpu.make_async_copy(v.out_here, v.out, v.r_own.at[2]).start()
    for row, total in zip((6, 7, 5), sums):
        v.vec[row : row + 1, :] = jnp.sum(total, axis=0, keepdims=True)

    def weight_grad(slots, right, into):
        def one(step, carry):
            other = (at.q + step) % 4
            total = jnp.zeros((256, 512), F32)
            for r in range(4):
                total += contract_rows(slots[at.chip(r), :, chip_rows(other)], right[r])
            into[2 * other] = total[0:128].astype(BF16)
            into[2 * other + 1] = total[128:256].astype(BF16)
            return carry

        lax.fori_loop(0, 4, one, 0)

    neighbours(gathers[1][0])
    hidden_grad(1, 0)
    hidden_grad(0, 1)
    neighbours(gathers[1][1])
    hidden_grad(0, 2)
    gathers[1][0].forward(3)
    hidden_grad(1, 1)
    hidden_grad(0, 3)
    gathers[1][1].forward(3)
    hidden_grad(1, 2)
    hidden_grad(1, 3)
    for one in done[-3:]:
        pass_on(scatters[1], *one)
    v.gbin[...] = jnp.sum(gbin[0], axis=0, keepdims=True)

    sums = tuple(jnp.zeros((8, 1024), F32) for _ in range(3))
    weight_grad(v.grad_slots, v.hid, v.g_back)
    wait_bytes(v.xs.at[pl.ds(0, 896)], v.s_ga.at[1])
    sum_back.begin((0,))
    scatters[1][0].relay()
    weight_grad(v.norm_slots, v.low, v.g_in)
    scatters[1][1].relay()
    for h in range(2):
        scatters[1][h].arrive()
        for i in range(2):
            rows = local(h, i)
            total = v.d2[rows] + terms[0, chip_part(h, i)] + peers(1, rows)
            unit = v.unit1[rows]
            d = norm_back(total * param(3), unit, v.scale1[rows][:, :1])
            v.d1[rows] = d
            low = d.astype(BF16)
            v.db[rows] = low
            sums = column_sums((total * unit, total, low.astype(F32)), sums)
        rows = pl.ds(64 * h, 64)
        v.da_send[rows] = contract_cols(v.db[rows], v.wo[...]).astype(BF16)
        for r in range(4):
            chip = at.chip(r)
            for plane in (h, h + 2):
                pair = 2 * (plane - h) + chip
                send_or_copy(
                    v.da_send.at[rows, lanes(pair)],
                    v.da.at[slot_rows(at.place)],
                    v.s_misc.at[4],
                    v.r_da.at[r],
                    (2 * chip + at.c, plane),
                    None if r else at.z == plane,
                )

    for row, total in zip((3, 4, 2), sums):
        v.vec[row : row + 1, :] = jnp.sum(total, axis=0, keepdims=True)
    v.vec[0:2, :] = jnp.zeros((2, 1024), F32)
    for i in range(3):
        if i:
            sum_back.begin((i,))
        sum_in.begin((i,))


def grads_phase(at, v, out_scatter, sum_in, sum_back):
    xs, wqkv, terms = v.xs, v.wqkv, v.terms
    parity, pair = at.parity, at.pair

    wait_bytes(xs.at[pl.ds(0, 896)], v.s_ex.at[0])
    for r in (3, 1, 2, 0):
        for core in (1 - at.c, at.c):
            part = contract_rows(v.db[:, lanes(2 * at.chip(r) + core)], v.att[...])
            if core is at.c:
                terms[r, 0:128] = part
            else:
                out_scatter.put(r, part)

    v.q_turned[...] = v.queries[...].astype(F32).T.astype(BF16)
    v.dk_turned[...] = jnp.zeros_like(v.dk_turned)
    v.dv_turned[...] = jnp.zeros_like(v.dv_turned)
    for r in (3, 1, 2):
        out_scatter.add(r, terms[r, 0:128])
    terms[0, 0:128] = out_scatter.add(0, terms[0, 0:128])
    sum_back.relay(1, 0)
    wait_bytes(v.da.at[chip_rows(at.q)], v.r_da.at[0])
    s_buf, d_buf, p_buf = v.scores, v.d_buf, v.p_buf

    def attend(step, carry):
        chip = ((at.y + step // 2) % 2) * 2 + (at.x + step % 2) % 2
        rows = chip_rows(chip)

        @pl.when(step > 0)
        def _():
            wait_bytes(v.da.at[rows], v.r_da.at[step])

        v.da_turned[:, rows] = v.da[rows].astype(F32).T.astype(BF16)
        parts = []
        for h in range(2):
            mask = head_mask(h)
            grad = v.da[rows].astype(F32) * mask
            delta = jnp.sum(grad * v.mixed[rows], axis=-1, keepdims=True)
            q = (v.queries[rows].astype(F32) * mask * HEAD_DIM**-0.5).astype(BF16)
            s_buf[...] = contract_cols(q, v.keys_all[...])
            d_buf[...] = contract_cols(grad.astype(BF16), v.values_all[...])
            logs = v.log_sums[rows][:, h * HEAD_DIM : h * HEAD_DIM + 1]
            probs = jnp.exp(s_buf[...] - logs)
            p_buf[...] = probs.astype(BF16)
            low = (probs * (d_buf[...] - delta)).astype(BF16)
            band = pl.ds(h * HEAD_DIM, HEAD_DIM)
            v.dv_turned[band] += dot_nn(v.da_turned[band, rows], p_buf[...])
            v.dk_turned[band] += dot_nn(v.q_turned[band, rows], low)
            parts.append(dot_nn(low, v.keys_all[...]))
        v.dq[rows] = jnp.where(head_mask(0) > 0.5, parts[0], parts[1]) * HEAD_DIM**-0.5

        @pl.when(step == 1)
        def _():
            out_scatter.relay()
            sum_back.relay(2, 0)
            sum_in.relay(1, 0)

        @pl.when(step == 3)
        def _():
            sum_back.relay(1, 1)

        return carry

    lax.fori_loop(0, 4, attend, 0)

    other = core_rows(1 - at.c)
    mine = core_rows(at.c)
    v.out_k[...] = v.dk_turned[:, other].T * HEAD_DIM**-0.5
    v.out_v[...] = v.dv_turned[:, other].T
    for k, (ref, into) in enumerate(((v.out_k, v.sib_k), (v.out_v, v.sib_v))):
        remote(ref, into, v.s_kv2.at[0], v.r_kv2.at[k], at.sibling()).start()
    dqkv = v.dqkv
    low = v.dq[...].astype(BF16)
    dqkv[:, 0:128] = low
    v.vec[0:1, lanes(pair)] = jnp.sum(low.astype(F32), axis=0, keepdims=True)
    out_scatter.arrive()
    peer_in = v.peer_in.at[0]

    def out_rows(rows):
        total = terms[0, rows] + peer_in[1, rows].astype(F32) + peer_in[2, rows].astype(F32)
        v.o_out[rows] = total.astype(BF16)

    by_rows(128, 32, out_rows)
    wide = pl.ds(pl.multiple_of(at.z * 256, 256), 256)
    pltpu.make_async_copy(v.o_out.at[:, wide], v.o_in.at[0], v.r_misc.at[8]).start()
    for dz in range(1, 4):
        plane = (at.z + dz) % 4
        remote(
            v.o_out.at[:, pl.ds(pl.multiple_of(plane * 256, 256), 256)],
            v.o_in.at[dz],
            v.s_misc.at[8],
            v.r_misc.at[8],
            (at.b, plane),
        ).start()

    own_k = v.dk_turned[:, mine].T * HEAD_DIM**-0.5
    wait_bytes(v.sib_k, v.r_kv2.at[0])
    dqkv[:, 128:256] = (own_k + v.sib_k[...]).astype(BF16)
    own_v = v.dv_turned[:, mine].T
    wait_bytes(v.sib_v, v.r_kv2.at[1])
    low = (own_v + v.sib_v[...]).astype(BF16)
    dqkv[:, 256:384] = low
    v.vec[1:2, lanes(pair)] = jnp.sum(low.astype(F32), axis=0, keepdims=True)

    notes = v.notes
    for b in range(8):
        notes[b, 0:8] = v.vec[:, 128 * b : 128 * b + 128]
        notes[b, 8:16] = jnp.zeros((8, 128), F32)
    row = lax.broadcasted_iota(jnp.int32, (8, 128), 0)
    for h in range(4):
        notes[2 * h + at.b // 4, 8:16] = jnp.where(
            row == at.b % 4, v.gbin[0:1, 128 * h : 128 * h + 128], 0.0
        )
    pltpu.make_async_copy(notes.at[at.b], v.notes_p.at[at.b], v.r_misc.at[5]).start()

    def spread(step, carry):
        to = (at.b + step) % 8
        remote(
            notes.at[to], v.notes_p.at[at.b], v.s_misc.at[5], v.r_misc.at[5], (to, at.z)
        ).start()
        return carry

    lax.fori_loop(1, 8, spread, 0)

    wait_bytes(xs.at[pl.ds(0, 896)], v.s_ga.at[0])
    x_out, x_in, x_via = v.norm_slots, v.grad_slots.at[0:2], v.grad_slots.at[2:4]
    for r in (3, 1, 2, 0):
        part = contract_cols(dqkv[chip_rows(at.chip(r))], wqkv[...])
        if r:
            x_out[r] = part.astype(BF16)
        else:
            v.x_sum[...] = part
    def piece(dz, k):
        return pl.ds(pl.multiple_of(((at.z + dz) % 4) * 64 + 32 * k, 32), 32)

    order = (2, 1, 3, 0)

    def send_dx(dz, via):
        for r, k in ((1, 0), (2, 1)):
            rows = piece(dz, k)
            remote(
                x_out.at[3 if via else r, rows],
                x_via.at[r - 1, rows] if via else x_in.at[r - 1, rows],
                v.s_dx.at[0],
                v.r_dx.at[dz, 0 if via else r, k],
                at.peer(r),
            ).start()

    def relay_dx(dz):
        for r, k in ((2, 0), (1, 1)):
            rows = piece(dz, k)
            wait_bytes(x_via.at[k, rows], v.r_dx.at[dz, 0, k])
            x_out[r, rows] = (
                x_out[r, rows].astype(F32) + x_via[k, rows].astype(F32)
            ).astype(BF16)
            remote(
                x_out.at[r, rows],
                x_in.at[r - 1, rows],
                v.s_dx.at[0],
                v.r_dx.at[dz, r, k],
                at.peer(r),
            ).start()

    z_out, z_in = v.z_out, v.z_in
    def column_dx(dz):
        plane = (at.z + dz) % 4
        rows = slot_rows(plane)
        for r in (1, 2):
            for k in range(2):
                wait_bytes(x_in.at[r - 1, piece(dz, k)], v.r_dx.at[dz, r, k])
        total = v.x_sum[rows] + x_in[0, rows].astype(F32) + x_in[1, rows].astype(F32)
        if dz:
            z_out[dz] = total.astype(BF16)
            remote(
                z_out.at[dz], z_in.at[dz], v.s_dz.at[0], v.r_dz.at[dz], (at.b, plane)
            ).start()
        else:
            v.x_own[...] = total

    def begin_dx(dz):
        send_dx(dz, True)
        send_dx(dz, False)

    begin_dx(2)
    begin_dx(1)
    def features(b):
        return contract_rows(xs[:, lanes(b)], dqkv[...])

    for r in range(4):
        v.w_sib_out[r] = features(2 * at.chip(r) + 1 - at.c)
        remote(
            v.w_sib_out.at[r], v.w_sib_in.at[r], v.s_ws.at[0], v.r_ws.at[r], at.sibling()
        ).start()
    relay_dx(2)
    begin_dx(3)
    sum_in.relay(1, 1)
    sum_in.relay(2, 0)
    relay_dx(1)
    begin_dx(0)
    column_dx(2)
    plane_w = 2 * (at.z // 2) + at.y
    for r in range(4):
        total = features(2 * at.chip(r) + at.c)
        wait_bytes(v.w_sib_in.at[r], v.r_ws.at[r])
        v.w_out[r] = (total + v.w_sib_in[r]).astype(BF16)
        send_or_copy(
            v.w_out.at[r],
            v.w_in.at[parity, at.x],
            v.s_misc.at[6],
            v.r_misc.at[6],
            at.peer(r)[:1] + (plane_w,),
            plane_w == at.z if r == 0 else None,
        )

    relay_dx(3)
    sum_back.finish(v.gs_back, v.fin_back, v.s_misc.at[7], v.r_misc.at[7])
    column_dx(1)
    relay_dx(0)
    sum_in.finish(v.gs_in, v.fin_in, v.s_misc.at[9], v.r_misc.at[9])
    column_dx(3)
    wait_bytes(v.notes_p, v.r_misc.at[5])
    total = v.notes_p[0]
    for b in range(1, 8):
        total += v.notes_p[b]
    v.notes_sum[...] = total
    mine = v.notes_in.at[at.z]
    pltpu.make_async_copy(v.notes_sum, mine, v.r_misc.at[11]).start()
    for dz in range(1, 4):
        remote(
            v.notes_sum, mine, v.s_misc.at[11], v.r_misc.at[11], (at.b, (at.z + dz) % 4)
        ).start()

    column_dx(0)
    for dz in (1, 2, 3):
        wait_bytes(z_in.at[dz], v.r_dz.at[dz])
    same = slot_rows(parity)
    v.gtok_here[same] = (v.d1[same] + v.x_own[...] + z_in[2].astype(F32)).astype(BF16)
    cross = slot_rows(1 - parity)
    v.gtok_here[cross] = (v.d1[cross] + z_in[1].astype(F32) + z_in[3].astype(F32)).astype(BF16)

    pltpu.make_async_copy(v.gtok_here, v.gtok, v.r_own.at[3]).start()
    wait_bytes(v.o_in, v.r_misc.at[8])
    wait_bytes(v.w_in, v.r_misc.at[6])
    wait_bytes(v.notes_in, v.r_misc.at[11])
    wait_bytes(v.fin_back, v.r_misc.at[7])
    wait_bytes(v.fin_in, v.r_misc.at[9])


def end_phase(at, v, ends):
    wait_bytes(v.out_here, v.r_own.at[2])
    for one in ends:
        one.end()

    def rows(n):
        return v.xs.at[pl.ds(0, n)]

    wait_bytes(rows(192), v.s_z.at[0])
    wait_bytes(rows(768), v.s_p.at[0])
    wait_bytes(rows(384), v.s_wo.at[0])
    wait_bytes(rows(608), v.s_o.at[0])
    wait_bytes(rows(256), v.s_kv.at[0])
    for i in (1, 2):
        wait_bytes(rows(896), v.s_ex.at[i])
    wait_bytes(rows(768), v.s_dx.at[0])
    wait_bytes(rows(192), v.s_dz.at[0])
    wait_bytes(v.w_sib_out, v.s_ws.at[0])
    wait_bytes(rows(512), v.s_kv2.at[0])
    wait_bytes(v.wqkv.at[pl.ds(0, 384)], v.s_w.at[0])
    wait_bytes(v.wqkv.at[pl.ds(0, 512)], v.s_w.at[1])
    wait_bytes(v.w_near, v.s_w.at[2])
    seven = v.wi.at[pl.ds(0, 896), pl.ds(0, 128)]
    for i in (0, 2, 7, 9):
        wait_bytes(seven, v.s_misc.at[i])
    wait_bytes(v.smalls.at[pl.ds(0, 3)], v.s_misc.at[1])
    wait_bytes(v.smalls.at[pl.ds(0, 7)], v.s_misc.at[10])
    for i in (3, 4):
        wait_bytes(v.att_send.at[pl.ds(0, 960)], v.s_misc.at[i])
    wait_bytes(v.notes.at[pl.ds(0, 7)], v.s_misc.at[5])
    wait_bytes(v.notes.at[pl.ds(0, 3)], v.s_misc.at[11])
    plane_w = 2 * (at.z // 2) + at.y

    @pl.when(plane_w == at.z)
    def _():
        wait_bytes(v.w_out.at[pl.ds(0, 3)], v.s_misc.at[6])

    @pl.when(plane_w != at.z)
    def _():
        wait_bytes(v.w_out, v.s_misc.at[6])

    wait_bytes(v.o_in.at[pl.ds(0, 3)], v.s_misc.at[8])
    wait_bytes(v.gtok_here, v.r_own.at[3])


def finish_kernel(
    place_ref,
    out_in,
    gtok_in,
    w_in,
    o_in,
    fin_in,
    fin_back,
    notes_in,
    out_ref,
    gtok_ref,
    gq_ref,
    gk_ref,
    gv_ref,
    gout_ref,
    gwin_ref,
    gwback_ref,
    bin_ref,
    *vector_refs,
):
    out_ref[...] = out_in[...]
    gtok_ref[...] = gtok_in[...]
    for x in range(2):
        total = w_in[0, x].astype(F32) + w_in[1, x].astype(F32)
        for k, ref in enumerate((gq_ref, gk_ref, gv_ref)):
            ref[:, 128 * x : 128 * x + 128] = total[:, 128 * k : 128 * k + 128]
    gout_ref[...] = (
        o_in[0].astype(F32) + o_in[1].astype(F32) + o_in[2].astype(F32) + o_in[3].astype(F32)
    ).T
    gwin_ref[...] = fin_in[...].astype(F32)
    gwback_ref[...] = fin_back[...].astype(F32)
    total = notes_in[0] + notes_in[1] + notes_in[2] + notes_in[3]
    z = place_ref[0]
    part = jnp.zeros((8, 32), F32)
    units = jnp.zeros((1, 128), F32)
    for k in range(4):
        part += jnp.where(z == k, total[0:8, 32 * k : 32 * k + 32], 0.0)
        units += jnp.where(z == k, total[8 + k : 9 + k], 0.0)
    for j, ref in enumerate(vector_refs):
        ref[...] = part[j]
    bin_ref[...] = units[0]


def vmem():
    return pl.BlockSpec(memory_space=pltpu.VMEM)


def run_layer(*args):
    results = [e for _, e in entries(Results)]
    scratch = [pltpu.VMEM(s, t) for _, (s, t) in entries(Scratch)]
    for _, shape in entries(Arrivals) + entries(Departures):
        scratch.append(DMA(shape))
    return pl.pallas_call(
        layer_kernel,
        out_shape=[jax.ShapeDtypeStruct(s, t) for s, t in results],
        in_specs=[vmem()] + [pl.BlockSpec(memory_space=pl.ANY)] * (len(args) - 1),
        out_specs=[pl.BlockSpec(memory_space=pl.ANY)] * len(results),
        scratch_shapes=scratch,
        compiler_params=pltpu.CompilerParams(
            collective_id=1, has_side_effects=True, vmem_limit_bytes=VMEM_LIMIT
        ),
    )(*args)


def run_finish(*args):
    shapes = (
        ((128, 1024), BF16),
        ((128, 1024), BF16),
        ((128, 256), F32),
        ((128, 256), F32),
        ((128, 256), F32),
        ((256, 128), F32),
        ((128, 1024), F32),
        ((128, 1024), F32),
        ((128,), F32),
    ) + (((32,), F32),) * 8
    return pl.pallas_call(
        finish_kernel,
        out_shape=[jax.ShapeDtypeStruct(s, t) for s, t in shapes],
        in_specs=[pl.BlockSpec(memory_space=pltpu.SMEM)] + [vmem()] * (len(args) - 1),
        out_specs=[vmem()] * len(shapes),
        compiler_params=pltpu.CompilerParams(vmem_limit_bytes=VMEM_LIMIT),
    )(*args)


DMA = pltpu.SemaphoreType.DMA


def fast_device(
    tokens,
    w_query,
    w_key,
    w_value,
    w_out,
    b_query,
    b_value,
    b_out,
    norm1_gain,
    norm1_shift,
    w_in,
    w_back,
    b_in,
    b_back,
    norm2_gain,
    norm2_shift,
    cotangent,
):
    head_id = lax.axis_index("head")
    token_shape = tokens.shape
    model_dim = tokens.shape[2]
    x = tokens.reshape(-1, model_dim)
    vectors = (
        b_query,
        b_value,
        b_out,
        norm1_gain,
        norm1_shift,
        b_back,
        norm2_gain,
        norm2_shift,
        b_in,
    )
    small = jnp.concatenate(vectors).astype(F32).reshape(1, -1)
    results = run_layer(
        small, x, cotangent.reshape(-1, model_dim), w_query, w_key, w_value, w_out, w_in, w_back
    )
    output, grad_tokens, gq, gk, gv, gout, gw_in, gw_back, gb_in, *own = run_finish(
        head_id.astype(jnp.int32).reshape(1), *results
    )
    return (
        output.reshape(token_shape),
        grad_tokens.reshape(token_shape),
        gq,
        gk,
        gv,
        gout,
        own[0],
        own[1],
        own[2],
        own[3],
        own[4],
        gw_in,
        gw_back,
        gb_in,
        own[5],
        own[6],
        own[7],
    )


def solution(mesh):
    in_specs = (
        P(None, ("blk", "head"), None),
        P("blk", "head"),
        P("blk", "head"),
        P("blk", "head"),
        P("head", "blk"),
        P(("blk", "head")),
        P(("blk", "head")),
        P(("blk", "head")),
        P(("blk", "head")),
        P(("blk", "head")),
        P("blk", "head"),
        P("blk", "head"),
        P(("blk", "head")),
        P(("blk", "head")),
        P(("blk", "head")),
        P(("blk", "head")),
        P(None, ("blk", "head"), None),
    )
    out_specs = (
        P(None, ("blk", "head"), None),
        P(None, ("blk", "head"), None),
        P("blk", "head"),
        P("blk", "head"),
        P("blk", "head"),
        P("head", "blk"),
        P(("blk", "head")),
        P(("blk", "head")),
        P(("blk", "head")),
        P(("blk", "head")),
        P(("blk", "head")),
        P("blk", "head"),
        P("blk", "head"),
        P(("blk", "head")),
        P(("blk", "head")),
        P(("blk", "head")),
        P(("blk", "head")),
    )
    sizes = (mesh.shape["blk"], mesh.shape["head"])
    body = fast_device if sizes == (8, 4) else per_device
    return jax.shard_map(
        body, mesh=mesh, in_specs=in_specs, out_specs=out_specs, check_vma=False
    )
```
